32 devices in a mesh: task: 4 (over x, core), dp: 8 (over z, y).
Axes of the slice: x: 2, y: 2, z: 4, core: 2. Of those that a mesh axis runs over, the one named last changes fastest.
Arguments:
- layer_input: float32 [4, 8, 1024, 384], P('task', 'dp'), may hold values from -6 to 6
- cotangent: float32 [4, 8, 1024, 384], P('task', 'dp'), may hold values from -6 to 6
- norm_gain: float32 [2, 384], replicated, may hold values from 0.1 to 1.9
- norm_bias: float32 [2, 384], replicated, may hold values from -2 to 2
- w_qkv: bfloat16 [384, 1152], P('dp'), may hold values from -0.5 to 0.5
- w_proj: bfloat16 [384, 384], P('dp'), may hold values from -0.3125 to 0.3125
- router: float32 [4, 384, 16], P('task'), may hold values from -0.15 to 0.15
- w_in: bfloat16 [16, 384, 1536], P('task', 'dp'), may hold values from -0.3125 to 0.3125
- w_out: bfloat16 [16, 1536, 384], P('task', 'dp'), may hold values from -1.25 to 1.25
- choices: int32 [4, 8, 1024, 4], P('task', 'dp'), may hold values from 0 to 15, all different within a row; in each aligned block of 1024 rows (0 to 1023, 1024 to 2047, ..., all dimensions but the last counted through in order) at most 320 rows name the same one
- top_count: int32 [4], P('task'), may hold values from 1 to 4, as said below
Outputs:
- activations: float32 [4, 8, 1024, 384], P('task', 'dp')
- input_grad: float32 [4, 8, 1024, 384], P('task', 'dp')
- grad_norm_gain: float32 [2, 384], replicated
- grad_norm_bias: float32 [2, 384], replicated
- grad_w_qkv: float32 [384, 1152], P('dp')
- grad_w_proj: float32 [384, 384], P('dp')
- grad_router: float32 [4, 384, 16], P('task')
- grad_w_in: float32 [16, 384, 1536], P('task', 'dp')
- grad_w_out: float32 [16, 1536, 384], P('task', 'dp')
The draws below stay inside these ranges and needn't reach their ends.
Inputs may be any that keep to these rules, and one draw needn't show every extreme that they name: `choices`: each token's row names 4 different experts and the token uses the first top_count of its task. Within the rows of one device no expert is named by more than 320 rows. `top_count`: the 4 tasks use different numbers of choices.
All inputs are finite; a program needn't handle non-finite values.
Results may differ from the reference program's by a relative error of at most 0.017.
The reference program's roundings to bfloat16 on the way count: a program that leaves them out, or rounds other values in their place, can miss the bound.
Values may be sent and summed in bfloat16 or wider, within the bound.
A program may use at most 192 MiB of HBM per device.

```python
import math
import jax
import jax.numpy as jnp
import numpy as np
from jax import lax

D = 384
HEADS = 6
HEAD_DIM = 64
FF = 1536
EXPERTS = 16
TOPMAX = 4
SEQ = 1024
IMG_DEV = 1
TASKS = 4
IMAGES = 8
CAP = 320
N_DP = 8


def draw_top_count(key, part):
    key = jax.random.fold_in(key, 7)
    return (jax.random.permutation(key, TASKS) % 4 + 1).astype(jnp.int32)


def level_of(own_key, extent, shards, smallest, largest):
    gain = 1.0
    for axis_at, shards_of in shards:
        steps = jax.random.uniform(jax.random.fold_in(jax.random.fold_in(own_key, 6), axis_at), (shards_of,), jnp.float32, smallest / len(shards), largest / len(shards))
        gain = gain * jnp.repeat(jnp.exp(steps), extent[axis_at] // shards_of).reshape((-1,) + (1,) * (len(extent) - 1 - axis_at))
    return gain


def assign_block(key, own, number, rows, amount, top, bound, slope):
    ranking = jax.random.permutation(key, amount)
    crowded, common = portions_of(amount, rows * top, bound, slope, True), portions_of(amount, rows * top, bound, slope, False)
    places = jnp.arange(amount)

    def named(lengths, rotation):
        used = int((lengths > 0).sum())
        fixed = max(1, used // 4)
        shifted = fixed + (places - fixed + rotation * (used - fixed)) % max(1, amount - fixed)
        return jnp.zeros((amount,), jnp.int32).at[ranking[jnp.where(places < fixed, places, shifted)]].set(jnp.asarray(lengths, jnp.int32))

    lengths = jnp.where(number % 4 == 0, named(crowded, number // 4), named(common, number - number // 4 - 1))
    mixed = jax.random.permutation(jax.random.fold_in(own, 3), amount)
    donor, receiver = mixed[0:amount // 2 * 2:2], mixed[1:amount // 2 * 2:2]
    slack = jnp.minimum(lengths[donor] - 1, bound - lengths[receiver]) // 2
    slack = jnp.where((donor == ranking[0]) | (receiver == ranking[0]) | (lengths[receiver] == 0), 0, jnp.maximum(slack, 0))
    shifted = jax.random.randint(jax.random.fold_in(own, 4), (amount // 2,), 0, 1 << 20) % (slack + 1)
    lengths = lengths.at[donor].add(-shifted).at[receiver].add(shifted)
    members = jnp.searchsorted(jnp.cumsum(lengths), jnp.arange(rows * top), side="right").astype(jnp.int32)
    grid = members.reshape(top, rows).T
    grid = grid[jax.random.permutation(jax.random.fold_in(own, 1), rows)]
    rotation = jax.random.randint(jax.random.fold_in(own, 2), (rows, 1), 0, top)
    return jnp.take_along_axis(grid, (jnp.arange(top)[None, :] + rotation) % top, axis=1)


def portions_of(number_of, total, bound, slope, full):
    loads = [(1 << 20) // math.isqrt(rank ** slope) + 1 for rank in range(1, number_of + 1)]
    largest = bound if full else min(bound, max(-(-total // number_of), total * loads[0] // sum(loads)))
    least = 1 if total - largest >= number_of - 1 else 0
    holding, rest = [largest] + [least] * (number_of - 1), total - largest - least * (number_of - 1)
    while rest > 0:
        movable = [i for i in range(1, number_of) if holding[i] < largest] or [i for i in range(1, number_of) if holding[i] < bound]
        whole, left = sum([loads[i] for i in movable]), rest
        for i in movable:
            more = min(bound - holding[i], max(1, left * loads[i] // whole), rest)
            holding[i] = holding[i] + more
            rest = rest - more
    return np.array(holding)


def noise(stream_key, extent, deviation, most, cuts=(), kind=jnp.bfloat16):
    drawn = deviation * jax.random.normal(stream_key, extent, jnp.float32)
    if cuts:
        drawn = drawn * level_of(stream_key, extent, cuts, -0.22, 0.18)
    return jnp.clip(drawn, -most, most).astype(kind)


def setup_inputs(seed: int = 0) -> dict:
    arg_keys = jax.random.split(jax.random.key(seed), 12)
    layer_input = noise(arg_keys[0], (TASKS, IMAGES, SEQ, D), 1.0, 6.0, ((0, 4), (1, 8)), jnp.float32)
    cotangent = noise(arg_keys[1], (TASKS, IMAGES, SEQ, D), 1.0, 6.0, ((0, 4), (1, 8)), jnp.float32)
    norm_gain = jnp.clip(1.0 + 0.18 * jax.random.normal(arg_keys[2], (2, D), jnp.float32), 0.1, 1.9)
    norm_bias = noise(arg_keys[3], (2, D), 0.3, 2.0, (), jnp.float32)
    w_qkv = noise(arg_keys[4], (D, 3 * D), (2 * D // 5) ** -0.5, 0.5, ((0, 8),))
    w_proj = noise(arg_keys[5], (D, D), D ** -0.5, 0.3125, ((0, 8),))
    router = noise(arg_keys[6], (TASKS, D, EXPERTS), 0.025, 0.15, ((0, 4),), jnp.float32)
    w_in = noise(arg_keys[7], (EXPERTS, D, FF), D ** -0.5, 0.3125, ((0, 4), (1, 8)))
    w_out = noise(arg_keys[8], (EXPERTS, FF, D), (FF // 64) ** -0.5, 1.25, ((0, 4), (1, 8)))
    choices_keys = jax.random.split(jax.random.fold_in(arg_keys[9], 1), TASKS * IMAGES * SEQ // (IMG_DEV * SEQ))
    choices_turns = jax.random.permutation(jax.random.fold_in(arg_keys[9], 3), TASKS * IMAGES * SEQ // (IMG_DEV * SEQ))
    choices = jax.vmap(lambda own, number: assign_block(jax.random.fold_in(arg_keys[9], 2), own, number, IMG_DEV * SEQ, EXPERTS, TOPMAX, CAP, 1))(choices_keys, choices_turns).reshape((TASKS, IMAGES, SEQ, TOPMAX))
    top_count = draw_top_count(jax.random.fold_in(arg_keys[11], 71), 0)
    return dict(layer_input=layer_input, cotangent=cotangent, norm_gain=norm_gain, norm_bias=norm_bias, w_qkv=w_qkv, w_proj=w_proj, router=router, w_in=w_in, w_out=w_out, choices=choices, top_count=top_count)


@jax.custom_vjp
def low(v):
    return lax.optimization_barrier(v.astype(jnp.bfloat16)).astype(jnp.float32)

@jax.custom_vjp
def low_back(v):
    return v

def low_keep(v):
    return (low(v), None)

def low_pass(kept, grad):
    return (grad,)

def back_keep(v):
    return (v, None)

def back_low(kept, grad):
    return (low(grad),)
low.defvjp(low_keep, low_pass)
low_back.defvjp(back_keep, back_low)
highest = lax.Precision.HIGHEST
epsilon = 1e-06

def layer_norm(inputs, norm_scale, norm_shift):
    mean_val = lax.optimization_barrier(jnp.mean(inputs, axis=-1, keepdims=True))
    centered = inputs - mean_val
    variance = lax.optimization_barrier(jnp.mean(centered * centered, axis=-1, keepdims=True))
    return centered * lax.rsqrt(variance + epsilon) * norm_scale + norm_shift

def softmax_rows(logit_rows):
    row_max = lax.optimization_barrier(jnp.max(logit_rows, axis=-1, keepdims=True))
    exp_rows = jnp.exp(logit_rows - row_max)
    return exp_rows / lax.optimization_barrier(jnp.sum(exp_rows, axis=-1, keepdims=True))

def attend_image(image_rows, gain_rows, bias_rows, weight_qkv, weight_proj):
    normed = layer_norm(image_rows, gain_rows[0], bias_rows[0])
    packed = jnp.dot(low(normed), weight_qkv, precision=highest)
    packed = low(low_back(packed))
    split_qkv = packed.reshape(SEQ, 3, HEADS, HEAD_DIM)
    score_scale = HEAD_DIM ** (-0.5)
    scores = jnp.einsum('qhd,khd->hqk', split_qkv[:, 0], split_qkv[:, 1], precision=highest) * score_scale
    scores = low_back(scores)
    prob_rows = softmax_rows(scores)
    mixed_rows = jnp.einsum('hqk,khd->qhd', low(prob_rows), split_qkv[:, 2], precision=highest).reshape(SEQ, D)
    mixed_rows = low(low_back(mixed_rows))
    branch = low_back(jnp.dot(mixed_rows, weight_proj, precision=highest))
    return image_rows + branch

def expert_apply(operands):
    rows_in, weight_in, weight_out = operands
    pre_act = low_back(jnp.dot(rows_in, weight_in, precision=highest))
    hidden_units = low(jax.nn.gelu(pre_act, approximate=False))
    return low(low_back(jnp.dot(hidden_units, weight_out, precision=highest)))

def scatter_rows(target_rows, value_rows):
    empty_rows = jnp.zeros((EXPERTS * CAP, D), value_rows.dtype)
    return empty_rows.at[target_rows].set(value_rows, mode='drop')

def pick_rows(table_rows, target_rows):
    return table_rows[target_rows]

def forward(inputs, gain_rows, bias_rows, weight_qkv, weight_proj, router_full, weight_in, weight_out, choices, top_count):
    row_dev = IMG_DEV * SEQ
    block_count = TASKS * N_DP
    images = inputs.reshape(TASKS * IMAGES, SEQ, D)

    def attend_one(image_rows):
        return attend_image(image_rows, gain_rows, bias_rows, weight_qkv, weight_proj)
    mid_rows = lax.map(jax.checkpoint(attend_one), images).reshape(TASKS, N_DP, row_dev, D)
    normed = layer_norm(mid_rows, gain_rows[1], bias_rows[1])
    logits = jnp.einsum('tnrd,tde->tnre', normed, router_full, precision=highest)
    route_probs = softmax_rows(logits)
    routes = choices.reshape(TASKS, N_DP, row_dev, TOPMAX)
    live_mask = jnp.arange(TOPMAX, dtype=jnp.int32)[None, None, None, :] < top_count[:, None, None, None]
    onehot = ((routes[..., None] == jnp.arange(EXPERTS, dtype=jnp.int32)) & live_mask[..., None]).astype(jnp.int32)
    gate_rows = lax.optimization_barrier(jnp.sum(route_probs[:, :, :, None, :] * onehot.astype(route_probs.dtype), axis=-1))
    flat_hot = onehot.reshape(TASKS, N_DP, row_dev * TOPMAX, EXPERTS)
    before = (jnp.cumsum(flat_hot, axis=2).astype(jnp.int32) - flat_hot).astype(jnp.int32)
    slot_rows = lax.optimization_barrier(jnp.sum(before * flat_hot, axis=-1)).astype(jnp.int32)
    live_flat = jnp.broadcast_to(live_mask, (TASKS, N_DP, row_dev, TOPMAX)).reshape(TASKS, N_DP, row_dev * TOPMAX)
    target = jnp.where(live_flat, routes.reshape(TASKS, N_DP, row_dev * TOPMAX) * CAP + slot_rows, EXPERTS * CAP).astype(jnp.int32).reshape(block_count, row_dev * TOPMAX)
    spread = jnp.broadcast_to(normed[:, :, :, None, :], (TASKS, N_DP, row_dev, TOPMAX, D))
    spread = spread.reshape(block_count, row_dev * TOPMAX, D)
    buffer = jax.vmap(scatter_rows)(target, spread)
    buffer = low(low_back(buffer))
    per_expert = buffer.reshape(block_count, EXPERTS, CAP, D).transpose(1, 0, 2, 3).reshape(EXPERTS, block_count * CAP, D)
    outputs = lax.map(jax.checkpoint(expert_apply), (per_expert, weight_in, weight_out))
    returned = outputs.reshape(EXPERTS, block_count, CAP, D).transpose(1, 0, 2, 3).reshape(block_count, EXPERTS * CAP, D)
    padded = jnp.concatenate([returned, jnp.zeros((block_count, 1, D), returned.dtype)], axis=1)
    picked = jax.vmap(pick_rows)(padded, target).reshape(TASKS, N_DP, row_dev, TOPMAX, D)
    mix_rows = lax.optimization_barrier(jnp.sum(gate_rows[..., None] * picked, axis=3))
    return (mid_rows + mix_rows).reshape(TASKS, IMAGES, SEQ, D)

def reference(layer_input, cotangent, norm_gain, norm_bias, w_qkv, w_proj, router, w_in, w_out, choices, top_count):

    def run_layer(inputs, gain_rows, bias_rows, weight_qkv, weight_proj, router_full, weight_in, weight_out):
        return forward(inputs, gain_rows, bias_rows, weight_qkv, weight_proj, router_full, weight_in, weight_out, choices, top_count)
    activations, pullback = jax.vjp(run_layer, layer_input, norm_gain, norm_bias, w_qkv.astype(jnp.float32), w_proj.astype(jnp.float32), router, w_in.astype(jnp.float32), w_out.astype(jnp.float32))
    gradients = pullback(cotangent)
    return (activations, gradients[0], gradients[1], gradients[2], gradients[3], gradients[4], gradients[5], gradients[6], gradients[7])
```

```python
import functools

import jax
import jax.numpy as jnp
from jax import lax
from jax.experimental import pallas as pl
from jax.experimental.pallas import tpu as pltpu
from jax.sharding import PartitionSpec as P

D = 384
FF = 1536
HEADS = 6
HEAD_DIM = 64
PAIR = 2 * HEAD_DIM
TOPMAX = 4
SEQ = 1024
CAP = 320

f32 = jnp.float32
bf16 = jnp.bfloat16
HIGHEST = lax.Precision.HIGHEST
EPSILON = 1e-06
ROOT_HALF = 0.7071067811865476
NORMAL = 0.3989422804014327

FF_TILE = 512
ROW_TILE = 640
QUERY_FWD = 512
QUERY_BWD = 256
ROWS = 256

VMEM = pl.BlockSpec(memory_space=pltpu.VMEM)
SMEM = pl.BlockSpec(memory_space=pltpu.SMEM)


def shape(*dims, dtype=f32):
    return jax.ShapeDtypeStruct(dims, dtype)


def params(**more):
    return pltpu.CompilerParams(vmem_limit_bytes=60 * 2**20, **more)


def dot(a, b):
    return lax.dot_general(a, b, (((1,), (0,)), ((), ())), preferred_element_type=f32)


def dot_rt(a, b):
    return lax.dot_general(a, b, (((1,), (1,)), ((), ())), preferred_element_type=f32)


def dot_lt(a, b):
    return lax.dot_general(a, b, (((0,), (0,)), ((), ())), preferred_element_type=f32)


def rows_at(index, size):
    return pl.ds(pl.multiple_of(index * size, size), size)


def normalize(rows):
    centered = rows - jnp.mean(rows, axis=1, keepdims=True)
    scale = lax.rsqrt(jnp.mean(centered * centered, axis=1, keepdims=True) + EPSILON)
    return centered * scale, scale


def norm_back(rows, grad_rows, gain):
    unit, scale = normalize(rows)
    scaled = grad_rows * gain
    grad_in = scale * (
        scaled
        - jnp.mean(scaled, axis=1, keepdims=True)
        - unit * jnp.mean(scaled * unit, axis=1, keepdims=True)
    )
    grad_gain = jnp.sum(grad_rows * unit, axis=0, keepdims=True)
    return grad_in, grad_gain, jnp.sum(grad_rows, axis=0, keepdims=True), unit


def half_lanes(rows, half):
    lanes = lax.broadcasted_iota(jnp.int32, (rows, PAIR), 1)
    return (lanes < HEAD_DIM) if half == 0 else (lanes >= HEAD_DIM)


def attend(packed, mixed, totals):
    zero = jnp.array(0, bf16)

    def head_pair(pair, _):
        queries, keys, values = (rows_at(pair + part * (D // PAIR), PAIR) for part in range(3))
        key_rows, value_rows = packed[:, keys], packed[:, values]

        def block(index, _):
            rows = rows_at(index, QUERY_FWD)
            query_rows = packed[rows, queries] * jnp.array(HEAD_DIM**-0.5, bf16)
            outs, logs = [], []
            for half in range(2):
                own = jnp.where(half_lanes(QUERY_FWD, half), query_rows, zero)
                scores = dot_rt(own, key_rows)
                top = jnp.max(scores, axis=1, keepdims=True)
                weights = jnp.exp(scores - top)
                total = jnp.sum(weights, axis=1, keepdims=True)
                outs.append(dot(weights.astype(bf16), value_rows) * (1.0 / total))
                logs.append(top + jnp.log(total))
            mixed[rows, queries] = jnp.where(half_lanes(QUERY_FWD, 0), outs[0], outs[1]).astype(
                bf16
            )
            lanes = lax.broadcasted_iota(jnp.int32, (QUERY_FWD, 8), 1)
            totals[rows, :] = jnp.where(
                lanes == 2 * pair,
                logs[0],
                jnp.where(lanes == 2 * pair + 1, logs[1], totals[rows, :]),
            )
            return 0

        return lax.fori_loop(0, SEQ // QUERY_FWD, block, 0)

    lax.fori_loop(0, HEADS // 2, head_pair, 0)


def forward_kernel(
    top_count,
    image,
    gain,
    bias,
    w_qkv,
    w_proj,
    router,
    choices,
    mid,
    packed,
    mixed,
    logs,
    normed,
    slots,
    gates,
    probs,
    normed_first,
    totals,
):
    experts = router.shape[0]

    def first_norm(index, _):
        rows = rows_at(index, ROWS)
        unit, _ = normalize(image[rows, :])
        normed_first[rows, :] = (unit * gain[0:1, :] + bias[0:1, :]).astype(bf16)
        return 0

    lax.fori_loop(0, SEQ // ROWS, first_norm, 0)
    named = choices[...].T
    numbers = lax.broadcasted_iota(jnp.int32, (experts, SEQ), 0)
    used = jnp.zeros((experts, SEQ), f32)
    for choice in range(TOPMAX):
        hit = (named[choice : choice + 1, :] == numbers) & (choice < top_count[0])
        used = used + jnp.where(hit, 1.0, 0.0)
    earlier = lax.broadcasted_iota(jnp.int32, (SEQ, SEQ), 0) < lax.broadcasted_iota(
        jnp.int32, (SEQ, SEQ), 1
    )
    before = dot(used.astype(bf16), jnp.where(earlier, 1.0, 0.0).astype(bf16))
    slots[...] = jnp.where(used > 0, before, -1.0).astype(jnp.int32)
    packed[...] = dot(normed_first[...], w_qkv[...]).astype(bf16)
    totals[...] = jnp.zeros_like(totals)
    attend(packed, mixed, totals)
    logs[...] = totals[...].T

    def second_norm(index, _):
        rows = rows_at(index, ROWS)
        mid_rows = image[rows, :] + dot(mixed[rows, :], w_proj[...])
        mid[rows, :] = mid_rows
        unit, _ = normalize(mid_rows)
        normed_rows = unit * gain[1:2, :] + bias[1:2, :]
        normed[rows, :] = normed_rows.astype(bf16)
        logits = lax.dot_general(
            router[...],
            normed_rows,
            (((1,), (1,)), ((), ())),
            precision=HIGHEST,
            preferred_element_type=f32,
        )
        powers = jnp.exp(logits - jnp.max(logits, axis=0, keepdims=True))
        probs[:, rows] = powers / jnp.sum(powers, axis=0, keepdims=True)
        return 0

    lax.fori_loop(0, SEQ // ROWS, second_norm, 0)
    gates[...] = jnp.where(slots[...] >= 0, probs[...], 0.0)


def forward_part(top_count, image, gain, bias, w_qkv, w_proj, router, choices):
    experts = router.shape[0]
    return pl.pallas_call(
        forward_kernel,
        out_shape=(
            shape(SEQ, D),
            shape(SEQ, 3 * D, dtype=bf16),
            shape(SEQ, D, dtype=bf16),
            shape(8, SEQ),
            shape(SEQ, D, dtype=bf16),
            shape(experts, SEQ, dtype=jnp.int32),
            shape(experts, SEQ),
            shape(experts, SEQ),
        ),
        in_specs=[SMEM] + [VMEM] * 7,
        out_specs=[VMEM] * 8,
        scratch_shapes=[pltpu.VMEM((SEQ, D), bf16), pltpu.VMEM((SEQ, 8), f32)],
        compiler_params=params(),
    )(top_count, image, gain, bias, w_qkv, w_proj, router, choices)


def slot_hits(slots, source, expert):
    return lax.broadcasted_iota(jnp.int32, (CAP, SEQ), 0) == slots[source, pl.ds(expert, 1), :]


def ones_at(hits):
    return jnp.where(hits, 1.0, 0.0).astype(bf16)


def expert_kernel(
    normed,
    cotangent,
    slots,
    gates,
    w_in,
    w_out,
    grad_in,
    grad_out,
    mixes,
    grad_normed,
    grad_gates,
    rows_in,
    rows_grad,
    rows_cot,
    rows_gate,
    hidden,
    grad_pre,
    sent,
    columns,
):
    groups, local_count = normed.shape[0], w_in.shape[0]
    width = groups * CAP

    def one_expert(expert, _):
        for source in range(groups):
            own = slice(source * CAP, (source + 1) * CAP)
            hits = slot_hits(slots, source, expert)
            picks = ones_at(hits)
            rows_in[own, :] = dot(picks, normed[source]).astype(bf16)
            cot_rows = dot(picks, cotangent[source])
            gate = jnp.sum(
                jnp.where(hits, gates[source, pl.ds(expert, 1), :], 0.0), axis=1, keepdims=True
            )
            rows_cot[own, :] = cot_rows.astype(bf16)
            rows_grad[own, :] = (gate * cot_rows).astype(bf16)
            rows_gate[own, :] = jnp.broadcast_to(gate, (CAP, 128))

        def tile(index, _):
            units = rows_at(index // (width // ROW_TILE), FF_TILE)
            rows = rows_at(lax.rem(index, width // ROW_TILE), ROW_TILE)
            pre = dot(rows_in[rows, :], w_in[expert, :, units])
            grad_hidden = dot_rt(rows_grad[rows, :], w_out[expert, units, :])
            share = 0.5 * lax.erf(pre * ROOT_HALF) + 0.5
            slope = share + pre * (NORMAL * jnp.exp(-0.5 * pre * pre))
            hidden[rows, units] = (pre * share).astype(bf16)
            grad_pre[rows, units] = (grad_hidden * slope).astype(bf16)
            return 0

        lax.fori_loop(0, (FF // FF_TILE) * (width // ROW_TILE), tile, 0)
        for source in range(groups):
            own = slice(source * CAP, (source + 1) * CAP)
            kept = rows_at(expert, CAP)
            out_rows = dot(hidden[own, :], w_out[expert]).astype(bf16).astype(f32)
            sent[source, kept, :D] = (rows_gate[own, 0:1] * out_rows).astype(bf16)
            sent[source, kept, D:] = dot_rt(grad_pre[own, :], w_in[expert]).astype(bf16)
            grad_gate = jnp.sum(rows_cot[own, :].astype(f32) * out_rows, axis=1, keepdims=True)
            hits = slot_hits(slots, source, expert)
            grad_gates[source, pl.ds(expert, 1), :] = jnp.sum(
                jnp.where(hits, grad_gate, 0.0), axis=0, keepdims=True
            )
        grad_in[expert] = dot_lt(rows_in[...], grad_pre[...]).astype(bf16)
        grad_out[expert] = dot_lt(rows_grad[...], hidden[...]).astype(bf16).T
        return 0

    lax.fori_loop(0, local_count, one_expert, 0)
    for source in range(groups):
        columns[...] = slots[source].T

        def combine(index, _):
            rows = rows_at(index, 512)
            lanes = lax.broadcasted_iota(jnp.int32, (512, CAP), 1)
            picks = jnp.concatenate(
                [ones_at(lanes == columns[rows, e : e + 1]) for e in range(local_count)], axis=1
            )
            back = dot(picks, sent[source])
            mixes[source, rows, :] = back[:, :D].astype(bf16)
            grad_normed[source, rows, :] = back[:, D:].astype(bf16)
            return 0

        lax.fori_loop(0, SEQ // 512, combine, 0)


def expert_part(normed, cotangent, slots, gates, w_in, w_out):
    groups, local_count = normed.shape[0], w_in.shape[0]
    width = groups * CAP
    return pl.pallas_call(
        expert_kernel,
        out_shape=(
            shape(local_count, D, FF, dtype=bf16),
            shape(local_count, FF, D, dtype=bf16),
            shape(groups, SEQ, D, dtype=bf16),
            shape(groups, SEQ, D, dtype=bf16),
            shape(groups, local_count, SEQ),
        ),
        in_specs=[VMEM] * 6,
        out_specs=[VMEM] * 5,
        scratch_shapes=[
            pltpu.VMEM((width, D), bf16),
            pltpu.VMEM((width, D), bf16),
            pltpu.VMEM((width, D), bf16),
            pltpu.VMEM((width, 128), f32),
            pltpu.VMEM((width, FF), bf16),
            pltpu.VMEM((width, FF), bf16),
            pltpu.VMEM((groups, local_count * CAP, 2 * D), bf16),
            pltpu.VMEM((SEQ, local_count), jnp.int32),
        ],
        compiler_params=params(),
    )(normed, cotangent, slots, gates, w_in, w_out)


def attend_back(packed, grad_mixed, logs, grad_packed, grad_keys, grad_values):
    zero = jnp.array(0, bf16)

    def head_pair(pair, _):
        queries, keys, values = (rows_at(pair + part * (D // PAIR), PAIR) for part in range(3))
        key_rows, value_rows = packed[:, keys], packed[:, values]

        def block(index, _):
            rows = rows_at(index, QUERY_BWD)
            query_rows = packed[rows, queries] * jnp.array(HEAD_DIM**-0.5, bf16)
            grad_rows = grad_mixed[rows, queries]
            grad_query, part_keys, part_values = [], 0.0, 0.0
            for half in range(2):
                lanes = half_lanes(QUERY_BWD, half)
                own = jnp.where(lanes, query_rows, zero)
                own_grad = jnp.where(lanes, grad_rows, zero)
                probs = jnp.exp(dot_rt(key_rows, own) - logs[pl.ds(2 * pair + half, 1), rows])
                grad_probs = dot_rt(value_rows, own_grad)
                mean = jnp.sum(probs * grad_probs, axis=0, keepdims=True)
                grad_scores = (probs * (grad_probs - mean)).astype(bf16)
                part_values += dot(probs.astype(bf16), own_grad)
                part_keys += dot(grad_scores, own)
                grad_query.append(dot_lt(grad_scores, key_rows))
            grad_packed[rows, queries] = (
                jnp.where(half_lanes(QUERY_BWD, 0), grad_query[0], grad_query[1])
                * HEAD_DIM**-0.5
            ).astype(bf16)
            grad_keys[...] = jnp.where(index == 0, part_keys, grad_keys[...] + part_keys)
            grad_values[...] = jnp.where(index == 0, part_values, grad_values[...] + part_values)
            return 0

        lax.fori_loop(0, SEQ // QUERY_BWD, block, 0)
        grad_packed[:, keys] = grad_keys[...].astype(bf16)
        grad_packed[:, values] = grad_values[...].astype(bf16)
        return 0

    lax.fori_loop(0, HEADS // 2, head_pair, 0)


def backward_kernel(
    image,
    cotangent,
    gain,
    bias,
    mid,
    w_qkv,
    w_proj,
    router,
    packed,
    mixed,
    logs,
    mixes,
    grad_normed,
    grad_gates,
    probs,
    activations,
    grad_image,
    grad_norm,
    grad_router,
    grad_shared,
    grad_mid,
    grad_low,
    grad_mixed,
    grad_packed,
    grad_keys,
    grad_values,
    normed_first,
):
    groups = mixes.shape[0]
    route = grad_gates[...]
    grad_logits = probs[...] * (route - jnp.sum(probs[...] * route, axis=0, keepdims=True))
    grad_norm[...] = jnp.zeros_like(grad_norm)
    grad_router[...] = jnp.zeros_like(grad_router)
    for index in range(SEQ // ROWS):
        rows = slice(index * ROWS, (index + 1) * ROWS)
        mid_rows = mid[rows, :]
        mix_rows, grad_rows = mixes[0, rows, :].astype(f32), grad_normed[0, rows, :].astype(f32)
        for source in range(1, groups):
            mix_rows += mixes[source, rows, :].astype(f32)
            grad_rows += grad_normed[source, rows, :].astype(f32)
        activations[rows, :] = mid_rows + mix_rows
        own_logits = grad_logits[:, rows]
        grad_rows += lax.dot_general(
            own_logits,
            router[...],
            (((0,), (0,)), ((), ())),
            precision=HIGHEST,
            preferred_element_type=f32,
        )
        grad_in, grad_gain, grad_bias, unit = norm_back(mid_rows, grad_rows, gain[1:2, :])
        grad_router[...] += jnp.dot(
            own_logits,
            unit * gain[1:2, :] + bias[1:2, :],
            precision=HIGHEST,
            preferred_element_type=f32,
        )
        grad_norm[1:2, :] += grad_gain
        grad_norm[3:4, :] += grad_bias
        grad_mid_rows = cotangent[rows, :] + grad_in
        grad_mid[rows, :] = grad_mid_rows
        low_rows = grad_mid_rows.astype(bf16)
        grad_low[rows, :] = low_rows
        grad_mixed[rows, :] = dot_rt(low_rows, w_proj[...]).astype(bf16)
    grad_shared[:, 3 * D :] = dot_lt(mixed[...], grad_low[...]).astype(bf16)
    attend_back(packed, grad_mixed, logs, grad_packed, grad_keys, grad_values)

    def first_norm(index, _):
        rows = rows_at(index, ROWS)
        grad_rows = dot_rt(grad_packed[rows, :], w_qkv[...])
        grad_in, grad_gain, grad_bias, unit = norm_back(image[rows, :], grad_rows, gain[0:1, :])
        normed_first[rows, :] = (unit * gain[0:1, :] + bias[0:1, :]).astype(bf16)
        grad_image[rows, :] = grad_mid[rows, :] + grad_in
        grad_norm[0:1, :] += grad_gain
        grad_norm[2:3, :] += grad_bias
        return 0

    lax.fori_loop(0, SEQ // ROWS, first_norm, 0)
    grad_shared[:, : 3 * D] = dot_lt(normed_first[...], grad_packed[...]).astype(bf16)


def backward_part(*operands):
    router = operands[7]
    return pl.pallas_call(
        backward_kernel,
        out_shape=(
            shape(SEQ, D),
            shape(SEQ, D),
            shape(4, D),
            shape(router.shape[0], D),
            shape(D, 4 * D, dtype=bf16),
        ),
        in_specs=[VMEM] * 15,
        out_specs=[VMEM] * 5,
        scratch_shapes=[
            pltpu.VMEM((SEQ, D), f32),
            pltpu.VMEM((SEQ, D), bf16),
            pltpu.VMEM((SEQ, D), bf16),
            pltpu.VMEM((SEQ, 3 * D), bf16),
            pltpu.VMEM((SEQ, PAIR), f32),
            pltpu.VMEM((SEQ, PAIR), f32),
            pltpu.VMEM((SEQ, D), bf16),
        ],
        compiler_params=params(),
    )(*operands)


def local(
    layer_input,
    cotangent,
    norm_gain,
    norm_bias,
    w_qkv,
    w_proj,
    router,
    w_in,
    w_out,
    choices,
    top_count,
):
    groups = lax.axis_size("task")
    local_count = w_in.shape[0]
    full_qkv, full_proj, full_in, full_out = (
        lax.all_gather(w_qkv, "dp", axis=0, tiled=True),
        lax.all_gather(w_proj, "dp", axis=0, tiled=True),
        lax.all_gather(w_in, "dp", axis=1, tiled=True),
        lax.all_gather(w_out, "dp", axis=1, tiled=True),
    )
    image = layer_input.reshape(SEQ, D)
    grad_rows = cotangent.reshape(SEQ, D)
    router_rows = router[0].T
    experts = router_rows.shape[0]
    mid, packed, mixed, logs, normed, slots, gates, probs = forward_part(
        top_count,
        image,
        norm_gain,
        norm_bias,
        full_qkv,
        full_proj,
        router_rows,
        choices.reshape(SEQ, TOPMAX),
    )

    def swap(array):
        return lax.all_to_all(array, "task", split_axis=0, concat_axis=0, tiled=True)

    grad_in, grad_out, mixes, grad_normed, grad_gates = expert_part(
        lax.all_gather(normed, "task"),
        lax.all_gather(grad_rows.astype(bf16), "task"),
        swap(slots.reshape(groups, local_count, SEQ)),
        swap(gates.reshape(groups, local_count, SEQ)),
        full_in,
        full_out,
    )
    activations, grad_image, grad_norm, grad_router, grad_shared = backward_part(
        image,
        grad_rows,
        norm_gain,
        norm_bias,
        mid,
        full_qkv,
        full_proj,
        router_rows,
        packed,
        mixed,
        logs,
        swap(mixes),
        swap(grad_normed),
        swap(grad_gates).reshape(experts, SEQ),
        probs,
    )
    grad_in = lax.psum_scatter(grad_in, "dp", scatter_dimension=1, tiled=True)
    grad_out = lax.psum_scatter(grad_out, "dp", scatter_dimension=1, tiled=True)
    grad_shared = lax.psum_scatter(grad_shared, "dp", scatter_dimension=0, tiled=True)
    grad_shared = lax.psum(grad_shared, "task").astype(f32)
    grad_router = lax.psum(grad_router, "dp")
    grad_norm = lax.psum(grad_norm, ("task", "dp"))
    return (
        activations.reshape(layer_input.shape),
        grad_image.reshape(layer_input.shape),
        grad_norm[:2],
        grad_norm[2:],
        grad_shared[:, : 3 * D],
        grad_shared[:, 3 * D :],
        grad_router.T[None],
        grad_in.astype(f32),
        grad_out.astype(f32),
    )


def solution(mesh):
    tokens = P("task", "dp", None, None)
    rows = P("dp", None)
    blocks = P("task", "dp", None)
    routed = P("task", None, None)
    return jax.shard_map(
        local,
        mesh=mesh,
        in_specs=(tokens, tokens, P(), P(), rows, rows, routed, blocks, blocks, tokens, P("task")),
        out_specs=(tokens, tokens, P(), P(), rows, rows, routed, blocks, blocks),
        check_vma=False,
    )
```

```python
import functools

import jax
import jax.numpy as jnp
from jax import lax
from jax.experimental import pallas as pl
from jax.experimental.pallas import tpu as pltpu
from jax.sharding import PartitionSpec as P

D = 384
FF = 1536
HEADS = 6
HEAD_DIM = 64
PAIR = 2 * HEAD_DIM
TOPMAX = 4
SEQ = 1024
CAP = 320

f32 = jnp.float32
bf16 = jnp.bfloat16
HIGHEST = lax.Precision.HIGHEST
EPSILON = 1e-06
ROOT_HALF = 0.7071067811865476
NORMAL = 0.3989422804014327

FF_TILE = 512
ROW_TILE = 640
QUERY_FWD = 256
QUERY_BWD = 256
ROWS = 256

VMEM = pl.BlockSpec(memory_space=pltpu.VMEM)
SMEM = pl.BlockSpec(memory_space=pltpu.SMEM)
ANY = pl.BlockSpec(memory_space=pl.ANY)


def shape(*dims, dtype=f32):
    return jax.ShapeDtypeStruct(dims, dtype)


def params(**more):
    return pltpu.CompilerParams(vmem_limit_bytes=60 * 2**20, **more)


def dot(a, b):
    return lax.dot_general(a, b, (((1,), (0,)), ((), ())), preferred_element_type=f32)


def dot_rt(a, b):
    return lax.dot_general(a, b, (((1,), (1,)), ((), ())), preferred_element_type=f32)


def dot_lt(a, b):
    return lax.dot_general(a, b, (((0,), (0,)), ((), ())), preferred_element_type=f32)


def rows_at(index, size):
    return pl.ds(pl.multiple_of(index * size, size), size)


def normalize(rows):
    centered = rows - jnp.mean(rows, axis=1, keepdims=True)
    scale = lax.rsqrt(jnp.mean(centered * centered, axis=1, keepdims=True) + EPSILON)
    return centered * scale, scale


def norm_back(rows, grad_rows, gain):
    unit, scale = normalize(rows)
    scaled = grad_rows * gain
    grad_in = scale * (
        scaled
        - jnp.mean(scaled, axis=1, keepdims=True)
        - unit * jnp.mean(scaled * unit, axis=1, keepdims=True)
    )
    grad_gain = jnp.sum(grad_rows * unit, axis=0, keepdims=True)
    return grad_in, grad_gain, jnp.sum(grad_rows, axis=0, keepdims=True), unit


def half_lanes(rows, half):
    lanes = lax.broadcasted_iota(jnp.int32, (rows, PAIR), 1)
    return (lanes < HEAD_DIM) if half == 0 else (lanes >= HEAD_DIM)


def remote(source, target, sent, landed, **device):
    return pltpu.make_async_remote_copy(
        src_ref=source,
        dst_ref=target,
        send_sem=sent,
        recv_sem=landed,
        device_id=device,
        device_id_type=pl.DeviceIdType.MESH,
    )


class Place:
    def __init__(self, outers):
        self.dp = lax.axis_index("dp")
        self.task = lax.axis_index("task")
        self.outers = outers
        self.outer, self.inner = self.dp // 2, self.dp % 2
        self.has_up, self.has_down = self.outer + 1 < outers, self.outer > 0
        self.up, self.down = self.dp + 2, self.dp - 2
        self.side = self.dp + 1 - 2 * self.inner
        self.core = self.task + 1 - 2 * (self.task % 2)
        self.across = self.task + 2 - 4 * (self.task // 2)

    def greet(self):
        barrier = pltpu.get_barrier_semaphore()

        def signal(**device):
            pl.semaphore_signal(
                barrier, inc=1, device_id=device, device_id_type=pl.DeviceIdType.MESH
            )

        pl.when(self.has_up)(lambda: signal(dp=self.up))
        pl.when(self.has_down)(lambda: signal(dp=self.down))
        signal(dp=self.side)
        signal(task=self.core)
        signal(task=self.across)
        pl.semaphore_wait(
            barrier, 3 + self.has_up.astype(jnp.int32) + self.has_down.astype(jnp.int32)
        )


class Gather:
    def __init__(self, place, shards, sent, landed, stay):
        self.place, self.shards = place, shards
        self.sent, self.landed, self.stay = sent, landed, stay

    def move(self, unit, source, way, device, first=False):
        own, full = self.shards[unit]
        return remote(
            own if first else full(source),
            full(source),
            self.sent.at[unit, source, way],
            self.landed.at[unit, source],
            dp=device,
        )

    def local(self, unit):
        own, full = self.shards[unit]
        return pltpu.make_async_copy(own, full(self.place.dp), self.stay.at[unit])

    def start(self, unit):
        place = self.place
        pl.when(place.has_up)(lambda: self.move(unit, place.dp, 0, place.up, True).start())
        pl.when(place.has_down)(lambda: self.move(unit, place.dp, 1, place.down, True).start())
        self.move(unit, place.dp, 2, place.side, True).start()
        self.local(unit).start()

    def step(self, unit, hop):
        place = self.place

        @pl.when(place.outer >= hop)
        def _():
            source = place.dp - 2 * hop
            self.move(unit, source, 0, place.dp).wait_recv()
            pl.when(place.has_up)(lambda: self.move(unit, source, 0, place.up).start())
            self.move(unit, source, 2, place.side).start()

        @pl.when(place.outer + hop < place.outers)
        def _():
            source = place.dp + 2 * hop
            self.move(unit, source, 1, place.dp).wait_recv()
            pl.when(place.has_down)(lambda: self.move(unit, source, 1, place.down).start())
            self.move(unit, source, 2, place.side).start()

    def finish(self, unit):
        place = self.place
        self.local(unit).wait()
        for outer in range(place.outers):
            own, other = 2 * outer + place.inner, 2 * outer + 1 - place.inner
            self.move(unit, other, 2, place.dp).wait_recv()
            self.move(unit, own, 2, place.side).wait_send()
            pl.when((outer <= place.outer) & place.has_up)(
                lambda own=own: self.move(unit, own, 0, place.up).wait_send()
            )
            pl.when((outer >= place.outer) & place.has_down)(
                lambda own=own: self.move(unit, own, 1, place.down).wait_send()
            )


class Share:
    def __init__(self, place, view, sent, landed):
        self.place, self.view, self.sent, self.landed = place, view, sent, landed

    def move(self, source, way, **device):
        return remote(
            self.view(source),
            self.view(source),
            self.sent.at[way],
            self.landed.at[way],
            **device,
        )

    def start(self):
        place = self.place
        self.move(place.task, 0, task=place.across).start()
        self.move(place.task, 1, task=place.core).start()

    def relay(self):
        place = self.place
        self.move(place.across, 0, task=place.across).wait_recv()
        self.move(place.across, 2, task=place.core).start()

    def finish(self):
        place = self.place
        self.move(place.task, 0, task=place.across).wait_send()
        self.move(place.core, 1, task=place.core).wait()
        self.move(place.across, 2, task=place.core).wait()


def attend(packed, mixed, totals, index):
    zero = jnp.array(0, bf16)
    rows = rows_at(index, QUERY_FWD)

    def head_pair(pair, _):
        queries, keys, values = (rows_at(pair + part * (D // PAIR), PAIR) for part in range(3))
        key_rows, value_rows = packed[:, keys], packed[:, values]
        query_rows = packed[rows, queries] * jnp.array(HEAD_DIM**-0.5, bf16)
        outs, logs = [], []
        for half in range(2):
            own = jnp.where(half_lanes(QUERY_FWD, half), query_rows, zero)
            scores = dot_rt(own, key_rows)
            top = jnp.max(scores, axis=1, keepdims=True)
            weights = jnp.exp(scores - top)
            total = jnp.sum(weights, axis=1, keepdims=True)
            outs.append(dot(weights.astype(bf16), value_rows) * (1.0 / total))
            logs.append(top + jnp.log(total))
        mixed[rows, queries] = jnp.where(half_lanes(QUERY_FWD, 0), outs[0], outs[1]).astype(bf16)
        lanes = lax.broadcasted_iota(jnp.int32, (QUERY_FWD, 8), 1)
        totals[rows, :] = jnp.where(
            lanes == 2 * pair,
            logs[0],
            jnp.where(lanes == 2 * pair + 1, logs[1], totals[rows, :]),
        )
        return 0

    lax.fori_loop(0, HEADS // 2, head_pair, 0)


def first_norm(image, gain, bias, normed_first):
    def block(index, _):
        rows = rows_at(index, ROWS)
        unit, _ = normalize(image[rows, :])
        normed_first[rows, :] = (unit * gain[0:1, :] + bias[0:1, :]).astype(bf16)
        return 0

    lax.fori_loop(0, SEQ // ROWS, block, 0)


def number_slots(choices, top_count, experts):
    named = choices[...].T
    numbers = lax.broadcasted_iota(jnp.int32, (experts, SEQ), 0)
    used = jnp.zeros((experts, SEQ), f32)
    for choice in range(TOPMAX):
        hit = (named[choice : choice + 1, :] == numbers) & (choice < top_count[0])
        used = used + jnp.where(hit, 1.0, 0.0)
    earlier = lax.broadcasted_iota(jnp.int32, (SEQ, SEQ), 0) < lax.broadcasted_iota(
        jnp.int32, (SEQ, SEQ), 1
    )
    before = dot(used.astype(bf16), jnp.where(earlier, 1.0, 0.0).astype(bf16))
    return jnp.where(used > 0, before, -1.0).astype(jnp.int32)


def mid_block(index, image, gain, bias, w_proj, router, mixed, mid, probs):
    rows = rows_at(index, QUERY_FWD)
    mid_rows = image[rows, :] + dot(mixed[rows, :], w_proj[...])
    mid[rows, :] = mid_rows
    unit, _ = normalize(mid_rows)
    normed_rows = unit * gain[1:2, :] + bias[1:2, :]
    logits = lax.dot_general(
        router[...],
        normed_rows,
        (((1,), (1,)), ((), ())),
        precision=HIGHEST,
        preferred_element_type=f32,
    )
    powers = jnp.exp(logits - jnp.max(logits, axis=0, keepdims=True))
    probs[:, rows] = powers / jnp.sum(powers, axis=0, keepdims=True)
    return normed_rows.astype(bf16)


def forward_kernel(
    top_count,
    image,
    gain,
    bias,
    w_qkv,
    w_proj,
    router,
    choices,
    mid,
    packed,
    mixed,
    logs,
    normed,
    slots,
    gates,
    probs,
    normed_first,
    totals,
):
    first_norm(image, gain, bias, normed_first)
    slots[...] = number_slots(choices, top_count, router.shape[0])
    packed[...] = dot(normed_first[...], w_qkv[...]).astype(bf16)
    totals[...] = jnp.zeros_like(totals)

    def block(index, _):
        attend(packed, mixed, totals, index)
        normed[rows_at(index, QUERY_FWD), :] = mid_block(
            index, image, gain, bias, w_proj, router, mixed, mid, probs
        )
        return 0

    lax.fori_loop(0, SEQ // QUERY_FWD, block, 0)
    logs[...] = totals[...].T
    gates[...] = jnp.where(slots[...] >= 0, probs[...], 0.0)


def forward_part(top_count, image, gain, bias, w_qkv, w_proj, router, choices):
    experts = router.shape[0]
    return pl.pallas_call(
        forward_kernel,
        out_shape=(
            shape(SEQ, D),
            shape(SEQ, 3 * D, dtype=bf16),
            shape(SEQ, D, dtype=bf16),
            shape(8, SEQ),
            shape(SEQ, D, dtype=bf16),
            shape(experts, SEQ, dtype=jnp.int32),
            shape(experts, SEQ),
            shape(experts, SEQ),
        ),
        in_specs=[SMEM] + [VMEM] * 7,
        out_specs=[VMEM] * 8,
        scratch_shapes=[pltpu.VMEM((SEQ, D), bf16), pltpu.VMEM((SEQ, 8), f32)],
        compiler_params=params(),
    )(top_count, image, gain, bias, w_qkv, w_proj, router, choices)


def forward_sending_kernel(
    outers,
    top_count,
    image,
    cotangent,
    gain,
    bias,
    w_qkv,
    w_proj,
    w_in,
    w_out,
    router,
    choices,
    mid,
    packed,
    mixed,
    logs,
    probs,
    normed_all,
    cot_all,
    slots_all,
    gates_all,
    full_qkv,
    full_proj,
    full_in,
    full_out,
    normed_first,
    totals,
    sent,
    landed,
    stay,
    share_sent,
    share_landed,
):
    place = Place(outers)
    task = place.task
    local_count = w_in.shape[0]

    def part(own, full, *lead):
        size = own.shape[-2]
        source = own.at[lead] if lead else own
        return source, lambda index: full.at[(*lead, rows_at(index, size))]

    shards = [part(w_qkv, full_qkv), part(w_proj, full_proj)]
    for expert in range(local_count):
        shards += [part(w_in, full_in, expert), part(w_out, full_out, expert)]
    gather = Gather(place, shards, sent, landed, stay)
    shared, routed = range(2), range(2, len(shards))
    cot_all[task] = cotangent[...].astype(bf16)
    place.greet()
    for unit in shared:
        gather.start(unit)

    def share(index, view):
        return Share(place, view, share_sent.at[index], share_landed.at[index])

    cot = share(0, lambda source: cot_all.at[source])
    slot = share(1, lambda source: slots_all.at[source])
    gate = share(2, lambda source: gates_all.at[source])
    cot.start()
    first_norm(image, gain, bias, normed_first)
    for hop in range(1, outers):
        for unit in shared:
            gather.step(unit, hop)
    for unit in routed:
        gather.start(unit)
    slots_all[task] = number_slots(choices, top_count, router.shape[0])
    slot.start()
    totals[...] = jnp.zeros_like(totals)
    for unit in shared:
        gather.finish(unit)
    packed[...] = dot(normed_first[...], full_qkv[...]).astype(bf16)
    cot.relay()
    slot.relay()

    def chunk(index):
        return share(3 + index, lambda source: normed_all.at[source, rows_at(index, QUERY_FWD)])

    blocks = SEQ // QUERY_FWD

    def block(index, _):
        attend(packed, mixed, totals, index)
        normed_all[task, rows_at(index, QUERY_FWD), :] = mid_block(
            index, image, gain, bias, full_proj, router, mixed, mid, probs
        )
        chunk(index).start()
        pl.when(index > 0)(lambda: chunk(index - 1).relay())
        for hop in range(1, outers):

            @pl.when(index == hop - 1)
            def _():
                for unit in routed:
                    gather.step(unit, hop)

        return 0

    lax.fori_loop(0, blocks, block, 0)
    for hop in range(blocks + 1, outers):
        for unit in routed:
            gather.step(unit, hop)
    gates_all[task] = jnp.where(slots_all[task] >= 0, probs[...], 0.0)
    gate.start()
    logs[...] = totals[...].T
    chunk(blocks - 1).relay()
    gate.relay()
    for one in [cot, slot, gate] + [chunk(index) for index in range(blocks)]:
        one.finish()
    for unit in routed:
        gather.finish(unit)


def forward_sending(top_count, image, cotangent, gain, bias, shards, router, choices):
    w_qkv, w_proj, w_in, w_out = shards
    experts, size = router.shape[0], lax.axis_size("dp")
    groups, local_count = lax.axis_size("task"), w_in.shape[0]
    units, shares = 2 + 2 * local_count, 3 + SEQ // QUERY_FWD
    return pl.pallas_call(
        functools.partial(forward_sending_kernel, size // 2),
        out_shape=(
            shape(SEQ, D),
            shape(SEQ, 3 * D, dtype=bf16),
            shape(SEQ, D, dtype=bf16),
            shape(8, SEQ),
            shape(experts, SEQ),
            shape(groups, SEQ, D, dtype=bf16),
            shape(groups, SEQ, D, dtype=bf16),
            shape(groups, experts, SEQ, dtype=jnp.int32),
            shape(groups, experts, SEQ),
            shape(D, 3 * D, dtype=bf16),
            shape(D, D, dtype=bf16),
            shape(local_count, D, FF, dtype=bf16),
            shape(local_count, FF, D, dtype=bf16),
        ),
        in_specs=[SMEM] + [VMEM] * 6 + [ANY] * 2 + [VMEM] * 2,
        out_specs=[VMEM] * 11 + [ANY] * 2,
        scratch_shapes=[
            pltpu.VMEM((SEQ, D), bf16),
            pltpu.VMEM((SEQ, 8), f32),
            pltpu.SemaphoreType.DMA((units, size, 3)),
            pltpu.SemaphoreType.DMA((units, size)),
            pltpu.SemaphoreType.DMA((units,)),
            pltpu.SemaphoreType.DMA((shares, 3)),
            pltpu.SemaphoreType.DMA((shares, 3)),
        ],
        compiler_params=params(collective_id=0, has_side_effects=True),
    )(top_count, image, cotangent, gain, bias, w_qkv, w_proj, w_in, w_out, router, choices)


def slot_hits(slots, source, expert):
    return lax.broadcasted_iota(jnp.int32, (CAP, SEQ), 0) == slots[source, pl.ds(expert, 1), :]


def ones_at(hits):
    return jnp.where(hits, 1.0, 0.0).astype(bf16)


def expert_kernel(
    normed,
    cotangent,
    slots,
    gates,
    w_in,
    w_out,
    grad_in,
    grad_out,
    mixes,
    grad_normed,
    grad_gates,
    rows_in,
    rows_grad,
    rows_cot,
    rows_gate,
    hidden,
    grad_pre,
    sent,
    columns,
):
    groups, local_count = normed.shape[0], w_in.shape[0]
    width = groups * CAP

    def one_expert(expert, _):
        for source in range(groups):
            own = slice(source * CAP, (source + 1) * CAP)
            hits = slot_hits(slots, source, expert)
            picks = ones_at(hits)
            rows_in[own, :] = dot(picks, normed[source]).astype(bf16)
            cot_rows = dot(picks, cotangent[source])
            gate = jnp.sum(
                jnp.where(hits, gates[source, pl.ds(expert, 1), :], 0.0), axis=1, keepdims=True
            )
            rows_cot[own, :] = cot_rows.astype(bf16)
            rows_grad[own, :] = (gate * cot_rows).astype(bf16)
            rows_gate[own, :] = jnp.broadcast_to(gate, (CAP, 128))

        def tile(index, _):
            units = rows_at(index // (width // ROW_TILE), FF_TILE)
            rows = rows_at(lax.rem(index, width // ROW_TILE), ROW_TILE)
            pre = dot(rows_in[rows, :], w_in[expert, :, units])
            grad_hidden = dot_rt(rows_grad[rows, :], w_out[expert, units, :])
            share = 0.5 * lax.erf(pre * ROOT_HALF) + 0.5
            slope = share + pre * (NORMAL * jnp.exp(-0.5 * pre * pre))
            hidden[rows, units] = (pre * share).astype(bf16)
            grad_pre[rows, units] = (grad_hidden * slope).astype(bf16)
            return 0

        lax.fori_loop(0, (FF // FF_TILE) * (width // ROW_TILE), tile, 0)
        for source in range(groups):
            own = slice(source * CAP, (source + 1) * CAP)
            kept = rows_at(expert, CAP)
            out_rows = dot(hidden[own, :], w_out[expert]).astype(bf16).astype(f32)
            sent[source, kept, :D] = (rows_gate[own, 0:1] * out_rows).astype(bf16)
            sent[source, kept, D:] = dot_rt(grad_pre[own, :], w_in[expert]).astype(bf16)
            grad_gate = jnp.sum(rows_cot[own, :].astype(f32) * out_rows, axis=1, keepdims=True)
            hits = slot_hits(slots, source, expert)
            grad_gates[source, pl.ds(expert, 1), :] = jnp.sum(
                jnp.where(hits, grad_gate, 0.0), axis=0, keepdims=True
            )
        grad_in[expert] = dot_lt(rows_in[...], grad_pre[...]).astype(bf16)
        grad_out[expert] = dot_lt(rows_grad[...], hidden[...]).astype(bf16).T
        return 0

    lax.fori_loop(0, local_count, one_expert, 0)
    for source in range(groups):
        columns[...] = slots[source].T

        def combine(index, _):
            rows = rows_at(index, 512)
            lanes = lax.broadcasted_iota(jnp.int32, (512, CAP), 1)
            picks = jnp.concatenate(
                [ones_at(lanes == columns[rows, e : e + 1]) for e in range(local_count)], axis=1
            )
            back = dot(picks, sent[source])
            mixes[source, rows, :] = back[:, :D].astype(bf16)
            grad_normed[source, rows, :] = back[:, D:].astype(bf16)
            return 0

        lax.fori_loop(0, SEQ // 512, combine, 0)


def expert_part(normed, cotangent, slots, gates, w_in, w_out):
    groups, local_count = normed.shape[0], w_in.shape[0]
    width = groups * CAP
    return pl.pallas_call(
        expert_kernel,
        out_shape=(
            shape(local_count, D, FF, dtype=bf16),
            shape(local_count, FF, D, dtype=bf16),
            shape(groups, SEQ, D, dtype=bf16),
            shape(groups, SEQ, D, dtype=bf16),
            shape(groups, local_count, SEQ),
        ),
        in_specs=[VMEM] * 6,
        out_specs=[VMEM] * 5,
        scratch_shapes=[
            pltpu.VMEM((width, D), bf16),
            pltpu.VMEM((width, D), bf16),
            pltpu.VMEM((width, D), bf16),
            pltpu.VMEM((width, 128), f32),
            pltpu.VMEM((width, FF), bf16),
            pltpu.VMEM((width, FF), bf16),
            pltpu.VMEM((groups, local_count * CAP, 2 * D), bf16),
            pltpu.VMEM((SEQ, local_count), jnp.int32),
        ],
        compiler_params=params(),
    )(normed, cotangent, slots, gates, w_in, w_out)


def attend_back(packed, grad_mixed, logs, grad_packed, grad_keys, grad_values):
    zero = jnp.array(0, bf16)

    def head_pair(pair, _):
        queries, keys, values = (rows_at(pair + part * (D // PAIR), PAIR) for part in range(3))
        key_rows, value_rows = packed[:, keys], packed[:, values]

        def block(index, _):
            rows = rows_at(index, QUERY_BWD)
            query_rows = packed[rows, queries] * jnp.array(HEAD_DIM**-0.5, bf16)
            grad_rows = grad_mixed[rows, queries]
            grad_query, part_keys, part_values = [], 0.0, 0.0
            for half in range(2):
                lanes = half_lanes(QUERY_BWD, half)
                own = jnp.where(lanes, query_rows, zero)
                own_grad = jnp.where(lanes, grad_rows, zero)
                probs = jnp.exp(dot_rt(key_rows, own) - logs[pl.ds(2 * pair + half, 1), rows])
                grad_probs = dot_rt(value_rows, own_grad)
                mean = jnp.sum(probs * grad_probs, axis=0, keepdims=True)
                grad_scores = (probs * (grad_probs - mean)).astype(bf16)
                part_values += dot(probs.astype(bf16), own_grad)
                part_keys += dot(grad_scores, own)
                grad_query.append(dot_lt(grad_scores, key_rows))
            grad_packed[rows, queries] = (
                jnp.where(half_lanes(QUERY_BWD, 0), grad_query[0], grad_query[1])
                * HEAD_DIM**-0.5
            ).astype(bf16)
            grad_keys[...] = jnp.where(index == 0, part_keys, grad_keys[...] + part_keys)
            grad_values[...] = jnp.where(index == 0, part_values, grad_values[...] + part_values)
            return 0

        lax.fori_loop(0, SEQ // QUERY_BWD, block, 0)
        grad_packed[:, keys] = grad_keys[...].astype(bf16)
        grad_packed[:, values] = grad_values[...].astype(bf16)
        return 0

    lax.fori_loop(0, HEADS // 2, head_pair, 0)


def backward_kernel(
    image,
    cotangent,
    gain,
    bias,
    mid,
    w_qkv,
    w_proj,
    router,
    packed,
    mixed,
    logs,
    mixes,
    grad_normed,
    grad_gates,
    probs,
    activations,
    grad_image,
    grad_norm,
    grad_router,
    grad_shared,
    grad_mid,
    grad_low,
    grad_mixed,
    grad_packed,
    grad_keys,
    grad_values,
    normed_first,
):
    groups = mixes.shape[0]
    route = grad_gates[...]
    grad_logits = probs[...] * (route - jnp.sum(probs[...] * route, axis=0, keepdims=True))
    grad_norm[...] = jnp.zeros_like(grad_norm)
    grad_router[...] = jnp.zeros_like(grad_router)
    for index in range(SEQ // ROWS):
        rows = slice(index * ROWS, (index + 1) * ROWS)
        mid_rows = mid[rows, :]
        mix_rows, grad_rows = mixes[0, rows, :].astype(f32), grad_normed[0, rows, :].astype(f32)
        for source in range(1, groups):
            mix_rows += mixes[source, rows, :].astype(f32)
            grad_rows += grad_normed[source, rows, :].astype(f32)
        activations[rows, :] = mid_rows + mix_rows
        own_logits = grad_logits[:, rows]
        grad_rows += lax.dot_general(
            own_logits,
            router[...],
            (((0,), (0,)), ((), ())),
            precision=HIGHEST,
            preferred_element_type=f32,
        )
        grad_in, grad_gain, grad_bias, unit = norm_back(mid_rows, grad_rows, gain[1:2, :])
        grad_router[...] += jnp.dot(
            own_logits,
            unit * gain[1:2, :] + bias[1:2, :],
            precision=HIGHEST,
            preferred_element_type=f32,
        )
        grad_norm[1:2, :] += grad_gain
        grad_norm[3:4, :] += grad_bias
        grad_mid_rows = cotangent[rows, :] + grad_in
        grad_mid[rows, :] = grad_mid_rows
        low_rows = grad_mid_rows.astype(bf16)
        grad_low[rows, :] = low_rows
        grad_mixed[rows, :] = dot_rt(low_rows, w_proj[...]).astype(bf16)
    grad_shared[:, 3 * D :] = dot_lt(mixed[...], grad_low[...]).astype(bf16)
    attend_back(packed, grad_mixed, logs, grad_packed, grad_keys, grad_values)

    def first_norm(index, _):
        rows = rows_at(index, ROWS)
        grad_rows = dot_rt(grad_packed[rows, :], w_qkv[...])
        grad_in, grad_gain, grad_bias, unit = norm_back(image[rows, :], grad_rows, gain[0:1, :])
        normed_first[rows, :] = (unit * gain[0:1, :] + bias[0:1, :]).astype(bf16)
        grad_image[rows, :] = grad_mid[rows, :] + grad_in
        grad_norm[0:1, :] += grad_gain
        grad_norm[2:3, :] += grad_bias
        return 0

    lax.fori_loop(0, SEQ // ROWS, first_norm, 0)
    grad_shared[:, : 3 * D] = dot_lt(normed_first[...], grad_packed[...]).astype(bf16)


def backward_part(*operands):
    router = operands[7]
    return pl.pallas_call(
        backward_kernel,
        out_shape=(
            shape(SEQ, D),
            shape(SEQ, D),
            shape(4, D),
            shape(router.shape[0], D),
            shape(D, 4 * D, dtype=bf16),
        ),
        in_specs=[VMEM] * 15,
        out_specs=[VMEM] * 5,
        scratch_shapes=[
            pltpu.VMEM((SEQ, D), f32),
            pltpu.VMEM((SEQ, D), bf16),
            pltpu.VMEM((SEQ, D), bf16),
            pltpu.VMEM((SEQ, 3 * D), bf16),
            pltpu.VMEM((SEQ, PAIR), f32),
            pltpu.VMEM((SEQ, PAIR), f32),
            pltpu.VMEM((SEQ, D), bf16),
        ],
        compiler_params=params(),
    )(*operands)


def local(
    layer_input,
    cotangent,
    norm_gain,
    norm_bias,
    w_qkv,
    w_proj,
    router,
    w_in,
    w_out,
    choices,
    top_count,
):
    groups = lax.axis_size("task")
    local_count = w_in.shape[0]
    image = layer_input.reshape(SEQ, D)
    grad_rows = cotangent.reshape(SEQ, D)
    router_rows = router[0].T
    experts = router_rows.shape[0]
    routes = choices.reshape(SEQ, TOPMAX)

    def swap(array):
        return lax.all_to_all(array, "task", split_axis=0, concat_axis=0, tiled=True)

    sending = groups == 4 and lax.axis_size("dp") in (4, 8) and w_in.shape[1] % 16 == 0
    if sending:
        (
            mid,
            packed,
            mixed,
            logs,
            probs,
            normed,
            cot_rows,
            slots,
            gates,
            full_qkv,
            full_proj,
            full_in,
            full_out,
        ) = forward_sending(
            top_count,
            image,
            grad_rows,
            norm_gain,
            norm_bias,
            (w_qkv, w_proj, w_in, w_out),
            router_rows,
            routes,
        )
        mine = lax.axis_index("task") * local_count
        slots = lax.dynamic_slice_in_dim(slots, mine, local_count, 1)
        gates = lax.dynamic_slice_in_dim(gates, mine, local_count, 1)
    else:
        full_qkv, full_proj, full_in, full_out = (
            lax.all_gather(w_qkv, "dp", axis=0, tiled=True),
            lax.all_gather(w_proj, "dp", axis=0, tiled=True),
            lax.all_gather(w_in, "dp", axis=1, tiled=True),
            lax.all_gather(w_out, "dp", axis=1, tiled=True),
        )
        mid, packed, mixed, logs, normed, slots, gates, probs = forward_part(
            top_count,
            image,
            norm_gain,
            norm_bias,
            full_qkv,
            full_proj,
            router_rows,
            routes,
        )
        normed = lax.all_gather(normed, "task")
        cot_rows = lax.all_gather(grad_rows.astype(bf16), "task")
        slots = swap(slots.reshape(groups, local_count, SEQ))
        gates = swap(gates.reshape(groups, local_count, SEQ))
    grad_in, grad_out, mixes, grad_normed, grad_gates = expert_part(
        normed, cot_rows, slots, gates, full_in, full_out
    )
    activations, grad_image, grad_norm, grad_router, grad_shared = backward_part(
        image,
        grad_rows,
        norm_gain,
        norm_bias,
        mid,
        full_qkv,
        full_proj,
        router_rows,
        packed,
        mixed,
        logs,
        swap(mixes),
        swap(grad_normed),
        swap(grad_gates).reshape(experts, SEQ),
        probs,
    )
    grad_in = lax.psum_scatter(grad_in, "dp", scatter_dimension=1, tiled=True)
    grad_out = lax.psum_scatter(grad_out, "dp", scatter_dimension=1, tiled=True)
    grad_shared = lax.psum_scatter(grad_shared, "dp", scatter_dimension=0, tiled=True)
    grad_shared = lax.psum(grad_shared, "task").astype(f32)
    grad_router = lax.psum(grad_router, "dp")
    grad_norm = lax.psum(grad_norm, ("task", "dp"))
    return (
        activations.reshape(layer_input.shape),
        grad_image.reshape(layer_input.shape),
        grad_norm[:2],
        grad_norm[2:],
        grad_shared[:, : 3 * D],
        grad_shared[:, 3 * D :],
        grad_router.T[None],
        grad_in.astype(f32),
        grad_out.astype(f32),
    )


def solution(mesh):
    tokens = P("task", "dp", None, None)
    rows = P("dp", None)
    blocks = P("task", "dp", None)
    routed = P("task", None, None)
    return jax.shard_map(
        local,
        mesh=mesh,
        in_specs=(tokens, tokens, P(), P(), rows, rows, routed, blocks, blocks, tokens, P("task")),
        out_specs=(tokens, tokens, P(), P(), rows, rows, routed, blocks, blocks),
        check_vma=False,
    )
```

```python
import functools

import jax
import jax.numpy as jnp
from jax import lax
from jax.experimental import pallas as pl
from jax.experimental.pallas import tpu as pltpu
from jax.sharding import PartitionSpec as P

D = 384
FF = 1536
HEADS = 6
HEAD_DIM = 64
PAIR = 2 * HEAD_DIM
TOPMAX = 4
SEQ = 1024
CAP = 320

f32 = jnp.float32
bf16 = jnp.bfloat16
HIGHEST = lax.Precision.HIGHEST
EPSILON = 1e-06
ROOT_HALF = 0.7071067811865476
NORMAL = 0.3989422804014327

FF_TILE = 512
ROW_TILE = 640
QUERY_FWD = 256
QUERY_BWD = 256
ROWS = 256
RETURNS = 2

VMEM = pl.BlockSpec(memory_space=pltpu.VMEM)
SMEM = pl.BlockSpec(memory_space=pltpu.SMEM)
ANY = pl.BlockSpec(memory_space=pl.ANY)


def shape(*dims, dtype=f32):
    return jax.ShapeDtypeStruct(dims, dtype)


def params(**more):
    return pltpu.CompilerParams(vmem_limit_bytes=62 * 2**20, **more)


def dot(a, b):
    return lax.dot_general(a, b, (((1,), (0,)), ((), ())), preferred_element_type=f32)


def dot_rt(a, b):
    return lax.dot_general(a, b, (((1,), (1,)), ((), ())), preferred_element_type=f32)


def dot_lt(a, b):
    return lax.dot_general(a, b, (((0,), (0,)), ((), ())), preferred_element_type=f32)


def rows_at(index, size):
    return pl.ds(pl.multiple_of(index * size, size), size)


def normalize(rows):
    centered = rows - jnp.mean(rows, axis=1, keepdims=True)
    scale = lax.rsqrt(jnp.mean(centered * centered, axis=1, keepdims=True) + EPSILON)
    return centered * scale, scale


def norm_back(rows, grad_rows, gain):
    unit, scale = normalize(rows)
    scaled = grad_rows * gain
    grad_in = scale * (
        scaled
        - jnp.mean(scaled, axis=1, keepdims=True)
        - unit * jnp.mean(scaled * unit, axis=1, keepdims=True)
    )
    grad_gain = jnp.sum(grad_rows * unit, axis=0, keepdims=True)
    return grad_in, grad_gain, jnp.sum(grad_rows, axis=0, keepdims=True), unit


def half_lanes(rows, half):
    lanes = lax.broadcasted_iota(jnp.int32, (rows, PAIR), 1)
    return (lanes < HEAD_DIM) if half == 0 else (lanes >= HEAD_DIM)


def remote(source, target, sent, landed, **device):
    return pltpu.make_async_remote_copy(
        src_ref=source,
        dst_ref=target,
        send_sem=sent,
        recv_sem=landed,
        device_id=device,
        device_id_type=pl.DeviceIdType.MESH,
    )


class Place:
    def __init__(self, outers):
        self.dp = lax.axis_index("dp")
        self.task = lax.axis_index("task")
        self.outers = outers
        self.outer, self.inner = self.dp // 2, self.dp % 2
        self.has_up, self.has_down = self.outer + 1 < outers, self.outer > 0
        self.up, self.down = self.dp + 2, self.dp - 2
        self.side = self.dp + 1 - 2 * self.inner
        self.core = self.task + 1 - 2 * (self.task % 2)
        self.across = self.task + 2 - 4 * (self.task // 2)
        self.far = self.across + 1 - 2 * (self.task % 2)

    def partner(self, bit):
        return self.dp + bit - 2 * bit * (self.dp // bit % 2)

    def greet(self, far=False, bits=()):
        barrier = pltpu.get_barrier_semaphore()

        def signal(**device):
            pl.semaphore_signal(
                barrier, inc=1, device_id=device, device_id_type=pl.DeviceIdType.MESH
            )

        pl.when(self.has_up)(lambda: signal(dp=self.up))
        pl.when(self.has_down)(lambda: signal(dp=self.down))
        signal(dp=self.side)
        signal(task=self.core)
        signal(task=self.across)
        if far:
            signal(task=self.far)
        for bit in bits:
            signal(dp=self.partner(bit))
        others = 3 + int(far) + len(bits)
        pl.semaphore_wait(
            barrier, others + self.has_up.astype(jnp.int32) + self.has_down.astype(jnp.int32)
        )


class Gather:
    def __init__(self, place, shards, sent, landed, stay):
        self.place, self.shards = place, shards
        self.sent, self.landed, self.stay = sent, landed, stay

    def move(self, unit, source, way, device, first=False):
        own, size, full = self.shards[unit]
        target = full.at[rows_at(source, size)]
        return remote(
            own if first else target,
            target,
            self.sent.at[unit, source, way],
            self.landed.at[unit, source],
            dp=device,
        )

    def local(self, unit):
        own, size, full = self.shards[unit]
        target = full.at[rows_at(self.place.dp, size)]
        return pltpu.make_async_copy(own, target, self.stay.at[unit])

    def start(self, unit):
        place = self.place
        pl.when(place.has_up)(lambda: self.move(unit, place.dp, 0, place.up, True).start())
        pl.when(place.has_down)(lambda: self.move(unit, place.dp, 1, place.down, True).start())
        self.move(unit, place.dp, 2, place.side, True).start()
        self.local(unit).start()

    def step(self, unit, hop):
        place = self.place

        @pl.when(place.outer >= hop)
        def _():
            source = place.dp - 2 * hop
            self.move(unit, source, 0, place.dp).wait_recv()
            pl.when(place.has_up)(lambda: self.move(unit, source, 0, place.up).start())
            self.move(unit, source, 2, place.side).start()

        @pl.when(place.outer + hop < place.outers)
        def _():
            source = place.dp + 2 * hop
            self.move(unit, source, 1, place.dp).wait_recv()
            pl.when(place.has_down)(lambda: self.move(unit, source, 1, place.down).start())
            self.move(unit, source, 2, place.side).start()

    def finish(self, unit):
        place = self.place
        self.local(unit).wait()
        for outer in range(place.outers):
            own, other = 2 * outer + place.inner, 2 * outer + 1 - place.inner
            self.move(unit, other, 2, place.dp).wait_recv()
            self.move(unit, own, 2, place.side).wait_send()
            pl.when((outer <= place.outer) & place.has_up)(
                lambda own=own: self.move(unit, own, 0, place.up).wait_send()
            )
            pl.when((outer >= place.outer) & place.has_down)(
                lambda own=own: self.move(unit, own, 1, place.down).wait_send()
            )


class Share:
    def __init__(self, place, view, sent, landed):
        self.place, self.view, self.sent, self.landed = place, view, sent, landed

    def move(self, source, way, **device):
        return remote(
            self.view(source),
            self.view(source),
            self.sent.at[way],
            self.landed.at[way],
            **device,
        )

    def start(self):
        place = self.place
        self.move(place.task, 0, task=place.across).start()
        self.move(place.task, 1, task=place.core).start()

    def relay(self):
        place = self.place
        self.move(place.across, 0, task=place.across).wait_recv()
        self.move(place.across, 2, task=place.core).start()

    def finish(self):
        place = self.place
        self.move(place.task, 0, task=place.across).wait_send()
        self.move(place.core, 1, task=place.core).wait()
        self.move(place.across, 2, task=place.core).wait()


class Scatter:
    def __init__(self, place, block, size, side, line, fold, sems):
        self.place, self.block, self.size = place, block, size
        self.side, self.line, self.fold = side, line, fold
        self.side_sent, self.side_landed, self.line_sent, self.line_landed = sems

    def own(self, outer, inner):
        return self.block(rows_at(2 * outer + inner, self.size))

    def to_side(self, outer):
        place = self.place
        return remote(
            self.own(outer, 1 - place.inner),
            self.side.at[outer],
            self.side_sent.at[outer],
            self.side_landed.at[outer],
            dp=place.side,
        )

    def along(self, outer, slot, device):
        return remote(
            self.fold.at[outer],
            self.line.at[slot],
            self.line_sent.at[outer],
            self.line_landed.at[slot],
            dp=device,
        )

    def start(self):
        outers = self.place.outers
        for near in range(outers // 2):
            self.to_side(outers - 1 - near).start()
            self.to_side(near).start()

    def total(self, outer, *slots):
        self.to_side(outer).wait_recv()
        rows = self.own(outer, self.place.inner)[...].astype(f32)
        rows += self.side[outer].astype(f32)
        for slot in slots:
            self.along(outer, slot, self.place.dp).wait_recv()
            rows += self.line[slot].astype(f32)
        return rows

    def hop(self, step):
        place, outers = self.place, self.place.outers

        @pl.when(place.outer == step)
        def _():
            for outer in range(outers - 1, step, -1):
                rows = self.total(outer, *([outer] if step else []))
                self.fold[outer] = rows.astype(bf16)
                self.along(outer, outer, place.up).start()

        @pl.when(place.outer == outers - 1 - step)
        def _():
            for outer in range(outers - 1 - step):
                rows = self.total(outer, *([outer] if step else []))
                self.fold[outer] = rows.astype(bf16)
                slot = outers if outer == outers - 2 - step else outer
                self.along(outer, slot, place.down).start()

    def finish(self, store):
        place, outers = self.place, self.place.outers
        for outer in range(outers):

            @pl.when(place.outer == outer)
            def _():
                below, above = [outer] * (outer > 0), [outers] * (outer < outers - 1)
                store(self.total(outer, *below, *above))
                for other in range(outers):
                    if other != outer:
                        self.along(other, other, place.dp).wait_send()

            self.to_side(outer).wait_send()


class PairSum:
    def __init__(self, stage, land, sent, landed):
        self.stage, self.land, self.sent, self.landed = stage, land, sent, landed

    def swap(self, step, **device):
        return remote(
            self.stage.at[step],
            self.land.at[step],
            self.sent.at[step],
            self.landed.at[step],
            **device,
        )

    def give(self, step, rows, **device):
        self.stage[step] = rows.astype(self.stage.dtype)
        self.swap(step, **device).start()

    def take(self, step, **device):
        self.swap(step, **device).wait()
        return self.stage[step].astype(f32) + self.land[step].astype(f32)


class Return:
    def __init__(self, place, parts, pieces, land, joint, sent, landed):
        self.place, self.parts, self.pieces = place, parts, pieces
        self.land, self.joint, self.sent, self.landed = land, joint, sent, landed
        self.size = SEQ // pieces

    def rows(self, piece):
        return pl.ds(piece * self.size, self.size)

    def move(self, way, piece):
        place, rows = self.place, self.rows(piece)
        source = [
            self.parts(place.core).at[rows],
            self.parts(place.far).at[rows],
            self.joint.at[rows],
        ][way]
        return remote(
            source,
            self.land.at[way, rows],
            self.sent.at[way, piece],
            self.landed.at[way, piece],
            task=place.across if way == 2 else place.core,
        )

    def to_core(self, piece):
        self.move(0, piece).start()

    def by_core(self, piece):
        self.move(1, piece).start()

    def to_across(self, piece):
        rows = self.rows(piece)
        self.move(1, piece).wait_recv()
        joint = self.parts(self.place.across)[rows, :].astype(f32)
        joint += self.land[1, rows, :].astype(f32)
        self.joint[rows, :] = joint.astype(bf16)
        self.move(2, piece).start()

    def finish(self, piece):
        rows = self.rows(piece)
        self.move(0, piece).wait()
        self.move(1, piece).wait_send()
        self.move(2, piece).wait()
        total = self.parts(self.place.task)[rows, :].astype(f32)
        return total + self.land[0, rows, :].astype(f32) + self.land[2, rows, :].astype(f32)


def attend(packed, mixed, totals, index):
    zero = jnp.array(0, bf16)
    rows = rows_at(index, QUERY_FWD)

    def head_pair(pair, _):
        queries, keys, values = (rows_at(pair + part * (D // PAIR), PAIR) for part in range(3))
        key_rows, value_rows = packed[:, keys], packed[:, values]
        query_rows = packed[rows, queries] * jnp.array(HEAD_DIM**-0.5, bf16)
        outs, logs = [], []
        for half in range(2):
            own = jnp.where(half_lanes(QUERY_FWD, half), query_rows, zero)
            scores = dot_rt(own, key_rows)
            top = jnp.max(scores, axis=1, keepdims=True)
            weights = jnp.exp(scores - top)
            total = jnp.sum(weights, axis=1, keepdims=True)
            outs.append(dot(weights.astype(bf16), value_rows) * (1.0 / total))
            logs.append(top + jnp.log(total))
        mixed[rows, queries] = jnp.where(half_lanes(QUERY_FWD, 0), outs[0], outs[1]).astype(bf16)
        lanes = lax.broadcasted_iota(jnp.int32, (QUERY_FWD, 8), 1)
        totals[rows, :] = jnp.where(
            lanes == 2 * pair,
            logs[0],
            jnp.where(lanes == 2 * pair + 1, logs[1], totals[rows, :]),
        )
        return 0

    lax.fori_loop(0, HEADS // 2, head_pair, 0)


def first_norm(image, gain, bias, normed_first):
    def block(index, _):
        rows = rows_at(index, ROWS)
        unit, _ = normalize(image[rows, :])
        normed_first[rows, :] = (unit * gain[0:1, :] + bias[0:1, :]).astype(bf16)
        return 0

    lax.fori_loop(0, SEQ // ROWS, block, 0)


def number_slots(choices, top_count, experts):
    named = choices[...].T
    numbers = lax.broadcasted_iota(jnp.int32, (experts, SEQ), 0)
    used = jnp.zeros((experts, SEQ), f32)
    for choice in range(TOPMAX):
        hit = (named[choice : choice + 1, :] == numbers) & (choice < top_count[0])
        used = used + jnp.where(hit, 1.0, 0.0)
    earlier = lax.broadcasted_iota(jnp.int32, (SEQ, SEQ), 0) < lax.broadcasted_iota(
        jnp.int32, (SEQ, SEQ), 1
    )
    before = dot(used.astype(bf16), jnp.where(earlier, 1.0, 0.0).astype(bf16))
    return jnp.where(used > 0, before, -1.0).astype(jnp.int32)


def mid_block(index, image, gain, bias, w_proj, router, mixed, mid, probs):
    rows = rows_at(index, QUERY_FWD)
    mid_rows = image[rows, :] + dot(mixed[rows, :], w_proj[...])
    mid[rows, :] = mid_rows
    unit, _ = normalize(mid_rows)
    normed_rows = unit * gain[1:2, :] + bias[1:2, :]
    logits = lax.dot_general(
        router[...],
        normed_rows,
        (((1,), (1,)), ((), ())),
        precision=HIGHEST,
        preferred_element_type=f32,
    )
    powers = jnp.exp(logits - jnp.max(logits, axis=0, keepdims=True))
    probs[:, rows] = powers / jnp.sum(powers, axis=0, keepdims=True)
    return normed_rows.astype(bf16)


def forward_kernel(
    top_count,
    image,
    gain,
    bias,
    w_qkv,
    w_proj,
    router,
    choices,
    mid,
    packed,
    mixed,
    logs,
    normed,
    slots,
    gates,
    probs,
    normed_first,
    totals,
):
    first_norm(image, gain, bias, normed_first)
    slots[...] = number_slots(choices, top_count, router.shape[0])
    packed[...] = dot(normed_first[...], w_qkv[...]).astype(bf16)
    totals[...] = jnp.zeros_like(totals)

    def block(index, _):
        attend(packed, mixed, totals, index)
        normed[rows_at(index, QUERY_FWD), :] = mid_block(
            index, image, gain, bias, w_proj, router, mixed, mid, probs
        )
        return 0

    lax.fori_loop(0, SEQ // QUERY_FWD, block, 0)
    logs[...] = totals[...].T
    gates[...] = jnp.where(slots[...] >= 0, probs[...], 0.0)


def forward_part(top_count, image, gain, bias, w_qkv, w_proj, router, choices):
    experts = router.shape[0]
    return pl.pallas_call(
        forward_kernel,
        out_shape=(
            shape(SEQ, D),
            shape(SEQ, 3 * D, dtype=bf16),
            shape(SEQ, D, dtype=bf16),
            shape(8, SEQ),
            shape(SEQ, D, dtype=bf16),
            shape(experts, SEQ, dtype=jnp.int32),
            shape(experts, SEQ),
            shape(experts, SEQ),
        ),
        in_specs=[SMEM] + [VMEM] * 7,
        out_specs=[VMEM] * 8,
        scratch_shapes=[pltpu.VMEM((SEQ, D), bf16), pltpu.VMEM((SEQ, 8), f32)],
        compiler_params=params(),
    )(top_count, image, gain, bias, w_qkv, w_proj, router, choices)


def forward_sending_kernel(
    outers,
    top_count,
    image,
    cotangent,
    gain,
    bias,
    w_qkv,
    w_proj,
    w_in,
    w_out,
    router,
    choices,
    mid,
    packed,
    mixed,
    logs,
    probs,
    normed_all,
    cot_all,
    slots_all,
    gates_all,
    full_qkv,
    full_proj,
    full_in,
    full_out,
    normed_first,
    totals,
    sent,
    landed,
    stay,
    share_sent,
    share_landed,
):
    place = Place(outers)
    task = place.task
    shards = [(w_qkv, w_qkv.shape[0], full_qkv), (w_proj, w_proj.shape[0], full_proj)]
    for expert in range(full_in.shape[0]):
        shards += [
            (w_in.at[expert], w_in.shape[1], full_in.at[expert]),
            (w_out.at[expert], w_out.shape[1], full_out.at[expert]),
        ]
    gather = Gather(place, shards, sent, landed, stay)
    shared, routed = range(2), range(2, len(shards))
    cot_all[task] = cotangent[...].astype(bf16)
    place.greet()
    for unit in shared:
        gather.start(unit)

    def share(index, view):
        return Share(place, view, share_sent.at[index], share_landed.at[index])

    cot = share(0, lambda source: cot_all.at[source])
    slot = share(1, lambda source: slots_all.at[source])
    gate = share(2, lambda source: gates_all.at[source])
    cot.start()
    first_norm(image, gain, bias, normed_first)
    for hop in range(1, outers):
        for unit in shared:
            gather.step(unit, hop)
    for unit in routed:
        gather.start(unit)
    slots_all[task] = number_slots(choices, top_count, router.shape[0])
    slot.start()
    totals[...] = jnp.zeros_like(totals)
    for unit in shared:
        gather.finish(unit)
    packed[...] = dot(normed_first[...], full_qkv[...]).astype(bf16)
    cot.relay()
    slot.relay()

    def chunk(index):
        return share(3 + index, lambda source: normed_all.at[source, rows_at(index, QUERY_FWD)])

    blocks = SEQ // QUERY_FWD

    def block(index, _):
        attend(packed, mixed, totals, index)
        normed_all[task, rows_at(index, QUERY_FWD), :] = mid_block(
            index, image, gain, bias, full_proj, router, mixed, mid, probs
        )
        chunk(index).start()
        pl.when(index > 0)(lambda: chunk(index - 1).relay())
        for hop in range(1, outers):

            @pl.when(index == hop - 1)
            def _():
                for unit in routed:
                    gather.step(unit, hop)

        return 0

    lax.fori_loop(0, blocks, block, 0)
    for hop in range(blocks + 1, outers):
        for unit in routed:
            gather.step(unit, hop)
    gates_all[task] = jnp.where(slots_all[task] >= 0, probs[...], 0.0)
    gate.start()
    logs[...] = totals[...].T
    chunk(blocks - 1).relay()
    gate.relay()
    for one in [cot, slot, gate] + [chunk(index) for index in range(blocks)]:
        one.finish()
    for unit in routed:
        gather.finish(unit)


def forward_sending(top_count, image, cotangent, gain, bias, shards, router, choices):
    w_qkv, w_proj, w_in, w_out = shards
    experts, size = router.shape[0], lax.axis_size("dp")
    groups, early = lax.axis_size("task"), w_in.shape[0] // 2
    units, shares = 2 + 2 * early, 3 + SEQ // QUERY_FWD
    return pl.pallas_call(
        functools.partial(forward_sending_kernel, size // 2),
        out_shape=(
            shape(SEQ, D),
            shape(SEQ, 3 * D, dtype=bf16),
            shape(SEQ, D, dtype=bf16),
            shape(8, SEQ),
            shape(experts, SEQ),
            shape(groups, SEQ, D, dtype=bf16),
            shape(groups, SEQ, D, dtype=bf16),
            shape(groups, experts, SEQ, dtype=jnp.int32),
            shape(groups, experts, SEQ),
            shape(D, 3 * D, dtype=bf16),
            shape(D, D, dtype=bf16),
            shape(early, D, FF, dtype=bf16),
            shape(early, FF, D, dtype=bf16),
        ),
        in_specs=[SMEM] + [VMEM] * 6 + [ANY] * 2 + [VMEM] * 2,
        out_specs=[VMEM] * 11 + [ANY] * 2,
        scratch_shapes=[
            pltpu.VMEM((SEQ, D), bf16),
            pltpu.VMEM((SEQ, 8), f32),
            pltpu.SemaphoreType.DMA((units, size, 3)),
            pltpu.SemaphoreType.DMA((units, size)),
            pltpu.SemaphoreType.DMA((units,)),
            pltpu.SemaphoreType.DMA((shares, 3)),
            pltpu.SemaphoreType.DMA((shares, 3)),
        ],
        compiler_params=params(collective_id=0, has_side_effects=True),
    )(top_count, image, cotangent, gain, bias, w_qkv, w_proj, w_in, w_out, router, choices)


def slot_hits(slots, source, expert):
    return lax.broadcasted_iota(jnp.int32, (CAP, SEQ), 0) == slots[source, pl.ds(expert, 1), :]


def ones_at(hits):
    return jnp.where(hits, 1.0, 0.0).astype(bf16)


def one_expert(operands, work, grads, expert, first, slot, between):
    normed, cotangent, slots, gates, w_in, w_out = operands
    rows_in, rows_grad, rows_cot, rows_gate, hidden, grad_pre, sent = work
    grad_in, grad_out, grad_gates = grads
    groups = normed.shape[0]
    width = groups * CAP
    for source in range(groups):
        own = slice(source * CAP, (source + 1) * CAP)
        hits = slot_hits(slots, source, first + expert)
        picks = ones_at(hits)
        rows_in[own, :] = dot(picks, normed[source]).astype(bf16)
        cot_rows = dot(picks, cotangent[source])
        gate = jnp.sum(
            jnp.where(hits, gates[source, pl.ds(first + expert, 1), :], 0.0),
            axis=1,
            keepdims=True,
        )
        rows_cot[own, :] = cot_rows.astype(bf16)
        rows_grad[own, :] = (gate * cot_rows).astype(bf16)
        rows_gate[own, :] = jnp.broadcast_to(gate, (CAP, 128))
    between(0)

    def tile(index, _):
        units = rows_at(index // (width // ROW_TILE), FF_TILE)
        rows = rows_at(lax.rem(index, width // ROW_TILE), ROW_TILE)
        pre = dot(rows_in[rows, :], w_in[slot, :, units])
        grad_hidden = dot_rt(rows_grad[rows, :], w_out[slot, units, :])
        share = 0.5 * lax.erf(pre * ROOT_HALF) + 0.5
        slope = share + pre * (NORMAL * jnp.exp(-0.5 * pre * pre))
        hidden[rows, units] = (pre * share).astype(bf16)
        grad_pre[rows, units] = (grad_hidden * slope).astype(bf16)
        return 0

    lax.fori_loop(0, (FF // FF_TILE) * (width // ROW_TILE), tile, 0)
    between(1)
    for source in range(groups):
        own = slice(source * CAP, (source + 1) * CAP)
        kept = rows_at(expert, CAP)
        out_rows = dot(hidden[own, :], w_out[slot]).astype(bf16).astype(f32)
        sent[source, kept, :D] = (rows_gate[own, 0:1] * out_rows).astype(bf16)
        sent[source, kept, D:] = dot_rt(grad_pre[own, :], w_in[slot]).astype(bf16)
        grad_gate = jnp.sum(rows_cot[own, :].astype(f32) * out_rows, axis=1, keepdims=True)
        hits = slot_hits(slots, source, first + expert)
        grad_gates[source, pl.ds(expert, 1), :] = jnp.sum(
            jnp.where(hits, grad_gate, 0.0), axis=0, keepdims=True
        )
    between(2)
    grad_in[expert] = dot_lt(rows_in[...], grad_pre[...]).astype(bf16)
    grad_out[expert] = dot_lt(rows_grad[...], hidden[...]).astype(bf16).T
    between(3)


def combine(slots, first, local_count, sent, columns, source, store):
    size = SEQ // RETURNS
    columns[...] = slots[source].T
    for piece in range(RETURNS):
        rows = pl.ds(piece * size, size)
        lanes = lax.broadcasted_iota(jnp.int32, (size, CAP), 1)
        mine = lax.broadcasted_iota(jnp.int32, (size, columns.shape[1]), 1)
        picks = []
        for expert in range(local_count):
            column = jnp.max(
                jnp.where(mine == first + expert, columns[rows, :], -1), axis=1, keepdims=True
            )
            picks.append(ones_at(lanes == column))
        back = dot(jnp.concatenate(picks, axis=1), sent[source])
        store(piece, rows, back[:, :D].astype(bf16), back[:, D:].astype(bf16))


def expert_scratch(groups, local_count, experts):
    width = groups * CAP
    return [
        pltpu.VMEM((width, D), bf16),
        pltpu.VMEM((width, D), bf16),
        pltpu.VMEM((width, D), bf16),
        pltpu.VMEM((width, 128), f32),
        pltpu.VMEM((width, FF), bf16),
        pltpu.VMEM((width, FF), bf16),
        pltpu.VMEM((groups, local_count * CAP, 2 * D), bf16),
        pltpu.VMEM((SEQ, experts), jnp.int32),
    ]


def expert_kernel(*refs):
    operands, grads, (mixes, grad_normed) = refs[:6], refs[6:9], refs[9:11]
    work, columns = refs[11:18], refs[18]
    groups, local_count = operands[0].shape[0], operands[4].shape[0]

    def body(expert, _):
        one_expert(operands, work, grads, expert, 0, expert, lambda point: None)
        return 0

    lax.fori_loop(0, local_count, body, 0)
    for source in range(groups):

        def store(piece, rows, mix, grad, source=source):
            mixes[source, rows, :] = mix
            grad_normed[source, rows, :] = grad

        combine(operands[2], 0, local_count, work[6], columns, source, store)


def expert_part(*operands):
    groups, local_count = operands[0].shape[0], operands[4].shape[0]
    return pl.pallas_call(
        expert_kernel,
        out_shape=(
            shape(local_count, D, FF, dtype=bf16),
            shape(local_count, FF, D, dtype=bf16),
            shape(groups, local_count, SEQ),
            shape(groups, SEQ, D, dtype=bf16),
            shape(groups, SEQ, D, dtype=bf16),
        ),
        in_specs=[VMEM] * 6,
        out_specs=[VMEM] * 5,
        scratch_shapes=expert_scratch(groups, local_count, operands[2].shape[1]),
        compiler_params=params(),
    )(*operands)


def expert_sending_kernel(outers, early, *refs):
    normed, cotangent, slots, gates, early_in, early_out, w_in, w_out = refs[:8]
    late_in, late_out, gate_all, mixes, grad_rows, shard_in, shard_out = refs[8:15]
    full_in, full_out = refs[15:17]
    work, columns = refs[17:24], refs[24]
    slot_in, slot_out, grad_in, grad_out, grad_gates, land = refs[25:31]
    in_bufs, out_bufs = refs[31:34], refs[34:37]
    sent, landed, gate_sent, gate_landed, mix_sem, late_sem, slot_sem = refs[37:44]
    gather_sems, scatter_sems = refs[44:47], refs[47:51]
    place = Place(outers)
    local_count, size = grad_in.shape[0], 2 * outers
    late = local_count - early
    first = place.task * local_count
    place.greet(far=True)

    shards = []
    for expert in range(late):
        shards += [
            (w_in.at[early + expert], w_in.shape[1], full_in.at[expert]),
            (w_out.at[early + expert], w_out.shape[1], full_out.at[expert]),
        ]
    gather = Gather(place, shards, *gather_sems)
    for unit in range(len(shards)):
        gather.start(unit)

    def load(source, expert, slot):
        return [
            pltpu.make_async_copy(source[0].at[expert], slot_in.at[slot], slot_sem.at[slot, 0]),
            pltpu.make_async_copy(source[1].at[expert], slot_out.at[slot], slot_sem.at[slot, 1]),
        ]

    for expert in range(early):
        for copy in load((early_in, early_out), expert, expert):
            copy.start()

    scatters, stores = [], []
    for expert in range(early):
        for source, bufs, shard in ((grad_in, in_bufs, shard_in), (grad_out, out_bufs, shard_out)):
            unit = len(scatters)
            scatters.append(
                Scatter(
                    place,
                    lambda rows, source=source, expert=expert: source.at[expert, rows],
                    shard.shape[1],
                    *[buf.at[expert] for buf in bufs],
                    [sem.at[unit] for sem in scatter_sems],
                )
            )

            def store(rows, shard=shard, expert=expert):
                shard[expert] = rows

            stores.append(store)

    def keep(expert):
        return [
            pltpu.make_async_copy(
                grad_in.at[early + expert], late_in.at[expert], late_sem.at[expert, 0]
            ),
            pltpu.make_async_copy(
                grad_out.at[early + expert], late_out.at[expert], late_sem.at[expert, 1]
            ),
        ]

    def plan(expert, point):
        steps = []
        if point == 0:
            if expert < early:
                steps += [copy.wait for copy in load((early_in, early_out), expert, expert)]
            else:
                steps += [
                    copy.wait
                    for copy in load((full_in, full_out), expert - early, expert - early)
                ]
        if expert == 0:
            for unit in range(len(shards)):
                hop = point - unit // 2 + 1
                if 0 < hop < outers:
                    steps.append(lambda unit=unit, hop=hop: gather.step(unit, hop))
        if expert == 1 and point == 0:
            for unit in range(len(shards)):
                for hop in range(5 - unit // 2, outers):
                    steps.append(lambda unit=unit, hop=hop: gather.step(unit, hop))
        if point == 3:
            if expert < early:
                steps += [scatters[2 * expert].start, scatters[2 * expert + 1].start]
            else:
                steps += [copy.start for copy in keep(expert - early)]
        return steps

    def body(expert, _):
        @pl.when(expert >= early)
        def _():
            for other in range(late):

                @pl.when(expert == early + other)
                def _():
                    gather.finish(2 * other)
                    gather.finish(2 * other + 1)
                    for copy in load((full_in, full_out), other, other):
                        copy.start()

        def between(point):
            for at in range(local_count):
                steps = plan(at, point)
                if steps:

                    @pl.when(expert == at)
                    def _():
                        for step in steps:
                            step()

        one_expert(
            (normed, cotangent, slots, gates, slot_in, slot_out),
            work,
            (grad_in, grad_out, grad_gates),
            expert,
            first,
            lax.rem(expert, early),
            between,
        )
        return 0

    lax.fori_loop(0, local_count, body, 0)
    gate_all[place.task] = grad_gates[place.task]
    peers = (place.core, place.across, place.far)

    def gate_move(way):
        return remote(
            grad_gates.at[peers[way]],
            gate_all.at[place.task],
            gate_sent.at[way],
            gate_landed.at[way],
            task=peers[way],
        )

    for way in range(3):
        gate_move(way).start()
    hidden, grad_pre, joint = work[4], work[5], work[2]

    def part(ref, source):
        return ref.at[pl.ds(0, SEQ), pl.ds(pl.multiple_of(source * D, 128), D)]

    back = Return(
        place, lambda source: part(hidden, source), RETURNS, land, joint, sent, landed
    )
    for source, after in (
        (place.far, back.by_core),
        (place.across, back.to_across),
        (place.core, back.to_core),
        (place.task, None),
    ):

        def store(piece, rows, mix, grad, source=source, after=after):
            part(grad_pre, source)[rows, :] = mix
            part(hidden, source)[rows, :] = grad
            if after:
                after(piece)

        combine(slots, first, local_count, work[6], columns, source, store)
    keeps = [
        pltpu.make_async_copy(part(grad_pre, source), mixes.at[source], mix_sem.at[source])
        for source in range(mixes.shape[0])
    ]
    for copy in keeps:
        copy.start()
    for turn in range(len(scatters) + outers):
        for step in range(outers - 1):
            if 0 <= turn - step < len(scatters):
                scatters[turn - step].hop(step)
        if 0 <= turn - outers + 1 < len(scatters):
            scatters[turn - outers + 1].finish(stores[turn - outers + 1])
    for piece in range(RETURNS):
        grad_rows[back.rows(piece), :] = back.finish(piece)
    for way in range(3):
        gate_move(way).wait()
    for copy in keeps:
        copy.wait()
    for expert in range(late):
        for copy in keep(expert):
            copy.wait()


def scatter_buffers(number, outers, *dims):
    return [pltpu.VMEM((number, slots, *dims), bf16) for slots in (outers, outers + 1, outers)]


def scatter_semaphores(units, outers):
    return [pltpu.SemaphoreType.DMA((units, outers))] * 3 + [
        pltpu.SemaphoreType.DMA((units, outers + 1))
    ]


def expert_sending(*operands):
    groups, experts = operands[2].shape[:2]
    local_count, thin = operands[6].shape[:2]
    wide, early = operands[7].shape[1], operands[4].shape[0]
    late, size = local_count - early, lax.axis_size("dp")
    outers = size // 2
    return pl.pallas_call(
        functools.partial(expert_sending_kernel, outers, early),
        out_shape=(
            shape(late, D, FF, dtype=bf16),
            shape(late, FF, D, dtype=bf16),
            shape(groups, local_count, SEQ),
            shape(groups, SEQ, D, dtype=bf16),
            shape(SEQ, D),
            shape(early, thin, FF),
            shape(early, wide, D),
            shape(late, D, FF, dtype=bf16),
            shape(late, FF, D, dtype=bf16),
        ),
        in_specs=[VMEM] * 4 + [ANY] * 4,
        out_specs=[ANY] * 2 + [VMEM, ANY, VMEM, VMEM, VMEM] + [ANY] * 2,
        scratch_shapes=expert_scratch(groups, local_count, experts)
        + [
            pltpu.VMEM((early, D, FF), bf16),
            pltpu.VMEM((early, FF, D), bf16),
            pltpu.VMEM((local_count, D, FF), bf16),
            pltpu.VMEM((local_count, FF, D), bf16),
            pltpu.VMEM((groups, local_count, SEQ), f32),
            pltpu.VMEM((3, SEQ, D), bf16),
        ]
        + scatter_buffers(early, outers, thin, FF)
        + scatter_buffers(early, outers, wide, D)
        + [
            pltpu.SemaphoreType.DMA((3, RETURNS)),
            pltpu.SemaphoreType.DMA((3, RETURNS)),
            pltpu.SemaphoreType.DMA((3,)),
            pltpu.SemaphoreType.DMA((3,)),
            pltpu.SemaphoreType.DMA((groups,)),
            pltpu.SemaphoreType.DMA((late, 2)),
            pltpu.SemaphoreType.DMA((early, 2)),
            pltpu.SemaphoreType.DMA((2 * late, size, 3)),
            pltpu.SemaphoreType.DMA((2 * late, size)),
            pltpu.SemaphoreType.DMA((2 * late,)),
        ]
        + scatter_semaphores(2 * early, outers),
        compiler_params=params(collective_id=1, has_side_effects=True),
    )(*operands)


def attend_back(packed, grad_mixed, logs, grad_packed, grad_keys, grad_values, between, done):
    zero = jnp.array(0, bf16)
    blocks = SEQ // QUERY_BWD

    def head_pair(pair):
        queries, keys, values = (
            slice(part * D + pair * PAIR, part * D + (pair + 1) * PAIR) for part in range(3)
        )
        key_rows, value_rows = packed[:, keys], packed[:, values]

        def block(index, _):
            rows = rows_at(index, QUERY_BWD)
            query_rows = packed[rows, queries] * jnp.array(HEAD_DIM**-0.5, bf16)
            grad_rows = grad_mixed[rows, queries]
            grad_query, part_keys, part_values = [], 0.0, 0.0
            for half in range(2):
                lanes = half_lanes(QUERY_BWD, half)
                own = jnp.where(lanes, query_rows, zero)
                own_grad = jnp.where(lanes, grad_rows, zero)
                head = 2 * pair + half
                probs = jnp.exp(dot_rt(key_rows, own) - logs[head : head + 1, rows])
                grad_probs = dot_rt(value_rows, own_grad)
                mean = jnp.sum(probs * grad_probs, axis=0, keepdims=True)
                grad_scores = (probs * (grad_probs - mean)).astype(bf16)
                part_values += dot(probs.astype(bf16), own_grad)
                part_keys += dot(grad_scores, own)
                grad_query.append(dot_lt(grad_scores, key_rows))
            grad_packed[rows, queries] = (
                jnp.where(half_lanes(QUERY_BWD, 0), grad_query[0], grad_query[1])
                * HEAD_DIM**-0.5
            ).astype(bf16)
            grad_keys[...] = jnp.where(index == 0, part_keys, grad_keys[...] + part_keys)
            grad_values[...] = jnp.where(index == 0, part_values, grad_values[...] + part_values)
            between(pair, index)
            return 0

        lax.fori_loop(0, blocks, block, 0)
        grad_packed[:, keys] = grad_keys[...].astype(bf16)
        grad_packed[:, values] = grad_values[...].astype(bf16)
        done(pair, (queries, keys, values))

    for pair in range(HEADS // 2):
        head_pair(pair)


def second_back(
    grad_rows, cotangent, gain, bias, mid, w_proj, router, grad_logits, grad_norm, grad_router, outs
):
    grad_mid, grad_low, grad_mixed = outs
    grad_norm[...] = jnp.zeros_like(grad_norm)
    grad_router[...] = jnp.zeros_like(grad_router)
    for index in range(SEQ // ROWS):
        rows = slice(index * ROWS, (index + 1) * ROWS)
        mid_rows = mid[rows, :]
        own_logits = grad_logits[:, rows]
        grad_in_rows = grad_rows(rows) + lax.dot_general(
            own_logits,
            router[...],
            (((0,), (0,)), ((), ())),
            precision=HIGHEST,
            preferred_element_type=f32,
        )
        grad_in, grad_gain, grad_bias, unit = norm_back(mid_rows, grad_in_rows, gain[1:2, :])
        grad_router[...] += jnp.dot(
            own_logits,
            unit * gain[1:2, :] + bias[1:2, :],
            precision=HIGHEST,
            preferred_element_type=f32,
        )
        grad_norm[1:2, :] += grad_gain
        grad_norm[3:4, :] += grad_bias
        grad_mid_rows = cotangent[rows, :] + grad_in
        grad_mid[rows, :] = grad_mid_rows
        low_rows = grad_mid_rows.astype(bf16)
        grad_low[rows, :] = low_rows
        grad_mixed[rows, :] = dot_rt(low_rows, w_proj[...]).astype(bf16)


def first_back(image, gain, w_qkv, grad_packed, grad_mid, grad_image, grad_norm):
    def block(index, _):
        rows = rows_at(index, ROWS)
        grad_rows = dot_rt(grad_packed[rows, :], w_qkv[...])
        grad_in, grad_gain, grad_bias, _ = norm_back(image[rows, :], grad_rows, gain[0:1, :])
        grad_image[rows, :] = grad_mid[rows, :] + grad_in
        grad_norm[0:1, :] += grad_gain
        grad_norm[2:3, :] += grad_bias
        return 0

    lax.fori_loop(0, SEQ // ROWS, block, 0)


def logit_grads(probs, grad_gates):
    route = jnp.concatenate([grad_gates[group] for group in range(grad_gates.shape[0])], axis=0)
    return probs[...] * (route - jnp.sum(probs[...] * route, axis=0, keepdims=True))


def backward_scratch():
    return [
        pltpu.VMEM((SEQ, D), f32),
        pltpu.VMEM((SEQ, D), bf16),
        pltpu.VMEM((SEQ, D), bf16),
        pltpu.VMEM((SEQ, 3 * D), bf16),
        pltpu.VMEM((SEQ, PAIR), f32),
        pltpu.VMEM((SEQ, PAIR), f32),
        pltpu.VMEM((SEQ, D), bf16),
    ]


def backward_kernel(*refs):
    image, cotangent, gain, bias, mid, w_qkv, w_proj, router = refs[:8]
    packed, mixed, logs, mixes, grad_normed, grad_gates, probs = refs[8:15]
    activations, grad_image, grad_norm, grad_router, grad_shared = refs[15:20]
    grad_mid, grad_low, grad_mixed, grad_packed, grad_keys, grad_values, normed_first = refs[20:]
    groups = mixes.shape[0]

    def added(parts, rows):
        total = parts[0, rows, :].astype(f32)
        for source in range(1, groups):
            total += parts[source, rows, :].astype(f32)
        return total

    activations[...] = mid[...] + added(mixes, slice(None))
    second_back(
        lambda rows: added(grad_normed, rows),
        cotangent,
        gain,
        bias,
        mid,
        w_proj,
        router,
        logit_grads(probs, grad_gates),
        grad_norm,
        grad_router,
        (grad_mid, grad_low, grad_mixed),
    )
    first_norm(image, gain, bias, normed_first)
    grad_shared[:, 3 * D :] = dot_lt(mixed[...], grad_low[...]).astype(bf16)
    attend_back(
        packed,
        grad_mixed,
        logs,
        grad_packed,
        grad_keys,
        grad_values,
        lambda pair, index: None,
        lambda pair, columns: None,
    )
    first_back(image, gain, w_qkv, grad_packed, grad_mid, grad_image, grad_norm)
    grad_shared[:, : 3 * D] = dot_lt(normed_first[...], grad_packed[...]).astype(bf16)


def backward_part(*operands):
    router = operands[7]
    return pl.pallas_call(
        backward_kernel,
        out_shape=(
            shape(SEQ, D),
            shape(SEQ, D),
            shape(4, D),
            shape(router.shape[0], D),
            shape(D, 4 * D, dtype=bf16),
        ),
        in_specs=[VMEM] * 15,
        out_specs=[VMEM] * 5,
        scratch_shapes=backward_scratch(),
        compiler_params=params(),
    )(*operands)


def backward_sending_kernel(outers, *refs):
    image, cotangent, gain, bias, mid, w_qkv, w_proj, router = refs[:8]
    packed, mixed, logs, mixes, grad_rows, grad_gates, probs, grad_in, grad_out = refs[8:17]
    activations, grad_image, grad_norm, grad_router, shard_qkv, shard_proj = refs[17:23]
    shard_in, shard_out = refs[23:25]
    grad_mid, grad_low, grad_mixed, grad_packed, grad_keys, grad_values, normed_first = refs[25:32]
    norm_sums, router_sums, shared = refs[32:35]
    land, joint, back_sent, back_landed = refs[35:39]
    in_bufs, out_bufs, shared_bufs = refs[39:42], refs[42:45], refs[45:48]
    scatter_sems = refs[48:52]
    norm_pair, router_pair, task_pair = refs[52:56], refs[56:60], refs[60:64]
    place = Place(outers)
    bits = [1 << step for step in range((2 * outers).bit_length() - 1)]
    place.greet(bits=bits[2:])
    count = grad_in.shape[0]

    def scatter(unit, block, size, bufs, at):
        return Scatter(
            place,
            block,
            size,
            *[buf.at[at] for buf in bufs],
            [sem.at[unit] for sem in scatter_sems],
        )

    big, stores = [], []
    for expert in range(count):
        for source, bufs, shard in ((grad_in, in_bufs, shard_in), (grad_out, out_bufs, shard_out)):
            big.append(
                scatter(
                    len(big),
                    lambda rows, source=source, expert=expert: source.at[expert, rows],
                    shard.shape[1],
                    bufs,
                    expert,
                )
            )

            def store(rows, shard=shard, expert=expert):
                shard[expert] = rows

            stores.append(store)
    pieces = HEADS // 2 + 1
    small = [
        scatter(
            len(big) + piece,
            lambda rows, piece=piece: shared.at[piece, rows],
            shard_proj.shape[0],
            shared_bufs,
            piece,
        )
        for piece in range(pieces)
    ]
    for unit in big:
        unit.start()
    back = Return(
        place, lambda source: mixes.at[source], 1, land, joint, back_sent, back_landed
    )
    back.by_core(0)
    back.to_core(0)
    second_back(
        lambda rows: grad_rows[rows, :],
        cotangent,
        gain,
        bias,
        mid,
        w_proj,
        router,
        logit_grads(probs, grad_gates),
        norm_sums,
        router_sums,
        (grad_mid, grad_low, grad_mixed),
    )
    back.to_across(0)
    first_norm(image, gain, bias, normed_first)
    shared[pieces - 1] = dot_lt(mixed[...], grad_low[...]).astype(bf16)
    small[pieces - 1].start()
    routers = PairSum(*router_pair)

    def between(pair, index):
        if pair == 1:
            for step, bit in enumerate(bits):

                @pl.when(index == step)
                def _():
                    if step:
                        rows = routers.take(step - 1, dp=place.partner(bits[step - 1]))
                    else:
                        rows = router_sums[...]
                    routers.give(step, rows, dp=place.partner(bit))

    def done(pair, columns):
        both = jnp.concatenate([grad_packed[:, part] for part in columns], axis=1)
        shared[pair] = dot_lt(normed_first[...], both).astype(bf16)
        small[pair].start()

    attend_back(
        packed, grad_mixed, logs, grad_packed, grad_keys, grad_values, between, done
    )
    first_back(image, gain, w_qkv, grad_packed, grad_mid, grad_image, norm_sums)
    norms = PairSum(*norm_pair)
    ways = [dict(dp=place.partner(bit)) for bit in bits]
    ways += [dict(task=place.core), dict(task=place.across)]
    norms.give(0, norm_sums[...], **ways[0])
    grad_router[...] = routers.take(len(bits) - 1, dp=place.partner(bits[-1]))
    activations[...] = mid[...] + back.finish(0)
    units = big + small
    for turn in range(len(units) + outers):
        if 0 < turn < len(ways):
            norms.give(turn, norms.take(turn - 1, **ways[turn - 1]), **ways[turn])
        for step in range(outers - 1):
            if 0 <= turn - step < len(units):
                units[turn - step].hop(step)
        if 0 <= turn - outers + 1 < len(big):
            big[turn - outers + 1].finish(stores[turn - outers + 1])
    grad_norm[...] = norms.take(len(ways) - 1, **ways[-1])
    tasks = PairSum(*task_pair)
    stage, land_task = task_pair[0], task_pair[1]
    for piece in range(pieces):

        def keep(rows, piece=piece):
            stage[0, :, piece * D : (piece + 1) * D] = rows.astype(bf16)

        small[piece].finish(keep)
    tasks.swap(0, task=place.core).start()
    rows = tasks.take(0, task=place.core)
    tasks.give(1, rows, task=place.across)
    rows = tasks.take(1, task=place.across)
    shard_proj[...] = rows[:, (pieces - 1) * D :]
    for pair in range(pieces - 1):
        for part in range(3):
            at = pair * D + part * PAIR
            shard_qkv[:, part * D + pair * PAIR : part * D + (pair + 1) * PAIR] = rows[
                :, at : at + PAIR
            ]


def backward_sending(*operands):
    router, grad_in = operands[7], operands[15]
    experts, size = router.shape[0], lax.axis_size("dp")
    outers, count = size // 2, grad_in.shape[0]
    thin, wide, pieces = D // size, FF // size, HEADS // 2 + 1
    units, steps = 2 * count + pieces, size.bit_length() - 1

    def pair_sum(steps, *dims, dtype=f32):
        return [pltpu.VMEM((steps, *dims), dtype)] * 2 + [pltpu.SemaphoreType.DMA((steps,))] * 2

    return pl.pallas_call(
        functools.partial(backward_sending_kernel, outers),
        out_shape=(
            shape(SEQ, D),
            shape(SEQ, D),
            shape(8, D),
            shape(experts, D),
            shape(thin, 3 * D),
            shape(thin, D),
            shape(count, thin, FF),
            shape(count, wide, D),
        ),
        in_specs=[VMEM] * 17,
        out_specs=[VMEM] * 8,
        scratch_shapes=backward_scratch()
        + [
            pltpu.VMEM((8, D), f32),
            pltpu.VMEM((experts, D), f32),
            pltpu.VMEM((pieces, D, D), bf16),
            pltpu.VMEM((3, SEQ, D), bf16),
            pltpu.VMEM((SEQ, D), bf16),
            pltpu.SemaphoreType.DMA((3, 1)),
            pltpu.SemaphoreType.DMA((3, 1)),
        ]
        + scatter_buffers(count, outers, thin, FF)
        + scatter_buffers(count, outers, wide, D)
        + scatter_buffers(pieces, outers, thin, D)
        + scatter_semaphores(units, outers)
        + pair_sum(steps + 2, 8, D)
        + pair_sum(steps, experts, D)
        + pair_sum(2, thin, 4 * D, dtype=bf16),
        compiler_params=params(collective_id=2, has_side_effects=True),
    )(*operands)


def local(
    layer_input,
    cotangent,
    norm_gain,
    norm_bias,
    w_qkv,
    w_proj,
    router,
    w_in,
    w_out,
    choices,
    top_count,
):
    groups = lax.axis_size("task")
    local_count = w_in.shape[0]
    image = layer_input.reshape(SEQ, D)
    grad_rows = cotangent.reshape(SEQ, D)
    router_rows = router[0].T
    experts = router_rows.shape[0]
    routes = choices.reshape(SEQ, TOPMAX)

    def swap(array):
        return lax.all_to_all(array, "task", split_axis=0, concat_axis=0, tiled=True)

    sending = groups == 4 and lax.axis_size("dp") in (4, 8) and w_in.shape[1] % 16 == 0
    if sending:
        (
            mid,
            packed,
            mixed,
            logs,
            probs,
            normed,
            cot_rows,
            slots,
            gates,
            full_qkv,
            full_proj,
            full_in,
            full_out,
        ) = forward_sending(
            top_count,
            image,
            grad_rows,
            norm_gain,
            norm_bias,
            (w_qkv, w_proj, w_in, w_out),
            router_rows,
            routes,
        )
        (
            late_in,
            late_out,
            grad_gates,
            mixes,
            grad_normed,
            early_in,
            early_out,
            _,
            _,
        ) = expert_sending(normed, cot_rows, slots, gates, full_in, full_out, w_in, w_out)
        (
            activations,
            grad_image,
            grad_norm,
            grad_router,
            grad_qkv,
            grad_proj,
            grad_in,
            grad_out,
        ) = backward_sending(
            image,
            grad_rows,
            norm_gain,
            norm_bias,
            mid,
            full_qkv,
            full_proj,
            router_rows,
            packed,
            mixed,
            logs,
            mixes,
            grad_normed,
            grad_gates,
            probs,
            late_in,
            late_out,
        )
        grad_in = jnp.concatenate([early_in, grad_in], axis=0)
        grad_out = jnp.concatenate([early_out, grad_out], axis=0)
    else:
        full_qkv, full_proj, full_in, full_out = (
            lax.all_gather(w_qkv, "dp", axis=0, tiled=True),
            lax.all_gather(w_proj, "dp", axis=0, tiled=True),
            lax.all_gather(w_in, "dp", axis=1, tiled=True),
            lax.all_gather(w_out, "dp", axis=1, tiled=True),
        )
        mid, packed, mixed, logs, normed, slots, gates, probs = forward_part(
            top_count,
            image,
            norm_gain,
            norm_bias,
            full_qkv,
            full_proj,
            router_rows,
            routes,
        )
        normed = lax.all_gather(normed, "task")
        cot_rows = lax.all_gather(grad_rows.astype(bf16), "task")
        slots = swap(slots.reshape(groups, local_count, SEQ))
        gates = swap(gates.reshape(groups, local_count, SEQ))
        grad_in, grad_out, grad_gates, mixes, grad_normed = expert_part(
            normed, cot_rows, slots, gates, full_in, full_out
        )
        activations, grad_image, grad_norm, grad_router, grad_shared = backward_part(
            image,
            grad_rows,
            norm_gain,
            norm_bias,
            mid,
            full_qkv,
            full_proj,
            router_rows,
            packed,
            mixed,
            logs,
            swap(mixes),
            swap(grad_normed),
            swap(grad_gates),
            probs,
        )
        grad_in = lax.psum_scatter(grad_in, "dp", scatter_dimension=1, tiled=True).astype(f32)
        grad_out = lax.psum_scatter(grad_out, "dp", scatter_dimension=1, tiled=True).astype(f32)
        grad_shared = lax.psum_scatter(grad_shared, "dp", scatter_dimension=0, tiled=True)
        grad_shared = lax.psum(grad_shared, "task").astype(f32)
        grad_qkv, grad_proj = grad_shared[:, : 3 * D], grad_shared[:, 3 * D :]
        grad_router = lax.psum(grad_router, "dp")
        grad_norm = lax.psum(grad_norm, ("task", "dp"))
    return (
        activations.reshape(layer_input.shape),
        grad_image.reshape(layer_input.shape),
        grad_norm[:2],
        grad_norm[2:4],
        grad_qkv,
        grad_proj,
        grad_router.T[None],
        grad_in,
        grad_out,
    )


def solution(mesh):
    tokens = P("task", "dp", None, None)
    rows = P("dp", None)
    blocks = P("task", "dp", None)
    routed = P("task", None, None)
    return jax.shard_map(
        local,
        mesh=mesh,
        in_specs=(tokens, tokens, P(), P(), rows, rows, routed, blocks, blocks, tokens, P("task")),
        out_specs=(tokens, tokens, P(), P(), rows, rows, routed, blocks, blocks),
        check_vma=False,
    )
```

```python
import functools

import jax
import jax.numpy as jnp
from jax import lax
from jax.experimental import pallas as pl
from jax.experimental.pallas import tpu as pltpu
from jax.sharding import PartitionSpec as P

D = 384
FF = 1536
HEADS = 6
HEAD_DIM = 64
PAIR = 2 * HEAD_DIM
TOPMAX = 4
SEQ = 1024
CAP = 320

f32 = jnp.float32
bf16 = jnp.bfloat16
HIGHEST = lax.Precision.HIGHEST
EPSILON = 1e-06
ROOT_HALF = 0.7071067811865476
NORMAL = 0.3989422804014327

FF_TILE = 512
ROW_TILE = 640
QUERY_FWD = 256
QUERY_BWD = 256
ROWS = 256
RETURNS = 2
TURNS = (3, 9)

VMEM = pl.BlockSpec(memory_space=pltpu.VMEM)
SMEM = pl.BlockSpec(memory_space=pltpu.SMEM)
ANY = pl.BlockSpec(memory_space=pl.ANY)


def shape(*dims, dtype=f32):
    return jax.ShapeDtypeStruct(dims, dtype)


def params(**more):
    return pltpu.CompilerParams(vmem_limit_bytes=62 * 2**20, **more)


def dot(a, b):
    return lax.dot_general(a, b, (((1,), (0,)), ((), ())), preferred_element_type=f32)


def dot_rt(a, b):
    return lax.dot_general(a, b, (((1,), (1,)), ((), ())), preferred_element_type=f32)


def dot_lt(a, b):
    return lax.dot_general(a, b, (((0,), (0,)), ((), ())), preferred_element_type=f32)


def rows_at(index, size):
    return pl.ds(pl.multiple_of(index * size, size), size)


def normalize(rows):
    centered = rows - jnp.mean(rows, axis=1, keepdims=True)
    scale = lax.rsqrt(jnp.mean(centered * centered, axis=1, keepdims=True) + EPSILON)
    return centered * scale, scale


def norm_back(rows, grad_rows, gain):
    unit, scale = normalize(rows)
    scaled = grad_rows * gain
    grad_in = scale * (
        scaled
        - jnp.mean(scaled, axis=1, keepdims=True)
        - unit * jnp.mean(scaled * unit, axis=1, keepdims=True)
    )
    grad_gain = jnp.sum(grad_rows * unit, axis=0, keepdims=True)
    return grad_in, grad_gain, jnp.sum(grad_rows, axis=0, keepdims=True), unit


def half_lanes(rows, half):
    lanes = lax.broadcasted_iota(jnp.int32, (rows, PAIR), 1)
    return (lanes < HEAD_DIM) if half == 0 else (lanes >= HEAD_DIM)


def remote(source, target, sent, landed, **device):
    return pltpu.make_async_remote_copy(
        src_ref=source,
        dst_ref=target,
        send_sem=sent,
        recv_sem=landed,
        device_id=device,
        device_id_type=pl.DeviceIdType.MESH,
    )


class Place:
    def __init__(self, outers):
        self.dp = lax.axis_index("dp")
        self.task = lax.axis_index("task")
        self.outers = outers
        self.outer, self.inner = self.dp // 2, self.dp % 2
        self.has_up, self.has_down = self.outer + 1 < outers, self.outer > 0
        self.up, self.down = self.dp + 2, self.dp - 2
        self.side = self.dp + 1 - 2 * self.inner
        self.core = self.task + 1 - 2 * (self.task % 2)
        self.across = self.task + 2 - 4 * (self.task // 2)
        self.far = self.across + 1 - 2 * (self.task % 2)

    def partner(self, bit):
        return self.dp + bit - 2 * bit * (self.dp // bit % 2)

    def greet(self, far=False, bits=()):
        barrier = pltpu.get_barrier_semaphore()

        def signal(**device):
            pl.semaphore_signal(
                barrier, inc=1, device_id=device, device_id_type=pl.DeviceIdType.MESH
            )

        pl.when(self.has_up)(lambda: signal(dp=self.up))
        pl.when(self.has_down)(lambda: signal(dp=self.down))
        signal(dp=self.side)
        signal(task=self.core)
        signal(task=self.across)
        if far:
            signal(task=self.far)
        for bit in bits:
            signal(dp=self.partner(bit))
        others = 3 + int(far) + len(bits)
        pl.semaphore_wait(
            barrier, others + self.has_up.astype(jnp.int32) + self.has_down.astype(jnp.int32)
        )


class Gather:
    def __init__(self, place, shards, sent, landed, stay):
        self.place, self.shards = place, shards
        self.sent, self.landed, self.stay = sent, landed, stay

    def move(self, unit, source, way, device, first=False):
        own, size, full = self.shards[unit]
        target = full.at[rows_at(source, size)]
        return remote(
            own if first else target,
            target,
            self.sent.at[unit, source, way],
            self.landed.at[unit, source],
            dp=device,
        )

    def local(self, unit):
        own, size, full = self.shards[unit]
        target = full.at[rows_at(self.place.dp, size)]
        return pltpu.make_async_copy(own, target, self.stay.at[unit])

    def start(self, unit):
        place = self.place
        pl.when(place.has_up)(lambda: self.move(unit, place.dp, 0, place.up, True).start())
        pl.when(place.has_down)(lambda: self.move(unit, place.dp, 1, place.down, True).start())
        self.move(unit, place.dp, 2, place.side, True).start()
        self.local(unit).start()

    def step(self, unit, hop):
        place = self.place

        @pl.when(place.outer >= hop)
        def _():
            source = place.dp - 2 * hop
            self.move(unit, source, 0, place.dp).wait_recv()
            pl.when(place.has_up)(lambda: self.move(unit, source, 0, place.up).start())
            self.move(unit, source, 2, place.side).start()

        @pl.when(place.outer + hop < place.outers)
        def _():
            source = place.dp + 2 * hop
            self.move(unit, source, 1, place.dp).wait_recv()
            pl.when(place.has_down)(lambda: self.move(unit, source, 1, place.down).start())
            self.move(unit, source, 2, place.side).start()

    def finish(self, unit):
        place = self.place
        self.local(unit).wait()
        for outer in range(place.outers):
            own, other = 2 * outer + place.inner, 2 * outer + 1 - place.inner
            self.move(unit, other, 2, place.dp).wait_recv()
            self.move(unit, own, 2, place.side).wait_send()
            pl.when((outer <= place.outer) & place.has_up)(
                lambda own=own: self.move(unit, own, 0, place.up).wait_send()
            )
            pl.when((outer >= place.outer) & place.has_down)(
                lambda own=own: self.move(unit, own, 1, place.down).wait_send()
            )


class Share:
    def __init__(self, place, view, sent, landed):
        self.place, self.view, self.sent, self.landed = place, view, sent, landed

    def move(self, source, way, **device):
        return remote(
            self.view(source),
            self.view(source),
            self.sent.at[way],
            self.landed.at[way],
            **device,
        )

    def start(self):
        place = self.place
        self.move(place.task, 0, task=place.across).start()
        self.move(place.task, 1, task=place.core).start()

    def relay(self):
        place = self.place
        self.move(place.across, 0, task=place.across).wait_recv()
        self.move(place.across, 2, task=place.core).start()

    def finish(self):
        place = self.place
        self.move(place.task, 0, task=place.across).wait_send()
        self.move(place.core, 1, task=place.core).wait()
        self.move(place.across, 2, task=place.core).wait()


class Scatter:
    def __init__(self, place, block, size, side, line, fold, sems):
        self.place, self.block, self.size = place, block, size
        self.side, self.line, self.fold = side, line, fold
        self.side_sent, self.side_landed, self.line_sent, self.line_landed = sems

    def own(self, outer, inner):
        return self.block(rows_at(2 * outer + inner, self.size))

    def to_side(self, outer):
        place = self.place
        return remote(
            self.own(outer, 1 - place.inner),
            self.side.at[outer],
            self.side_sent.at[outer],
            self.side_landed.at[outer],
            dp=place.side,
        )

    def along(self, outer, slot, device):
        return remote(
            self.fold.at[outer],
            self.line.at[slot],
            self.line_sent.at[outer],
            self.line_landed.at[slot],
            dp=device,
        )

    def start(self):
        outers = self.place.outers
        for near in range(outers // 2):
            self.to_side(outers - 1 - near).start()
            self.to_side(near).start()

    def total(self, outer, *slots):
        self.to_side(outer).wait_recv()
        rows = self.own(outer, self.place.inner)[...].astype(f32)
        rows += self.side[outer].astype(f32)
        for slot in slots:
            self.along(outer, slot, self.place.dp).wait_recv()
            rows += self.line[slot].astype(f32)
        return rows

    def hop(self, step):
        place, outers = self.place, self.place.outers

        @pl.when(place.outer == step)
        def _():
            for outer in range(outers - 1, step, -1):
                rows = self.total(outer, *([outer] if step else []))
                self.fold[outer] = rows.astype(bf16)
                self.along(outer, outer, place.up).start()

        @pl.when(place.outer == outers - 1 - step)
        def _():
            for outer in range(outers - 1 - step):
                rows = self.total(outer, *([outer] if step else []))
                self.fold[outer] = rows.astype(bf16)
                slot = outers if outer == outers - 2 - step else outer
                self.along(outer, slot, place.down).start()

    def finish(self, store):
        place, outers = self.place, self.place.outers
        for outer in range(outers):

            @pl.when(place.outer == outer)
            def _():
                below, above = [outer] * (outer > 0), [outers] * (outer < outers - 1)
                store(self.total(outer, *below, *above))
                for other in range(outers):
                    if other != outer:
                        self.along(other, other, place.dp).wait_send()

            self.to_side(outer).wait_send()


def scatter_turn(units, stores, turn):
    outers = units[0].place.outers
    for step in range(outers - 1):
        if 0 <= turn - step < len(units):
            units[turn - step].hop(step)
    last = turn - outers + 1
    if 0 <= last < len(units) and stores[last]:
        units[last].finish(stores[last])


class PairSum:
    def __init__(self, stage, land, sent, landed):
        self.stage, self.land, self.sent, self.landed = stage, land, sent, landed

    def swap(self, step, **device):
        return remote(
            self.stage.at[step],
            self.land.at[step],
            self.sent.at[step],
            self.landed.at[step],
            **device,
        )

    def give(self, step, rows, **device):
        self.stage[step] = rows.astype(self.stage.dtype)
        self.swap(step, **device).start()

    def take(self, step, **device):
        self.swap(step, **device).wait()
        return self.stage[step].astype(f32) + self.land[step].astype(f32)


class Return:
    def __init__(self, place, parts, pieces, land, joint, sent, landed):
        self.place, self.parts, self.pieces = place, parts, pieces
        self.land, self.joint, self.sent, self.landed = land, joint, sent, landed
        self.size = SEQ // pieces

    def rows(self, piece):
        return pl.ds(piece * self.size, self.size)

    def move(self, way, piece):
        place, rows = self.place, self.rows(piece)
        source = [
            self.parts(place.core).at[rows],
            self.parts(place.far).at[rows],
            self.joint.at[rows],
        ][way]
        return remote(
            source,
            self.land.at[way, rows],
            self.sent.at[way, piece],
            self.landed.at[way, piece],
            task=place.across if way == 2 else place.core,
        )

    def to_core(self, piece):
        self.move(0, piece).start()

    def by_core(self, piece):
        self.move(1, piece).start()

    def to_across(self, piece):
        rows = self.rows(piece)
        self.move(1, piece).wait_recv()
        joint = self.parts(self.place.across)[rows, :].astype(f32)
        joint += self.land[1, rows, :].astype(f32)
        self.joint[rows, :] = joint.astype(bf16)
        self.move(2, piece).start()

    def finish(self, piece):
        rows = self.rows(piece)
        self.move(0, piece).wait()
        self.move(1, piece).wait_send()
        self.move(2, piece).wait()
        total = self.parts(self.place.task)[rows, :].astype(f32)
        return total + self.land[0, rows, :].astype(f32) + self.land[2, rows, :].astype(f32)


def attend(packed, mixed, totals, index):
    zero = jnp.array(0, bf16)
    rows = rows_at(index, QUERY_FWD)

    def head_pair(pair, _):
        queries, keys, values = (rows_at(pair + part * (D // PAIR), PAIR) for part in range(3))
        key_rows, value_rows = packed[:, keys], packed[:, values]
        query_rows = packed[rows, queries] * jnp.array(HEAD_DIM**-0.5, bf16)
        outs, logs = [], []
        for half in range(2):
            own = jnp.where(half_lanes(QUERY_FWD, half), query_rows, zero)
            scores = dot_rt(own, key_rows)
            top = jnp.max(scores, axis=1, keepdims=True)
            weights = jnp.exp(scores - top)
            total = jnp.sum(weights, axis=1, keepdims=True)
            outs.append(dot(weights.astype(bf16), value_rows) * (1.0 / total))
            logs.append(top + jnp.log(total))
        mixed[rows, queries] = jnp.where(half_lanes(QUERY_FWD, 0), outs[0], outs[1]).astype(bf16)
        lanes = lax.broadcasted_iota(jnp.int32, (QUERY_FWD, 8), 1)
        totals[rows, :] = jnp.where(
            lanes == 2 * pair,
            logs[0],
            jnp.where(lanes == 2 * pair + 1, logs[1], totals[rows, :]),
        )
        return 0

    lax.fori_loop(0, HEADS // 2, head_pair, 0)


def first_norm(image, gain, bias, normed_first):
    def block(index, _):
        rows = rows_at(index, ROWS)
        unit, _ = normalize(image[rows, :])
        normed_first[rows, :] = (unit * gain[0:1, :] + bias[0:1, :]).astype(bf16)
        return 0

    lax.fori_loop(0, SEQ // ROWS, block, 0)


def number_slots(choices, top_count, experts):
    named = choices[...].T
    numbers = lax.broadcasted_iota(jnp.int32, (experts, SEQ), 0)
    used = jnp.zeros((experts, SEQ), f32)
    for choice in range(TOPMAX):
        hit = (named[choice : choice + 1, :] == numbers) & (choice < top_count[0])
        used = used + jnp.where(hit, 1.0, 0.0)
    earlier = lax.broadcasted_iota(jnp.int32, (SEQ, SEQ), 0) < lax.broadcasted_iota(
        jnp.int32, (SEQ, SEQ), 1
    )
    before = dot(used.astype(bf16), jnp.where(earlier, 1.0, 0.0).astype(bf16))
    return jnp.where(used > 0, before, -1.0).astype(jnp.int32)


def mid_block(index, image, gain, bias, w_proj, router, mixed, mid, probs):
    rows = rows_at(index, QUERY_FWD)
    mid_rows = image[rows, :] + dot(mixed[rows, :], w_proj[...])
    mid[rows, :] = mid_rows
    unit, _ = normalize(mid_rows)
    normed_rows = unit * gain[1:2, :] + bias[1:2, :]
    logits = lax.dot_general(
        router[...],
        normed_rows,
        (((1,), (1,)), ((), ())),
        precision=HIGHEST,
        preferred_element_type=f32,
    )
    powers = jnp.exp(logits - jnp.max(logits, axis=0, keepdims=True))
    probs[:, rows] = powers / jnp.sum(powers, axis=0, keepdims=True)
    return normed_rows.astype(bf16)


def forward_kernel(
    top_count,
    image,
    gain,
    bias,
    w_qkv,
    w_proj,
    router,
    choices,
    mid,
    packed,
    mixed,
    logs,
    normed,
    slots,
    gates,
    probs,
    normed_first,
    totals,
):
    first_norm(image, gain, bias, normed_first)
    slots[...] = number_slots(choices, top_count, router.shape[0])
    packed[...] = dot(normed_first[...], w_qkv[...]).astype(bf16)
    totals[...] = jnp.zeros_like(totals)

    def block(index, _):
        attend(packed, mixed, totals, index)
        normed[rows_at(index, QUERY_FWD), :] = mid_block(
            index, image, gain, bias, w_proj, router, mixed, mid, probs
        )
        return 0

    lax.fori_loop(0, SEQ // QUERY_FWD, block, 0)
    logs[...] = totals[...].T
    gates[...] = jnp.where(slots[...] >= 0, probs[...], 0.0)


def forward_part(top_count, image, gain, bias, w_qkv, w_proj, router, choices):
    experts = router.shape[0]
    return pl.pallas_call(
        forward_kernel,
        out_shape=(
            shape(SEQ, D),
            shape(SEQ, 3 * D, dtype=bf16),
            shape(SEQ, D, dtype=bf16),
            shape(8, SEQ),
            shape(SEQ, D, dtype=bf16),
            shape(experts, SEQ, dtype=jnp.int32),
            shape(experts, SEQ),
            shape(experts, SEQ),
        ),
        in_specs=[SMEM] + [VMEM] * 7,
        out_specs=[VMEM] * 8,
        scratch_shapes=[pltpu.VMEM((SEQ, D), bf16), pltpu.VMEM((SEQ, 8), f32)],
        compiler_params=params(),
    )(top_count, image, gain, bias, w_qkv, w_proj, router, choices)


def forward_sending_kernel(
    outers,
    top_count,
    image,
    cotangent,
    gain,
    bias,
    w_qkv,
    w_proj,
    w_in,
    w_out,
    router,
    choices,
    mid,
    packed,
    mixed,
    logs,
    probs,
    normed_all,
    cot_all,
    slots_all,
    gates_all,
    full_qkv,
    full_proj,
    full_in,
    full_out,
    normed_first,
    totals,
    sent,
    landed,
    stay,
    share_sent,
    share_landed,
):
    place = Place(outers)
    task = place.task
    shards = [(w_qkv, w_qkv.shape[0], full_qkv), (w_proj, w_proj.shape[0], full_proj)]
    for expert in range(full_in.shape[0]):
        shards += [
            (w_in.at[expert], w_in.shape[1], full_in.at[expert]),
            (w_out.at[expert], w_out.shape[1], full_out.at[expert]),
        ]
    gather = Gather(place, shards, sent, landed, stay)
    shared, routed = range(2), range(2, len(shards))
    cot_all[task] = cotangent[...].astype(bf16)
    place.greet()
    for unit in shared:
        gather.start(unit)

    def share(index, view):
        return Share(place, view, share_sent.at[index], share_landed.at[index])

    cot = share(0, lambda source: cot_all.at[source])
    slot = share(1, lambda source: slots_all.at[source])
    gate = share(2, lambda source: gates_all.at[source])
    cot.start()
    first_norm(image, gain, bias, normed_first)
    for hop in range(1, outers):
        for unit in shared:
            gather.step(unit, hop)
    for unit in routed:
        gather.start(unit)
    slots_all[task] = number_slots(choices, top_count, router.shape[0])
    slot.start()
    totals[...] = jnp.zeros_like(totals)
    for unit in shared:
        gather.finish(unit)
    packed[...] = dot(normed_first[...], full_qkv[...]).astype(bf16)
    cot.relay()
    slot.relay()

    def chunk(index):
        return share(3 + index, lambda source: normed_all.at[source, rows_at(index, QUERY_FWD)])

    blocks = SEQ // QUERY_FWD

    def block(index, _):
        attend(packed, mixed, totals, index)
        normed_all[task, rows_at(index, QUERY_FWD), :] = mid_block(
            index, image, gain, bias, full_proj, router, mixed, mid, probs
        )
        chunk(index).start()
        pl.when(index > 0)(lambda: chunk(index - 1).relay())
        for hop in range(1, outers):

            @pl.when(index == hop - 1)
            def _():
                for unit in routed:
                    gather.step(unit, hop)

        return 0

    lax.fori_loop(0, blocks, block, 0)
    for hop in range(blocks + 1, outers):
        for unit in routed:
            gather.step(unit, hop)
    gates_all[task] = jnp.where(slots_all[task] >= 0, probs[...], 0.0)
    gate.start()
    logs[...] = totals[...].T
    chunk(blocks - 1).relay()
    gate.relay()
    for one in [cot, slot, gate] + [chunk(index) for index in range(blocks)]:
        one.finish()
    for unit in routed:
        gather.finish(unit)


def forward_sending(top_count, image, cotangent, gain, bias, shards, router, choices):
    w_qkv, w_proj, w_in, w_out = shards
    experts, size = router.shape[0], lax.axis_size("dp")
    groups, early = lax.axis_size("task"), w_in.shape[0] // 2
    units, shares = 2 + 2 * early, 3 + SEQ // QUERY_FWD
    return pl.pallas_call(
        functools.partial(forward_sending_kernel, size // 2),
        out_shape=(
            shape(SEQ, D),
            shape(SEQ, 3 * D, dtype=bf16),
            shape(SEQ, D, dtype=bf16),
            shape(8, SEQ),
            shape(experts, SEQ),
            shape(groups, SEQ, D, dtype=bf16),
            shape(groups, SEQ, D, dtype=bf16),
            shape(groups, experts, SEQ, dtype=jnp.int32),
            shape(groups, experts, SEQ),
            shape(D, 3 * D, dtype=bf16),
            shape(D, D, dtype=bf16),
            shape(early, D, FF, dtype=bf16),
            shape(early, FF, D, dtype=bf16),
        ),
        in_specs=[SMEM] + [VMEM] * 6 + [ANY] * 2 + [VMEM] * 2,
        out_specs=[VMEM] * 11 + [ANY] * 2,
        scratch_shapes=[
            pltpu.VMEM((SEQ, D), bf16),
            pltpu.VMEM((SEQ, 8), f32),
            pltpu.SemaphoreType.DMA((units, size, 3)),
            pltpu.SemaphoreType.DMA((units, size)),
            pltpu.SemaphoreType.DMA((units,)),
            pltpu.SemaphoreType.DMA((shares, 3)),
            pltpu.SemaphoreType.DMA((shares, 3)),
        ],
        compiler_params=params(collective_id=0, has_side_effects=True),
    )(top_count, image, cotangent, gain, bias, w_qkv, w_proj, w_in, w_out, router, choices)


def slot_hits(slots, source, expert):
    return lax.broadcasted_iota(jnp.int32, (CAP, SEQ), 0) == slots[source, pl.ds(expert, 1), :]


def ones_at(hits):
    return jnp.where(hits, 1.0, 0.0).astype(bf16)


def one_expert(operands, work, grads, expert, first, slot, between):
    normed, cotangent, slots, gates, w_in, w_out = operands
    rows_in, rows_grad, rows_cot, rows_gate, hidden, grad_pre, sent = work
    grad_in, grad_out, grad_gates = grads
    groups = normed.shape[0]
    width = groups * CAP
    for source in range(groups):
        own = slice(source * CAP, (source + 1) * CAP)
        hits = slot_hits(slots, source, first + expert)
        picks = ones_at(hits)
        rows_in[own, :] = dot(picks, normed[source]).astype(bf16)
        cot_rows = dot(picks, cotangent[source])
        gate = jnp.sum(
            jnp.where(hits, gates[source, pl.ds(first + expert, 1), :], 0.0),
            axis=1,
            keepdims=True,
        )
        rows_cot[own, :] = cot_rows.astype(bf16)
        rows_grad[own, :] = (gate * cot_rows).astype(bf16)
        rows_gate[own, :] = jnp.broadcast_to(gate, (CAP, 128))
    between(0)

    def tile(index, _):
        units = rows_at(index // (width // ROW_TILE), FF_TILE)
        rows = rows_at(lax.rem(index, width // ROW_TILE), ROW_TILE)
        pre = dot(rows_in[rows, :], w_in[slot, :, units])
        grad_hidden = dot_rt(rows_grad[rows, :], w_out[slot, units, :])
        share = 0.5 * lax.erf(pre * ROOT_HALF) + 0.5
        slope = share + pre * (NORMAL * jnp.exp(-0.5 * pre * pre))
        hidden[rows, units] = (pre * share).astype(bf16)
        grad_pre[rows, units] = (grad_hidden * slope).astype(bf16)
        return 0

    lax.fori_loop(0, (FF // FF_TILE) * (width // ROW_TILE), tile, 0)
    between(1)
    for source in range(groups):
        own = slice(source * CAP, (source + 1) * CAP)
        kept = rows_at(expert, CAP)
        out_rows = dot(hidden[own, :], w_out[slot]).astype(bf16).astype(f32)
        sent[source, kept, :D] = (rows_gate[own, 0:1] * out_rows).astype(bf16)
        sent[source, kept, D:] = dot_rt(grad_pre[own, :], w_in[slot]).astype(bf16)
        grad_gate = jnp.sum(rows_cot[own, :].astype(f32) * out_rows, axis=1, keepdims=True)
        hits = slot_hits(slots, source, first + expert)
        grad_gates[source, pl.ds(expert, 1), :] = jnp.sum(
            jnp.where(hits, grad_gate, 0.0), axis=0, keepdims=True
        )
    between(2)
    grad_in[expert] = dot_lt(rows_in[...], grad_pre[...]).astype(bf16)
    grad_out[expert] = dot_lt(rows_grad[...], hidden[...]).astype(bf16).T
    between(3)


def combine(slots, first, local_count, sent, columns, source, store):
    size = SEQ // RETURNS
    columns[...] = slots[source].T
    for piece in range(RETURNS):
        rows = pl.ds(piece * size, size)
        lanes = lax.broadcasted_iota(jnp.int32, (size, CAP), 1)
        mine = lax.broadcasted_iota(jnp.int32, (size, columns.shape[1]), 1)
        picks = []
        for expert in range(local_count):
            column = jnp.max(
                jnp.where(mine == first + expert, columns[rows, :], -1), axis=1, keepdims=True
            )
            picks.append(ones_at(lanes == column))
        back = dot(jnp.concatenate(picks, axis=1), sent[source])
        store(piece, rows, back[:, :D].astype(bf16), back[:, D:].astype(bf16))


def expert_scratch(groups, local_count, experts):
    width = groups * CAP
    return [
        pltpu.VMEM((width, D), bf16),
        pltpu.VMEM((width, D), bf16),
        pltpu.VMEM((width, D), bf16),
        pltpu.VMEM((width, 128), f32),
        pltpu.VMEM((width, FF), bf16),
        pltpu.VMEM((width, FF), bf16),
        pltpu.VMEM((groups, local_count * CAP, 2 * D), bf16),
        pltpu.VMEM((SEQ, experts), jnp.int32),
    ]


def expert_kernel(*refs):
    operands, grads, (mixes, grad_normed) = refs[:6], refs[6:9], refs[9:11]
    work, columns = refs[11:18], refs[18]
    groups, local_count = operands[0].shape[0], operands[4].shape[0]

    def body(expert, _):
        one_expert(operands, work, grads, expert, 0, expert, lambda point: None)
        return 0

    lax.fori_loop(0, local_count, body, 0)
    for source in range(groups):

        def store(piece, rows, mix, grad, source=source):
            mixes[source, rows, :] = mix
            grad_normed[source, rows, :] = grad

        combine(operands[2], 0, local_count, work[6], columns, source, store)


def expert_part(*operands):
    groups, local_count = operands[0].shape[0], operands[4].shape[0]
    return pl.pallas_call(
        expert_kernel,
        out_shape=(
            shape(local_count, D, FF, dtype=bf16),
            shape(local_count, FF, D, dtype=bf16),
            shape(groups, local_count, SEQ),
            shape(groups, SEQ, D, dtype=bf16),
            shape(groups, SEQ, D, dtype=bf16),
        ),
        in_specs=[VMEM] * 6,
        out_specs=[VMEM] * 5,
        scratch_shapes=expert_scratch(groups, local_count, operands[2].shape[1]),
        compiler_params=params(),
    )(*operands)


def expert_sending_kernel(outers, early, *refs):
    normed, cotangent, slots, gates, early_in, early_out, w_in, w_out = refs[:8]
    late_in, late_out, gate_all, mixes, grad_rows, shard_in, shard_out = refs[8:15]
    full_in, full_out = refs[15:17]
    work, columns = refs[17:24], refs[24]
    slot_in, slot_out, grad_in, grad_out, grad_gates, land = refs[25:31]
    in_bufs, out_bufs = refs[31:34], refs[34:37]
    sent, landed, gate_sent, gate_landed, mix_sem, late_sem, slot_sem = refs[37:44]
    gather_sems, scatter_sems = refs[44:47], refs[47:51]
    place = Place(outers)
    local_count, size = grad_in.shape[0], 2 * outers
    late = local_count - early
    first = place.task * local_count
    place.greet(far=True)

    shards = []
    for expert in range(late):
        shards += [
            (w_in.at[early + expert], w_in.shape[1], full_in.at[expert]),
            (w_out.at[early + expert], w_out.shape[1], full_out.at[expert]),
        ]
    gather = Gather(place, shards, *gather_sems)
    for unit in range(len(shards)):
        gather.start(unit)

    def load(source, expert, slot):
        return [
            pltpu.make_async_copy(source[0].at[expert], slot_in.at[slot], slot_sem.at[slot, 0]),
            pltpu.make_async_copy(source[1].at[expert], slot_out.at[slot], slot_sem.at[slot, 1]),
        ]

    for expert in range(early):
        for copy in load((early_in, early_out), expert, expert):
            copy.start()

    scatters, stores = [], []
    for expert in range(early):
        for source, bufs, shard in ((grad_in, in_bufs, shard_in), (grad_out, out_bufs, shard_out)):
            unit = len(scatters)
            scatters.append(
                Scatter(
                    place,
                    lambda rows, source=source, expert=expert: source.at[expert, rows],
                    shard.shape[1],
                    *[buf.at[expert] for buf in bufs],
                    [sem.at[unit] for sem in scatter_sems],
                )
            )

            def store(rows, shard=shard, expert=expert):
                shard[expert] = rows

            stores.append(store)

    def keep(expert):
        return [
            pltpu.make_async_copy(
                grad_in.at[early + expert], late_in.at[expert], late_sem.at[expert, 0]
            ),
            pltpu.make_async_copy(
                grad_out.at[early + expert], late_out.at[expert], late_sem.at[expert, 1]
            ),
        ]

    def plan(expert, point):
        steps = []
        if point == 0:
            if expert < early:
                steps += [copy.wait for copy in load((early_in, early_out), expert, expert)]
            else:
                steps += [
                    copy.wait
                    for copy in load((full_in, full_out), expert - early, expert - early)
                ]
        if expert == 0:
            for unit in range(len(shards)):
                hop = point - unit // 2 + 1
                if 0 < hop < outers:
                    steps.append(lambda unit=unit, hop=hop: gather.step(unit, hop))
        if expert == 1 and point == 0:
            for unit in range(len(shards)):
                for hop in range(5 - unit // 2, outers):
                    steps.append(lambda unit=unit, hop=hop: gather.step(unit, hop))
        if point == 3:
            if expert < early:
                steps += [scatters[2 * expert].start, scatters[2 * expert + 1].start]
            else:
                steps += [copy.start for copy in keep(expert - early)]
        if expert == local_count - 1 and point in (0, 2):
            steps.append(lambda: scatter_turn(scatters, stores, point // 2))
        return steps

    def body(expert, _):
        @pl.when(expert >= early)
        def _():
            for other in range(late):

                @pl.when(expert == early + other)
                def _():
                    gather.finish(2 * other)
                    gather.finish(2 * other + 1)
                    for copy in load((full_in, full_out), other, other):
                        copy.start()

        def between(point):
            for at in range(local_count):
                steps = plan(at, point)
                if steps:

                    @pl.when(expert == at)
                    def _():
                        for step in steps:
                            step()

        one_expert(
            (normed, cotangent, slots, gates, slot_in, slot_out),
            work,
            (grad_in, grad_out, grad_gates),
            expert,
            first,
            lax.rem(expert, early),
            between,
        )
        return 0

    lax.fori_loop(0, local_count, body, 0)
    gate_all[place.task] = grad_gates[place.task]
    peers = (place.core, place.across, place.far)

    def gate_move(way):
        return remote(
            grad_gates.at[peers[way]],
            gate_all.at[place.task],
            gate_sent.at[way],
            gate_landed.at[way],
            task=peers[way],
        )

    for way in range(3):
        gate_move(way).start()
    hidden, grad_pre, joint = work[4], work[5], work[2]

    def part(ref, source):
        return ref.at[pl.ds(0, SEQ), pl.ds(pl.multiple_of(source * D, 128), D)]

    back = Return(
        place, lambda source: part(hidden, source), RETURNS, land, joint, sent, landed
    )
    for order, (source, after) in enumerate(
        (
            (place.far, back.by_core),
            (place.across, back.to_across),
            (place.core, back.to_core),
            (place.task, None),
        )
    ):

        def store(piece, rows, mix, grad, source=source, after=after):
            part(grad_pre, source)[rows, :] = mix
            part(hidden, source)[rows, :] = grad
            if after:
                after(piece)

        combine(slots, first, local_count, work[6], columns, source, store)
        if order:
            scatter_turn(scatters, stores, 1 + order)
    keeps = [
        pltpu.make_async_copy(part(grad_pre, source), mixes.at[source], mix_sem.at[source])
        for source in range(mixes.shape[0])
    ]
    for copy in keeps:
        copy.start()
    for turn in range(5, len(scatters) + outers):
        scatter_turn(scatters, stores, turn)
    for piece in range(RETURNS):
        grad_rows[back.rows(piece), :] = back.finish(piece)
    for way in range(3):
        gate_move(way).wait()
    for copy in keeps:
        copy.wait()
    for expert in range(late):
        for copy in keep(expert):
            copy.wait()


def scatter_buffers(number, outers, *dims):
    return [pltpu.VMEM((number, slots, *dims), bf16) for slots in (outers, outers + 1, outers)]


def scatter_semaphores(units, outers):
    return [pltpu.SemaphoreType.DMA((units, outers))] * 3 + [
        pltpu.SemaphoreType.DMA((units, outers + 1))
    ]


def expert_sending(*operands):
    groups, experts = operands[2].shape[:2]
    local_count, thin = operands[6].shape[:2]
    wide, early = operands[7].shape[1], operands[4].shape[0]
    late, size = local_count - early, lax.axis_size("dp")
    outers = size // 2
    return pl.pallas_call(
        functools.partial(expert_sending_kernel, outers, early),
        out_shape=(
            shape(late, D, FF, dtype=bf16),
            shape(late, FF, D, dtype=bf16),
            shape(groups, local_count, SEQ),
            shape(groups, SEQ, D, dtype=bf16),
            shape(SEQ, D),
            shape(early, thin, FF),
            shape(early, wide, D),
            shape(late, D, FF, dtype=bf16),
            shape(late, FF, D, dtype=bf16),
        ),
        in_specs=[VMEM] * 4 + [ANY] * 4,
        out_specs=[ANY] * 2 + [VMEM, ANY, VMEM, VMEM, VMEM] + [ANY] * 2,
        scratch_shapes=expert_scratch(groups, local_count, experts)
        + [
            pltpu.VMEM((early, D, FF), bf16),
            pltpu.VMEM((early, FF, D), bf16),
            pltpu.VMEM((local_count, D, FF), bf16),
            pltpu.VMEM((local_count, FF, D), bf16),
            pltpu.VMEM((groups, local_count, SEQ), f32),
            pltpu.VMEM((3, SEQ, D), bf16),
        ]
        + scatter_buffers(early, outers, thin, FF)
        + scatter_buffers(early, outers, wide, D)
        + [
            pltpu.SemaphoreType.DMA((3, RETURNS)),
            pltpu.SemaphoreType.DMA((3, RETURNS)),
            pltpu.SemaphoreType.DMA((3,)),
            pltpu.SemaphoreType.DMA((3,)),
            pltpu.SemaphoreType.DMA((groups,)),
            pltpu.SemaphoreType.DMA((late, 2)),
            pltpu.SemaphoreType.DMA((early, 2)),
            pltpu.SemaphoreType.DMA((2 * late, size, 3)),
            pltpu.SemaphoreType.DMA((2 * late, size)),
            pltpu.SemaphoreType.DMA((2 * late,)),
        ]
        + scatter_semaphores(2 * early, outers),
        compiler_params=params(collective_id=1, has_side_effects=True),
    )(*operands)


def attend_back(packed, grad_mixed, logs, grad_packed, grad_keys, grad_values, between, done):
    zero = jnp.array(0, bf16)
    blocks = SEQ // QUERY_BWD

    def head_pair(pair):
        queries, keys, values = (
            slice(part * D + pair * PAIR, part * D + (pair + 1) * PAIR) for part in range(3)
        )
        key_rows, value_rows = packed[:, keys], packed[:, values]

        def block(index, _):
            rows = rows_at(index, QUERY_BWD)
            query_rows = packed[rows, queries] * jnp.array(HEAD_DIM**-0.5, bf16)
            grad_rows = grad_mixed[rows, queries]
            grad_query, part_keys, part_values = [], 0.0, 0.0
            for half in range(2):
                lanes = half_lanes(QUERY_BWD, half)
                own = jnp.where(lanes, query_rows, zero)
                own_grad = jnp.where(lanes, grad_rows, zero)
                head = 2 * pair + half
                probs = jnp.exp(dot_rt(key_rows, own) - logs[head : head + 1, rows])
                grad_probs = dot_rt(value_rows, own_grad)
                mean = jnp.sum(probs * grad_probs, axis=0, keepdims=True)
                grad_scores = (probs * (grad_probs - mean)).astype(bf16)
                part_values += dot(probs.astype(bf16), own_grad)
                part_keys += dot(grad_scores, own)
                grad_query.append(dot_lt(grad_scores, key_rows))
            grad_packed[rows, queries] = (
                jnp.where(half_lanes(QUERY_BWD, 0), grad_query[0], grad_query[1])
                * HEAD_DIM**-0.5
            ).astype(bf16)
            grad_keys[...] = jnp.where(index == 0, part_keys, grad_keys[...] + part_keys)
            grad_values[...] = jnp.where(index == 0, part_values, grad_values[...] + part_values)
            between(pair, index)
            return 0

        lax.fori_loop(0, blocks, block, 0)
        grad_packed[:, keys] = grad_keys[...].astype(bf16)
        grad_packed[:, values] = grad_values[...].astype(bf16)
        done(pair, (queries, keys, values))

    for pair in range(HEADS // 2):
        head_pair(pair)


def second_back(
    grad_rows, cotangent, gain, bias, mid, w_proj, router, grad_logits, grad_norm, grad_router, outs
):
    grad_mid, grad_low, grad_mixed = outs
    grad_norm[...] = jnp.zeros_like(grad_norm)
    grad_router[...] = jnp.zeros_like(grad_router)
    for index in range(SEQ // ROWS):
        rows = slice(index * ROWS, (index + 1) * ROWS)
        mid_rows = mid[rows, :]
        own_logits = grad_logits[:, rows]
        grad_in_rows = grad_rows(rows) + lax.dot_general(
            own_logits,
            router[...],
            (((0,), (0,)), ((), ())),
            precision=HIGHEST,
            preferred_element_type=f32,
        )
        grad_in, grad_gain, grad_bias, unit = norm_back(mid_rows, grad_in_rows, gain[1:2, :])
        grad_router[...] += jnp.dot(
            own_logits,
            unit * gain[1:2, :] + bias[1:2, :],
            precision=HIGHEST,
            preferred_element_type=f32,
        )
        grad_norm[1:2, :] += grad_gain
        grad_norm[3:4, :] += grad_bias
        grad_mid_rows = cotangent[rows, :] + grad_in
        grad_mid[rows, :] = grad_mid_rows
        low_rows = grad_mid_rows.astype(bf16)
        grad_low[rows, :] = low_rows
        grad_mixed[rows, :] = dot_rt(low_rows, w_proj[...]).astype(bf16)


def first_back(image, gain, w_qkv, grad_packed, grad_mid, grad_image, grad_norm):
    def block(index, _):
        rows = rows_at(index, ROWS)
        grad_rows = dot_rt(grad_packed[rows, :], w_qkv[...])
        grad_in, grad_gain, grad_bias, _ = norm_back(image[rows, :], grad_rows, gain[0:1, :])
        grad_image[rows, :] = grad_mid[rows, :] + grad_in
        grad_norm[0:1, :] += grad_gain
        grad_norm[2:3, :] += grad_bias
        return 0

    lax.fori_loop(0, SEQ // ROWS, block, 0)


def logit_grads(probs, grad_gates):
    route = jnp.concatenate([grad_gates[group] for group in range(grad_gates.shape[0])], axis=0)
    return probs[...] * (route - jnp.sum(probs[...] * route, axis=0, keepdims=True))


def backward_scratch():
    return [
        pltpu.VMEM((SEQ, D), f32),
        pltpu.VMEM((SEQ, D), bf16),
        pltpu.VMEM((SEQ, D), bf16),
        pltpu.VMEM((SEQ, 3 * D), bf16),
        pltpu.VMEM((SEQ, PAIR), f32),
        pltpu.VMEM((SEQ, PAIR), f32),
        pltpu.VMEM((SEQ, D), bf16),
    ]


def backward_kernel(*refs):
    image, cotangent, gain, bias, mid, w_qkv, w_proj, router = refs[:8]
    packed, mixed, logs, mixes, grad_normed, grad_gates, probs = refs[8:15]
    activations, grad_image, grad_norm, grad_router, grad_shared = refs[15:20]
    grad_mid, grad_low, grad_mixed, grad_packed, grad_keys, grad_values, normed_first = refs[20:]
    groups = mixes.shape[0]

    def added(parts, rows):
        total = parts[0, rows, :].astype(f32)
        for source in range(1, groups):
            total += parts[source, rows, :].astype(f32)
        return total

    activations[...] = mid[...] + added(mixes, slice(None))
    second_back(
        lambda rows: added(grad_normed, rows),
        cotangent,
        gain,
        bias,
        mid,
        w_proj,
        router,
        logit_grads(probs, grad_gates),
        grad_norm,
        grad_router,
        (grad_mid, grad_low, grad_mixed),
    )
    first_norm(image, gain, bias, normed_first)
    grad_shared[:, 3 * D :] = dot_lt(mixed[...], grad_low[...]).astype(bf16)
    attend_back(
        packed,
        grad_mixed,
        logs,
        grad_packed,
        grad_keys,
        grad_values,
        lambda pair, index: None,
        lambda pair, columns: None,
    )
    first_back(image, gain, w_qkv, grad_packed, grad_mid, grad_image, grad_norm)
    grad_shared[:, : 3 * D] = dot_lt(normed_first[...], grad_packed[...]).astype(bf16)


def backward_part(*operands):
    router = operands[7]
    return pl.pallas_call(
        backward_kernel,
        out_shape=(
            shape(SEQ, D),
            shape(SEQ, D),
            shape(4, D),
            shape(router.shape[0], D),
            shape(D, 4 * D, dtype=bf16),
        ),
        in_specs=[VMEM] * 15,
        out_specs=[VMEM] * 5,
        scratch_shapes=backward_scratch(),
        compiler_params=params(),
    )(*operands)


def backward_sending_kernel(outers, *refs):
    image, cotangent, gain, bias, mid, w_qkv, w_proj, router = refs[:8]
    packed, mixed, logs, mixes, grad_rows, grad_gates, probs, grad_in, grad_out = refs[8:17]
    activations, grad_image, grad_norm, grad_router, shard_qkv, shard_proj = refs[17:23]
    shard_in, shard_out = refs[23:25]
    grad_mid, grad_low, grad_mixed, grad_packed, grad_keys, grad_values, normed_first = refs[25:32]
    norm_sums, router_sums, shared = refs[32:35]
    land, joint, back_sent, back_landed = refs[35:39]
    in_bufs, out_bufs, shared_bufs = refs[39:42], refs[42:45], refs[45:48]
    scatter_sems = refs[48:52]
    norm_pair, router_pair, task_pair = refs[52:56], refs[56:60], refs[60:64]
    place = Place(outers)
    bits = [1 << step for step in range((2 * outers).bit_length() - 1)]
    place.greet(bits=bits[2:])
    count = grad_in.shape[0]

    def scatter(unit, block, size, bufs, at):
        return Scatter(
            place,
            block,
            size,
            *[buf.at[at] for buf in bufs],
            [sem.at[unit] for sem in scatter_sems],
        )

    big, stores = [], []
    for expert in range(count):
        for source, bufs, shard in ((grad_in, in_bufs, shard_in), (grad_out, out_bufs, shard_out)):
            big.append(
                scatter(
                    len(big),
                    lambda rows, source=source, expert=expert: source.at[expert, rows],
                    shard.shape[1],
                    bufs,
                    expert,
                )
            )

            def store(rows, shard=shard, expert=expert):
                shard[expert] = rows

            stores.append(store)
    pieces = HEADS // 2 + 1
    small = [
        scatter(
            len(big) + piece,
            lambda rows, piece=piece: shared.at[piece, rows],
            shard_proj.shape[0],
            shared_bufs,
            piece,
        )
        for piece in range(pieces)
    ]
    for unit in big:
        unit.start()
    back = Return(
        place, lambda source: mixes.at[source], 1, land, joint, back_sent, back_landed
    )
    back.by_core(0)
    back.to_core(0)
    second_back(
        lambda rows: grad_rows[rows, :],
        cotangent,
        gain,
        bias,
        mid,
        w_proj,
        router,
        logit_grads(probs, grad_gates),
        norm_sums,
        router_sums,
        (grad_mid, grad_low, grad_mixed),
    )
    back.to_across(0)
    first_norm(image, gain, bias, normed_first)
    shared[pieces - 1] = dot_lt(mixed[...], grad_low[...]).astype(bf16)
    small[pieces - 1].start()
    routers = PairSum(*router_pair)
    blocks = SEQ // QUERY_BWD

    units, keeps = big + small, stores + [None] * pieces

    def between(pair, index):
        for turn, at in enumerate(TURNS):
            if at // blocks == pair:
                pl.when(index == at % blocks)(lambda turn=turn: scatter_turn(units, keeps, turn))
        if pair == 1:
            for step, bit in enumerate(bits):

                @pl.when(index == step)
                def _():
                    if step:
                        rows = routers.take(step - 1, dp=place.partner(bits[step - 1]))
                    else:
                        rows = router_sums[...]
                    routers.give(step, rows, dp=place.partner(bit))

    def done(pair, columns):
        both = jnp.concatenate([grad_packed[:, part] for part in columns], axis=1)
        shared[pair] = dot_lt(normed_first[...], both).astype(bf16)
        small[pair].start()

    attend_back(
        packed, grad_mixed, logs, grad_packed, grad_keys, grad_values, between, done
    )
    first_back(image, gain, w_qkv, grad_packed, grad_mid, grad_image, norm_sums)
    norms = PairSum(*norm_pair)
    ways = [dict(dp=place.partner(bit)) for bit in bits]
    ways += [dict(task=place.core), dict(task=place.across)]
    norms.give(0, norm_sums[...], **ways[0])
    grad_router[...] = routers.take(len(bits) - 1, dp=place.partner(bits[-1]))
    activations[...] = mid[...] + back.finish(0)
    for turn in range(len(TURNS), len(units) + outers):
        step = turn - len(TURNS) + 1
        if step < len(ways):
            norms.give(step, norms.take(step - 1, **ways[step - 1]), **ways[step])
        scatter_turn(units, keeps, turn)
    grad_norm[...] = norms.take(len(ways) - 1, **ways[-1])
    tasks = PairSum(*task_pair)
    stage, land_task = task_pair[0], task_pair[1]
    for piece in range(pieces):

        def keep(rows, piece=piece):
            stage[0, :, piece * D : (piece + 1) * D] = rows.astype(bf16)

        small[piece].finish(keep)
    tasks.swap(0, task=place.core).start()
    rows = tasks.take(0, task=place.core)
    tasks.give(1, rows, task=place.across)
    rows = tasks.take(1, task=place.across)
    shard_proj[...] = rows[:, (pieces - 1) * D :]
    for pair in range(pieces - 1):
        for part in range(3):
            at = pair * D + part * PAIR
            shard_qkv[:, part * D + pair * PAIR : part * D + (pair + 1) * PAIR] = rows[
                :, at : at + PAIR
            ]


def backward_sending(*operands):
    router, grad_in = operands[7], operands[15]
    experts, size = router.shape[0], lax.axis_size("dp")
    outers, count = size // 2, grad_in.shape[0]
    thin, wide, pieces = D // size, FF // size, HEADS // 2 + 1
    units, steps = 2 * count + pieces, size.bit_length() - 1

    def pair_sum(steps, *dims, dtype=f32):
        return [pltpu.VMEM((steps, *dims), dtype)] * 2 + [pltpu.SemaphoreType.DMA((steps,))] * 2

    return pl.pallas_call(
        functools.partial(backward_sending_kernel, outers),
        out_shape=(
            shape(SEQ, D),
            shape(SEQ, D),
            shape(8, D),
            shape(experts, D),
            shape(thin, 3 * D),
            shape(thin, D),
            shape(count, thin, FF),
            shape(count, wide, D),
        ),
        in_specs=[VMEM] * 17,
        out_specs=[VMEM] * 8,
        scratch_shapes=backward_scratch()
        + [
            pltpu.VMEM((8, D), f32),
            pltpu.VMEM((experts, D), f32),
            pltpu.VMEM((pieces, D, D), bf16),
            pltpu.VMEM((3, SEQ, D), bf16),
            pltpu.VMEM((SEQ, D), bf16),
            pltpu.SemaphoreType.DMA((3, 1)),
            pltpu.SemaphoreType.DMA((3, 1)),
        ]
        + scatter_buffers(count, outers, thin, FF)
        + scatter_buffers(count, outers, wide, D)
        + scatter_buffers(pieces, outers, thin, D)
        + scatter_semaphores(units, outers)
        + pair_sum(steps + 2, 8, D)
        + pair_sum(steps, experts, D)
        + pair_sum(2, thin, 4 * D, dtype=bf16),
        compiler_params=params(collective_id=2, has_side_effects=True),
    )(*operands)


def local(
    layer_input,
    cotangent,
    norm_gain,
    norm_bias,
    w_qkv,
    w_proj,
    router,
    w_in,
    w_out,
    choices,
    top_count,
):
    groups = lax.axis_size("task")
    local_count = w_in.shape[0]
    image = layer_input.reshape(SEQ, D)
    grad_rows = cotangent.reshape(SEQ, D)
    router_rows = router[0].T
    experts = router_rows.shape[0]
    routes = choices.reshape(SEQ, TOPMAX)

    def swap(array):
        return lax.all_to_all(array, "task", split_axis=0, concat_axis=0, tiled=True)

    sending = groups == 4 and lax.axis_size("dp") in (4, 8) and w_in.shape[1] % 16 == 0
    if sending:
        (
            mid,
            packed,
            mixed,
            logs,
            probs,
            normed,
            cot_rows,
            slots,
            gates,
            full_qkv,
            full_proj,
            full_in,
            full_out,
        ) = forward_sending(
            top_count,
            image,
            grad_rows,
            norm_gain,
            norm_bias,
            (w_qkv, w_proj, w_in, w_out),
            router_rows,
            routes,
        )
        (
            late_in,
            late_out,
            grad_gates,
            mixes,
            grad_normed,
            early_in,
            early_out,
            _,
            _,
        ) = expert_sending(normed, cot_rows, slots, gates, full_in, full_out, w_in, w_out)
        (
            activations,
            grad_image,
            grad_norm,
            grad_router,
            grad_qkv,
            grad_proj,
            grad_in,
            grad_out,
        ) = backward_sending(
            image,
            grad_rows,
            norm_gain,
            norm_bias,
            mid,
            full_qkv,
            full_proj,
            router_rows,
            packed,
            mixed,
            logs,
            mixes,
            grad_normed,
            grad_gates,
            probs,
            late_in,
            late_out,
        )
        grad_in = jnp.concatenate([early_in, grad_in], axis=0)
        grad_out = jnp.concatenate([early_out, grad_out], axis=0)
    else:
        full_qkv, full_proj, full_in, full_out = (
            lax.all_gather(w_qkv, "dp", axis=0, tiled=True),
            lax.all_gather(w_proj, "dp", axis=0, tiled=True),
            lax.all_gather(w_in, "dp", axis=1, tiled=True),
            lax.all_gather(w_out, "dp", axis=1, tiled=True),
        )
        mid, packed, mixed, logs, normed, slots, gates, probs = forward_part(
            top_count,
            image,
            norm_gain,
            norm_bias,
            full_qkv,
            full_proj,
            router_rows,
            routes,
        )
        normed = lax.all_gather(normed, "task")
        cot_rows = lax.all_gather(grad_rows.astype(bf16), "task")
        slots = swap(slots.reshape(groups, local_count, SEQ))
        gates = swap(gates.reshape(groups, local_count, SEQ))
        grad_in, grad_out, grad_gates, mixes, grad_normed = expert_part(
            normed, cot_rows, slots, gates, full_in, full_out
        )
        activations, grad_image, grad_norm, grad_router, grad_shared = backward_part(
            image,
            grad_rows,
            norm_gain,
            norm_bias,
            mid,
            full_qkv,
            full_proj,
            router_rows,
            packed,
            mixed,
            logs,
            swap(mixes),
            swap(grad_normed),
            swap(grad_gates),
            probs,
        )
        grad_in = lax.psum_scatter(grad_in, "dp", scatter_dimension=1, tiled=True).astype(f32)
        grad_out = lax.psum_scatter(grad_out, "dp", scatter_dimension=1, tiled=True).astype(f32)
        grad_shared = lax.psum_scatter(grad_shared, "dp", scatter_dimension=0, tiled=True)
        grad_shared = lax.psum(grad_shared, "task").astype(f32)
        grad_qkv, grad_proj = grad_shared[:, : 3 * D], grad_shared[:, 3 * D :]
        grad_router = lax.psum(grad_router, "dp")
        grad_norm = lax.psum(grad_norm, ("task", "dp"))
    return (
        activations.reshape(layer_input.shape),
        grad_image.reshape(layer_input.shape),
        grad_norm[:2],
        grad_norm[2:4],
        grad_qkv,
        grad_proj,
        grad_router.T[None],
        grad_in,
        grad_out,
    )


def solution(mesh):
    tokens = P("task", "dp", None, None)
    rows = P("dp", None)
    blocks = P("task", "dp", None)
    routed = P("task", None, None)
    return jax.shard_map(
        local,
        mesh=mesh,
        in_specs=(tokens, tokens, P(), P(), rows, rows, routed, blocks, blocks, tokens, P("task")),
        out_specs=(tokens, tokens, P(), P(), rows, rows, routed, blocks, blocks),
        check_vma=False,
    )
```

```python
import functools

import jax
import jax.numpy as jnp
from jax import lax
from jax.experimental import pallas as pl
from jax.experimental.pallas import tpu as pltpu
from jax.sharding import PartitionSpec as P

D = 384
FF = 1536
HEADS = 6
HEAD_DIM = 64
PAIR = 2 * HEAD_DIM
TOPMAX = 4
SEQ = 1024
CAP = 320

f32 = jnp.float32
bf16 = jnp.bfloat16
HIGHEST = lax.Precision.HIGHEST
EPSILON = 1e-06
ROOT_HALF = 0.7071067811865476
NORMAL = 0.3989422804014327

FF_TILE = 512
ROW_TILE = 640
QUERY_FWD = 256
QUERY_BWD = 256
ROWS = 256
RETURNS = 2
TURNS = (2, 5, 8, 11)

VMEM = pl.BlockSpec(memory_space=pltpu.VMEM)
SMEM = pl.BlockSpec(memory_space=pltpu.SMEM)
ANY = pl.BlockSpec(memory_space=pl.ANY)


def shape(*dims, dtype=f32):
    return jax.ShapeDtypeStruct(dims, dtype)


def params(**more):
    return pltpu.CompilerParams(vmem_limit_bytes=62 * 2**20, **more)


def dot(a, b):
    return lax.dot_general(a, b, (((1,), (0,)), ((), ())), preferred_element_type=f32)


def dot_rt(a, b):
    return lax.dot_general(a, b, (((1,), (1,)), ((), ())), preferred_element_type=f32)


def dot_lt(a, b):
    return lax.dot_general(a, b, (((0,), (0,)), ((), ())), preferred_element_type=f32)


def rows_at(index, size):
    return pl.ds(pl.multiple_of(index * size, size), size)


def normalize(rows):
    centered = rows - jnp.mean(rows, axis=1, keepdims=True)
    scale = lax.rsqrt(jnp.mean(centered * centered, axis=1, keepdims=True) + EPSILON)
    return centered * scale, scale


def norm_back(rows, grad_rows, gain):
    unit, scale = normalize(rows)
    scaled = grad_rows * gain
    grad_in = scale * (
        scaled
        - jnp.mean(scaled, axis=1, keepdims=True)
        - unit * jnp.mean(scaled * unit, axis=1, keepdims=True)
    )
    grad_gain = jnp.sum(grad_rows * unit, axis=0, keepdims=True)
    return grad_in, grad_gain, jnp.sum(grad_rows, axis=0, keepdims=True), unit


def half_lanes(rows, half):
    lanes = lax.broadcasted_iota(jnp.int32, (rows, PAIR), 1)
    return (lanes < HEAD_DIM) if half == 0 else (lanes >= HEAD_DIM)


def remote(source, target, sent, landed, **device):
    return pltpu.make_async_remote_copy(
        src_ref=source,
        dst_ref=target,
        send_sem=sent,
        recv_sem=landed,
        device_id=device,
        device_id_type=pl.DeviceIdType.MESH,
    )


class Place:
    def __init__(self, outers):
        self.dp = lax.axis_index("dp")
        self.task = lax.axis_index("task")
        self.outers = outers
        self.outer, self.inner = self.dp // 2, self.dp % 2
        self.has_up, self.has_down = self.outer + 1 < outers, self.outer > 0
        self.up, self.down = self.dp + 2, self.dp - 2
        self.side = self.dp + 1 - 2 * self.inner
        self.core = self.task + 1 - 2 * (self.task % 2)
        self.across = self.task + 2 - 4 * (self.task // 2)
        self.far = self.across + 1 - 2 * (self.task % 2)

    def signal(self, **device):
        pl.semaphore_signal(
            pltpu.get_barrier_semaphore(),
            inc=1,
            device_id=device,
            device_id_type=pl.DeviceIdType.MESH,
        )

    def greet(self, far=False):
        pl.when(self.has_up)(lambda: self.signal(dp=self.up))
        pl.when(self.has_down)(lambda: self.signal(dp=self.down))
        self.signal(dp=self.side)
        self.signal(task=self.core)
        self.signal(task=self.across)
        if far:
            self.signal(task=self.far)
        others = 3 + int(far) + self.has_up.astype(jnp.int32) + self.has_down.astype(jnp.int32)
        pl.semaphore_wait(pltpu.get_barrier_semaphore(), others)

    def greet_all(self, groups):
        size = 2 * self.outers
        for ahead in range(1, size):
            self.signal(dp=lax.rem(self.dp + ahead, size))
        for ahead in range(1, groups):
            self.signal(task=lax.rem(self.task + ahead, groups))
        pl.semaphore_wait(pltpu.get_barrier_semaphore(), size + groups - 2)


class Gather:
    def __init__(self, place, shards, sent, landed, stay):
        self.place, self.shards = place, shards
        self.sent, self.landed, self.stay = sent, landed, stay

    def move(self, unit, source, way, device, first=False):
        own, size, full = self.shards[unit]
        target = full.at[rows_at(source, size)]
        return remote(
            own if first else target,
            target,
            self.sent.at[unit, source, way],
            self.landed.at[unit, source],
            dp=device,
        )

    def local(self, unit):
        own, size, full = self.shards[unit]
        target = full.at[rows_at(self.place.dp, size)]
        return pltpu.make_async_copy(own, target, self.stay.at[unit])

    def start(self, unit):
        place = self.place
        pl.when(place.has_up)(lambda: self.move(unit, place.dp, 0, place.up, True).start())
        pl.when(place.has_down)(lambda: self.move(unit, place.dp, 1, place.down, True).start())
        self.move(unit, place.dp, 2, place.side, True).start()
        self.local(unit).start()

    def step(self, unit, hop):
        place = self.place

        @pl.when(place.outer >= hop)
        def _():
            source = place.dp - 2 * hop
            self.move(unit, source, 0, place.dp).wait_recv()
            pl.when(place.has_up)(lambda: self.move(unit, source, 0, place.up).start())
            self.move(unit, source, 2, place.side).start()

        @pl.when(place.outer + hop < place.outers)
        def _():
            source = place.dp + 2 * hop
            self.move(unit, source, 1, place.dp).wait_recv()
            pl.when(place.has_down)(lambda: self.move(unit, source, 1, place.down).start())
            self.move(unit, source, 2, place.side).start()

    def finish(self, unit):
        place = self.place
        self.local(unit).wait()
        for outer in range(place.outers):
            own, other = 2 * outer + place.inner, 2 * outer + 1 - place.inner
            self.move(unit, other, 2, place.dp).wait_recv()
            self.move(unit, own, 2, place.side).wait_send()
            pl.when((outer <= place.outer) & place.has_up)(
                lambda own=own: self.move(unit, own, 0, place.up).wait_send()
            )
            pl.when((outer >= place.outer) & place.has_down)(
                lambda own=own: self.move(unit, own, 1, place.down).wait_send()
            )


class Share:
    def __init__(self, place, view, sent, landed):
        self.place, self.view, self.sent, self.landed = place, view, sent, landed

    def move(self, source, way, **device):
        return remote(
            self.view(source),
            self.view(source),
            self.sent.at[way],
            self.landed.at[way],
            **device,
        )

    def start(self):
        place = self.place
        self.move(place.task, 0, task=place.across).start()
        self.move(place.task, 1, task=place.core).start()

    def relay(self):
        place = self.place
        self.move(place.across, 0, task=place.across).wait_recv()
        self.move(place.across, 2, task=place.core).start()

    def finish(self):
        place = self.place
        self.move(place.task, 0, task=place.across).wait_send()
        self.move(place.core, 1, task=place.core).wait()
        self.move(place.across, 2, task=place.core).wait()


class Scatter:
    def __init__(self, place, block, size, side, line, fold, sems):
        self.place, self.block, self.size = place, block, size
        self.side, self.line, self.fold = side, line, fold
        self.side_sent, self.side_landed, self.line_sent, self.line_landed = sems

    def own(self, outer, inner):
        return self.block(rows_at(2 * outer + inner, self.size))

    def to_side(self, outer):
        place = self.place
        return remote(
            self.own(outer, 1 - place.inner),
            self.side.at[outer],
            self.side_sent.at[outer],
            self.side_landed.at[outer],
            dp=place.side,
        )

    def along(self, outer, slot, device):
        return remote(
            self.fold.at[outer],
            self.line.at[slot],
            self.line_sent.at[outer],
            self.line_landed.at[slot],
            dp=device,
        )

    def start(self):
        outers = self.place.outers
        for near in range(outers // 2):
            self.to_side(outers - 1 - near).start()
            self.to_side(near).start()

    def total(self, outer, *slots):
        self.to_side(outer).wait_recv()
        rows = self.own(outer, self.place.inner)[...].astype(f32)
        rows += self.side[outer].astype(f32)
        for slot in slots:
            self.along(outer, slot, self.place.dp).wait_recv()
            rows += self.line[slot].astype(f32)
        return rows

    def hop(self, step):
        place, outers = self.place, self.place.outers

        @pl.when(place.outer == step)
        def _():
            for outer in range(outers - 1, step, -1):
                rows = self.total(outer, *([outer] if step else []))
                self.fold[outer] = rows.astype(bf16)
                self.along(outer, outer, place.up).start()

        @pl.when(place.outer == outers - 1 - step)
        def _():
            for outer in range(outers - 1 - step):
                rows = self.total(outer, *([outer] if step else []))
                self.fold[outer] = rows.astype(bf16)
                slot = outers if outer == outers - 2 - step else outer
                self.along(outer, slot, place.down).start()

    def finish(self, store):
        place, outers = self.place, self.place.outers
        for outer in range(outers):

            @pl.when(place.outer == outer)
            def _():
                below, above = [outer] * (outer > 0), [outers] * (outer < outers - 1)
                store(self.total(outer, *below, *above))
                for other in range(outers):
                    if other != outer:
                        self.along(other, other, place.dp).wait_send()

            self.to_side(outer).wait_send()


def scatter_turn(units, stores, turn):
    outers = units[0].place.outers
    for step in range(outers - 1):
        if 0 <= turn - step < len(units):
            units[turn - step].hop(step)
    last = turn - outers + 1
    if 0 <= last < len(units):
        units[last].finish(stores[last])


class Spread:
    def __init__(self, axis, place, count, land, sent, landed):
        self.axis, self.me, self.count = axis, getattr(place, axis), count
        self.land, self.sent, self.landed = land, sent, landed

    def move(self, source, ahead):
        return remote(
            self.land.at[source],
            self.land.at[source],
            self.sent.at[ahead - 1],
            self.landed.at[ahead - 1],
            **{self.axis: lax.rem(self.me + ahead, self.count)},
        )

    def give(self, rows):
        self.land[self.me] = rows.astype(self.land.dtype)
        for ahead in range(1, self.count):
            self.move(self.me, ahead).start()

    def take(self):
        for ahead in range(1, self.count):
            self.move(lax.rem(self.me + self.count - ahead, self.count), ahead).wait_recv()
            self.move(self.me, ahead).wait_send()
        total = self.land[0].astype(f32)
        for index in range(1, self.count):
            total += self.land[index].astype(f32)
        return total


class Return:
    def __init__(self, place, parts, pieces, land, joint, sent, landed):
        self.place, self.parts, self.pieces = place, parts, pieces
        self.land, self.joint, self.sent, self.landed = land, joint, sent, landed
        self.size = SEQ // pieces

    def rows(self, piece):
        return pl.ds(piece * self.size, self.size)

    def move(self, way, piece):
        place, rows = self.place, self.rows(piece)
        source = [
            self.parts(place.core).at[rows],
            self.parts(place.far).at[rows],
            self.joint.at[rows],
        ][way]
        return remote(
            source,
            self.land.at[way, rows],
            self.sent.at[way, piece],
            self.landed.at[way, piece],
            task=place.across if way == 2 else place.core,
        )

    def to_core(self, piece):
        self.move(0, piece).start()

    def by_core(self, piece):
        self.move(1, piece).start()

    def to_across(self, piece):
        rows = self.rows(piece)
        self.move(1, piece).wait_recv()
        joint = self.parts(self.place.across)[rows, :].astype(f32)
        joint += self.land[1, rows, :].astype(f32)
        self.joint[rows, :] = joint.astype(bf16)
        self.move(2, piece).start()

    def finish(self, piece):
        rows = self.rows(piece)
        self.move(0, piece).wait()
        self.move(1, piece).wait_send()
        self.move(2, piece).wait()
        total = self.parts(self.place.task)[rows, :].astype(f32)
        return total + self.land[0, rows, :].astype(f32) + self.land[2, rows, :].astype(f32)


def attend(packed, mixed, totals, index):
    zero = jnp.array(0, bf16)
    rows = rows_at(index, QUERY_FWD)

    def head_pair(pair, _):
        queries, keys, values = (rows_at(pair + part * (D // PAIR), PAIR) for part in range(3))
        key_rows, value_rows = packed[:, keys], packed[:, values]
        query_rows = packed[rows, queries] * jnp.array(HEAD_DIM**-0.5, bf16)
        outs, logs = [], []
        for half in range(2):
            own = jnp.where(half_lanes(QUERY_FWD, half), query_rows, zero)
            scores = dot_rt(own, key_rows)
            top = jnp.max(scores, axis=1, keepdims=True)
            weights = jnp.exp(scores - top)
            total = jnp.sum(weights, axis=1, keepdims=True)
            outs.append(dot(weights.astype(bf16), value_rows) * (1.0 / total))
            logs.append(top + jnp.log(total))
        mixed[rows, queries] = jnp.where(half_lanes(QUERY_FWD, 0), outs[0], outs[1]).astype(bf16)
        lanes = lax.broadcasted_iota(jnp.int32, (QUERY_FWD, 8), 1)
        totals[rows, :] = jnp.where(
            lanes == 2 * pair,
            logs[0],
            jnp.where(lanes == 2 * pair + 1, logs[1], totals[rows, :]),
        )
        return 0

    lax.fori_loop(0, HEADS // 2, head_pair, 0)


def first_norm(image, gain, bias, normed_first):
    def block(index, _):
        rows = rows_at(index, ROWS)
        unit, _ = normalize(image[rows, :])
        normed_first[rows, :] = (unit * gain[0:1, :] + bias[0:1, :]).astype(bf16)
        return 0

    lax.fori_loop(0, SEQ // ROWS, block, 0)


def number_slots(choices, top_count, experts):
    named = choices[...].T
    numbers = lax.broadcasted_iota(jnp.int32, (experts, SEQ), 0)
    used = jnp.zeros((experts, SEQ), f32)
    for choice in range(TOPMAX):
        hit = (named[choice : choice + 1, :] == numbers) & (choice < top_count[0])
        used = used + jnp.where(hit, 1.0, 0.0)
    earlier = lax.broadcasted_iota(jnp.int32, (SEQ, SEQ), 0) < lax.broadcasted_iota(
        jnp.int32, (SEQ, SEQ), 1
    )
    before = dot(used.astype(bf16), jnp.where(earlier, 1.0, 0.0).astype(bf16))
    return jnp.where(used > 0, before, -1.0).astype(jnp.int32)


def mid_block(index, image, gain, bias, w_proj, router, mixed, mid, probs):
    rows = rows_at(index, QUERY_FWD)
    mid_rows = image[rows, :] + dot(mixed[rows, :], w_proj[...])
    mid[rows, :] = mid_rows
    unit, _ = normalize(mid_rows)
    normed_rows = unit * gain[1:2, :] + bias[1:2, :]
    logits = lax.dot_general(
        router[...],
        normed_rows,
        (((1,), (1,)), ((), ())),
        precision=HIGHEST,
        preferred_element_type=f32,
    )
    powers = jnp.exp(logits - jnp.max(logits, axis=0, keepdims=True))
    probs[:, rows] = powers / jnp.sum(powers, axis=0, keepdims=True)
    return normed_rows.astype(bf16)


def forward_kernel(
    top_count,
    image,
    gain,
    bias,
    w_qkv,
    w_proj,
    router,
    choices,
    mid,
    packed,
    mixed,
    logs,
    normed,
    slots,
    gates,
    probs,
    normed_first,
    totals,
):
    first_norm(image, gain, bias, normed_first)
    slots[...] = number_slots(choices, top_count, router.shape[0])
    packed[...] = dot(normed_first[...], w_qkv[...]).astype(bf16)
    totals[...] = jnp.zeros_like(totals)

    def block(index, _):
        attend(packed, mixed, totals, index)
        normed[rows_at(index, QUERY_FWD), :] = mid_block(
            index, image, gain, bias, w_proj, router, mixed, mid, probs
        )
        return 0

    lax.fori_loop(0, SEQ // QUERY_FWD, block, 0)
    logs[...] = totals[...].T
    gates[...] = jnp.where(slots[...] >= 0, probs[...], 0.0)


def forward_part(top_count, image, gain, bias, w_qkv, w_proj, router, choices):
    experts = router.shape[0]
    return pl.pallas_call(
        forward_kernel,
        out_shape=(
            shape(SEQ, D),
            shape(SEQ, 3 * D, dtype=bf16),
            shape(SEQ, D, dtype=bf16),
            shape(8, SEQ),
            shape(SEQ, D, dtype=bf16),
            shape(experts, SEQ, dtype=jnp.int32),
            shape(experts, SEQ),
            shape(experts, SEQ),
        ),
        in_specs=[SMEM] + [VMEM] * 7,
        out_specs=[VMEM] * 8,
        scratch_shapes=[pltpu.VMEM((SEQ, D), bf16), pltpu.VMEM((SEQ, 8), f32)],
        compiler_params=params(),
    )(top_count, image, gain, bias, w_qkv, w_proj, router, choices)


def forward_sending_kernel(
    outers,
    top_count,
    image,
    cotangent,
    gain,
    bias,
    w_qkv,
    w_proj,
    w_in,
    w_out,
    router,
    choices,
    mid,
    packed,
    mixed,
    logs,
    probs,
    normed_all,
    cot_all,
    slots_all,
    gates_all,
    full_qkv,
    full_proj,
    full_in,
    full_out,
    normed_first,
    totals,
    sent,
    landed,
    stay,
    share_sent,
    share_landed,
):
    place = Place(outers)
    task = place.task
    shards = [(w_qkv, w_qkv.shape[0], full_qkv), (w_proj, w_proj.shape[0], full_proj)]
    for expert in range(full_in.shape[0]):
        shards += [
            (w_in.at[expert], w_in.shape[1], full_in.at[expert]),
            (w_out.at[expert], w_out.shape[1], full_out.at[expert]),
        ]
    gather = Gather(place, shards, sent, landed, stay)
    shared, routed = range(2), range(2, len(shards))
    cot_all[task] = cotangent[...].astype(bf16)
    place.greet()
    for unit in shared:
        gather.start(unit)

    def share(index, view):
        return Share(place, view, share_sent.at[index], share_landed.at[index])

    cot = share(0, lambda source: cot_all.at[source])
    slot = share(1, lambda source: slots_all.at[source])
    gate = share(2, lambda source: gates_all.at[source])
    cot.start()
    first_norm(image, gain, bias, normed_first)
    for hop in range(1, outers):
        for unit in shared:
            gather.step(unit, hop)
    for unit in routed:
        gather.start(unit)
    slots_all[task] = number_slots(choices, top_count, router.shape[0])
    slot.start()
    totals[...] = jnp.zeros_like(totals)
    for unit in shared:
        gather.finish(unit)
    packed[...] = dot(normed_first[...], full_qkv[...]).astype(bf16)
    cot.relay()
    slot.relay()

    def chunk(index):
        return share(3 + index, lambda source: normed_all.at[source, rows_at(index, QUERY_FWD)])

    blocks = SEQ // QUERY_FWD

    def block(index, _):
        attend(packed, mixed, totals, index)
        normed_all[task, rows_at(index, QUERY_FWD), :] = mid_block(
            index, image, gain, bias, full_proj, router, mixed, mid, probs
        )
        chunk(index).start()
        pl.when(index > 0)(lambda: chunk(index - 1).relay())
        for hop in range(1, outers):

            @pl.when(index == hop - 1)
            def _():
                for unit in routed:
                    gather.step(unit, hop)

        return 0

    lax.fori_loop(0, blocks, block, 0)
    for hop in range(blocks + 1, outers):
        for unit in routed:
            gather.step(unit, hop)
    gates_all[task] = jnp.where(slots_all[task] >= 0, probs[...], 0.0)
    gate.start()
    logs[...] = totals[...].T
    chunk(blocks - 1).relay()
    gate.relay()
    for one in [cot, slot, gate] + [chunk(index) for index in range(blocks)]:
        one.finish()
    for unit in routed:
        gather.finish(unit)


def forward_sending(top_count, image, cotangent, gain, bias, shards, router, choices):
    w_qkv, w_proj, w_in, w_out = shards
    experts, size = router.shape[0], lax.axis_size("dp")
    groups, early = lax.axis_size("task"), w_in.shape[0] // 2
    units, shares = 2 + 2 * early, 3 + SEQ // QUERY_FWD
    return pl.pallas_call(
        functools.partial(forward_sending_kernel, size // 2),
        out_shape=(
            shape(SEQ, D),
            shape(SEQ, 3 * D, dtype=bf16),
            shape(SEQ, D, dtype=bf16),
            shape(8, SEQ),
            shape(experts, SEQ),
            shape(groups, SEQ, D, dtype=bf16),
            shape(groups, SEQ, D, dtype=bf16),
            shape(groups, experts, SEQ, dtype=jnp.int32),
            shape(groups, experts, SEQ),
            shape(D, 3 * D, dtype=bf16),
            shape(D, D, dtype=bf16),
            shape(early, D, FF, dtype=bf16),
            shape(early, FF, D, dtype=bf16),
        ),
        in_specs=[SMEM] + [VMEM] * 6 + [ANY] * 2 + [VMEM] * 2,
        out_specs=[VMEM] * 11 + [ANY] * 2,
        scratch_shapes=[
            pltpu.VMEM((SEQ, D), bf16),
            pltpu.VMEM((SEQ, 8), f32),
            pltpu.SemaphoreType.DMA((units, size, 3)),
            pltpu.SemaphoreType.DMA((units, size)),
            pltpu.SemaphoreType.DMA((units,)),
            pltpu.SemaphoreType.DMA((shares, 3)),
            pltpu.SemaphoreType.DMA((shares, 3)),
        ],
        compiler_params=params(collective_id=0, has_side_effects=True),
    )(top_count, image, cotangent, gain, bias, w_qkv, w_proj, w_in, w_out, router, choices)


def slot_hits(slots, source, expert):
    return lax.broadcasted_iota(jnp.int32, (CAP, SEQ), 0) == slots[source, pl.ds(expert, 1), :]


def ones_at(hits):
    return jnp.where(hits, 1.0, 0.0).astype(bf16)


def one_expert(operands, work, grads, expert, first, slot, between):
    normed, cotangent, slots, gates, w_in, w_out = operands
    rows_in, rows_grad, rows_cot, rows_gate, hidden, grad_pre, sent = work
    grad_in, grad_out, grad_gates = grads
    groups = normed.shape[0]
    width = groups * CAP
    for source in range(groups):
        own = slice(source * CAP, (source + 1) * CAP)
        hits = slot_hits(slots, source, first + expert)
        picks = ones_at(hits)
        rows_in[own, :] = dot(picks, normed[source]).astype(bf16)
        cot_rows = dot(picks, cotangent[source])
        gate = jnp.sum(
            jnp.where(hits, gates[source, pl.ds(first + expert, 1), :], 0.0),
            axis=1,
            keepdims=True,
        )
        rows_cot[own, :] = cot_rows.astype(bf16)
        rows_grad[own, :] = (gate * cot_rows).astype(bf16)
        rows_gate[own, :] = jnp.broadcast_to(gate, (CAP, 128))
    between(0)

    def tile(index, _):
        units = rows_at(index // (width // ROW_TILE), FF_TILE)
        rows = rows_at(lax.rem(index, width // ROW_TILE), ROW_TILE)
        pre = dot(rows_in[rows, :], w_in[slot, :, units])
        grad_hidden = dot_rt(rows_grad[rows, :], w_out[slot, units, :])
        share = 0.5 * lax.erf(pre * ROOT_HALF) + 0.5
        slope = share + pre * (NORMAL * jnp.exp(-0.5 * pre * pre))
        hidden[rows, units] = (pre * share).astype(bf16)
        grad_pre[rows, units] = (grad_hidden * slope).astype(bf16)
        return 0

    lax.fori_loop(0, (FF // FF_TILE) * (width // ROW_TILE), tile, 0)
    between(1)
    for source in range(groups):
        own = slice(source * CAP, (source + 1) * CAP)
        kept = rows_at(expert, CAP)
        out_rows = dot(hidden[own, :], w_out[slot]).astype(bf16).astype(f32)
        sent[source, kept, :D] = (rows_gate[own, 0:1] * out_rows).astype(bf16)
        sent[source, kept, D:] = dot_rt(grad_pre[own, :], w_in[slot]).astype(bf16)
        grad_gate = jnp.sum(rows_cot[own, :].astype(f32) * out_rows, axis=1, keepdims=True)
        hits = slot_hits(slots, source, first + expert)
        grad_gates[source, pl.ds(expert, 1), :] = jnp.sum(
            jnp.where(hits, grad_gate, 0.0), axis=0, keepdims=True
        )
    between(2)
    grad_in[expert] = dot_lt(rows_in[...], grad_pre[...]).astype(bf16)
    grad_out[expert] = dot_lt(rows_grad[...], hidden[...]).astype(bf16).T
    between(3)


def combine(slots, first, local_count, sent, columns, source, store):
    size = SEQ // RETURNS
    columns[...] = slots[source].T
    for piece in range(RETURNS):
        rows = pl.ds(piece * size, size)
        lanes = lax.broadcasted_iota(jnp.int32, (size, CAP), 1)
        mine = lax.broadcasted_iota(jnp.int32, (size, columns.shape[1]), 1)
        picks = []
        for expert in range(local_count):
            column = jnp.max(
                jnp.where(mine == first + expert, columns[rows, :], -1), axis=1, keepdims=True
            )
            picks.append(ones_at(lanes == column))
        back = dot(jnp.concatenate(picks, axis=1), sent[source])
        store(piece, rows, back[:, :D].astype(bf16), back[:, D:].astype(bf16))


def expert_scratch(groups, local_count, experts):
    width = groups * CAP
    return [
        pltpu.VMEM((width, D), bf16),
        pltpu.VMEM((width, D), bf16),
        pltpu.VMEM((width, D), bf16),
        pltpu.VMEM((width, 128), f32),
        pltpu.VMEM((width, FF), bf16),
        pltpu.VMEM((width, FF), bf16),
        pltpu.VMEM((groups, local_count * CAP, 2 * D), bf16),
        pltpu.VMEM((SEQ, experts), jnp.int32),
    ]


def expert_kernel(*refs):
    operands, grads, (mixes, grad_normed) = refs[:6], refs[6:9], refs[9:11]
    work, columns = refs[11:18], refs[18]
    groups, local_count = operands[0].shape[0], operands[4].shape[0]

    def body(expert, _):
        one_expert(operands, work, grads, expert, 0, expert, lambda point: None)
        return 0

    lax.fori_loop(0, local_count, body, 0)
    for source in range(groups):

        def store(piece, rows, mix, grad, source=source):
            mixes[source, rows, :] = mix
            grad_normed[source, rows, :] = grad

        combine(operands[2], 0, local_count, work[6], columns, source, store)


def expert_part(*operands):
    groups, local_count = operands[0].shape[0], operands[4].shape[0]
    return pl.pallas_call(
        expert_kernel,
        out_shape=(
            shape(local_count, D, FF, dtype=bf16),
            shape(local_count, FF, D, dtype=bf16),
            shape(groups, local_count, SEQ),
            shape(groups, SEQ, D, dtype=bf16),
            shape(groups, SEQ, D, dtype=bf16),
        ),
        in_specs=[VMEM] * 6,
        out_specs=[VMEM] * 5,
        scratch_shapes=expert_scratch(groups, local_count, operands[2].shape[1]),
        compiler_params=params(),
    )(*operands)


def expert_sending_kernel(outers, early, *refs):
    normed, cotangent, slots, gates, early_in, early_out, w_in, w_out = refs[:8]
    late_in, late_out, gate_all, mixes, grad_rows, shard_in, shard_out = refs[8:15]
    full_in, full_out = refs[15:17]
    work, columns = refs[17:24], refs[24]
    slot_in, slot_out, grad_in, grad_out, grad_gates, land = refs[25:31]
    in_bufs, out_bufs = refs[31:34], refs[34:37]
    sent, landed, gate_sent, gate_landed, mix_sem, late_sem, slot_sem = refs[37:44]
    gather_sems, scatter_sems = refs[44:47], refs[47:51]
    place = Place(outers)
    local_count, size = grad_in.shape[0], 2 * outers
    late = local_count - early
    first = place.task * local_count
    place.greet(far=True)

    shards = []
    for expert in range(late):
        shards += [
            (w_in.at[early + expert], w_in.shape[1], full_in.at[expert]),
            (w_out.at[early + expert], w_out.shape[1], full_out.at[expert]),
        ]
    gather = Gather(place, shards, *gather_sems)
    for unit in range(len(shards)):
        gather.start(unit)

    def load(source, expert, slot):
        return [
            pltpu.make_async_copy(source[0].at[expert], slot_in.at[slot], slot_sem.at[slot, 0]),
            pltpu.make_async_copy(source[1].at[expert], slot_out.at[slot], slot_sem.at[slot, 1]),
        ]

    for expert in range(early):
        for copy in load((early_in, early_out), expert, expert):
            copy.start()

    scatters, stores = [], []
    for expert in range(early):
        for source, bufs, shard in ((grad_in, in_bufs, shard_in), (grad_out, out_bufs, shard_out)):
            unit = len(scatters)
            scatters.append(
                Scatter(
                    place,
                    lambda rows, source=source, expert=expert: source.at[expert, rows],
                    shard.shape[1],
                    *[buf.at[expert] for buf in bufs],
                    [sem.at[unit] for sem in scatter_sems],
                )
            )

            def store(rows, shard=shard, expert=expert):
                shard[expert] = rows

            stores.append(store)

    def keep(expert):
        return [
            pltpu.make_async_copy(
                grad_in.at[early + expert], late_in.at[expert], late_sem.at[expert, 0]
            ),
            pltpu.make_async_copy(
                grad_out.at[early + expert], late_out.at[expert], late_sem.at[expert, 1]
            ),
        ]

    def plan(expert, point):
        steps = []
        if point == 0:
            if expert < early:
                steps += [copy.wait for copy in load((early_in, early_out), expert, expert)]
            else:
                steps += [
                    copy.wait
                    for copy in load((full_in, full_out), expert - early, expert - early)
                ]
        if expert == 0:
            for unit in range(len(shards)):
                hop = point - unit // 2 + 1
                if 0 < hop < outers:
                    steps.append(lambda unit=unit, hop=hop: gather.step(unit, hop))
        if expert == 1 and point == 0:
            for unit in range(len(shards)):
                for hop in range(5 - unit // 2, outers):
                    steps.append(lambda unit=unit, hop=hop: gather.step(unit, hop))
        if point == 3:
            if expert < early:
                steps += [scatters[2 * expert].start, scatters[2 * expert + 1].start]
            else:
                steps += [copy.start for copy in keep(expert - early)]
        if expert == local_count - 1 and point in (0, 2):
            steps.append(lambda: scatter_turn(scatters, stores, point // 2))
        return steps

    def body(expert, _):
        @pl.when(expert >= early)
        def _():
            for other in range(late):

                @pl.when(expert == early + other)
                def _():
                    gather.finish(2 * other)
                    gather.finish(2 * other + 1)
                    for copy in load((full_in, full_out), other, other):
                        copy.start()

        def between(point):
            for at in range(local_count):
                steps = plan(at, point)
                if steps:

                    @pl.when(expert == at)
                    def _():
                        for step in steps:
                            step()

        one_expert(
            (normed, cotangent, slots, gates, slot_in, slot_out),
            work,
            (grad_in, grad_out, grad_gates),
            expert,
            first,
            lax.rem(expert, early),
            between,
        )
        return 0

    lax.fori_loop(0, local_count, body, 0)
    gate_all[place.task] = grad_gates[place.task]
    peers = (place.core, place.across, place.far)

    def gate_move(way):
        return remote(
            grad_gates.at[peers[way]],
            gate_all.at[place.task],
            gate_sent.at[way],
            gate_landed.at[way],
            task=peers[way],
        )

    for way in range(3):
        gate_move(way).start()
    hidden, grad_pre, joint = work[4], work[5], work[2]

    def part(ref, source):
        return ref.at[pl.ds(0, SEQ), pl.ds(pl.multiple_of(source * D, 128), D)]

    back = Return(
        place, lambda source: part(hidden, source), RETURNS, land, joint, sent, landed
    )
    for order, (source, after) in enumerate(
        (
            (place.far, back.by_core),
            (place.across, back.to_across),
            (place.core, back.to_core),
            (place.task, None),
        )
    ):

        def store(piece, rows, mix, grad, source=source, after=after):
            part(grad_pre, source)[rows, :] = mix
            part(hidden, source)[rows, :] = grad
            if after:
                after(piece)

        combine(slots, first, local_count, work[6], columns, source, store)
        if order:
            scatter_turn(scatters, stores, 1 + order)
    keeps = [
        pltpu.make_async_copy(part(grad_pre, source), mixes.at[source], mix_sem.at[source])
        for source in range(mixes.shape[0])
    ]
    for copy in keeps:
        copy.start()
    for turn in range(5, len(scatters) + outers):
        scatter_turn(scatters, stores, turn)
    for piece in range(RETURNS):
        grad_rows[back.rows(piece), :] = back.finish(piece)
    for way in range(3):
        gate_move(way).wait()
    for copy in keeps:
        copy.wait()
    for expert in range(late):
        for copy in keep(expert):
            copy.wait()


def scatter_buffers(number, outers, *dims):
    return [pltpu.VMEM((number, slots, *dims), bf16) for slots in (outers, outers + 1, outers)]


def scatter_semaphores(units, outers):
    return [pltpu.SemaphoreType.DMA((units, outers))] * 3 + [
        pltpu.SemaphoreType.DMA((units, outers + 1))
    ]


def expert_sending(*operands):
    groups, experts = operands[2].shape[:2]
    local_count, thin = operands[6].shape[:2]
    wide, early = operands[7].shape[1], operands[4].shape[0]
    late, size = local_count - early, lax.axis_size("dp")
    outers = size // 2
    return pl.pallas_call(
        functools.partial(expert_sending_kernel, outers, early),
        out_shape=(
            shape(late, D, FF, dtype=bf16),
            shape(late, FF, D, dtype=bf16),
            shape(groups, local_count, SEQ),
            shape(groups, SEQ, D, dtype=bf16),
            shape(SEQ, D),
            shape(early, thin, FF),
            shape(early, wide, D),
            shape(late, D, FF, dtype=bf16),
            shape(late, FF, D, dtype=bf16),
        ),
        in_specs=[VMEM] * 4 + [ANY] * 4,
        out_specs=[ANY] * 2 + [VMEM, ANY, VMEM, VMEM, VMEM] + [ANY] * 2,
        scratch_shapes=expert_scratch(groups, local_count, experts)
        + [
            pltpu.VMEM((early, D, FF), bf16),
            pltpu.VMEM((early, FF, D), bf16),
            pltpu.VMEM((local_count, D, FF), bf16),
            pltpu.VMEM((local_count, FF, D), bf16),
            pltpu.VMEM((groups, local_count, SEQ), f32),
            pltpu.VMEM((3, SEQ, D), bf16),
        ]
        + scatter_buffers(early, outers, thin, FF)
        + scatter_buffers(early, outers, wide, D)
        + [
            pltpu.SemaphoreType.DMA((3, RETURNS)),
            pltpu.SemaphoreType.DMA((3, RETURNS)),
            pltpu.SemaphoreType.DMA((3,)),
            pltpu.SemaphoreType.DMA((3,)),
            pltpu.SemaphoreType.DMA((groups,)),
            pltpu.SemaphoreType.DMA((late, 2)),
            pltpu.SemaphoreType.DMA((early, 2)),
            pltpu.SemaphoreType.DMA((2 * late, size, 3)),
            pltpu.SemaphoreType.DMA((2 * late, size)),
            pltpu.SemaphoreType.DMA((2 * late,)),
        ]
        + scatter_semaphores(2 * early, outers),
        compiler_params=params(collective_id=1, has_side_effects=True),
    )(*operands)


def attend_back(packed, grad_mixed, logs, grad_packed, grad_keys, grad_values, between, done):
    zero = jnp.array(0, bf16)
    blocks = SEQ // QUERY_BWD

    def head_pair(pair):
        queries, keys, values = (
            slice(part * D + pair * PAIR, part * D + (pair + 1) * PAIR) for part in range(3)
        )
        key_rows, value_rows = packed[:, keys], packed[:, values]

        def block(index, _):
            rows = rows_at(index, QUERY_BWD)
            query_rows = packed[rows, queries] * jnp.array(HEAD_DIM**-0.5, bf16)
            grad_rows = grad_mixed[rows, queries]
            grad_query, part_keys, part_values = [], 0.0, 0.0
            for half in range(2):
                lanes = half_lanes(QUERY_BWD, half)
                own = jnp.where(lanes, query_rows, zero)
                own_grad = jnp.where(lanes, grad_rows, zero)
                head = 2 * pair + half
                probs = jnp.exp(dot_rt(key_rows, own) - logs[head : head + 1, rows])
                grad_probs = dot_rt(value_rows, own_grad)
                mean = jnp.sum(probs * grad_probs, axis=0, keepdims=True)
                grad_scores = (probs * (grad_probs - mean)).astype(bf16)
                part_values += dot(probs.astype(bf16), own_grad)
                part_keys += dot(grad_scores, own)
                grad_query.append(dot_lt(grad_scores, key_rows))
            grad_packed[rows, queries] = (
                jnp.where(half_lanes(QUERY_BWD, 0), grad_query[0], grad_query[1])
                * HEAD_DIM**-0.5
            ).astype(bf16)
            grad_keys[...] = jnp.where(index == 0, part_keys, grad_keys[...] + part_keys)
            grad_values[...] = jnp.where(index == 0, part_values, grad_values[...] + part_values)
            between(pair, index)
            return 0

        lax.fori_loop(0, blocks, block, 0)
        grad_packed[:, keys] = grad_keys[...].astype(bf16)
        grad_packed[:, values] = grad_values[...].astype(bf16)
        done(pair, (queries, keys, values))

    for pair in range(HEADS // 2):
        head_pair(pair)


def second_back(
    grad_rows, cotangent, gain, bias, mid, w_proj, router, grad_logits, grad_norm, grad_router, outs
):
    grad_mid, grad_low, grad_mixed = outs
    grad_norm[...] = jnp.zeros_like(grad_norm)
    grad_router[...] = jnp.zeros_like(grad_router)
    for index in range(SEQ // ROWS):
        rows = slice(index * ROWS, (index + 1) * ROWS)
        mid_rows = mid[rows, :]
        own_logits = grad_logits[:, rows]
        grad_in_rows = grad_rows(rows) + lax.dot_general(
            own_logits,
            router[...],
            (((0,), (0,)), ((), ())),
            precision=HIGHEST,
            preferred_element_type=f32,
        )
        grad_in, grad_gain, grad_bias, unit = norm_back(mid_rows, grad_in_rows, gain[1:2, :])
        grad_router[...] += jnp.dot(
            own_logits,
            unit * gain[1:2, :] + bias[1:2, :],
            precision=HIGHEST,
            preferred_element_type=f32,
        )
        grad_norm[1:2, :] += grad_gain
        grad_norm[3:4, :] += grad_bias
        grad_mid_rows = cotangent[rows, :] + grad_in
        grad_mid[rows, :] = grad_mid_rows
        low_rows = grad_mid_rows.astype(bf16)
        grad_low[rows, :] = low_rows
        grad_mixed[rows, :] = dot_rt(low_rows, w_proj[...]).astype(bf16)


def first_back(image, gain, w_qkv, grad_packed, grad_mid, grad_image, grad_norm):
    def block(index, _):
        rows = rows_at(index, ROWS)
        grad_rows = dot_rt(grad_packed[rows, :], w_qkv[...])
        grad_in, grad_gain, grad_bias, _ = norm_back(image[rows, :], grad_rows, gain[0:1, :])
        grad_image[rows, :] = grad_mid[rows, :] + grad_in
        grad_norm[0:1, :] += grad_gain
        grad_norm[2:3, :] += grad_bias
        return 0

    lax.fori_loop(0, SEQ // ROWS, block, 0)


def logit_grads(probs, grad_gates):
    route = jnp.concatenate([grad_gates[group] for group in range(grad_gates.shape[0])], axis=0)
    return probs[...] * (route - jnp.sum(probs[...] * route, axis=0, keepdims=True))


def backward_scratch():
    return [
        pltpu.VMEM((SEQ, D), f32),
        pltpu.VMEM((SEQ, D), bf16),
        pltpu.VMEM((SEQ, D), bf16),
        pltpu.VMEM((SEQ, 3 * D), bf16),
        pltpu.VMEM((SEQ, PAIR), f32),
        pltpu.VMEM((SEQ, PAIR), f32),
        pltpu.VMEM((SEQ, D), bf16),
    ]


def backward_kernel(*refs):
    image, cotangent, gain, bias, mid, w_qkv, w_proj, router = refs[:8]
    packed, mixed, logs, mixes, grad_normed, grad_gates, probs = refs[8:15]
    activations, grad_image, grad_norm, grad_router, grad_shared = refs[15:20]
    grad_mid, grad_low, grad_mixed, grad_packed, grad_keys, grad_values, normed_first = refs[20:]
    groups = mixes.shape[0]

    def added(parts, rows):
        total = parts[0, rows, :].astype(f32)
        for source in range(1, groups):
            total += parts[source, rows, :].astype(f32)
        return total

    activations[...] = mid[...] + added(mixes, slice(None))
    second_back(
        lambda rows: added(grad_normed, rows),
        cotangent,
        gain,
        bias,
        mid,
        w_proj,
        router,
        logit_grads(probs, grad_gates),
        grad_norm,
        grad_router,
        (grad_mid, grad_low, grad_mixed),
    )
    first_norm(image, gain, bias, normed_first)
    grad_shared[:, 3 * D :] = dot_lt(mixed[...], grad_low[...]).astype(bf16)
    attend_back(
        packed,
        grad_mixed,
        logs,
        grad_packed,
        grad_keys,
        grad_values,
        lambda pair, index: None,
        lambda pair, columns: None,
    )
    first_back(image, gain, w_qkv, grad_packed, grad_mid, grad_image, grad_norm)
    grad_shared[:, : 3 * D] = dot_lt(normed_first[...], grad_packed[...]).astype(bf16)


def backward_part(*operands):
    router = operands[7]
    return pl.pallas_call(
        backward_kernel,
        out_shape=(
            shape(SEQ, D),
            shape(SEQ, D),
            shape(4, D),
            shape(router.shape[0], D),
            shape(D, 4 * D, dtype=bf16),
        ),
        in_specs=[VMEM] * 15,
        out_specs=[VMEM] * 5,
        scratch_shapes=backward_scratch(),
        compiler_params=params(),
    )(*operands)


def backward_sending_kernel(outers, *refs):
    image, cotangent, gain, bias, mid, w_qkv, w_proj, router = refs[:8]
    packed, mixed, logs, mixes, grad_rows, grad_gates, probs, grad_in, grad_out = refs[8:17]
    activations, grad_image, grad_norm, grad_router, shard_qkv, shard_proj = refs[17:23]
    shard_in, shard_out = refs[23:25]
    grad_mid, grad_low, grad_mixed, grad_packed, grad_keys, grad_values, normed_first = refs[25:32]
    norm_sums, router_sums, shared = refs[32:35]
    land, joint, back_sent, back_landed = refs[35:39]
    in_bufs, out_bufs, shared_bufs = refs[39:42], refs[42:45], refs[45:48]
    scatter_sems = refs[48:52]
    place = Place(outers)
    count, groups, size = grad_in.shape[0], mixes.shape[0], 2 * outers
    place.greet_all(groups)
    norms = Spread("dp", place, size, *refs[52:55])
    norms_task = Spread("task", place, groups, *refs[55:58])
    routers = Spread("dp", place, size, *refs[58:61])
    task_refs = refs[61:64]

    def scatter(unit, block, size, bufs, at):
        return Scatter(
            place,
            block,
            size,
            *[buf.at[at] for buf in bufs],
            [sem.at[unit] for sem in scatter_sems],
        )

    big, stores = [], []
    for expert in range(count):
        for source, bufs, shard in ((grad_in, in_bufs, shard_in), (grad_out, out_bufs, shard_out)):
            big.append(
                scatter(
                    len(big),
                    lambda rows, source=source, expert=expert: source.at[expert, rows],
                    shard.shape[1],
                    bufs,
                    expert,
                )
            )

            def store(rows, shard=shard, expert=expert):
                shard[expert] = rows

            stores.append(store)
    pieces = HEADS // 2 + 1
    small = [
        scatter(
            len(big) + piece,
            lambda rows, piece=piece: shared.at[piece, rows],
            shard_proj.shape[0],
            shared_bufs,
            piece,
        )
        for piece in range(pieces)
    ]
    for unit in big:
        unit.start()
    back = Return(
        place, lambda source: mixes.at[source], 1, land, joint, back_sent, back_landed
    )
    back.by_core(0)
    back.to_core(0)
    second_back(
        lambda rows: grad_rows[rows, :],
        cotangent,
        gain,
        bias,
        mid,
        w_proj,
        router,
        logit_grads(probs, grad_gates),
        norm_sums,
        router_sums,
        (grad_mid, grad_low, grad_mixed),
    )
    back.to_across(0)
    first_norm(image, gain, bias, normed_first)
    shared[pieces - 1] = dot_lt(mixed[...], grad_low[...]).astype(bf16)
    small[pieces - 1].start()
    routers.give(router_sums[...])
    blocks = SEQ // QUERY_BWD
    totals = [
        Spread("task", place, groups, *[ref.at[piece] for ref in task_refs])
        for piece in range(pieces)
    ]
    units, keeps = big + small, stores + [one.give for one in totals]

    def between(pair, index):
        for turn, at in enumerate(TURNS):
            if at // blocks == pair:
                pl.when(index == at % blocks)(lambda turn=turn: scatter_turn(units, keeps, turn))

    def done(pair, columns):
        both = jnp.concatenate([grad_packed[:, part] for part in columns], axis=1)
        shared[pair] = dot_lt(normed_first[...], both).astype(bf16)
        small[pair].start()

    attend_back(
        packed, grad_mixed, logs, grad_packed, grad_keys, grad_values, between, done
    )
    first_back(image, gain, w_qkv, grad_packed, grad_mid, grad_image, norm_sums)
    norms.give(norm_sums[...])
    activations[...] = mid[...] + back.finish(0)
    grad_router[...] = routers.take()
    for turn in range(len(TURNS), len(units) + outers - 1):
        scatter_turn(units, keeps, turn)
        if turn == len(units) - 1:
            norms_task.give(norms.take())
    grad_norm[...] = norms_task.take()
    for piece in range(pieces):
        rows = totals[piece].take()
        if piece == pieces - 1:
            shard_proj[...] = rows
        else:
            for part in range(3):
                at = part * D + piece * PAIR
                shard_qkv[:, at : at + PAIR] = rows[:, part * PAIR : (part + 1) * PAIR]


def backward_sending(*operands):
    router, grad_in = operands[7], operands[15]
    experts, size = router.shape[0], lax.axis_size("dp")
    outers, count = size // 2, grad_in.shape[0]
    thin, wide, pieces = D // size, FF // size, HEADS // 2 + 1
    units, groups = 2 * count + pieces, lax.axis_size("task")

    def spread(peers, *dims, lead=(), dtype=f32):
        return [pltpu.VMEM((*lead, peers, *dims), dtype)] + [
            pltpu.SemaphoreType.DMA((*lead, peers - 1))
        ] * 2

    return pl.pallas_call(
        functools.partial(backward_sending_kernel, outers),
        out_shape=(
            shape(SEQ, D),
            shape(SEQ, D),
            shape(8, D),
            shape(experts, D),
            shape(thin, 3 * D),
            shape(thin, D),
            shape(count, thin, FF),
            shape(count, wide, D),
        ),
        in_specs=[VMEM] * 17,
        out_specs=[VMEM] * 8,
        scratch_shapes=backward_scratch()
        + [
            pltpu.VMEM((8, D), f32),
            pltpu.VMEM((experts, D), f32),
            pltpu.VMEM((pieces, D, D), bf16),
            pltpu.VMEM((3, SEQ, D), bf16),
            pltpu.VMEM((SEQ, D), bf16),
            pltpu.SemaphoreType.DMA((3, 1)),
            pltpu.SemaphoreType.DMA((3, 1)),
        ]
        + scatter_buffers(count, outers, thin, FF)
        + scatter_buffers(count, outers, wide, D)
        + scatter_buffers(pieces, outers, thin, D)
        + scatter_semaphores(units, outers)
        + spread(size, 8, D)
        + spread(groups, 8, D)
        + spread(size, experts, D)
        + spread(groups, thin, D, lead=(pieces,), dtype=bf16),
        compiler_params=params(collective_id=2, has_side_effects=True),
    )(*operands)


def local(
    layer_input,
    cotangent,
    norm_gain,
    norm_bias,
    w_qkv,
    w_proj,
    router,
    w_in,
    w_out,
    choices,
    top_count,
):
    groups = lax.axis_size("task")
    local_count = w_in.shape[0]
    image = layer_input.reshape(SEQ, D)
    grad_rows = cotangent.reshape(SEQ, D)
    router_rows = router[0].T
    experts = router_rows.shape[0]
    routes = choices.reshape(SEQ, TOPMAX)

    def swap(array):
        return lax.all_to_all(array, "task", split_axis=0, concat_axis=0, tiled=True)

    sending = groups == 4 and lax.axis_size("dp") in (4, 8) and w_in.shape[1] % 16 == 0
    if sending:
        (
            mid,
            packed,
            mixed,
            logs,
            probs,
            normed,
            cot_rows,
            slots,
            gates,
            full_qkv,
            full_proj,
            full_in,
            full_out,
        ) = forward_sending(
            top_count,
            image,
            grad_rows,
            norm_gain,
            norm_bias,
            (w_qkv, w_proj, w_in, w_out),
            router_rows,
            routes,
        )
        (
            late_in,
            late_out,
            grad_gates,
            mixes,
            grad_normed,
            early_in,
            early_out,
            _,
            _,
        ) = expert_sending(normed, cot_rows, slots, gates, full_in, full_out, w_in, w_out)
        (
            activations,
            grad_image,
            grad_norm,
            grad_router,
            grad_qkv,
            grad_proj,
            grad_in,
            grad_out,
        ) = backward_sending(
            image,
            grad_rows,
            norm_gain,
            norm_bias,
            mid,
            full_qkv,
            full_proj,
            router_rows,
            packed,
            mixed,
            logs,
            mixes,
            grad_normed,
            grad_gates,
            probs,
            late_in,
            late_out,
        )
        grad_in = jnp.concatenate([early_in, grad_in], axis=0)
        grad_out = jnp.concatenate([early_out, grad_out], axis=0)
    else:
        full_qkv, full_proj, full_in, full_out = (
            lax.all_gather(w_qkv, "dp", axis=0, tiled=True),
            lax.all_gather(w_proj, "dp", axis=0, tiled=True),
            lax.all_gather(w_in, "dp", axis=1, tiled=True),
            lax.all_gather(w_out, "dp", axis=1, tiled=True),
        )
        mid, packed, mixed, logs, normed, slots, gates, probs = forward_part(
            top_count,
            image,
            norm_gain,
            norm_bias,
            full_qkv,
            full_proj,
            router_rows,
            routes,
        )
        normed = lax.all_gather(normed, "task")
        cot_rows = lax.all_gather(grad_rows.astype(bf16), "task")
        slots = swap(slots.reshape(groups, local_count, SEQ))
        gates = swap(gates.reshape(groups, local_count, SEQ))
        grad_in, grad_out, grad_gates, mixes, grad_normed = expert_part(
            normed, cot_rows, slots, gates, full_in, full_out
        )
        activations, grad_image, grad_norm, grad_router, grad_shared = backward_part(
            image,
            grad_rows,
            norm_gain,
            norm_bias,
            mid,
            full_qkv,
            full_proj,
            router_rows,
            packed,
            mixed,
            logs,
            swap(mixes),
            swap(grad_normed),
            swap(grad_gates),
            probs,
        )
        grad_in = lax.psum_scatter(grad_in, "dp", scatter_dimension=1, tiled=True).astype(f32)
        grad_out = lax.psum_scatter(grad_out, "dp", scatter_dimension=1, tiled=True).astype(f32)
        grad_shared = lax.psum_scatter(grad_shared, "dp", scatter_dimension=0, tiled=True)
        grad_shared = lax.psum(grad_shared, "task").astype(f32)
        grad_qkv, grad_proj = grad_shared[:, : 3 * D], grad_shared[:, 3 * D :]
        grad_router = lax.psum(grad_router, "dp")
        grad_norm = lax.psum(grad_norm, ("task", "dp"))
    return (
        activations.reshape(layer_input.shape),
        grad_image.reshape(layer_input.shape),
        grad_norm[:2],
        grad_norm[2:4],
        grad_qkv,
        grad_proj,
        grad_router.T[None],
        grad_in,
        grad_out,
    )


def solution(mesh):
    tokens = P("task", "dp", None, None)
    rows = P("dp", None)
    blocks = P("task", "dp", None)
    routed = P("task", None, None)
    return jax.shard_map(
        local,
        mesh=mesh,
        in_specs=(tokens, tokens, P(), P(), rows, rows, routed, blocks, blocks, tokens, P("task")),
        out_specs=(tokens, tokens, P(), P(), rows, rows, routed, blocks, blocks),
        check_vma=False,
    )
```

```python
import functools

import jax
import jax.numpy as jnp
from jax import lax
from jax.experimental import pallas as pl
from jax.experimental.pallas import tpu as pltpu
from jax.sharding import PartitionSpec as P

D = 384
FF = 1536
HEADS = 6
HEAD_DIM = 64
PAIR = 2 * HEAD_DIM
TOPMAX = 4
SEQ = 1024
CAP = 320

f32 = jnp.float32
bf16 = jnp.bfloat16
HIGHEST = lax.Precision.HIGHEST
EPSILON = 1e-06
ROOT_HALF = 0.7071067811865476
NORMAL = 0.3989422804014327

FF_TILE = 512
ROW_TILE = 640
QUERY_FWD = 256
QUERY_BWD = 256
ROWS = 256
RETURNS = 2

GATHER_WHOLE = ((0, 0), (0, 1), (1, 0), (1, 1))
GATHER_SPLIT = ((2, 0), (2, 1))
GATHER_LATE = ((3, 0), (3, 1))
SCATTER_EARLY = ((0, 0), (0, 1), (1, 0))
SCATTER_SPLIT = ((1, 1), (2, 0))
SCATTER_LATE = ((2, 1), (3, 0), (3, 1))
EARLY_EXPERTS = 2

GATHER_POINTS = ((0, 2), (1, 1), (1, 4))
SCATTER_POINTS = ((3, 1), (3, 3))
COMBINE_TURNS = (1, 2, 3)

BACKWARD_POINTS = {
    3: ("s1", "u0",),
    8: ("t1", "s2", "v0",),
    11: ("u1",),
}
BACKWARD_THEN = (
    ("w0", "t2", "s3", "v1", "u2", "30", "00", "10",),
    ("w1", "t3", "v2", "u3", "20", "31", "01", "11", "w2", "v3", "21", "32", "02", "12", "33", "03", "22", "13", "23", "w3",),
)


VMEM = pl.BlockSpec(memory_space=pltpu.VMEM)
SMEM = pl.BlockSpec(memory_space=pltpu.SMEM)
ANY = pl.BlockSpec(memory_space=pl.ANY)


def shape(*dims, dtype=f32):
    return jax.ShapeDtypeStruct(dims, dtype)


def params(**more):
    return pltpu.CompilerParams(vmem_limit_bytes=62 * 2**20, **more)


def dot(a, b):
    return lax.dot_general(a, b, (((1,), (0,)), ((), ())), preferred_element_type=f32)


def dot_rt(a, b):
    return lax.dot_general(a, b, (((1,), (1,)), ((), ())), preferred_element_type=f32)


def dot_lt(a, b):
    return lax.dot_general(a, b, (((0,), (0,)), ((), ())), preferred_element_type=f32)


def rows_at(index, size):
    return pl.ds(pl.multiple_of(index * size, size), size)


def normalize(rows):
    centered = rows - jnp.mean(rows, axis=1, keepdims=True)
    scale = lax.rsqrt(jnp.mean(centered * centered, axis=1, keepdims=True) + EPSILON)
    return centered * scale, scale


def norm_back(rows, grad_rows, gain):
    unit, scale = normalize(rows)
    scaled = grad_rows * gain
    grad_in = scale * (
        scaled
        - jnp.mean(scaled, axis=1, keepdims=True)
        - unit * jnp.mean(scaled * unit, axis=1, keepdims=True)
    )
    grad_gain = jnp.sum(grad_rows * unit, axis=0, keepdims=True)
    return grad_in, grad_gain, jnp.sum(grad_rows, axis=0, keepdims=True), unit


def half_lanes(rows, half):
    lanes = lax.broadcasted_iota(jnp.int32, (rows, PAIR), 1)
    return (lanes < HEAD_DIM) if half == 0 else (lanes >= HEAD_DIM)


def remote(source, target, sent, landed, **device):
    return pltpu.make_async_remote_copy(
        src_ref=source,
        dst_ref=target,
        send_sem=sent,
        recv_sem=landed,
        device_id=device,
        device_id_type=pl.DeviceIdType.MESH,
    )


class Place:
    def __init__(self, outers):
        self.dp = lax.axis_index("dp")
        self.task = lax.axis_index("task")
        self.outers = outers
        self.outer, self.inner = self.dp // 2, self.dp % 2
        self.has_up, self.has_down = self.outer + 1 < outers, self.outer > 0
        self.up, self.down = self.dp + 2, self.dp - 2
        self.side = self.dp + 1 - 2 * self.inner
        self.core = self.task + 1 - 2 * (self.task % 2)
        self.across = self.task + 2 - 4 * (self.task // 2)
        self.far = self.across + 1 - 2 * (self.task % 2)

    def signal(self, **device):
        pl.semaphore_signal(
            pltpu.get_barrier_semaphore(),
            inc=1,
            device_id=device,
            device_id_type=pl.DeviceIdType.MESH,
        )

    def greet(self, far=False):
        pl.when(self.has_up)(lambda: self.signal(dp=self.up))
        pl.when(self.has_down)(lambda: self.signal(dp=self.down))
        self.signal(dp=self.side)
        self.signal(task=self.core)
        self.signal(task=self.across)
        if far:
            self.signal(task=self.far)
        others = 3 + int(far) + self.has_up.astype(jnp.int32) + self.has_down.astype(jnp.int32)
        pl.semaphore_wait(pltpu.get_barrier_semaphore(), others)

    def greet_all(self, groups):
        size = 2 * self.outers
        for ahead in range(1, size):
            self.signal(dp=lax.rem(self.dp + ahead, size))
        for ahead in range(1, groups):
            self.signal(task=lax.rem(self.task + ahead, groups))
        pl.semaphore_wait(pltpu.get_barrier_semaphore(), size + groups - 2)


class Gather:
    def __init__(self, place, shards, sent, landed, stay):
        self.place, self.shards = place, shards
        self.sent, self.landed, self.stay = sent, landed, stay

    def move(self, unit, source, way, device, first=None):
        _, size, full, _ = self.shards[unit]
        target = full.at[rows_at(source, size)]
        return remote(
            target if first is None else first,
            target,
            self.sent.at[unit, source, way],
            self.landed.at[unit, source],
            dp=device,
        )

    def local(self, unit, outer):
        own, size, full, mode = self.shards[unit]
        rows = rows_at(2 * outer + self.place.inner, size)
        source = own.at[rows] if mode == "side" else own
        return pltpu.make_async_copy(source, full.at[rows], self.stay.at[unit, outer])

    def along(self, unit, source, up, down):
        place = self.place
        if up:
            pl.when(place.has_up)(lambda: self.move(unit, source, 0, place.up).start())
        if down:
            pl.when(place.has_down)(lambda: self.move(unit, source, 1, place.down).start())

    def to_side(self, unit, outer):
        own, size = self.shards[unit][:2]
        source = 2 * outer + self.place.inner
        return self.move(unit, source, 2, self.place.side, own.at[rows_at(source, size)])

    def start(self, unit):
        place = self.place
        own, mode = self.shards[unit][0], self.shards[unit][3]
        if mode == "side":
            for outer in range(place.outers):
                self.to_side(unit, outer).start()
                self.local(unit, outer).start()
            return
        if mode == "turned":
            self.move(unit, place.dp, 2, place.side, own).start()
        pl.when(place.has_up)(lambda: self.move(unit, place.dp, 0, place.up, own).start())
        pl.when(place.has_down)(lambda: self.move(unit, place.dp, 1, place.down, own).start())
        if mode == "both":
            self.move(unit, place.dp, 2, place.side, own).start()
        self.local(unit, place.outer).start()

    def step(self, unit, hop):
        place, mode = self.place, self.shards[unit][3]
        if hop == 0:
            self.move(unit, place.side, 0, place.dp).wait_recv()
            self.along(unit, place.side, True, True)
            return
        for column in (place.dp, place.side) if mode == "turned" else (place.dp,):

            @pl.when(place.outer >= hop)
            def _():
                self.move(unit, column - 2 * hop, 0, place.dp).wait_recv()
                self.along(unit, column - 2 * hop, True, False)
                if mode == "both":
                    self.move(unit, column - 2 * hop, 2, place.side).start()

            @pl.when(place.outer + hop < place.outers)
            def _():
                self.move(unit, column + 2 * hop, 1, place.dp).wait_recv()
                self.along(unit, column + 2 * hop, False, True)
                if mode == "both":
                    self.move(unit, column + 2 * hop, 2, place.side).start()

    def finish(self, unit):
        place, mode = self.place, self.shards[unit][3]
        if mode != "side":
            self.local(unit, place.outer).wait()
        if mode == "turned":
            self.move(unit, place.dp, 2, place.side).wait_send()
        for outer in range(place.outers):
            own, other = 2 * outer + place.inner, 2 * outer + 1 - place.inner
            if mode == "side":
                self.local(unit, outer).wait()
            if mode in ("both", "side"):
                self.move(unit, other, 2, place.dp).wait_recv()
                self.move(unit, own, 2, place.side).wait_send()
            if mode == "side":
                continue
            for source in (own, other) if mode == "turned" else (own,):
                pl.when((outer <= place.outer) & place.has_up)(
                    lambda source=source: self.move(unit, source, 0, place.up).wait_send()
                )
                pl.when((outer >= place.outer) & place.has_down)(
                    lambda source=source: self.move(unit, source, 1, place.down).wait_send()
                )


def gather_semaphores(units, size):
    return [
        pltpu.SemaphoreType.DMA((units, size, 3)),
        pltpu.SemaphoreType.DMA((units, size)),
        pltpu.SemaphoreType.DMA((units, size // 2)),
    ]


class Share:
    def __init__(self, place, view, sent, landed):
        self.place, self.view, self.sent, self.landed = place, view, sent, landed

    def move(self, source, way, **device):
        return remote(
            self.view(source),
            self.view(source),
            self.sent.at[way],
            self.landed.at[way],
            **device,
        )

    def start(self):
        place = self.place
        self.move(place.task, 0, task=place.across).start()
        self.move(place.task, 1, task=place.core).start()

    def relay(self):
        place = self.place
        self.move(place.across, 0, task=place.across).wait_recv()
        self.move(place.across, 2, task=place.core).start()

    def finish(self):
        place = self.place
        self.move(place.task, 0, task=place.across).wait_send()
        self.move(place.core, 1, task=place.core).wait()
        self.move(place.across, 2, task=place.core).wait()


class Scatter:
    def __init__(self, place, mine, theirs, side, line, fold, sems):
        self.place, self.mine, self.theirs = place, mine, theirs
        self.side, self.line, self.fold = side, line, fold
        self.side_sent, self.side_landed, self.line_sent, self.line_landed = sems

    def to_side(self, outer):
        return remote(
            self.theirs(outer),
            self.side.at[outer],
            self.side_sent.at[outer],
            self.side_landed.at[outer],
            dp=self.place.side,
        )

    def along(self, outer, slot, device):
        return remote(
            self.fold.at[outer],
            self.line.at[slot],
            self.line_sent.at[outer],
            self.line_landed.at[slot],
            dp=device,
        )

    def start(self):
        outers = self.place.outers
        for near in range(outers // 2):
            self.to_side(outers - 1 - near).start()
            self.to_side(near).start()

    def total(self, outer, *slots):
        rows = self.mine(outer)[...].astype(f32)
        if self.side is not None:
            self.to_side(outer).wait_recv()
            rows += self.side[outer].astype(f32)
        for slot in slots:
            self.along(outer, slot, self.place.dp).wait_recv()
            rows += self.line[slot].astype(f32)
        return rows

    def settle(self, store):
        for outer in range(self.place.outers):
            store(outer, self.total(outer).astype(bf16))
            self.to_side(outer).wait_send()

    def hop(self, step):
        place, outers = self.place, self.place.outers

        @pl.when(place.outer == step)
        def _():
            for outer in range(outers - 1, step, -1):
                rows = self.total(outer, *([outer] if step else []))
                self.fold[outer] = rows.astype(bf16)
                self.along(outer, outer, place.up).start()

        @pl.when(place.outer == outers - 1 - step)
        def _():
            for outer in range(outers - 1 - step):
                rows = self.total(outer, *([outer] if step else []))
                self.fold[outer] = rows.astype(bf16)
                slot = outers if outer == outers - 2 - step else outer
                self.along(outer, slot, place.down).start()

    def finish(self, store):
        place, outers = self.place, self.place.outers
        for outer in range(outers):

            @pl.when(place.outer == outer)
            def _():
                below, above = [outer] * (outer > 0), [outers] * (outer < outers - 1)
                store(self.total(outer, *below, *above))
                for other in range(outers):
                    if other != outer:
                        self.along(other, other, place.dp).wait_send()

            if self.side is not None:
                self.to_side(outer).wait_send()


def scatter_turn(units, stores, turn):
    outers = units[0].place.outers
    for step in range(outers - 1):
        if 0 <= turn - step < len(units):
            units[turn - step].hop(step)
    last = turn - outers + 1
    if 0 <= last < len(units):
        units[last].finish(stores[last])


def blocks_of(place, ref, size):
    return (
        lambda outer: ref.at[rows_at(2 * outer + place.inner, size)],
        lambda outer: ref.at[rows_at(2 * outer + 1 - place.inner, size)],
    )


def tile_of(kind, thin, wide):
    return (wide, D) if kind else (thin, FF)


def scatter_scratch(units, outers, tiles, side=True, line=True):
    scratch = []
    for unit in units:
        tile = tiles[unit[1]] if isinstance(unit, tuple) else tiles
        for asked, slots in ((side, outers), (line, outers + 1), (line, outers)):
            if asked:
                scratch.append(pltpu.VMEM((slots, *tile), bf16))
        for asked, count in ((side, outers), (side, outers), (line, outers), (line, outers + 1)):
            if asked:
                scratch.append(pltpu.SemaphoreType.DMA((count,)))
    return scratch


def make_scatters(place, blocks, refs, side=True, line=True):
    count = 3 * side + 4 * line
    scatters = []
    for index, (mine, theirs) in enumerate(blocks):
        own = list(refs[index * count : (index + 1) * count])
        buffers = [own.pop(0) if asked else None for asked in (side, line, line)]
        sems = [own.pop(0) if asked else None for asked in (side, side, line, line)]
        scatters.append(Scatter(place, mine, theirs, *buffers, sems))
    return scatters


class Spread:
    def __init__(self, axis, place, count, land, sent, landed):
        self.axis, self.me, self.count = axis, getattr(place, axis), count
        self.land, self.sent, self.landed = land, sent, landed

    def move(self, source, ahead):
        return remote(
            self.land.at[source],
            self.land.at[source],
            self.sent.at[ahead - 1],
            self.landed.at[ahead - 1],
            **{self.axis: lax.rem(self.me + ahead, self.count)},
        )

    def give(self, rows):
        self.land[self.me] = rows.astype(self.land.dtype)
        for ahead in range(1, self.count):
            self.move(self.me, ahead).start()

    def take(self):
        for ahead in range(1, self.count):
            self.move(lax.rem(self.me + self.count - ahead, self.count), ahead).wait_recv()
            self.move(self.me, ahead).wait_send()
        total = self.land[0].astype(f32)
        for index in range(1, self.count):
            total += self.land[index].astype(f32)
        return total


class Return:
    def __init__(self, place, parts, pieces, land, joint, sent, landed):
        self.place, self.parts, self.pieces = place, parts, pieces
        self.land, self.joint, self.sent, self.landed = land, joint, sent, landed
        self.size = SEQ // pieces

    def rows(self, piece):
        return pl.ds(piece * self.size, self.size)

    def move(self, way, piece):
        place, rows = self.place, self.rows(piece)
        source = [
            self.parts(place.core).at[rows],
            self.parts(place.far).at[rows],
            self.joint.at[rows],
        ][way]
        return remote(
            source,
            self.land.at[way, rows],
            self.sent.at[way, piece],
            self.landed.at[way, piece],
            task=place.across if way == 2 else place.core,
        )

    def to_core(self, piece):
        self.move(0, piece).start()

    def by_core(self, piece):
        self.move(1, piece).start()

    def to_across(self, piece):
        rows = self.rows(piece)
        self.move(1, piece).wait_recv()
        joint = self.parts(self.place.across)[rows, :].astype(f32)
        joint += self.land[1, rows, :].astype(f32)
        self.joint[rows, :] = joint.astype(bf16)
        self.move(2, piece).start()

    def finish(self, piece):
        rows = self.rows(piece)
        self.move(0, piece).wait()
        self.move(1, piece).wait_send()
        self.move(2, piece).wait()
        total = self.parts(self.place.task)[rows, :].astype(f32)
        return total + self.land[0, rows, :].astype(f32) + self.land[2, rows, :].astype(f32)


def attend(packed, mixed, totals, index):
    zero = jnp.array(0, bf16)
    rows = rows_at(index, QUERY_FWD)

    def head_pair(pair, _):
        queries, keys, values = (rows_at(pair + part * (D // PAIR), PAIR) for part in range(3))
        key_rows, value_rows = packed[:, keys], packed[:, values]
        query_rows = packed[rows, queries] * jnp.array(HEAD_DIM**-0.5, bf16)
        outs, logs = [], []
        for half in range(2):
            own = jnp.where(half_lanes(QUERY_FWD, half), query_rows, zero)
            scores = dot_rt(own, key_rows)
            top = jnp.max(scores, axis=1, keepdims=True)
            weights = jnp.exp(scores - top)
            total = jnp.sum(weights, axis=1, keepdims=True)
            outs.append(dot(weights.astype(bf16), value_rows) * (1.0 / total))
            logs.append(top + jnp.log(total))
        mixed[rows, queries] = jnp.where(half_lanes(QUERY_FWD, 0), outs[0], outs[1]).astype(bf16)
        lanes = lax.broadcasted_iota(jnp.int32, (QUERY_FWD, 8), 1)
        totals[rows, :] = jnp.where(
            lanes == 2 * pair,
            logs[0],
            jnp.where(lanes == 2 * pair + 1, logs[1], totals[rows, :]),
        )
        return 0

    lax.fori_loop(0, HEADS // 2, head_pair, 0)


def first_norm(image, gain, bias, normed_first):
    def block(index, _):
        rows = rows_at(index, ROWS)
        unit, _ = normalize(image[rows, :])
        normed_first[rows, :] = (unit * gain[0:1, :] + bias[0:1, :]).astype(bf16)
        return 0

    lax.fori_loop(0, SEQ // ROWS, block, 0)


def number_slots(choices, top_count, experts):
    named = choices[...].T
    numbers = lax.broadcasted_iota(jnp.int32, (experts, SEQ), 0)
    used = jnp.zeros((experts, SEQ), f32)
    for choice in range(TOPMAX):
        hit = (named[choice : choice + 1, :] == numbers) & (choice < top_count[0])
        used = used + jnp.where(hit, 1.0, 0.0)
    earlier = lax.broadcasted_iota(jnp.int32, (SEQ, SEQ), 0) < lax.broadcasted_iota(
        jnp.int32, (SEQ, SEQ), 1
    )
    before = dot(used.astype(bf16), jnp.where(earlier, 1.0, 0.0).astype(bf16))
    return jnp.where(used > 0, before, -1.0).astype(jnp.int32)


def mid_block(index, image, gain, bias, w_proj, router, mixed, mid, probs):
    rows = rows_at(index, QUERY_FWD)
    mid_rows = image[rows, :] + dot(mixed[rows, :], w_proj[...])
    mid[rows, :] = mid_rows
    unit, _ = normalize(mid_rows)
    normed_rows = unit * gain[1:2, :] + bias[1:2, :]
    logits = lax.dot_general(
        router[...],
        normed_rows,
        (((1,), (1,)), ((), ())),
        precision=HIGHEST,
        preferred_element_type=f32,
    )
    powers = jnp.exp(logits - jnp.max(logits, axis=0, keepdims=True))
    probs[:, rows] = powers / jnp.sum(powers, axis=0, keepdims=True)
    return normed_rows.astype(bf16)


def forward_kernel(
    top_count,
    image,
    gain,
    bias,
    w_qkv,
    w_proj,
    router,
    choices,
    mid,
    packed,
    mixed,
    logs,
    normed,
    slots,
    gates,
    probs,
    normed_first,
    totals,
):
    first_norm(image, gain, bias, normed_first)
    slots[...] = number_slots(choices, top_count, router.shape[0])
    packed[...] = dot(normed_first[...], w_qkv[...]).astype(bf16)
    totals[...] = jnp.zeros_like(totals)

    def block(index, _):
        attend(packed, mixed, totals, index)
        normed[rows_at(index, QUERY_FWD), :] = mid_block(
            index, image, gain, bias, w_proj, router, mixed, mid, probs
        )
        return 0

    lax.fori_loop(0, SEQ // QUERY_FWD, block, 0)
    logs[...] = totals[...].T
    gates[...] = jnp.where(slots[...] >= 0, probs[...], 0.0)


def forward_part(top_count, image, gain, bias, w_qkv, w_proj, router, choices):
    experts = router.shape[0]
    return pl.pallas_call(
        forward_kernel,
        out_shape=(
            shape(SEQ, D),
            shape(SEQ, 3 * D, dtype=bf16),
            shape(SEQ, D, dtype=bf16),
            shape(8, SEQ),
            shape(SEQ, D, dtype=bf16),
            shape(experts, SEQ, dtype=jnp.int32),
            shape(experts, SEQ),
            shape(experts, SEQ),
        ),
        in_specs=[SMEM] + [VMEM] * 7,
        out_specs=[VMEM] * 8,
        scratch_shapes=[pltpu.VMEM((SEQ, D), bf16), pltpu.VMEM((SEQ, 8), f32)],
        compiler_params=params(),
    )(top_count, image, gain, bias, w_qkv, w_proj, router, choices)


def forward_sending_kernel(
    outers,
    top_count,
    image,
    cotangent,
    gain,
    bias,
    w_qkv,
    w_proj,
    w_in,
    w_out,
    router,
    choices,
    mid,
    packed,
    mixed,
    logs,
    probs,
    normed_all,
    cot_all,
    slots_all,
    gates_all,
    full_qkv,
    full_proj,
    full_in,
    full_out,
    normed_first,
    totals,
    sent,
    landed,
    stay,
    share_sent,
    share_landed,
):
    place = Place(outers)
    task = place.task
    shards = [
        (w_qkv, w_qkv.shape[0], full_qkv, "both"),
        (w_proj, w_proj.shape[0], full_proj, "both"),
    ]
    for expert, kind in GATHER_WHOLE + GATHER_SPLIT:
        own, full = ((w_in, full_in), (w_out, full_out))[kind]
        mode = "line" if (expert, kind) in GATHER_SPLIT else "both"
        shards.append((own.at[expert], own.shape[1], full.at[expert], mode))
    gather = Gather(place, shards, sent, landed, stay)
    shared, routed = range(2), range(2, len(shards))
    cot_all[task] = cotangent[...].astype(bf16)
    place.greet()
    for unit in shared:
        gather.start(unit)

    def share(index, view):
        return Share(place, view, share_sent.at[index], share_landed.at[index])

    cot = share(0, lambda source: cot_all.at[source])
    slot = share(1, lambda source: slots_all.at[source])
    gate = share(2, lambda source: gates_all.at[source])
    cot.start()
    first_norm(image, gain, bias, normed_first)
    for hop in range(1, outers):
        for unit in shared:
            gather.step(unit, hop)
    for unit in routed:
        gather.start(unit)
    slots_all[task] = number_slots(choices, top_count, router.shape[0])
    slot.start()
    totals[...] = jnp.zeros_like(totals)
    for unit in shared:
        gather.finish(unit)
    packed[...] = dot(normed_first[...], full_qkv[...]).astype(bf16)
    cot.relay()
    slot.relay()

    def chunk(index):
        return share(3 + index, lambda source: normed_all.at[source, rows_at(index, QUERY_FWD)])

    blocks = SEQ // QUERY_FWD

    def block(index, _):
        attend(packed, mixed, totals, index)
        normed_all[task, rows_at(index, QUERY_FWD), :] = mid_block(
            index, image, gain, bias, full_proj, router, mixed, mid, probs
        )
        chunk(index).start()
        pl.when(index > 0)(lambda: chunk(index - 1).relay())
        for hop in range(1, outers):

            @pl.when(index == hop - 1)
            def _():
                for unit in routed:
                    gather.step(unit, hop)

        return 0

    lax.fori_loop(0, blocks, block, 0)
    for hop in range(blocks + 1, outers):
        for unit in routed:
            gather.step(unit, hop)
    gates_all[task] = jnp.where(slots_all[task] >= 0, probs[...], 0.0)
    gate.start()
    logs[...] = totals[...].T
    chunk(blocks - 1).relay()
    gate.relay()
    for one in [cot, slot, gate] + [chunk(index) for index in range(blocks)]:
        one.finish()
    for unit in routed:
        gather.finish(unit)


def forward_sending(top_count, image, cotangent, gain, bias, shards, router, choices):
    w_qkv, w_proj, w_in, w_out = shards
    experts, size = router.shape[0], lax.axis_size("dp")
    groups, early = lax.axis_size("task"), 1 + GATHER_SPLIT[-1][0]
    units, shares = 2 + len(GATHER_WHOLE + GATHER_SPLIT), 3 + SEQ // QUERY_FWD
    return pl.pallas_call(
        functools.partial(forward_sending_kernel, size // 2),
        out_shape=(
            shape(SEQ, D),
            shape(SEQ, 3 * D, dtype=bf16),
            shape(SEQ, D, dtype=bf16),
            shape(8, SEQ),
            shape(experts, SEQ),
            shape(groups, SEQ, D, dtype=bf16),
            shape(groups, SEQ, D, dtype=bf16),
            shape(groups, experts, SEQ, dtype=jnp.int32),
            shape(groups, experts, SEQ),
            shape(D, 3 * D, dtype=bf16),
            shape(D, D, dtype=bf16),
            shape(early, D, FF, dtype=bf16),
            shape(early, FF, D, dtype=bf16),
        ),
        in_specs=[SMEM] + [VMEM] * 6 + [ANY] * 2 + [VMEM] * 2,
        out_specs=[VMEM] * 11 + [ANY] * 2,
        scratch_shapes=[
            pltpu.VMEM((SEQ, D), bf16),
            pltpu.VMEM((SEQ, 8), f32),
            *gather_semaphores(units, size),
            pltpu.SemaphoreType.DMA((shares, 3)),
            pltpu.SemaphoreType.DMA((shares, 3)),
        ],
        compiler_params=params(collective_id=0, has_side_effects=True),
    )(top_count, image, cotangent, gain, bias, w_qkv, w_proj, w_in, w_out, router, choices)


def slot_hits(slots, source, expert):
    return lax.broadcasted_iota(jnp.int32, (CAP, SEQ), 0) == slots[source, pl.ds(expert, 1), :]


def ones_at(hits):
    return jnp.where(hits, 1.0, 0.0).astype(bf16)


def one_expert(operands, work, grads, expert, first, slot, between):
    normed, cotangent, slots, gates, w_in, w_out = operands
    rows_in, rows_grad, rows_cot, rows_gate, hidden, grad_pre, sent = work
    grad_in, grad_out, grad_gates = grads
    groups = normed.shape[0]
    width = groups * CAP
    between(0)
    for source in range(groups):
        own = slice(source * CAP, (source + 1) * CAP)
        hits = slot_hits(slots, source, first + expert)
        picks = ones_at(hits)
        rows_in[own, :] = dot(picks, normed[source]).astype(bf16)
        cot_rows = dot(picks, cotangent[source])
        gate = jnp.sum(
            jnp.where(hits, gates[source, pl.ds(first + expert, 1), :], 0.0),
            axis=1,
            keepdims=True,
        )
        rows_cot[own, :] = cot_rows.astype(bf16)
        rows_grad[own, :] = (gate * cot_rows).astype(bf16)
        rows_gate[own, :] = jnp.broadcast_to(gate, (CAP, 128))
    between(1)

    def tile(index, _):
        units = rows_at(index // (width // ROW_TILE), FF_TILE)
        rows = rows_at(lax.rem(index, width // ROW_TILE), ROW_TILE)
        pre = dot(rows_in[rows, :], w_in[slot, :, units])
        grad_hidden = dot_rt(rows_grad[rows, :], w_out[slot, units, :])
        share = 0.5 * lax.erf(pre * ROOT_HALF) + 0.5
        slope = share + pre * (NORMAL * jnp.exp(-0.5 * pre * pre))
        hidden[rows, units] = (pre * share).astype(bf16)
        grad_pre[rows, units] = (grad_hidden * slope).astype(bf16)
        return 0

    lax.fori_loop(0, (FF // FF_TILE) * (width // ROW_TILE), tile, 0)
    between(2)
    for source in range(groups):
        own = slice(source * CAP, (source + 1) * CAP)
        kept = rows_at(expert, CAP)
        out_rows = dot(hidden[own, :], w_out[slot]).astype(bf16).astype(f32)
        sent[source, kept, :D] = (rows_gate[own, 0:1] * out_rows).astype(bf16)
        sent[source, kept, D:] = dot_rt(grad_pre[own, :], w_in[slot]).astype(bf16)
        grad_gate = jnp.sum(rows_cot[own, :].astype(f32) * out_rows, axis=1, keepdims=True)
        hits = slot_hits(slots, source, first + expert)
        grad_gates[source, pl.ds(expert, 1), :] = jnp.sum(
            jnp.where(hits, grad_gate, 0.0), axis=0, keepdims=True
        )
    between(3)
    grad_in[expert] = dot_lt(rows_in[...], grad_pre[...]).astype(bf16)
    grad_out[expert] = dot_lt(rows_grad[...], hidden[...]).astype(bf16).T
    between(4)


def combine(slots, first, local_count, sent, columns, source, store):
    size = SEQ // RETURNS
    columns[...] = slots[source].T
    for piece in range(RETURNS):
        rows = pl.ds(piece * size, size)
        lanes = lax.broadcasted_iota(jnp.int32, (size, CAP), 1)
        mine = lax.broadcasted_iota(jnp.int32, (size, columns.shape[1]), 1)
        picks = []
        for expert in range(local_count):
            column = jnp.max(
                jnp.where(mine == first + expert, columns[rows, :], -1), axis=1, keepdims=True
            )
            picks.append(ones_at(lanes == column))
        back = dot(jnp.concatenate(picks, axis=1), sent[source])
        store(piece, rows, back[:, :D].astype(bf16), back[:, D:].astype(bf16))


def expert_scratch(groups, local_count, experts):
    width = groups * CAP
    return [
        pltpu.VMEM((width, D), bf16),
        pltpu.VMEM((width, D), bf16),
        pltpu.VMEM((width, D), bf16),
        pltpu.VMEM((width, 128), f32),
        pltpu.VMEM((width, FF), bf16),
        pltpu.VMEM((width, FF), bf16),
        pltpu.VMEM((groups, local_count * CAP, 2 * D), bf16),
        pltpu.VMEM((SEQ, experts), jnp.int32),
    ]


def expert_kernel(*refs):
    operands, grads, (mixes, grad_normed) = refs[:6], refs[6:9], refs[9:11]
    work, columns = refs[11:18], refs[18]
    groups, local_count = operands[0].shape[0], operands[4].shape[0]

    def body(expert, _):
        one_expert(operands, work, grads, expert, 0, expert, lambda point: None)
        return 0

    lax.fori_loop(0, local_count, body, 0)
    for source in range(groups):

        def store(piece, rows, mix, grad, source=source):
            mixes[source, rows, :] = mix
            grad_normed[source, rows, :] = grad

        combine(operands[2], 0, local_count, work[6], columns, source, store)


def expert_part(*operands):
    groups, local_count = operands[0].shape[0], operands[4].shape[0]
    return pl.pallas_call(
        expert_kernel,
        out_shape=(
            shape(local_count, D, FF, dtype=bf16),
            shape(local_count, FF, D, dtype=bf16),
            shape(groups, local_count, SEQ),
            shape(groups, SEQ, D, dtype=bf16),
            shape(groups, SEQ, D, dtype=bf16),
        ),
        in_specs=[VMEM] * 6,
        out_specs=[VMEM] * 5,
        scratch_shapes=expert_scratch(groups, local_count, operands[2].shape[1]),
        compiler_params=params(),
    )(*operands)


def expert_sending_kernel(outers, *refs):
    normed_all, cot_all, slots, gates, early_in, early_out, w_in, w_out = refs[:8]
    late_in, late_out, gate_all, mixes, grad_rows, shard_in, shard_out, parts_in, parts_out = refs[8:17]
    full_in, full_out = refs[17:19]
    work, columns = refs[19:26], refs[26]
    normed, cotangent, slot_in, slot_out, grad_in, grad_out, grad_gates, land = refs[27:35]
    sent, landed, gate_sent, gate_landed, mix_sem, late_sem, slot_sem, token_sem = refs[35:43]
    gather_sems, scatter_refs = refs[43:46], refs[46:]
    place = Place(outers)
    groups, local_count, size = normed.shape[0], grad_in.shape[0], 2 * outers
    late = local_count - EARLY_EXPERTS
    first = place.task * local_count
    grads, shares = (grad_in, grad_out), (w_in.shape[1], w_out.shape[1])

    def tokens():
        return [
            pltpu.make_async_copy(whole.at[source], ref.at[source], token_sem.at[kind, source])
            for source in range(groups)
            for kind, (whole, ref) in enumerate(((normed_all, normed), (cot_all, cotangent)))
        ]

    def load(expert):
        slot = expert % EARLY_EXPERTS
        whole = (early_in, early_out) if expert < EARLY_EXPERTS else (full_in, full_out)
        place_in = expert if expert < EARLY_EXPERTS else expert - EARLY_EXPERTS
        return [
            pltpu.make_async_copy(
                whole[kind].at[place_in], (slot_in, slot_out)[kind].at[slot], slot_sem.at[slot, kind]
            )
            for kind in range(2)
        ]

    def keep(expert):
        return [
            pltpu.make_async_copy(
                grads[kind].at[EARLY_EXPERTS + expert],
                (late_in, late_out)[kind].at[expert],
                late_sem.at[expert, kind],
            )
            for kind in range(2)
        ]

    for copy in tokens() + load(0):
        copy.start()
    place.greet(far=True)
    shards = []
    for expert, kind in GATHER_LATE + GATHER_SPLIT:
        full = (full_in, full_out)[kind].at[expert - EARLY_EXPERTS]
        if (expert, kind) in GATHER_SPLIT:
            shards.append(((early_in, early_out)[kind].at[expert], shares[kind], full, "side"))
        else:
            shards.append(((w_in, w_out)[kind].at[expert], shares[kind], full, "turned"))
    gather = Gather(place, shards, *gather_sems)
    turned = range(len(GATHER_LATE))
    for unit in range(len(shards)):
        gather.start(unit)
    for copy in load(1):
        copy.start()
    per_full, per_side = 7 * len(SCATTER_EARLY), 3 * len(SCATTER_SPLIT)

    def scatters(units, refs, **parts):
        return make_scatters(
            place,
            [blocks_of(place, grads[kind].at[expert], shares[kind]) for expert, kind in units],
            refs,
            **parts,
        )

    whole = scatters(SCATTER_EARLY, scatter_refs[:per_full])
    split = scatters(SCATTER_SPLIT, scatter_refs[per_full : per_full + per_side], line=False)
    stores, keeps = [], []
    for expert, kind in SCATTER_EARLY:

        def store(rows, shard=(shard_in, shard_out)[kind], expert=expert):
            shard[expert] = rows

        stores.append(store)
    for index, (_, kind) in enumerate(SCATTER_SPLIT):
        at = [other[1] for other in SCATTER_SPLIT[:index]].count(kind)

        def settle(outer, rows, parts=(parts_in, parts_out)[kind], at=at):
            parts[at, outer] = rows

        keeps.append(settle)
    steps = {}

    def plan(expert, point, *acts):
        steps.setdefault((expert, point), []).extend(acts)

    plan(0, 0, *[copy.wait for copy in tokens()])
    for expert in range(EARLY_EXPERTS):
        plan(expert, 1, *[copy.wait for copy in load(expert)])
    for hop in range(outers):
        at = GATHER_POINTS[hop] if hop < outers - 1 else (3, 0)
        plan(*at, *[lambda unit=unit, hop=hop: gather.step(unit, hop) for unit in turned])
    for expert in range(EARLY_EXPERTS, local_count):
        units = [
            unit
            for unit, (owner, _) in enumerate(GATHER_LATE + GATHER_SPLIT)
            if owner == expert
        ]
        plan(expert, 0, *[lambda unit=unit: gather.finish(unit) for unit in units])
        plan(expert, 0, *[copy.start for copy in load(expert)])
        plan(expert, 1, *[copy.wait for copy in load(expert)])
        plan(expert, 4, *[copy.start for copy in keep(expert - EARLY_EXPERTS)])
    for index, (expert, _) in enumerate(SCATTER_EARLY):
        plan(expert, 4, whole[index].start)
    for index, (expert, _) in enumerate(SCATTER_SPLIT):
        plan(expert, 4, split[index].start)
    for turn, at in enumerate(SCATTER_POINTS):
        plan(*at, lambda turn=turn: scatter_turn(whole, stores, turn))

    def body(expert, _):
        def between(point):
            for at in range(local_count):
                acts = steps.get((at, point))
                if acts:

                    @pl.when(expert == at)
                    def _():
                        for act in acts:
                            act()

        one_expert(
            (normed, cotangent, slots, gates, slot_in, slot_out),
            work,
            (grad_in, grad_out, grad_gates),
            expert,
            first,
            lax.rem(expert, EARLY_EXPERTS),
            between,
        )
        return 0

    lax.fori_loop(0, local_count, body, 0)
    gate_all[place.task] = grad_gates[place.task]
    peers = (place.core, place.across, place.far)

    def gate_move(way):
        return remote(
            grad_gates.at[peers[way]],
            gate_all.at[place.task],
            gate_sent.at[way],
            gate_landed.at[way],
            task=peers[way],
        )

    for way in range(3):
        gate_move(way).start()
    hidden, grad_pre, joint = work[4], work[5], work[2]

    def part(ref, source):
        return ref.at[pl.ds(0, SEQ), pl.ds(pl.multiple_of(source * D, 128), D)]

    back = Return(
        place, lambda source: part(hidden, source), RETURNS, land, joint, sent, landed
    )
    turns = list(range(len(SCATTER_POINTS), len(whole) + outers - 1))
    for order, (source, after) in enumerate(
        (
            (place.far, back.by_core),
            (place.across, back.to_across),
            (place.core, back.to_core),
            (place.task, None),
        )
    ):

        def store(piece, rows, mix, grad, source=source, after=after):
            part(grad_pre, source)[rows, :] = mix
            part(hidden, source)[rows, :] = grad
            if after:
                after(piece)

        combine(slots, first, local_count, work[6], columns, source, store)
        pltpu.make_async_copy(part(grad_pre, source), mixes.at[source], mix_sem.at[order]).start()
        if order in COMBINE_TURNS and turns:
            scatter_turn(whole, stores, turns.pop(0))
    for turn in turns:
        scatter_turn(whole, stores, turn)
    for index, one in enumerate(split):
        one.settle(keeps[index])
    for piece in range(RETURNS):
        grad_rows[back.rows(piece), :] = back.finish(piece)
    for way in range(3):
        gate_move(way).wait()
    for order in range(groups):
        pltpu.make_async_copy(
            part(grad_pre, place.task), mixes.at[place.task], mix_sem.at[order]
        ).wait()
    for expert in range(late):
        for copy in keep(expert):
            copy.wait()


def kinds(units, kind):
    return [unit for unit in units if unit[1] == kind]


def expert_sending(*operands):
    groups, experts = operands[2].shape[:2]
    local_count, thin = operands[6].shape[:2]
    wide, size = operands[7].shape[1], lax.axis_size("dp")
    late, outers = local_count - EARLY_EXPERTS, size // 2
    tiles = ((thin, FF), (wide, D))
    return pl.pallas_call(
        functools.partial(expert_sending_kernel, outers),
        out_shape=(
            shape(late, D, FF, dtype=bf16),
            shape(late, FF, D, dtype=bf16),
            shape(groups, local_count, SEQ),
            shape(groups, SEQ, D, dtype=bf16),
            shape(SEQ, D),
            *[shape(len(kinds(SCATTER_EARLY, kind)), *tiles[kind]) for kind in range(2)],
            *[
                shape(len(kinds(SCATTER_SPLIT, kind)), outers, *tiles[kind], dtype=bf16)
                for kind in range(2)
            ],
            shape(late, D, FF, dtype=bf16),
            shape(late, FF, D, dtype=bf16),
        ),
        in_specs=[ANY] * 2 + [VMEM] * 2 + [ANY] * 4,
        out_specs=[ANY] * 2 + [VMEM, ANY] + [VMEM] * 5 + [ANY] * 2,
        scratch_shapes=expert_scratch(groups, local_count, experts)
        + [
            pltpu.VMEM((groups, SEQ, D), bf16),
            pltpu.VMEM((groups, SEQ, D), bf16),
            pltpu.VMEM((EARLY_EXPERTS, D, FF), bf16),
            pltpu.VMEM((EARLY_EXPERTS, FF, D), bf16),
            pltpu.VMEM((local_count, D, FF), bf16),
            pltpu.VMEM((local_count, FF, D), bf16),
            pltpu.VMEM((groups, local_count, SEQ), f32),
            pltpu.VMEM((3, SEQ, D), bf16),
            pltpu.SemaphoreType.DMA((3, RETURNS)),
            pltpu.SemaphoreType.DMA((3, RETURNS)),
            pltpu.SemaphoreType.DMA((3,)),
            pltpu.SemaphoreType.DMA((3,)),
            pltpu.SemaphoreType.DMA((groups,)),
            pltpu.SemaphoreType.DMA((late, 2)),
            pltpu.SemaphoreType.DMA((EARLY_EXPERTS, 2)),
            pltpu.SemaphoreType.DMA((2, groups)),
        ]
        + gather_semaphores(len(GATHER_LATE + GATHER_SPLIT), size)
        + scatter_scratch(SCATTER_EARLY, outers, tiles)
        + scatter_scratch(SCATTER_SPLIT, outers, tiles, line=False),
        compiler_params=params(collective_id=1, has_side_effects=True),
    )(*operands)


def attend_back(packed, grad_mixed, logs, grad_packed, grad_keys, grad_values, between, done):
    zero = jnp.array(0, bf16)
    blocks = SEQ // QUERY_BWD

    def head_pair(pair):
        queries, keys, values = (
            slice(part * D + pair * PAIR, part * D + (pair + 1) * PAIR) for part in range(3)
        )
        key_rows, value_rows = packed[:, keys], packed[:, values]

        def block(index, _):
            rows = rows_at(index, QUERY_BWD)
            query_rows = packed[rows, queries] * jnp.array(HEAD_DIM**-0.5, bf16)
            grad_rows = grad_mixed[rows, queries]
            grad_query, part_keys, part_values = [], 0.0, 0.0
            for half in range(2):
                lanes = half_lanes(QUERY_BWD, half)
                own = jnp.where(lanes, query_rows, zero)
                own_grad = jnp.where(lanes, grad_rows, zero)
                head = 2 * pair + half
                probs = jnp.exp(dot_rt(key_rows, own) - logs[head : head + 1, rows])
                grad_probs = dot_rt(value_rows, own_grad)
                mean = jnp.sum(probs * grad_probs, axis=0, keepdims=True)
                grad_scores = (probs * (grad_probs - mean)).astype(bf16)
                part_values += dot(probs.astype(bf16), own_grad)
                part_keys += dot(grad_scores, own)
                grad_query.append(dot_lt(grad_scores, key_rows))
            grad_packed[rows, queries] = (
                jnp.where(half_lanes(QUERY_BWD, 0), grad_query[0], grad_query[1])
                * HEAD_DIM**-0.5
            ).astype(bf16)
            grad_keys[...] = jnp.where(index == 0, part_keys, grad_keys[...] + part_keys)
            grad_values[...] = jnp.where(index == 0, part_values, grad_values[...] + part_values)
            between(pair, index)
            return 0

        lax.fori_loop(0, blocks, block, 0)
        grad_packed[:, keys] = grad_keys[...].astype(bf16)
        grad_packed[:, values] = grad_values[...].astype(bf16)
        done(pair, (queries, keys, values))

    for pair in range(HEADS // 2):
        head_pair(pair)


def second_back(
    grad_rows, cotangent, gain, bias, mid, w_proj, router, grad_logits, grad_norm, grad_router, outs
):
    grad_mid, grad_low, grad_mixed = outs
    grad_norm[...] = jnp.zeros_like(grad_norm)
    grad_router[...] = jnp.zeros_like(grad_router)
    for index in range(SEQ // ROWS):
        rows = slice(index * ROWS, (index + 1) * ROWS)
        mid_rows = mid[rows, :]
        own_logits = grad_logits[:, rows]
        grad_in_rows = grad_rows(rows) + lax.dot_general(
            own_logits,
            router[...],
            (((0,), (0,)), ((), ())),
            precision=HIGHEST,
            preferred_element_type=f32,
        )
        grad_in, grad_gain, grad_bias, unit = norm_back(mid_rows, grad_in_rows, gain[1:2, :])
        grad_router[...] += jnp.dot(
            own_logits,
            unit * gain[1:2, :] + bias[1:2, :],
            precision=HIGHEST,
            preferred_element_type=f32,
        )
        grad_norm[1:2, :] += grad_gain
        grad_norm[3:4, :] += grad_bias
        grad_mid_rows = cotangent[rows, :] + grad_in
        grad_mid[rows, :] = grad_mid_rows
        low_rows = grad_mid_rows.astype(bf16)
        grad_low[rows, :] = low_rows
        grad_mixed[rows, :] = dot_rt(low_rows, w_proj[...]).astype(bf16)


def first_back(image, gain, w_qkv, grad_packed, grad_mid, grad_image, grad_norm):
    def block(index, _):
        rows = rows_at(index, ROWS)
        grad_rows = dot_rt(grad_packed[rows, :], w_qkv[...])
        grad_in, grad_gain, grad_bias, _ = norm_back(image[rows, :], grad_rows, gain[0:1, :])
        grad_image[rows, :] = grad_mid[rows, :] + grad_in
        grad_norm[0:1, :] += grad_gain
        grad_norm[2:3, :] += grad_bias
        return 0

    lax.fori_loop(0, SEQ // ROWS, block, 0)


def logit_grads(probs, grad_gates):
    route = jnp.concatenate([grad_gates[group] for group in range(grad_gates.shape[0])], axis=0)
    return probs[...] * (route - jnp.sum(probs[...] * route, axis=0, keepdims=True))


def backward_scratch():
    return [
        pltpu.VMEM((SEQ, D), f32),
        pltpu.VMEM((SEQ, D), bf16),
        pltpu.VMEM((SEQ, D), bf16),
        pltpu.VMEM((SEQ, 3 * D), bf16),
        pltpu.VMEM((SEQ, PAIR), f32),
        pltpu.VMEM((SEQ, PAIR), f32),
        pltpu.VMEM((SEQ, D), bf16),
    ]


def backward_kernel(*refs):
    image, cotangent, gain, bias, mid, w_qkv, w_proj, router = refs[:8]
    packed, mixed, logs, mixes, grad_normed, grad_gates, probs = refs[8:15]
    activations, grad_image, grad_norm, grad_router, grad_shared = refs[15:20]
    grad_mid, grad_low, grad_mixed, grad_packed, grad_keys, grad_values, normed_first = refs[20:]
    groups = mixes.shape[0]

    def added(parts, rows):
        total = parts[0, rows, :].astype(f32)
        for source in range(1, groups):
            total += parts[source, rows, :].astype(f32)
        return total

    activations[...] = mid[...] + added(mixes, slice(None))
    second_back(
        lambda rows: added(grad_normed, rows),
        cotangent,
        gain,
        bias,
        mid,
        w_proj,
        router,
        logit_grads(probs, grad_gates),
        grad_norm,
        grad_router,
        (grad_mid, grad_low, grad_mixed),
    )
    first_norm(image, gain, bias, normed_first)
    grad_shared[:, 3 * D :] = dot_lt(mixed[...], grad_low[...]).astype(bf16)
    attend_back(
        packed,
        grad_mixed,
        logs,
        grad_packed,
        grad_keys,
        grad_values,
        lambda pair, index: None,
        lambda pair, columns: None,
    )
    first_back(image, gain, w_qkv, grad_packed, grad_mid, grad_image, grad_norm)
    grad_shared[:, : 3 * D] = dot_lt(normed_first[...], grad_packed[...]).astype(bf16)


def backward_part(*operands):
    router = operands[7]
    return pl.pallas_call(
        backward_kernel,
        out_shape=(
            shape(SEQ, D),
            shape(SEQ, D),
            shape(4, D),
            shape(router.shape[0], D),
            shape(D, 4 * D, dtype=bf16),
        ),
        in_specs=[VMEM] * 15,
        out_specs=[VMEM] * 5,
        scratch_shapes=backward_scratch(),
        compiler_params=params(),
    )(*operands)


def backward_sending_kernel(outers, groups, *refs):
    image, cotangent, gain, bias, mid, w_qkv, w_proj, router = refs[:8]
    packed, mixed, logs, mixes_all, grad_rows, grad_gates, probs, late_in, late_out = refs[8:17]
    parts_in, parts_out = refs[17:19]
    activations, grad_image, grad_norm, grad_router, shard_qkv, shard_proj = refs[19:25]
    shard_in, shard_out = refs[25:27]
    grad_mid, grad_low, grad_mixed, grad_packed, grad_keys, grad_values, normed_first = refs[27:34]
    norm_sums, router_sums, shared, mixes, land, joint, back_sent, back_landed = refs[34:42]
    mix_sem, grad_sem, grad_refs = refs[42], refs[43], refs[44 : 44 + len(SCATTER_LATE)]
    refs = refs[44 + len(SCATTER_LATE) :]
    place = Place(outers)
    size, pieces = 2 * outers, HEADS // 2 + 1
    shards = (shard_in, shard_out)
    loads = [
        pltpu.make_async_copy(
            (late_in, late_out)[kind].at[expert - EARLY_EXPERTS],
            grad_refs[index],
            grad_sem.at[index],
        )
        for index, (expert, kind) in enumerate(SCATTER_LATE)
    ]
    mix_load = pltpu.make_async_copy(mixes_all, mixes, mix_sem)
    for copy in (*loads, mix_load):
        copy.start()
    place.greet_all(groups)
    at = 7 * len(SCATTER_LATE)
    late = make_scatters(
        place,
        [
            blocks_of(place, grad_refs[index], shards[kind].shape[1])
            for index, (_, kind) in enumerate(SCATTER_LATE)
        ],
        refs[:at],
    )
    split_blocks = []
    for index, (_, kind) in enumerate(SCATTER_SPLIT):
        number = [other[1] for other in SCATTER_SPLIT[:index]].count(kind)
        split_blocks.append(
            (
                lambda outer, parts=(parts_in, parts_out)[kind], number=number: parts.at[
                    number, outer
                ],
                None,
            )
        )
    split = make_scatters(place, split_blocks, refs[at:], side=False)
    at += 4 * len(SCATTER_SPLIT)
    small = make_scatters(
        place,
        [blocks_of(place, shared.at[piece], shard_proj.shape[0]) for piece in range(pieces)],
        refs[at:],
    )
    at += 7 * pieces
    norms = Spread("dp", place, size, *refs[at : at + 3])
    norms_task = Spread("task", place, groups, *refs[at + 3 : at + 6])
    routers = Spread("dp", place, size, *refs[at + 6 : at + 9])
    totals = [
        Spread("task", place, groups, *[ref.at[piece] for ref in refs[at + 9 : at + 12]])
        for piece in range(pieces)
    ]
    stores = []
    for unit in SCATTER_SPLIT + SCATTER_LATE:
        number = sorted(kinds(SCATTER_SPLIT + SCATTER_LATE, unit[1])).index(unit)

        def store(rows, shard=shards[unit[1]], number=number):
            shard[number] = rows

        stores.append(store)
    for one in split:
        one.hop(0)
    for copy, one in zip(loads, late):
        copy.wait()
        one.start()
    mix_load.wait()
    back = Return(
        place, lambda source: mixes.at[source], 1, land, joint, back_sent, back_landed
    )
    back.by_core(0)
    back.to_core(0)
    second_back(
        lambda rows: grad_rows[rows, :],
        cotangent,
        gain,
        bias,
        mid,
        w_proj,
        router,
        logit_grads(probs, grad_gates),
        norm_sums,
        router_sums,
        (grad_mid, grad_low, grad_mixed),
    )
    back.to_across(0)
    first_norm(image, gain, bias, normed_first)
    shared[pieces - 1] = dot_lt(mixed[...], grad_low[...]).astype(bf16)
    small[pieces - 1].start()
    routers.give(router_sums[...])
    blocks = SEQ // QUERY_BWD
    units, keeps = split + late, stores
    names = dict(zip("stuvwxyz", range(len(units))))
    names.update({str(piece): len(units) + piece for piece in range(pieces)})
    units, keeps = units + small, keeps + [one.give for one in totals]

    def run(acts):
        for act in acts:
            unit, hop = names[act[0]], int(act[1])
            if hop < outers - 1:
                units[unit].hop(hop)
            else:
                units[unit].finish(keeps[unit])

    def between(pair, index):
        for at, acts in BACKWARD_POINTS.items():
            if at // blocks == pair:
                pl.when(index == at % blocks)(lambda acts=acts: run(acts))

    def done(pair, columns):
        both = jnp.concatenate([grad_packed[:, part] for part in columns], axis=1)
        shared[pair] = dot_lt(normed_first[...], both).astype(bf16)
        small[pair].start()

    attend_back(
        packed, grad_mixed, logs, grad_packed, grad_keys, grad_values, between, done
    )
    first_back(image, gain, w_qkv, grad_packed, grad_mid, grad_image, norm_sums)
    norms.give(norm_sums[...])
    activations[...] = mid[...] + back.finish(0)
    run(BACKWARD_THEN[0])
    grad_router[...] = routers.take()
    norms_task.give(norms.take())
    run(BACKWARD_THEN[1])
    grad_norm[...] = norms_task.take()
    for piece in (pieces - 1, *range(pieces - 1)):
        rows = totals[piece].take()
        if piece == pieces - 1:
            shard_proj[...] = rows
        else:
            for part in range(3):
                column = part * D + piece * PAIR
                shard_qkv[:, column : column + PAIR] = rows[:, part * PAIR : (part + 1) * PAIR]


def backward_sending(*operands):
    router = operands[7]
    experts, size = router.shape[0], lax.axis_size("dp")
    outers, thin, wide, pieces = size // 2, D // size, FF // size, HEADS // 2 + 1
    groups = lax.axis_size("task")
    tiles, wholes = ((thin, FF), (wide, D)), ((D, FF), (FF, D))
    ends = SCATTER_SPLIT + SCATTER_LATE

    def spread(peers, *dims, lead=(), dtype=f32):
        return [pltpu.VMEM((*lead, peers, *dims), dtype)] + [
            pltpu.SemaphoreType.DMA((*lead, peers - 1))
        ] * 2

    return pl.pallas_call(
        functools.partial(backward_sending_kernel, outers, groups),
        out_shape=(
            shape(SEQ, D),
            shape(SEQ, D),
            shape(8, D),
            shape(experts, D),
            shape(thin, 3 * D),
            shape(thin, D),
            *[shape(len(kinds(ends, kind)), *tiles[kind]) for kind in range(2)],
        ),
        in_specs=[VMEM] * 11 + [ANY] + [VMEM] * 3 + [ANY] * 2 + [VMEM] * 2,
        out_specs=[VMEM] * 8,
        scratch_shapes=backward_scratch()
        + [
            pltpu.VMEM((8, D), f32),
            pltpu.VMEM((experts, D), f32),
            pltpu.VMEM((pieces, D, D), bf16),
            pltpu.VMEM((groups, SEQ, D), bf16),
            pltpu.VMEM((3, SEQ, D), bf16),
            pltpu.VMEM((SEQ, D), bf16),
            pltpu.SemaphoreType.DMA((3, 1)),
            pltpu.SemaphoreType.DMA((3, 1)),
            pltpu.SemaphoreType.DMA,
            pltpu.SemaphoreType.DMA((len(SCATTER_LATE),)),
        ]
        + [pltpu.VMEM(wholes[kind], bf16) for _, kind in SCATTER_LATE]
        + scatter_scratch(SCATTER_LATE, outers, tiles)
        + scatter_scratch(SCATTER_SPLIT, outers, tiles, side=False)
        + scatter_scratch(range(pieces), outers, (thin, D))
        + spread(size, 8, D)
        + spread(groups, 8, D)
        + spread(size, experts, D)
        + spread(groups, thin, D, lead=(pieces,), dtype=bf16),
        compiler_params=params(collective_id=2, has_side_effects=True),
    )(*operands)


def local(
    layer_input,
    cotangent,
    norm_gain,
    norm_bias,
    w_qkv,
    w_proj,
    router,
    w_in,
    w_out,
    choices,
    top_count,
):
    groups = lax.axis_size("task")
    local_count = w_in.shape[0]
    image = layer_input.reshape(SEQ, D)
    grad_rows = cotangent.reshape(SEQ, D)
    router_rows = router[0].T
    experts = router_rows.shape[0]
    routes = choices.reshape(SEQ, TOPMAX)

    def swap(array):
        return lax.all_to_all(array, "task", split_axis=0, concat_axis=0, tiled=True)

    sending = groups == 4 and lax.axis_size("dp") == 8 and local_count == 4
    if sending:
        (
            mid,
            packed,
            mixed,
            logs,
            probs,
            normed,
            cot_rows,
            slots,
            gates,
            full_qkv,
            full_proj,
            full_in,
            full_out,
        ) = forward_sending(
            top_count,
            image,
            grad_rows,
            norm_gain,
            norm_bias,
            (w_qkv, w_proj, w_in, w_out),
            router_rows,
            routes,
        )
        (
            late_in,
            late_out,
            grad_gates,
            mixes,
            grad_normed,
            early_in,
            early_out,
            parts_in,
            parts_out,
            _,
            _,
        ) = expert_sending(normed, cot_rows, slots, gates, full_in, full_out, w_in, w_out)
        (
            activations,
            grad_image,
            grad_norm,
            grad_router,
            grad_qkv,
            grad_proj,
            grad_in,
            grad_out,
        ) = backward_sending(
            image,
            grad_rows,
            norm_gain,
            norm_bias,
            mid,
            full_qkv,
            full_proj,
            router_rows,
            packed,
            mixed,
            logs,
            mixes,
            grad_normed,
            grad_gates,
            probs,
            late_in,
            late_out,
            parts_in,
            parts_out,
        )
        grad_in = jnp.concatenate([early_in, grad_in], axis=0)
        grad_out = jnp.concatenate([early_out, grad_out], axis=0)
    else:
        full_qkv, full_proj, full_in, full_out = (
            lax.all_gather(w_qkv, "dp", axis=0, tiled=True),
            lax.all_gather(w_proj, "dp", axis=0, tiled=True),
            lax.all_gather(w_in, "dp", axis=1, tiled=True),
            lax.all_gather(w_out, "dp", axis=1, tiled=True),
        )
        mid, packed, mixed, logs, normed, slots, gates, probs = forward_part(
            top_count,
            image,
            norm_gain,
            norm_bias,
            full_qkv,
            full_proj,
            router_rows,
            routes,
        )
        normed = lax.all_gather(normed, "task")
        cot_rows = lax.all_gather(grad_rows.astype(bf16), "task")
        slots = swap(slots.reshape(groups, local_count, SEQ))
        gates = swap(gates.reshape(groups, local_count, SEQ))
        grad_in, grad_out, grad_gates, mixes, grad_normed = expert_part(
            normed, cot_rows, slots, gates, full_in, full_out
        )
        activations, grad_image, grad_norm, grad_router, grad_shared = backward_part(
            image,
            grad_rows,
            norm_gain,
            norm_bias,
            mid,
            full_qkv,
            full_proj,
            router_rows,
            packed,
            mixed,
            logs,
            swap(mixes),
            swap(grad_normed),
            swap(grad_gates),
            probs,
        )
        grad_in = lax.psum_scatter(grad_in, "dp", scatter_dimension=1, tiled=True).astype(f32)
        grad_out = lax.psum_scatter(grad_out, "dp", scatter_dimension=1, tiled=True).astype(f32)
        grad_shared = lax.psum_scatter(grad_shared, "dp", scatter_dimension=0, tiled=True)
        grad_shared = lax.psum(grad_shared, "task").astype(f32)
        grad_qkv, grad_proj = grad_shared[:, : 3 * D], grad_shared[:, 3 * D :]
        grad_router = lax.psum(grad_router, "dp")
        grad_norm = lax.psum(grad_norm, ("task", "dp"))
    return (
        activations.reshape(layer_input.shape),
        grad_image.reshape(layer_input.shape),
        grad_norm[:2],
        grad_norm[2:4],
        grad_qkv,
        grad_proj,
        grad_router.T[None],
        grad_in,
        grad_out,
    )


def solution(mesh):
    tokens = P("task", "dp", None, None)
    rows = P("dp", None)
    blocks = P("task", "dp", None)
    routed = P("task", None, None)
    return jax.shard_map(
        local,
        mesh=mesh,
        in_specs=(tokens, tokens, P(), P(), rows, rows, routed, blocks, blocks, tokens, P("task")),
        out_specs=(tokens, tokens, P(), P(), rows, rows, routed, blocks, blocks),
        check_vma=False,
    )
```

```python
import functools

import jax
import jax.numpy as jnp
from jax import lax
from jax.experimental import pallas as pl
from jax.experimental.pallas import tpu as pltpu
from jax.sharding import PartitionSpec as P

D = 384
FF = 1536
HEADS = 6
HEAD_DIM = 64
PAIR = 2 * HEAD_DIM
TOPMAX = 4
SEQ = 1024
CAP = 320

f32 = jnp.float32
bf16 = jnp.bfloat16
HIGHEST = lax.Precision.HIGHEST
EPSILON = 1e-06
ROOT_HALF = 0.7071067811865476
NORMAL = 0.3989422804014327

FF_TILE = 512
ROW_TILE = 640
QUERY_FWD = 256
QUERY_BWD = 256
ROWS = 256
RETURNS = 2

GATHER_WHOLE = ((0, 0), (0, 1), (1, 0), (1, 1))
GATHER_SPLIT = ((2, 0), (2, 1))
GATHER_LATE = ((3, 0), (3, 1))
SCATTER_EARLY = ((0, 0), (0, 1), (1, 0))
SCATTER_SPLIT = ((1, 1), (2, 0))
SCATTER_LATE = ((2, 1), (3, 0), (3, 1))
EARLY_EXPERTS = 2

GATHER_POINTS = {2: ((0, 1), (0, 3), (1, 0), (1, 4)), 3: ((0, 2), (1, 1), (1, 4), (3, 0))}
SCATTER_POINTS = ((3, 1), (3, 3))
COMBINE_TURNS = (1, 2, 3)

AHEAD = 2
FORWARD_FIRST = ((0, 1), (1, 1))
FORWARD_POINTS = {
    0: ((2, 1), (3, 1)),
    3: ((4, 1), (5, 1)),
    8: ((0, 2), (1, 2)),
    11: ((2, 2), (3, 2)),
}
FORWARD_THEN = (((4, 2), (5, 2)), ((0, 3), (1, 3), (2, 3), (3, 3), (4, 3), (5, 3)))

BACKWARD_POINTS = {
    3: ("s1", "u0",),
    8: ("t1", "s2", "v0",),
    11: ("u1",),
}
BACKWARD_THEN = (
    ("w0", "t2", "s3", "v1", "u2", "30", "00", "10",),
    ("w1", "t3", "v2", "u3", "20", "31", "01", "11", "w2", "v3", "21", "32", "02", "12", "33", "03", "22", "13", "23", "w3",),
)


VMEM = pl.BlockSpec(memory_space=pltpu.VMEM)
SMEM = pl.BlockSpec(memory_space=pltpu.SMEM)
ANY = pl.BlockSpec(memory_space=pl.ANY)


def shape(*dims, dtype=f32):
    return jax.ShapeDtypeStruct(dims, dtype)


def params(**more):
    return pltpu.CompilerParams(vmem_limit_bytes=62 * 2**20, **more)


def dot(a, b):
    return lax.dot_general(a, b, (((1,), (0,)), ((), ())), preferred_element_type=f32)


def dot_rt(a, b):
    return lax.dot_general(a, b, (((1,), (1,)), ((), ())), preferred_element_type=f32)


def dot_lt(a, b):
    return lax.dot_general(a, b, (((0,), (0,)), ((), ())), preferred_element_type=f32)


def rows_at(index, size):
    return pl.ds(pl.multiple_of(index * size, size), size)


def normalize(rows):
    centered = rows - jnp.mean(rows, axis=1, keepdims=True)
    scale = lax.rsqrt(jnp.mean(centered * centered, axis=1, keepdims=True) + EPSILON)
    return centered * scale, scale


def norm_back(rows, grad_rows, gain):
    unit, scale = normalize(rows)
    scaled = grad_rows * gain
    grad_in = scale * (
        scaled
        - jnp.mean(scaled, axis=1, keepdims=True)
        - unit * jnp.mean(scaled * unit, axis=1, keepdims=True)
    )
    grad_gain = jnp.sum(grad_rows * unit, axis=0, keepdims=True)
    return grad_in, grad_gain, jnp.sum(grad_rows, axis=0, keepdims=True), unit


def half_lanes(rows, half):
    lanes = lax.broadcasted_iota(jnp.int32, (rows, PAIR), 1)
    return (lanes < HEAD_DIM) if half == 0 else (lanes >= HEAD_DIM)


def remote(source, target, sent, landed, **device):
    return pltpu.make_async_remote_copy(
        src_ref=source,
        dst_ref=target,
        send_sem=sent,
        recv_sem=landed,
        device_id=device,
        device_id_type=pl.DeviceIdType.MESH,
    )


class Place:
    def __init__(self, outers):
        self.dp = lax.axis_index("dp")
        self.task = lax.axis_index("task")
        self.outers = outers
        self.outer, self.inner = self.dp // 2, self.dp % 2
        self.has_up, self.has_down = self.outer + 1 < outers, self.outer > 0
        self.up, self.down = self.dp + 2, self.dp - 2
        self.side = self.dp + 1 - 2 * self.inner
        self.core = self.task + 1 - 2 * (self.task % 2)
        self.across = self.task + 2 - 4 * (self.task // 2)
        self.far = self.across + 1 - 2 * (self.task % 2)

    def signal(self, **device):
        pl.semaphore_signal(
            pltpu.get_barrier_semaphore(),
            inc=1,
            device_id=device,
            device_id_type=pl.DeviceIdType.MESH,
        )

    def greet(self, far=False):
        pl.when(self.has_up)(lambda: self.signal(dp=self.up))
        pl.when(self.has_down)(lambda: self.signal(dp=self.down))
        self.signal(dp=self.side)
        self.signal(task=self.core)
        self.signal(task=self.across)
        if far:
            self.signal(task=self.far)
        others = 3 + int(far) + self.has_up.astype(jnp.int32) + self.has_down.astype(jnp.int32)
        pl.semaphore_wait(pltpu.get_barrier_semaphore(), others)

    def greet_all(self, groups):
        size = 2 * self.outers
        for ahead in range(1, size):
            self.signal(dp=lax.rem(self.dp + ahead, size))
        for ahead in range(1, groups):
            self.signal(task=lax.rem(self.task + ahead, groups))
        pl.semaphore_wait(pltpu.get_barrier_semaphore(), size + groups - 2)


class Gather:
    def __init__(self, place, shards, sent, landed, stay):
        self.place, self.shards = place, shards
        self.sent, self.landed, self.stay = sent, landed, stay

    def move(self, unit, source, way, device, first=None):
        _, size, full, _ = self.shards[unit]
        target = full.at[rows_at(source, size)]
        return remote(
            target if first is None else first,
            target,
            self.sent.at[unit, source, way],
            self.landed.at[unit, source],
            dp=device,
        )

    def local(self, unit):
        own, size, full, _ = self.shards[unit]
        target = full.at[rows_at(self.place.dp, size)]
        return pltpu.make_async_copy(own, target, self.stay.at[unit])

    def along(self, unit, source, up, down):
        place = self.place
        if up:
            pl.when(place.has_up)(lambda: self.move(unit, source, 0, place.up).start())
        if down:
            pl.when(place.has_down)(lambda: self.move(unit, source, 1, place.down).start())

    def to_side(self, unit, outer):
        own, size = self.shards[unit][:2]
        source = 2 * outer + self.place.inner
        return self.move(unit, source, 2, self.place.side, own.at[rows_at(source, size)])

    def start(self, unit):
        place = self.place
        own, mode = self.shards[unit][0], self.shards[unit][3]
        if mode == "side":
            for outer in range(place.outers):
                self.to_side(unit, outer).start()
            return
        if mode == "turned":
            self.move(unit, place.dp, 2, place.side, own).start()
        pl.when(place.has_up)(lambda: self.move(unit, place.dp, 0, place.up, own).start())
        pl.when(place.has_down)(lambda: self.move(unit, place.dp, 1, place.down, own).start())
        if mode == "both":
            self.move(unit, place.dp, 2, place.side, own).start()
        if self.stay is not None:
            self.local(unit).start()

    def step(self, unit, hop):
        place, mode = self.place, self.shards[unit][3]
        if hop == 0:
            self.move(unit, place.side, 0, place.dp).wait_recv()
            self.along(unit, place.side, True, True)
            return
        for column in (place.dp, place.side) if mode == "turned" else (place.dp,):

            @pl.when(place.outer >= hop)
            def _():
                self.move(unit, column - 2 * hop, 0, place.dp).wait_recv()
                self.along(unit, column - 2 * hop, True, False)
                if mode == "both":
                    self.move(unit, column - 2 * hop, 2, place.side).start()

            @pl.when(place.outer + hop < place.outers)
            def _():
                self.move(unit, column + 2 * hop, 1, place.dp).wait_recv()
                self.along(unit, column + 2 * hop, False, True)
                if mode == "both":
                    self.move(unit, column + 2 * hop, 2, place.side).start()

    def finish(self, unit):
        place, mode = self.place, self.shards[unit][3]
        if self.stay is not None:
            self.local(unit).wait()
        if mode == "turned":
            self.move(unit, place.dp, 2, place.side).wait_send()
        for outer in range(place.outers):
            own, other = 2 * outer + place.inner, 2 * outer + 1 - place.inner
            if mode in ("both", "side"):
                self.move(unit, other, 2, place.dp).wait_recv()
                self.move(unit, own, 2, place.side).wait_send()
            if mode == "side":
                continue
            for source in (own, other) if mode == "turned" else (own,):
                pl.when((outer <= place.outer) & place.has_up)(
                    lambda source=source: self.move(unit, source, 0, place.up).wait_send()
                )
                pl.when((outer >= place.outer) & place.has_down)(
                    lambda source=source: self.move(unit, source, 1, place.down).wait_send()
                )


def gather_semaphores(units, size):
    return [
        pltpu.SemaphoreType.DMA((units, size, 3)),
        pltpu.SemaphoreType.DMA((units, size)),
    ]


class Share:
    def __init__(self, place, view, sent, landed):
        self.place, self.view, self.sent, self.landed = place, view, sent, landed

    def move(self, source, way, **device):
        return remote(
            self.view(source),
            self.view(source),
            self.sent.at[way],
            self.landed.at[way],
            **device,
        )

    def start(self):
        place = self.place
        self.move(place.task, 0, task=place.across).start()
        self.move(place.task, 1, task=place.core).start()

    def relay(self):
        place = self.place
        self.move(place.across, 0, task=place.across).wait_recv()
        self.move(place.across, 2, task=place.core).start()

    def finish(self):
        place = self.place
        self.move(place.task, 0, task=place.across).wait_send()
        self.move(place.core, 1, task=place.core).wait()
        self.move(place.across, 2, task=place.core).wait()


class Scatter:
    def __init__(self, place, mine, theirs, side, line, fold, sems):
        self.place, self.mine, self.theirs = place, mine, theirs
        self.side, self.line, self.fold = side, line, fold
        self.side_sent, self.side_landed, self.line_sent, self.line_landed = sems

    def to_side(self, outer):
        return remote(
            self.theirs(outer),
            self.side.at[outer],
            self.side_sent.at[outer],
            self.side_landed.at[outer],
            dp=self.place.side,
        )

    def along(self, outer, slot, device):
        return remote(
            self.fold.at[outer],
            self.line.at[slot],
            self.line_sent.at[outer],
            self.line_landed.at[slot],
            dp=device,
        )

    def start(self):
        outers = self.place.outers
        for near in range(outers // 2):
            self.to_side(outers - 1 - near).start()
            self.to_side(near).start()

    def total(self, outer, *slots):
        rows = self.mine(outer)[...].astype(f32)
        if self.side is not None:
            self.to_side(outer).wait_recv()
            rows += self.side[outer].astype(f32)
        for slot in slots:
            self.along(outer, slot, self.place.dp).wait_recv()
            rows += self.line[slot].astype(f32)
        return rows

    def settle(self, store):
        for outer in range(self.place.outers):
            store(outer, self.total(outer).astype(bf16))
            self.to_side(outer).wait_send()

    def hop(self, step):
        place, outers = self.place, self.place.outers

        @pl.when(place.outer == step)
        def _():
            for outer in range(outers - 1, step, -1):
                rows = self.total(outer, *([outer] if step else []))
                self.fold[outer] = rows.astype(bf16)
                self.along(outer, outer, place.up).start()

        @pl.when(place.outer == outers - 1 - step)
        def _():
            for outer in range(outers - 1 - step):
                rows = self.total(outer, *([outer] if step else []))
                self.fold[outer] = rows.astype(bf16)
                slot = outers if outer == outers - 2 - step else outer
                self.along(outer, slot, place.down).start()

    def finish(self, store):
        place, outers = self.place, self.place.outers
        for outer in range(outers):

            @pl.when(place.outer == outer)
            def _():
                below, above = [outer] * (outer > 0), [outers] * (outer < outers - 1)
                store(self.total(outer, *below, *above))
                for other in range(outers):
                    if other != outer:
                        self.along(other, other, place.dp).wait_send()

            if self.side is not None:
                self.to_side(outer).wait_send()


def scatter_turn(units, stores, turn):
    outers = units[0].place.outers
    for step in range(outers - 1):
        if 0 <= turn - step < len(units):
            units[turn - step].hop(step)
    last = turn - outers + 1
    if 0 <= last < len(units):
        units[last].finish(stores[last])


def blocks_of(place, ref, size):
    return (
        lambda outer: ref.at[rows_at(2 * outer + place.inner, size)],
        lambda outer: ref.at[rows_at(2 * outer + 1 - place.inner, size)],
    )


def tile_of(kind, thin, wide):
    return (wide, D) if kind else (thin, FF)


def scatter_scratch(units, outers, tiles, side=True, line=True):
    scratch = []
    for unit in units:
        tile = tiles[unit[1]] if isinstance(unit, tuple) else tiles
        for asked, slots in ((side, outers), (line, outers + 1), (line, outers)):
            if asked:
                scratch.append(pltpu.VMEM((slots, *tile), bf16))
        for asked, count in ((side, outers), (side, outers), (line, outers), (line, outers + 1)):
            if asked:
                scratch.append(pltpu.SemaphoreType.DMA((count,)))
    return scratch


def make_scatters(place, blocks, refs, side=True, line=True):
    count = 3 * side + 4 * line
    scatters = []
    for index, (mine, theirs) in enumerate(blocks):
        own = list(refs[index * count : (index + 1) * count])
        buffers = [own.pop(0) if asked else None for asked in (side, line, line)]
        sems = [own.pop(0) if asked else None for asked in (side, side, line, line)]
        scatters.append(Scatter(place, mine, theirs, *buffers, sems))
    return scatters


class Spread:
    def __init__(self, axis, place, count, land, sent, landed):
        self.axis, self.me, self.count = axis, getattr(place, axis), count
        self.land, self.sent, self.landed = land, sent, landed

    def move(self, source, ahead):
        return remote(
            self.land.at[source],
            self.land.at[source],
            self.sent.at[ahead - 1],
            self.landed.at[ahead - 1],
            **{self.axis: lax.rem(self.me + ahead, self.count)},
        )

    def give(self, rows):
        self.land[self.me] = rows.astype(self.land.dtype)
        for ahead in range(1, self.count):
            self.move(self.me, ahead).start()

    def take(self):
        for ahead in range(1, self.count):
            self.move(lax.rem(self.me + self.count - ahead, self.count), ahead).wait_recv()
            self.move(self.me, ahead).wait_send()
        total = self.land[0].astype(f32)
        for index in range(1, self.count):
            total += self.land[index].astype(f32)
        return total


class Return:
    def __init__(self, place, parts, pieces, land, joint, sent, landed):
        self.place, self.parts, self.pieces = place, parts, pieces
        self.land, self.joint, self.sent, self.landed = land, joint, sent, landed
        self.size = SEQ // pieces

    def rows(self, piece):
        return pl.ds(piece * self.size, self.size)

    def move(self, way, piece):
        place, rows = self.place, self.rows(piece)
        source = [
            self.parts(place.core).at[rows],
            self.parts(place.far).at[rows],
            self.joint.at[rows],
        ][way]
        return remote(
            source,
            self.land.at[way, rows],
            self.sent.at[way, piece],
            self.landed.at[way, piece],
            task=place.across if way == 2 else place.core,
        )

    def to_core(self, piece):
        self.move(0, piece).start()

    def by_core(self, piece):
        self.move(1, piece).start()

    def to_across(self, piece):
        rows = self.rows(piece)
        self.move(1, piece).wait_recv()
        joint = self.parts(self.place.across)[rows, :].astype(f32)
        joint += self.land[1, rows, :].astype(f32)
        self.joint[rows, :] = joint.astype(bf16)
        self.move(2, piece).start()

    def finish(self, piece):
        rows = self.rows(piece)
        self.move(0, piece).wait()
        self.move(1, piece).wait_send()
        self.move(2, piece).wait()
        total = self.parts(self.place.task)[rows, :].astype(f32)
        return total + self.land[0, rows, :].astype(f32) + self.land[2, rows, :].astype(f32)


def attend(packed, mixed, totals, index, between):
    zero = jnp.array(0, bf16)
    rows = rows_at(index, QUERY_FWD)

    def head_pair(pair, _):
        queries, keys, values = (rows_at(pair + part * (D // PAIR), PAIR) for part in range(3))
        key_rows, value_rows = packed[:, keys], packed[:, values]
        query_rows = packed[rows, queries] * jnp.array(HEAD_DIM**-0.5, bf16)
        outs, logs = [], []
        for half in range(2):
            own = jnp.where(half_lanes(QUERY_FWD, half), query_rows, zero)
            scores = dot_rt(own, key_rows)
            top = jnp.max(scores, axis=1, keepdims=True)
            weights = jnp.exp(scores - top)
            total = jnp.sum(weights, axis=1, keepdims=True)
            outs.append(dot(weights.astype(bf16), value_rows) * (1.0 / total))
            logs.append(top + jnp.log(total))
        mixed[rows, queries] = jnp.where(half_lanes(QUERY_FWD, 0), outs[0], outs[1]).astype(bf16)
        lanes = lax.broadcasted_iota(jnp.int32, (QUERY_FWD, 8), 1)
        totals[rows, :] = jnp.where(
            lanes == 2 * pair,
            logs[0],
            jnp.where(lanes == 2 * pair + 1, logs[1], totals[rows, :]),
        )
        between(index * (HEADS // 2) + pair)
        return 0

    lax.fori_loop(0, HEADS // 2, head_pair, 0)


def first_norm(image, gain, bias, normed_first):
    def block(index, _):
        rows = rows_at(index, ROWS)
        unit, _ = normalize(image[rows, :])
        normed_first[rows, :] = (unit * gain[0:1, :] + bias[0:1, :]).astype(bf16)
        return 0

    lax.fori_loop(0, SEQ // ROWS, block, 0)


def number_slots(choices, top_count, experts):
    named = choices[...].T
    numbers = lax.broadcasted_iota(jnp.int32, (experts, SEQ), 0)
    used = jnp.zeros((experts, SEQ), f32)
    for choice in range(TOPMAX):
        hit = (named[choice : choice + 1, :] == numbers) & (choice < top_count[0])
        used = used + jnp.where(hit, 1.0, 0.0)
    earlier = lax.broadcasted_iota(jnp.int32, (SEQ, SEQ), 0) < lax.broadcasted_iota(
        jnp.int32, (SEQ, SEQ), 1
    )
    before = dot(used.astype(bf16), jnp.where(earlier, 1.0, 0.0).astype(bf16))
    return jnp.where(used > 0, before, -1.0).astype(jnp.int32)


def mid_block(index, image, gain, bias, w_proj, router, mixed, mid, probs):
    rows = rows_at(index, QUERY_FWD)
    mid_rows = image[rows, :] + dot(mixed[rows, :], w_proj[...])
    mid[rows, :] = mid_rows
    unit, _ = normalize(mid_rows)
    normed_rows = unit * gain[1:2, :] + bias[1:2, :]
    logits = lax.dot_general(
        router[...],
        normed_rows,
        (((1,), (1,)), ((), ())),
        precision=HIGHEST,
        preferred_element_type=f32,
    )
    powers = jnp.exp(logits - jnp.max(logits, axis=0, keepdims=True))
    probs[:, rows] = powers / jnp.sum(powers, axis=0, keepdims=True)
    return normed_rows.astype(bf16)


def forward_kernel(
    top_count,
    image,
    gain,
    bias,
    w_qkv,
    w_proj,
    router,
    choices,
    mid,
    packed,
    mixed,
    logs,
    normed,
    slots,
    gates,
    probs,
    normed_first,
    totals,
):
    first_norm(image, gain, bias, normed_first)
    slots[...] = number_slots(choices, top_count, router.shape[0])
    packed[...] = dot(normed_first[...], w_qkv[...]).astype(bf16)
    totals[...] = jnp.zeros_like(totals)

    def block(index, _):
        attend(packed, mixed, totals, index, lambda point: None)
        normed[rows_at(index, QUERY_FWD), :] = mid_block(
            index, image, gain, bias, w_proj, router, mixed, mid, probs
        )
        return 0

    lax.fori_loop(0, SEQ // QUERY_FWD, block, 0)
    logs[...] = totals[...].T
    gates[...] = jnp.where(slots[...] >= 0, probs[...], 0.0)


def forward_part(top_count, image, gain, bias, w_qkv, w_proj, router, choices):
    experts = router.shape[0]
    return pl.pallas_call(
        forward_kernel,
        out_shape=(
            shape(SEQ, D),
            shape(SEQ, 3 * D, dtype=bf16),
            shape(SEQ, D, dtype=bf16),
            shape(8, SEQ),
            shape(SEQ, D, dtype=bf16),
            shape(experts, SEQ, dtype=jnp.int32),
            shape(experts, SEQ),
            shape(experts, SEQ),
        ),
        in_specs=[SMEM] + [VMEM] * 7,
        out_specs=[VMEM] * 8,
        scratch_shapes=[pltpu.VMEM((SEQ, D), bf16), pltpu.VMEM((SEQ, 8), f32)],
        compiler_params=params(),
    )(top_count, image, gain, bias, w_qkv, w_proj, router, choices)


def forward_sending_kernel(
    outers,
    top_count,
    image,
    cotangent,
    gain,
    bias,
    w_qkv,
    w_proj,
    w_in,
    w_out,
    router,
    choices,
    mid,
    packed,
    mixed,
    logs,
    probs,
    normed_all,
    cot_all,
    slots_all,
    gates_all,
    full_qkv,
    full_proj,
    full_in,
    full_out,
    normed_first,
    totals,
    sent,
    landed,
    stay,
    share_sent,
    share_landed,
):
    place = Place(outers)
    task = place.task
    shards = [
        (w_qkv, w_qkv.shape[0], full_qkv, "both"),
        (w_proj, w_proj.shape[0], full_proj, "both"),
    ]
    for expert, kind in GATHER_WHOLE + GATHER_SPLIT:
        own, full = ((w_in, full_in), (w_out, full_out))[kind]
        mode = "line" if (expert, kind) in GATHER_SPLIT else "both"
        shards.append((own.at[expert], own.shape[1], full.at[expert], mode))
    gather = Gather(place, shards, sent, landed, stay)
    shared, routed = range(2), range(2, len(shards))
    cot_all[task] = cotangent[...].astype(bf16)
    place.greet()
    for unit in shared:
        gather.start(unit)

    def share(index, view):
        return Share(place, view, share_sent.at[index], share_landed.at[index])

    cot = share(0, lambda source: cot_all.at[source])
    slot = share(1, lambda source: slots_all.at[source])
    gate = share(2, lambda source: gates_all.at[source])
    for unit in routed[:AHEAD]:
        gather.start(unit)
    cot.start()
    first_norm(image, gain, bias, normed_first)
    for hop in range(1, outers):
        for unit in shared:
            gather.step(unit, hop)
    for unit in routed[AHEAD:]:
        gather.start(unit)
    slots_all[task] = number_slots(choices, top_count, router.shape[0])
    slot.start()
    totals[...] = jnp.zeros_like(totals)
    for unit in shared:
        gather.finish(unit)
    packed[...] = dot(normed_first[...], full_qkv[...]).astype(bf16)
    cot.relay()
    slot.relay()

    def chunk(index):
        return share(3 + index, lambda source: normed_all.at[source, rows_at(index, QUERY_FWD)])

    def run(acts):
        for unit, hop in acts:
            if unit < len(routed):
                gather.step(routed[unit], hop)

    blocks = SEQ // QUERY_FWD
    run(FORWARD_FIRST)

    def block(index, _):
        def between(point):
            for at, acts in FORWARD_POINTS.items():
                pl.when(point == at)(lambda acts=acts: run(acts))

        attend(packed, mixed, totals, index, between)
        normed_all[task, rows_at(index, QUERY_FWD), :] = mid_block(
            index, image, gain, bias, full_proj, router, mixed, mid, probs
        )
        chunk(index).start()
        pl.when(index > 0)(lambda: chunk(index - 1).relay())
        return 0

    lax.fori_loop(0, blocks, block, 0)
    gates_all[task] = jnp.where(slots_all[task] >= 0, probs[...], 0.0)
    gate.start()
    logs[...] = totals[...].T
    run(FORWARD_THEN[0])
    chunk(blocks - 1).relay()
    gate.relay()
    run(FORWARD_THEN[1])
    for one in [cot, slot, gate] + [chunk(index) for index in range(blocks)]:
        one.finish()
    for unit in routed:
        gather.finish(unit)


def forward_sending(top_count, image, cotangent, gain, bias, shards, router, choices):
    w_qkv, w_proj, w_in, w_out = shards
    experts, size = router.shape[0], lax.axis_size("dp")
    groups, early = lax.axis_size("task"), 1 + GATHER_SPLIT[-1][0]
    units, shares = 2 + len(GATHER_WHOLE + GATHER_SPLIT), 3 + SEQ // QUERY_FWD
    return pl.pallas_call(
        functools.partial(forward_sending_kernel, size // 2),
        out_shape=(
            shape(SEQ, D),
            shape(SEQ, 3 * D, dtype=bf16),
            shape(SEQ, D, dtype=bf16),
            shape(8, SEQ),
            shape(experts, SEQ),
            shape(groups, SEQ, D, dtype=bf16),
            shape(groups, SEQ, D, dtype=bf16),
            shape(groups, experts, SEQ, dtype=jnp.int32),
            shape(groups, experts, SEQ),
            shape(D, 3 * D, dtype=bf16),
            shape(D, D, dtype=bf16),
            shape(early, D, FF, dtype=bf16),
            shape(early, FF, D, dtype=bf16),
        ),
        in_specs=[SMEM] + [VMEM] * 10,
        out_specs=[VMEM] * 11 + [ANY] * 2,
        scratch_shapes=[
            pltpu.VMEM((SEQ, D), bf16),
            pltpu.VMEM((SEQ, 8), f32),
            *gather_semaphores(units, size),
            pltpu.SemaphoreType.DMA((units,)),
            pltpu.SemaphoreType.DMA((shares, 3)),
            pltpu.SemaphoreType.DMA((shares, 3)),
        ],
        compiler_params=params(collective_id=0, has_side_effects=True),
    )(top_count, image, cotangent, gain, bias, w_qkv, w_proj, w_in, w_out, router, choices)


def slot_hits(slots, source, expert):
    return lax.broadcasted_iota(jnp.int32, (CAP, SEQ), 0) == slots[source, pl.ds(expert, 1), :]


def ones_at(hits):
    return jnp.where(hits, 1.0, 0.0).astype(bf16)


def one_expert(operands, work, grads, expert, first, slot, between):
    normed, cotangent, slots, gates, w_in, w_out = operands
    rows_in, rows_grad, rows_cot, rows_gate, hidden, grad_pre, sent = work
    grad_in, grad_out, grad_gates = grads
    groups = normed.shape[0]
    width = groups * CAP
    between(0)
    for source in range(groups):
        own = slice(source * CAP, (source + 1) * CAP)
        hits = slot_hits(slots, source, first + expert)
        picks = ones_at(hits)
        rows_in[own, :] = dot(picks, normed[source]).astype(bf16)
        cot_rows = dot(picks, cotangent[source])
        gate = jnp.sum(
            jnp.where(hits, gates[source, pl.ds(first + expert, 1), :], 0.0),
            axis=1,
            keepdims=True,
        )
        rows_cot[own, :] = cot_rows.astype(bf16)
        rows_grad[own, :] = (gate * cot_rows).astype(bf16)
        rows_gate[own, :] = jnp.broadcast_to(gate, (CAP, 128))
    between(1)

    def tile(index, _):
        units = rows_at(index // (width // ROW_TILE), FF_TILE)
        rows = rows_at(lax.rem(index, width // ROW_TILE), ROW_TILE)
        pre = dot(rows_in[rows, :], w_in[slot, :, units])
        grad_hidden = dot_rt(rows_grad[rows, :], w_out[slot, units, :])
        share = 0.5 * lax.erf(pre * ROOT_HALF) + 0.5
        slope = share + pre * (NORMAL * jnp.exp(-0.5 * pre * pre))
        hidden[rows, units] = (pre * share).astype(bf16)
        grad_pre[rows, units] = (grad_hidden * slope).astype(bf16)
        return 0

    lax.fori_loop(0, (FF // FF_TILE) * (width // ROW_TILE), tile, 0)
    between(2)
    for source in range(groups):
        own = slice(source * CAP, (source + 1) * CAP)
        kept = rows_at(expert, CAP)
        out_rows = dot(hidden[own, :], w_out[slot]).astype(bf16).astype(f32)
        sent[source, kept, :D] = (rows_gate[own, 0:1] * out_rows).astype(bf16)
        sent[source, kept, D:] = dot_rt(grad_pre[own, :], w_in[slot]).astype(bf16)
        grad_gate = jnp.sum(rows_cot[own, :].astype(f32) * out_rows, axis=1, keepdims=True)
        hits = slot_hits(slots, source, first + expert)
        grad_gates[source, pl.ds(expert, 1), :] = jnp.sum(
            jnp.where(hits, grad_gate, 0.0), axis=0, keepdims=True
        )
    between(3)
    grad_in[expert] = dot_lt(rows_in[...], grad_pre[...]).astype(bf16)
    grad_out[expert] = dot_lt(rows_grad[...], hidden[...]).astype(bf16).T
    between(4)


def combine(slots, first, local_count, sent, columns, source, store):
    size = SEQ // RETURNS
    columns[...] = slots[source].T
    for piece in range(RETURNS):
        rows = pl.ds(piece * size, size)
        lanes = lax.broadcasted_iota(jnp.int32, (size, CAP), 1)
        mine = lax.broadcasted_iota(jnp.int32, (size, columns.shape[1]), 1)
        picks = []
        for expert in range(local_count):
            column = jnp.max(
                jnp.where(mine == first + expert, columns[rows, :], -1), axis=1, keepdims=True
            )
            picks.append(ones_at(lanes == column))
        back = dot(jnp.concatenate(picks, axis=1), sent[source])
        store(piece, rows, back[:, :D].astype(bf16), back[:, D:].astype(bf16))


def expert_scratch(groups, local_count, experts):
    width = groups * CAP
    return [
        pltpu.VMEM((width, D), bf16),
        pltpu.VMEM((width, D), bf16),
        pltpu.VMEM((width, D), bf16),
        pltpu.VMEM((width, 128), f32),
        pltpu.VMEM((width, FF), bf16),
        pltpu.VMEM((width, FF), bf16),
        pltpu.VMEM((groups, local_count * CAP, 2 * D), bf16),
        pltpu.VMEM((SEQ, experts), jnp.int32),
    ]


def expert_kernel(*refs):
    operands, grads, (mixes, grad_normed) = refs[:6], refs[6:9], refs[9:11]
    work, columns = refs[11:18], refs[18]
    groups, local_count = operands[0].shape[0], operands[4].shape[0]

    def body(expert, _):
        one_expert(operands, work, grads, expert, 0, expert, lambda point: None)
        return 0

    lax.fori_loop(0, local_count, body, 0)
    for source in range(groups):

        def store(piece, rows, mix, grad, source=source):
            mixes[source, rows, :] = mix
            grad_normed[source, rows, :] = grad

        combine(operands[2], 0, local_count, work[6], columns, source, store)


def expert_part(*operands):
    groups, local_count = operands[0].shape[0], operands[4].shape[0]
    return pl.pallas_call(
        expert_kernel,
        out_shape=(
            shape(local_count, D, FF, dtype=bf16),
            shape(local_count, FF, D, dtype=bf16),
            shape(groups, local_count, SEQ),
            shape(groups, SEQ, D, dtype=bf16),
            shape(groups, SEQ, D, dtype=bf16),
        ),
        in_specs=[VMEM] * 6,
        out_specs=[VMEM] * 5,
        scratch_shapes=expert_scratch(groups, local_count, operands[2].shape[1]),
        compiler_params=params(),
    )(*operands)


def expert_sending_kernel(outers, *refs):
    normed_all, cot_all, slots, gates, early_in, early_out, w_in, w_out = refs[:8]
    late_in, late_out, gate_all, mixes, grad_rows, shard_in, shard_out, parts_in, parts_out = refs[8:17]
    full_in, full_out = refs[17:19]
    work, columns = refs[19:26], refs[26]
    normed, cotangent, slot_in, slot_out, grad_in, grad_out, grad_gates, land = refs[27:35]
    sent, landed, gate_sent, gate_landed, mix_sem, late_sem, slot_sem, token_sem = refs[35:43]
    gather_sems, scatter_refs = refs[43:45], refs[45:]
    place = Place(outers)
    groups, local_count, size = normed.shape[0], grad_in.shape[0], 2 * outers
    late = local_count - EARLY_EXPERTS
    first = place.task * local_count
    grads, shares = (grad_in, grad_out), (w_in.shape[1], w_out.shape[1])

    def tokens():
        return [
            pltpu.make_async_copy(whole.at[source], ref.at[source], token_sem.at[kind, source])
            for source in range(groups)
            for kind, (whole, ref) in enumerate(((normed_all, normed), (cot_all, cotangent)))
        ]

    def load(expert):
        slot, copies = expert % EARLY_EXPERTS, []
        for kind in range(2):
            target, sem = (slot_in, slot_out)[kind].at[slot], slot_sem.at[slot, kind]
            early, own = (early_in, early_out)[kind], (w_in, w_out)[kind]
            full = (full_in, full_out)[kind]
            if expert < EARLY_EXPERTS:
                copies.append(pltpu.make_async_copy(early.at[expert], target, sem.at[0]))
                continue
            for ahead in range(size):
                block = lax.rem(place.dp + ahead, size)
                rows = rows_at(block, shares[kind])
                source = full.at[expert - EARLY_EXPERTS, rows]
                if (expert, kind) in GATHER_SPLIT:
                    if ahead % 2 == 0:
                        source = early.at[expert, rows]
                elif ahead == 0:
                    source = own.at[expert]
                copies.append(pltpu.make_async_copy(source, target.at[rows], sem.at[ahead]))
        return copies

    def keep(expert):
        return [
            pltpu.make_async_copy(
                grads[kind].at[EARLY_EXPERTS + expert],
                (late_in, late_out)[kind].at[expert],
                late_sem.at[expert, kind],
            )
            for kind in range(2)
        ]

    for copy in tokens() + load(0):
        copy.start()
    place.greet(far=True)
    shards = []
    for expert, kind in GATHER_LATE + GATHER_SPLIT:
        full = (full_in, full_out)[kind].at[expert - EARLY_EXPERTS]
        if (expert, kind) in GATHER_SPLIT:
            shards.append(((early_in, early_out)[kind].at[expert], shares[kind], full, "side"))
        else:
            shards.append(((w_in, w_out)[kind].at[expert], shares[kind], full, "turned"))
    gather = Gather(place, shards, *gather_sems, None)
    turned = range(len(GATHER_LATE))
    for unit in range(len(shards)):
        gather.start(unit)
    for copy in load(1):
        copy.start()
    per_full, per_side = 7 * len(SCATTER_EARLY), 3 * len(SCATTER_SPLIT)

    def scatters(units, refs, **parts):
        return make_scatters(
            place,
            [blocks_of(place, grads[kind].at[expert], shares[kind]) for expert, kind in units],
            refs,
            **parts,
        )

    whole = scatters(SCATTER_EARLY, scatter_refs[:per_full])
    split = scatters(SCATTER_SPLIT, scatter_refs[per_full : per_full + per_side], line=False)
    stores, keeps = [], []
    for expert, kind in SCATTER_EARLY:

        def store(rows, shard=(shard_in, shard_out)[kind], expert=expert):
            shard[expert] = rows

        stores.append(store)
    for index, (_, kind) in enumerate(SCATTER_SPLIT):
        at = [other[1] for other in SCATTER_SPLIT[:index]].count(kind)

        def settle(outer, rows, parts=(parts_in, parts_out)[kind], at=at):
            parts[at, outer] = rows

        keeps.append(settle)
    steps = {}

    def plan(expert, point, *acts):
        steps.setdefault((expert, point), []).extend(acts)

    plan(0, 0, *[copy.wait for copy in tokens()])
    for expert in range(EARLY_EXPERTS):
        plan(expert, 1, *[copy.wait for copy in load(expert)])
    for unit in turned:
        for hop, at in enumerate(GATHER_POINTS[GATHER_LATE[unit][0]]):
            plan(*at, lambda unit=unit, hop=hop: gather.step(unit, hop))
    for expert in range(EARLY_EXPERTS, local_count):
        units = [
            unit
            for unit, (owner, _) in enumerate(GATHER_LATE + GATHER_SPLIT)
            if owner == expert
        ]
        plan(expert, 0, *[lambda unit=unit: gather.finish(unit) for unit in units])
        plan(expert, 0, *[copy.start for copy in load(expert)])
        plan(expert, 1, *[copy.wait for copy in load(expert)])
        plan(expert, 4, *[copy.start for copy in keep(expert - EARLY_EXPERTS)])
    for index, (expert, _) in enumerate(SCATTER_EARLY):
        plan(expert, 4, whole[index].start)
    for index, (expert, _) in enumerate(SCATTER_SPLIT):
        plan(expert, 4, split[index].start)
    for turn, at in enumerate(SCATTER_POINTS):
        plan(*at, lambda turn=turn: scatter_turn(whole, stores, turn))

    def body(expert, _):
        def between(point):
            for at in range(local_count):
                acts = steps.get((at, point))
                if acts:

                    @pl.when(expert == at)
                    def _():
                        for act in acts:
                            act()

        one_expert(
            (normed, cotangent, slots, gates, slot_in, slot_out),
            work,
            (grad_in, grad_out, grad_gates),
            expert,
            first,
            lax.rem(expert, EARLY_EXPERTS),
            between,
        )
        return 0

    lax.fori_loop(0, local_count, body, 0)
    gate_all[place.task] = grad_gates[place.task]
    peers = (place.core, place.across, place.far)

    def gate_move(way):
        return remote(
            grad_gates.at[peers[way]],
            gate_all.at[place.task],
            gate_sent.at[way],
            gate_landed.at[way],
            task=peers[way],
        )

    for way in range(3):
        gate_move(way).start()
    hidden, grad_pre, joint = work[4], work[5], work[2]

    def part(ref, source):
        return ref.at[pl.ds(0, SEQ), pl.ds(pl.multiple_of(source * D, 128), D)]

    back = Return(
        place, lambda source: part(hidden, source), RETURNS, land, joint, sent, landed
    )
    turns = list(range(len(SCATTER_POINTS), len(whole) + outers - 1))
    for order, (source, after) in enumerate(
        (
            (place.far, back.by_core),
            (place.across, back.to_across),
            (place.core, back.to_core),
            (place.task, None),
        )
    ):

        def store(piece, rows, mix, grad, source=source, after=after):
            part(grad_pre, source)[rows, :] = mix
            part(hidden, source)[rows, :] = grad
            if after:
                after(piece)

        combine(slots, first, local_count, work[6], columns, source, store)
        pltpu.make_async_copy(part(grad_pre, source), mixes.at[source], mix_sem.at[order]).start()
        if order in COMBINE_TURNS and turns:
            scatter_turn(whole, stores, turns.pop(0))
    for turn in turns:
        scatter_turn(whole, stores, turn)
    for index, one in enumerate(split):
        one.settle(keeps[index])
    for piece in range(RETURNS):
        grad_rows[back.rows(piece), :] = back.finish(piece)
    for way in range(3):
        gate_move(way).wait()
    for order in range(groups):
        pltpu.make_async_copy(
            part(grad_pre, place.task), mixes.at[place.task], mix_sem.at[order]
        ).wait()
    for expert in range(late):
        for copy in keep(expert):
            copy.wait()


def kinds(units, kind):
    return [unit for unit in units if unit[1] == kind]


def expert_sending(*operands):
    groups, experts = operands[2].shape[:2]
    local_count, thin = operands[6].shape[:2]
    wide, size = operands[7].shape[1], lax.axis_size("dp")
    late, outers = local_count - EARLY_EXPERTS, size // 2
    tiles = ((thin, FF), (wide, D))
    return pl.pallas_call(
        functools.partial(expert_sending_kernel, outers),
        out_shape=(
            shape(late, D, FF, dtype=bf16),
            shape(late, FF, D, dtype=bf16),
            shape(groups, local_count, SEQ),
            shape(groups, SEQ, D, dtype=bf16),
            shape(SEQ, D),
            *[shape(len(kinds(SCATTER_EARLY, kind)), *tiles[kind]) for kind in range(2)],
            *[
                shape(len(kinds(SCATTER_SPLIT, kind)), outers, *tiles[kind], dtype=bf16)
                for kind in range(2)
            ],
            shape(late, D, FF, dtype=bf16),
            shape(late, FF, D, dtype=bf16),
        ),
        in_specs=[ANY] * 2 + [VMEM] * 2 + [ANY] * 4,
        out_specs=[ANY] * 2 + [VMEM, ANY] + [VMEM] * 5 + [ANY] * 2,
        scratch_shapes=expert_scratch(groups, local_count, experts)
        + [
            pltpu.VMEM((groups, SEQ, D), bf16),
            pltpu.VMEM((groups, SEQ, D), bf16),
            pltpu.VMEM((EARLY_EXPERTS, D, FF), bf16),
            pltpu.VMEM((EARLY_EXPERTS, FF, D), bf16),
            pltpu.VMEM((local_count, D, FF), bf16),
            pltpu.VMEM((local_count, FF, D), bf16),
            pltpu.VMEM((groups, local_count, SEQ), f32),
            pltpu.VMEM((3, SEQ, D), bf16),
            pltpu.SemaphoreType.DMA((3, RETURNS)),
            pltpu.SemaphoreType.DMA((3, RETURNS)),
            pltpu.SemaphoreType.DMA((3,)),
            pltpu.SemaphoreType.DMA((3,)),
            pltpu.SemaphoreType.DMA((groups,)),
            pltpu.SemaphoreType.DMA((late, 2)),
            pltpu.SemaphoreType.DMA((EARLY_EXPERTS, 2, size)),
            pltpu.SemaphoreType.DMA((2, groups)),
        ]
        + gather_semaphores(len(GATHER_LATE + GATHER_SPLIT), size)
        + scatter_scratch(SCATTER_EARLY, outers, tiles)
        + scatter_scratch(SCATTER_SPLIT, outers, tiles, line=False),
        compiler_params=params(collective_id=1, has_side_effects=True),
    )(*operands)


def attend_back(packed, grad_mixed, logs, grad_packed, grad_keys, grad_values, between, done):
    zero = jnp.array(0, bf16)
    blocks = SEQ // QUERY_BWD

    def head_pair(pair):
        queries, keys, values = (
            slice(part * D + pair * PAIR, part * D + (pair + 1) * PAIR) for part in range(3)
        )
        key_rows, value_rows = packed[:, keys], packed[:, values]

        def block(index, _):
            rows = rows_at(index, QUERY_BWD)
            query_rows = packed[rows, queries] * jnp.array(HEAD_DIM**-0.5, bf16)
            grad_rows = grad_mixed[rows, queries]
            grad_query, part_keys, part_values = [], 0.0, 0.0
            for half in range(2):
                lanes = half_lanes(QUERY_BWD, half)
                own = jnp.where(lanes, query_rows, zero)
                own_grad = jnp.where(lanes, grad_rows, zero)
                head = 2 * pair + half
                probs = jnp.exp(dot_rt(key_rows, own) - logs[head : head + 1, rows])
                grad_probs = dot_rt(value_rows, own_grad)
                mean = jnp.sum(probs * grad_probs, axis=0, keepdims=True)
                grad_scores = (probs * (grad_probs - mean)).astype(bf16)
                part_values += dot(probs.astype(bf16), own_grad)
                part_keys += dot(grad_scores, own)
                grad_query.append(dot_lt(grad_scores, key_rows))
            grad_packed[rows, queries] = (
                jnp.where(half_lanes(QUERY_BWD, 0), grad_query[0], grad_query[1])
                * HEAD_DIM**-0.5
            ).astype(bf16)
            grad_keys[...] = jnp.where(index == 0, part_keys, grad_keys[...] + part_keys)
            grad_values[...] = jnp.where(index == 0, part_values, grad_values[...] + part_values)
            between(pair, index)
            return 0

        lax.fori_loop(0, blocks, block, 0)
        grad_packed[:, keys] = grad_keys[...].astype(bf16)
        grad_packed[:, values] = grad_values[...].astype(bf16)
        done(pair, (queries, keys, values))

    for pair in range(HEADS // 2):
        head_pair(pair)


def second_back(
    grad_rows, cotangent, gain, bias, mid, w_proj, router, grad_logits, grad_norm, grad_router, outs
):
    grad_mid, grad_low, grad_mixed = outs
    grad_norm[...] = jnp.zeros_like(grad_norm)
    grad_router[...] = jnp.zeros_like(grad_router)
    for index in range(SEQ // ROWS):
        rows = slice(index * ROWS, (index + 1) * ROWS)
        mid_rows = mid[rows, :]
        own_logits = grad_logits[:, rows]
        grad_in_rows = grad_rows(rows) + lax.dot_general(
            own_logits,
            router[...],
            (((0,), (0,)), ((), ())),
            precision=HIGHEST,
            preferred_element_type=f32,
        )
        grad_in, grad_gain, grad_bias, unit = norm_back(mid_rows, grad_in_rows, gain[1:2, :])
        grad_router[...] += jnp.dot(
            own_logits,
            unit * gain[1:2, :] + bias[1:2, :],
            precision=HIGHEST,
            preferred_element_type=f32,
        )
        grad_norm[1:2, :] += grad_gain
        grad_norm[3:4, :] += grad_bias
        grad_mid_rows = cotangent[rows, :] + grad_in
        grad_mid[rows, :] = grad_mid_rows
        low_rows = grad_mid_rows.astype(bf16)
        grad_low[rows, :] = low_rows
        grad_mixed[rows, :] = dot_rt(low_rows, w_proj[...]).astype(bf16)


def first_back(image, gain, w_qkv, grad_packed, grad_mid, grad_image, grad_norm):
    def block(index, _):
        rows = rows_at(index, ROWS)
        grad_rows = dot_rt(grad_packed[rows, :], w_qkv[...])
        grad_in, grad_gain, grad_bias, _ = norm_back(image[rows, :], grad_rows, gain[0:1, :])
        grad_image[rows, :] = grad_mid[rows, :] + grad_in
        grad_norm[0:1, :] += grad_gain
        grad_norm[2:3, :] += grad_bias
        return 0

    lax.fori_loop(0, SEQ // ROWS, block, 0)


def logit_grads(probs, grad_gates):
    route = jnp.concatenate([grad_gates[group] for group in range(grad_gates.shape[0])], axis=0)
    return probs[...] * (route - jnp.sum(probs[...] * route, axis=0, keepdims=True))


def backward_scratch():
    return [
        pltpu.VMEM((SEQ, D), f32),
        pltpu.VMEM((SEQ, D), bf16),
        pltpu.VMEM((SEQ, D), bf16),
        pltpu.VMEM((SEQ, 3 * D), bf16),
        pltpu.VMEM((SEQ, PAIR), f32),
        pltpu.VMEM((SEQ, PAIR), f32),
        pltpu.VMEM((SEQ, D), bf16),
    ]


def backward_kernel(*refs):
    image, cotangent, gain, bias, mid, w_qkv, w_proj, router = refs[:8]
    packed, mixed, logs, mixes, grad_normed, grad_gates, probs = refs[8:15]
    activations, grad_image, grad_norm, grad_router, grad_shared = refs[15:20]
    grad_mid, grad_low, grad_mixed, grad_packed, grad_keys, grad_values, normed_first = refs[20:]
    groups = mixes.shape[0]

    def added(parts, rows):
        total = parts[0, rows, :].astype(f32)
        for source in range(1, groups):
            total += parts[source, rows, :].astype(f32)
        return total

    activations[...] = mid[...] + added(mixes, slice(None))
    second_back(
        lambda rows: added(grad_normed, rows),
        cotangent,
        gain,
        bias,
        mid,
        w_proj,
        router,
        logit_grads(probs, grad_gates),
        grad_norm,
        grad_router,
        (grad_mid, grad_low, grad_mixed),
    )
    first_norm(image, gain, bias, normed_first)
    grad_shared[:, 3 * D :] = dot_lt(mixed[...], grad_low[...]).astype(bf16)
    attend_back(
        packed,
        grad_mixed,
        logs,
        grad_packed,
        grad_keys,
        grad_values,
        lambda pair, index: None,
        lambda pair, columns: None,
    )
    first_back(image, gain, w_qkv, grad_packed, grad_mid, grad_image, grad_norm)
    grad_shared[:, : 3 * D] = dot_lt(normed_first[...], grad_packed[...]).astype(bf16)


def backward_part(*operands):
    router = operands[7]
    return pl.pallas_call(
        backward_kernel,
        out_shape=(
            shape(SEQ, D),
            shape(SEQ, D),
            shape(4, D),
            shape(router.shape[0], D),
            shape(D, 4 * D, dtype=bf16),
        ),
        in_specs=[VMEM] * 15,
        out_specs=[VMEM] * 5,
        scratch_shapes=backward_scratch(),
        compiler_params=params(),
    )(*operands)


def backward_sending_kernel(outers, groups, *refs):
    image, cotangent, gain, bias, mid, w_qkv, w_proj, router = refs[:8]
    packed, mixed, logs, mixes_all, grad_rows, grad_gates, probs, late_in, late_out = refs[8:17]
    parts_in, parts_out = refs[17:19]
    activations, grad_image, grad_norm, grad_router, shard_qkv, shard_proj = refs[19:25]
    shard_in, shard_out = refs[25:27]
    grad_mid, grad_low, grad_mixed, grad_packed, grad_keys, grad_values, normed_first = refs[27:34]
    norm_sums, router_sums, shared, mixes, land, joint, back_sent, back_landed = refs[34:42]
    mix_sem, grad_sem, grad_refs = refs[42], refs[43], refs[44 : 44 + len(SCATTER_LATE)]
    refs = refs[44 + len(SCATTER_LATE) :]
    place = Place(outers)
    size, pieces = 2 * outers, HEADS // 2 + 1
    shards = (shard_in, shard_out)
    loads = [
        pltpu.make_async_copy(
            (late_in, late_out)[kind].at[expert - EARLY_EXPERTS],
            grad_refs[index],
            grad_sem.at[index],
        )
        for index, (expert, kind) in enumerate(SCATTER_LATE)
    ]
    mix_load = pltpu.make_async_copy(mixes_all, mixes, mix_sem)
    for copy in (*loads, mix_load):
        copy.start()
    place.greet_all(groups)
    at = 7 * len(SCATTER_LATE)
    late = make_scatters(
        place,
        [
            blocks_of(place, grad_refs[index], shards[kind].shape[1])
            for index, (_, kind) in enumerate(SCATTER_LATE)
        ],
        refs[:at],
    )
    split_blocks = []
    for index, (_, kind) in enumerate(SCATTER_SPLIT):
        number = [other[1] for other in SCATTER_SPLIT[:index]].count(kind)
        split_blocks.append(
            (
                lambda outer, parts=(parts_in, parts_out)[kind], number=number: parts.at[
                    number, outer
                ],
                None,
            )
        )
    split = make_scatters(place, split_blocks, refs[at:], side=False)
    at += 4 * len(SCATTER_SPLIT)
    small = make_scatters(
        place,
        [blocks_of(place, shared.at[piece], shard_proj.shape[0]) for piece in range(pieces)],
        refs[at:],
    )
    at += 7 * pieces
    norms = Spread("dp", place, size, *refs[at : at + 3])
    norms_task = Spread("task", place, groups, *refs[at + 3 : at + 6])
    routers = Spread("dp", place, size, *refs[at + 6 : at + 9])
    totals = [
        Spread("task", place, groups, *[ref.at[piece] for ref in refs[at + 9 : at + 12]])
        for piece in range(pieces)
    ]
    stores = []
    for unit in SCATTER_SPLIT + SCATTER_LATE:
        number = sorted(kinds(SCATTER_SPLIT + SCATTER_LATE, unit[1])).index(unit)

        def store(rows, shard=shards[unit[1]], number=number):
            shard[number] = rows

        stores.append(store)
    for one in split:
        one.hop(0)
    for copy, one in zip(loads, late):
        copy.wait()
        one.start()
    mix_load.wait()
    back = Return(
        place, lambda source: mixes.at[source], 1, land, joint, back_sent, back_landed
    )
    back.by_core(0)
    back.to_core(0)
    second_back(
        lambda rows: grad_rows[rows, :],
        cotangent,
        gain,
        bias,
        mid,
        w_proj,
        router,
        logit_grads(probs, grad_gates),
        norm_sums,
        router_sums,
        (grad_mid, grad_low, grad_mixed),
    )
    back.to_across(0)
    first_norm(image, gain, bias, normed_first)
    shared[pieces - 1] = dot_lt(mixed[...], grad_low[...]).astype(bf16)
    small[pieces - 1].start()
    routers.give(router_sums[...])
    blocks = SEQ // QUERY_BWD
    units, keeps = split + late, stores
    names = dict(zip("stuvwxyz", range(len(units))))
    names.update({str(piece): len(units) + piece for piece in range(pieces)})
    units, keeps = units + small, keeps + [one.give for one in totals]

    def run(acts):
        for act in acts:
            unit, hop = names[act[0]], int(act[1])
            if hop < outers - 1:
                units[unit].hop(hop)
            else:
                units[unit].finish(keeps[unit])

    def between(pair, index):
        for at, acts in BACKWARD_POINTS.items():
            if at // blocks == pair:
                pl.when(index == at % blocks)(lambda acts=acts: run(acts))

    def done(pair, columns):
        both = jnp.concatenate([grad_packed[:, part] for part in columns], axis=1)
        shared[pair] = dot_lt(normed_first[...], both).astype(bf16)
        small[pair].start()

    attend_back(
        packed, grad_mixed, logs, grad_packed, grad_keys, grad_values, between, done
    )
    first_back(image, gain, w_qkv, grad_packed, grad_mid, grad_image, norm_sums)
    norms.give(norm_sums[...])
    activations[...] = mid[...] + back.finish(0)
    run(BACKWARD_THEN[0])
    grad_router[...] = routers.take()
    norms_task.give(norms.take())
    run(BACKWARD_THEN[1])
    grad_norm[...] = norms_task.take()
    for piece in (pieces - 1, *range(pieces - 1)):
        rows = totals[piece].take()
        if piece == pieces - 1:
            shard_proj[...] = rows
        else:
            for part in range(3):
                column = part * D + piece * PAIR
                shard_qkv[:, column : column + PAIR] = rows[:, part * PAIR : (part + 1) * PAIR]


def backward_sending(*operands):
    router = operands[7]
    experts, size = router.shape[0], lax.axis_size("dp")
    outers, thin, wide, pieces = size // 2, D // size, FF // size, HEADS // 2 + 1
    groups = lax.axis_size("task")
    tiles, wholes = ((thin, FF), (wide, D)), ((D, FF), (FF, D))
    ends = SCATTER_SPLIT + SCATTER_LATE

    def spread(peers, *dims, lead=(), dtype=f32):
        return [pltpu.VMEM((*lead, peers, *dims), dtype)] + [
            pltpu.SemaphoreType.DMA((*lead, peers - 1))
        ] * 2

    return pl.pallas_call(
        functools.partial(backward_sending_kernel, outers, groups),
        out_shape=(
            shape(SEQ, D),
            shape(SEQ, D),
            shape(8, D),
            shape(experts, D),
            shape(thin, 3 * D),
            shape(thin, D),
            *[shape(len(kinds(ends, kind)), *tiles[kind]) for kind in range(2)],
        ),
        in_specs=[VMEM] * 11 + [ANY] + [VMEM] * 3 + [ANY] * 2 + [VMEM] * 2,
        out_specs=[VMEM] * 8,
        scratch_shapes=backward_scratch()
        + [
            pltpu.VMEM((8, D), f32),
            pltpu.VMEM((experts, D), f32),
            pltpu.VMEM((pieces, D, D), bf16),
            pltpu.VMEM((groups, SEQ, D), bf16),
            pltpu.VMEM((3, SEQ, D), bf16),
            pltpu.VMEM((SEQ, D), bf16),
            pltpu.SemaphoreType.DMA((3, 1)),
            pltpu.SemaphoreType.DMA((3, 1)),
            pltpu.SemaphoreType.DMA,
            pltpu.SemaphoreType.DMA((len(SCATTER_LATE),)),
        ]
        + [pltpu.VMEM(wholes[kind], bf16) for _, kind in SCATTER_LATE]
        + scatter_scratch(SCATTER_LATE, outers, tiles)
        + scatter_scratch(SCATTER_SPLIT, outers, tiles, side=False)
        + scatter_scratch(range(pieces), outers, (thin, D))
        + spread(size, 8, D)
        + spread(groups, 8, D)
        + spread(size, experts, D)
        + spread(groups, thin, D, lead=(pieces,), dtype=bf16),
        compiler_params=params(collective_id=2, has_side_effects=True),
    )(*operands)


def local(
    layer_input,
    cotangent,
    norm_gain,
    norm_bias,
    w_qkv,
    w_proj,
    router,
    w_in,
    w_out,
    choices,
    top_count,
):
    groups = lax.axis_size("task")
    local_count = w_in.shape[0]
    image = layer_input.reshape(SEQ, D)
    grad_rows = cotangent.reshape(SEQ, D)
    router_rows = router[0].T
    experts = router_rows.shape[0]
    routes = choices.reshape(SEQ, TOPMAX)

    def swap(array):
        return lax.all_to_all(array, "task", split_axis=0, concat_axis=0, tiled=True)

    sending = groups == 4 and lax.axis_size("dp") == 8 and local_count == 4
    if sending:
        (
            mid,
            packed,
            mixed,
            logs,
            probs,
            normed,
            cot_rows,
            slots,
            gates,
            full_qkv,
            full_proj,
            full_in,
            full_out,
        ) = forward_sending(
            top_count,
            image,
            grad_rows,
            norm_gain,
            norm_bias,
            (w_qkv, w_proj, w_in, w_out),
            router_rows,
            routes,
        )
        (
            late_in,
            late_out,
            grad_gates,
            mixes,
            grad_normed,
            early_in,
            early_out,
            parts_in,
            parts_out,
            _,
            _,
        ) = expert_sending(normed, cot_rows, slots, gates, full_in, full_out, w_in, w_out)
        (
            activations,
            grad_image,
            grad_norm,
            grad_router,
            grad_qkv,
            grad_proj,
            grad_in,
            grad_out,
        ) = backward_sending(
            image,
            grad_rows,
            norm_gain,
            norm_bias,
            mid,
            full_qkv,
            full_proj,
            router_rows,
            packed,
            mixed,
            logs,
            mixes,
            grad_normed,
            grad_gates,
            probs,
            late_in,
            late_out,
            parts_in,
            parts_out,
        )
        grad_in = jnp.concatenate([early_in, grad_in], axis=0)
        grad_out = jnp.concatenate([early_out, grad_out], axis=0)
    else:
        full_qkv, full_proj, full_in, full_out = (
            lax.all_gather(w_qkv, "dp", axis=0, tiled=True),
            lax.all_gather(w_proj, "dp", axis=0, tiled=True),
            lax.all_gather(w_in, "dp", axis=1, tiled=True),
            lax.all_gather(w_out, "dp", axis=1, tiled=True),
        )
        mid, packed, mixed, logs, normed, slots, gates, probs = forward_part(
            top_count,
            image,
            norm_gain,
            norm_bias,
            full_qkv,
            full_proj,
            router_rows,
            routes,
        )
        normed = lax.all_gather(normed, "task")
        cot_rows = lax.all_gather(grad_rows.astype(bf16), "task")
        slots = swap(slots.reshape(groups, local_count, SEQ))
        gates = swap(gates.reshape(groups, local_count, SEQ))
        grad_in, grad_out, grad_gates, mixes, grad_normed = expert_part(
            normed, cot_rows, slots, gates, full_in, full_out
        )
        activations, grad_image, grad_norm, grad_router, grad_shared = backward_part(
            image,
            grad_rows,
            norm_gain,
            norm_bias,
            mid,
            full_qkv,
            full_proj,
            router_rows,
            packed,
            mixed,
            logs,
            swap(mixes),
            swap(grad_normed),
            swap(grad_gates),
            probs,
        )
        grad_in = lax.psum_scatter(grad_in, "dp", scatter_dimension=1, tiled=True).astype(f32)
        grad_out = lax.psum_scatter(grad_out, "dp", scatter_dimension=1, tiled=True).astype(f32)
        grad_shared = lax.psum_scatter(grad_shared, "dp", scatter_dimension=0, tiled=True)
        grad_shared = lax.psum(grad_shared, "task").astype(f32)
        grad_qkv, grad_proj = grad_shared[:, : 3 * D], grad_shared[:, 3 * D :]
        grad_router = lax.psum(grad_router, "dp")
        grad_norm = lax.psum(grad_norm, ("task", "dp"))
    return (
        activations.reshape(layer_input.shape),
        grad_image.reshape(layer_input.shape),
        grad_norm[:2],
        grad_norm[2:4],
        grad_qkv,
        grad_proj,
        grad_router.T[None],
        grad_in,
        grad_out,
    )


def solution(mesh):
    tokens = P("task", "dp", None, None)
    rows = P("dp", None)
    blocks = P("task", "dp", None)
    routed = P("task", None, None)
    return jax.shard_map(
        local,
        mesh=mesh,
        in_specs=(tokens, tokens, P(), P(), rows, rows, routed, blocks, blocks, tokens, P("task")),
        out_specs=(tokens, tokens, P(), P(), rows, rows, routed, blocks, blocks),
        check_vma=False,
    )
```

```python
import functools

import jax
import jax.numpy as jnp
from jax import lax
from jax.experimental import pallas as pl
from jax.experimental.pallas import tpu as pltpu
from jax.sharding import PartitionSpec as P

D = 384
FF = 1536
HEADS = 6
HEAD_DIM = 64
PAIR = 2 * HEAD_DIM
TOPMAX = 4
SEQ = 1024
CAP = 320

f32 = jnp.float32
bf16 = jnp.bfloat16
HIGHEST = lax.Precision.HIGHEST
EPSILON = 1e-06
ROOT_HALF = 0.7071067811865476
NORMAL = 0.3989422804014327

FF_TILE = 512
ROW_TILE = 640
QUERY_FWD = 256
QUERY_BWD = 256
ROWS = 256
RETURNS = 2

GATHER_WHOLE = ((0, 0), (0, 1), (1, 0), (1, 1))
GATHER_SPLIT = ((2, 0), (2, 1))
GATHER_LATE = ((3, 0), (3, 1))
SCATTER_EARLY = ((0, 0), (0, 1), (1, 0))
SCATTER_SPLIT = ((1, 1), (2, 0))
SCATTER_LATE = ((2, 1), (3, 0), (3, 1, 0), (3, 1, 1))
EARLY_EXPERTS = 2

GATHER_POINTS = {2: ((0, 1), (0, 3), (1, 0), (1, 4)), 3: ((0, 2), (1, 1), (1, 4), (3, 0))}
SCATTER_POINTS = {1: (2, 4), 3: (3, 6)}

AHEAD = 2
FORWARD_FIRST = ((0, 1), (1, 1))
FORWARD_POINTS = {
    0: ((2, 1),),
    1: ((3, 1),),
    2: ((4, 1),),
    3: ((5, 1),),
    5: ((0, 2),),
    6: ((1, 2),),
    8: ((2, 2),),
    9: ((3, 2),),
    10: ((4, 2),),
    11: ((5, 2),),
}
FORWARD_THEN = (((0, 3), (1, 3)), ((2, 3), (3, 3), (4, 3), (5, 3)))

BACKWARD_POINTS = {
    3: ("s1", "u0",),
    8: ("t1", "s2", "v0",),
    11: ("u1",),
}
BACKWARD_THEN = (
    ("t2", "s3", "v1", "u2", "w0"),
    ("x0", "t3", "v2", "u3", "w1", "00", "x1", "01", "v3", "w2", "02", "x2", "w3", "03"),
    ("x3",),
)


VMEM = pl.BlockSpec(memory_space=pltpu.VMEM)
SMEM = pl.BlockSpec(memory_space=pltpu.SMEM)
ANY = pl.BlockSpec(memory_space=pl.ANY)


def shape(*dims, dtype=f32):
    return jax.ShapeDtypeStruct(dims, dtype)


def params(**more):
    return pltpu.CompilerParams(vmem_limit_bytes=63 * 2**20, **more)


def dot(a, b):
    return lax.dot_general(a, b, (((1,), (0,)), ((), ())), preferred_element_type=f32)


def dot_rt(a, b):
    return lax.dot_general(a, b, (((1,), (1,)), ((), ())), preferred_element_type=f32)


def dot_lt(a, b):
    return lax.dot_general(a, b, (((0,), (0,)), ((), ())), preferred_element_type=f32)


def rows_at(index, size):
    return pl.ds(pl.multiple_of(index * size, size), size)


def normalize(rows):
    centered = rows - jnp.mean(rows, axis=1, keepdims=True)
    scale = lax.rsqrt(jnp.mean(centered * centered, axis=1, keepdims=True) + EPSILON)
    return centered * scale, scale


def norm_back(rows, grad_rows, gain):
    unit, scale = normalize(rows)
    scaled = grad_rows * gain
    grad_in = scale * (
        scaled
        - jnp.mean(scaled, axis=1, keepdims=True)
        - unit * jnp.mean(scaled * unit, axis=1, keepdims=True)
    )
    grad_gain = jnp.sum(grad_rows * unit, axis=0, keepdims=True)
    return grad_in, grad_gain, jnp.sum(grad_rows, axis=0, keepdims=True), unit


def half_lanes(rows, half):
    lanes = lax.broadcasted_iota(jnp.int32, (rows, PAIR), 1)
    return (lanes < HEAD_DIM) if half == 0 else (lanes >= HEAD_DIM)


def remote(source, target, sent, landed, **device):
    return pltpu.make_async_remote_copy(
        src_ref=source,
        dst_ref=target,
        send_sem=sent,
        recv_sem=landed,
        device_id=device,
        device_id_type=pl.DeviceIdType.MESH,
    )


class Place:
    def __init__(self, outers):
        self.dp = lax.axis_index("dp")
        self.task = lax.axis_index("task")
        self.outers = outers
        self.outer, self.inner = self.dp // 2, self.dp % 2
        self.has_up, self.has_down = self.outer + 1 < outers, self.outer > 0
        self.up, self.down = self.dp + 2, self.dp - 2
        self.side = self.dp + 1 - 2 * self.inner
        self.core = self.task + 1 - 2 * (self.task % 2)
        self.across = self.task + 2 - 4 * (self.task // 2)
        self.far = self.across + 1 - 2 * (self.task % 2)

    def signal(self, **device):
        pl.semaphore_signal(
            pltpu.get_barrier_semaphore(),
            inc=1,
            device_id=device,
            device_id_type=pl.DeviceIdType.MESH,
        )

    def greet(self, far=False):
        pl.when(self.has_up)(lambda: self.signal(dp=self.up))
        pl.when(self.has_down)(lambda: self.signal(dp=self.down))
        self.signal(dp=self.side)
        self.signal(task=self.core)
        self.signal(task=self.across)
        if far:
            self.signal(task=self.far)
        others = 3 + int(far) + self.has_up.astype(jnp.int32) + self.has_down.astype(jnp.int32)
        pl.semaphore_wait(pltpu.get_barrier_semaphore(), others)

    def greet_all(self, groups):
        size = 2 * self.outers
        for ahead in range(1, size):
            self.signal(dp=lax.rem(self.dp + ahead, size))
        for ahead in range(1, groups):
            self.signal(task=lax.rem(self.task + ahead, groups))
        pl.semaphore_wait(pltpu.get_barrier_semaphore(), size + groups - 2)


class Gather:
    def __init__(self, place, shards, sent, landed, stay):
        self.place, self.shards = place, shards
        self.sent, self.landed, self.stay = sent, landed, stay

    def move(self, unit, source, way, device, first=None):
        _, size, full, _ = self.shards[unit]
        target = full.at[rows_at(source, size)]
        return remote(
            target if first is None else first,
            target,
            self.sent.at[unit, source, way],
            self.landed.at[unit, source],
            dp=device,
        )

    def local(self, unit):
        own, size, full, _ = self.shards[unit]
        target = full.at[rows_at(self.place.dp, size)]
        return pltpu.make_async_copy(own, target, self.stay.at[unit])

    def along(self, unit, source, up, down):
        place = self.place
        if up:
            pl.when(place.has_up)(lambda: self.move(unit, source, 0, place.up).start())
        if down:
            pl.when(place.has_down)(lambda: self.move(unit, source, 1, place.down).start())

    def to_side(self, unit, outer):
        own, size = self.shards[unit][:2]
        source = 2 * outer + self.place.inner
        return self.move(unit, source, 2, self.place.side, own.at[rows_at(source, size)])

    def start(self, unit):
        place = self.place
        own, mode = self.shards[unit][0], self.shards[unit][3]
        if mode == "side":
            for outer in range(place.outers):
                self.to_side(unit, outer).start()
            return
        if mode == "turned":
            self.move(unit, place.dp, 2, place.side, own).start()
        pl.when(place.has_up)(lambda: self.move(unit, place.dp, 0, place.up, own).start())
        pl.when(place.has_down)(lambda: self.move(unit, place.dp, 1, place.down, own).start())
        if mode == "both":
            self.move(unit, place.dp, 2, place.side, own).start()
        if self.stay is not None:
            self.local(unit).start()

    def step(self, unit, hop):
        place, mode = self.place, self.shards[unit][3]
        if hop == 0:
            self.move(unit, place.side, 0, place.dp).wait_recv()
            self.along(unit, place.side, True, True)
            return
        for column in (place.dp, place.side) if mode == "turned" else (place.dp,):

            @pl.when(place.outer >= hop)
            def _():
                self.move(unit, column - 2 * hop, 0, place.dp).wait_recv()
                self.along(unit, column - 2 * hop, True, False)
                if mode == "both":
                    self.move(unit, column - 2 * hop, 2, place.side).start()

            @pl.when(place.outer + hop < place.outers)
            def _():
                self.move(unit, column + 2 * hop, 1, place.dp).wait_recv()
                self.along(unit, column + 2 * hop, False, True)
                if mode == "both":
                    self.move(unit, column + 2 * hop, 2, place.side).start()

    def finish(self, unit):
        place, mode = self.place, self.shards[unit][3]
        if self.stay is not None:
            self.local(unit).wait()
        if mode == "turned":
            self.move(unit, place.dp, 2, place.side).wait_send()
        for outer in range(place.outers):
            own, other = 2 * outer + place.inner, 2 * outer + 1 - place.inner
            if mode in ("both", "side"):
                self.move(unit, other, 2, place.dp).wait_recv()
                self.move(unit, own, 2, place.side).wait_send()
            if mode == "side":
                continue
            for source in (own, other) if mode == "turned" else (own,):
                pl.when((outer <= place.outer) & place.has_up)(
                    lambda source=source: self.move(unit, source, 0, place.up).wait_send()
                )
                pl.when((outer >= place.outer) & place.has_down)(
                    lambda source=source: self.move(unit, source, 1, place.down).wait_send()
                )


def gather_semaphores(units, size):
    return [
        pltpu.SemaphoreType.DMA((units, size, 3)),
        pltpu.SemaphoreType.DMA((units, size)),
    ]


class Share:
    def __init__(self, place, view, sent, landed):
        self.place, self.view, self.sent, self.landed = place, view, sent, landed

    def move(self, source, way, **device):
        return remote(
            self.view(source),
            self.view(source),
            self.sent.at[way],
            self.landed.at[way],
            **device,
        )

    def start(self):
        place = self.place
        self.move(place.task, 0, task=place.across).start()
        self.move(place.task, 1, task=place.core).start()

    def relay(self):
        place = self.place
        self.move(place.across, 0, task=place.across).wait_recv()
        self.move(place.across, 2, task=place.core).start()

    def finish(self):
        place = self.place
        self.move(place.task, 0, task=place.across).wait_send()
        self.move(place.core, 1, task=place.core).wait()
        self.move(place.across, 2, task=place.core).wait()


class Scatter:
    def __init__(self, place, mine, theirs, side, line, sems):
        self.place, self.mine, self.theirs = place, mine, theirs
        self.side, self.line = side, line
        self.side_sent, self.side_landed, self.line_sent, self.line_landed = sems

    def to_side(self, outer):
        return remote(
            self.theirs(outer),
            self.side.at[outer],
            self.side_sent.at[outer],
            self.side_landed.at[outer],
            dp=self.place.side,
        )

    def fold(self, outer):
        return self.mine(outer) if self.side is None else self.side.at[outer]

    def along(self, outer, slot, device):
        return remote(
            self.fold(outer),
            self.line.at[slot],
            self.line_sent.at[outer],
            self.line_landed.at[slot],
            dp=device,
        )

    def start(self):
        outers = self.place.outers
        for near in range(outers // 2):
            self.to_side(outers - 1 - near).start()
            self.to_side(near).start()

    def total(self, outer, *slots):
        rows = self.mine(outer)[...].astype(f32)
        if self.side is not None:
            self.to_side(outer).wait_recv()
            rows += self.side[outer].astype(f32)
        for slot in slots:
            self.along(outer, slot, self.place.dp).wait_recv()
            rows += self.line[slot].astype(f32)
        return rows

    def settle(self, parts, sem):
        for outer in range(self.place.outers):
            self.fold(outer)[...] = self.total(outer).astype(bf16)
            self.to_side(outer).wait_send()
        copy = pltpu.make_async_copy(self.side, parts, sem)
        copy.start()
        return copy

    def hop(self, step):
        place, outers = self.place, self.place.outers

        @pl.when(place.outer == step)
        def _():
            for outer in range(outers - 1, step, -1):
                rows = self.total(outer, *([outer] if step else []))
                self.fold(outer)[...] = rows.astype(bf16)
                self.along(outer, outer, place.up).start()

        @pl.when(place.outer == outers - 1 - step)
        def _():
            for outer in range(outers - 1 - step):
                rows = self.total(outer, *([outer] if step else []))
                self.fold(outer)[...] = rows.astype(bf16)
                slot = outers if outer == outers - 2 - step else outer
                self.along(outer, slot, place.down).start()

    def finish(self, store):
        place, outers = self.place, self.place.outers
        for outer in range(outers):

            @pl.when(place.outer == outer)
            def _():
                below, above = [outer] * (outer > 0), [outers] * (outer < outers - 1)
                store(self.total(outer, *below, *above))
                for other in range(outers):
                    if other != outer:
                        self.along(other, other, place.dp).wait_send()

            if self.side is not None:
                self.to_side(outer).wait_send()


class Turned:
    def __init__(self, place, mine, theirs, refs):
        self.place = place
        self.own = Scatter(place, mine, None, None, refs[0], (None, None, *refs[1:3]))
        self.other = Scatter(place, theirs, None, None, refs[3], (None, None, *refs[4:6]))
        self.stage, self.land, self.sent, self.landed = refs[6:]

    def move(self):
        return remote(self.stage, self.land, self.sent, self.landed, dp=self.place.side)

    def start(self):
        self.own.hop(0)
        self.other.hop(0)

    def hop(self, step):
        if step:
            self.own.hop(step)
            self.other.hop(step)

    def finish(self, store):
        def send(rows):
            self.stage[...] = rows.astype(bf16)
            self.move().start()

        self.other.finish(send)
        self.own.finish(store)

    def add(self, shard):
        self.move().wait()
        shard[...] += self.land[...].astype(f32)


def turned_scratch(outers, tile):
    line = [pltpu.VMEM((outers + 1, *tile), bf16)]
    line += [pltpu.SemaphoreType.DMA((count,)) for count in (outers, outers + 1)]
    return line * 2 + [pltpu.VMEM(tile, bf16)] * 2 + [pltpu.SemaphoreType.DMA] * 2


def scatter_turn(units, stores, turn):
    outers = units[0].place.outers
    for step in range(outers - 1):
        if 0 <= turn - step < len(units):
            units[turn - step].hop(step)
    last = turn - outers + 1
    if 0 <= last < len(units):
        units[last].finish(stores[last])


def blocks_of(place, ref, size, half=()):
    def block(index):
        if half:
            return ref.at[rows_at(2 * index + half[0], size // 2)]
        return ref.at[rows_at(index, size)]

    return (
        lambda outer: block(2 * outer + place.inner),
        lambda outer: block(2 * outer + 1 - place.inner),
    )


def scatter_scratch(units, outers, tiles, side=True, line=True):
    scratch = []
    for unit in units:
        tile = tiles[unit[1]] if isinstance(unit, tuple) else tiles
        if isinstance(unit, tuple) and len(unit) > 2:
            tile = (tile[0] // 2, tile[1])
        for asked, slots in ((side, outers), (line, outers + 1)):
            if asked:
                scratch.append(pltpu.VMEM((slots, *tile), bf16))
        for asked, count in ((side, outers), (side, outers), (line, outers), (line, outers + 1)):
            if asked:
                scratch.append(pltpu.SemaphoreType.DMA((count,)))
    return scratch


def make_scatters(place, blocks, refs, side=True, line=True):
    count = 3 * side + 3 * line
    scatters = []
    for index, (mine, theirs) in enumerate(blocks):
        own = list(refs[index * count : (index + 1) * count])
        buffers = [own.pop(0) if asked else None for asked in (side, line)]
        sems = [own.pop(0) if asked else None for asked in (side, side, line, line)]
        scatters.append(Scatter(place, mine, theirs, *buffers, sems))
    return scatters


class Spread:
    def __init__(self, axis, place, count, land, sent, landed):
        self.axis, self.me, self.count = axis, getattr(place, axis), count
        self.land, self.sent, self.landed = land, sent, landed

    def move(self, source, ahead):
        return remote(
            self.land.at[source],
            self.land.at[source],
            self.sent.at[ahead - 1],
            self.landed.at[ahead - 1],
            **{self.axis: lax.rem(self.me + ahead, self.count)},
        )

    def give(self, rows):
        self.land[self.me] = rows.astype(self.land.dtype)
        for ahead in range(1, self.count):
            self.move(self.me, ahead).start()

    def arrive(self):
        for ahead in range(1, self.count):
            self.move(lax.rem(self.me + self.count - ahead, self.count), ahead).wait_recv()
            self.move(self.me, ahead).wait_send()

    def take(self):
        self.arrive()
        total = self.land[0].astype(f32)
        for index in range(1, self.count):
            total += self.land[index].astype(f32)
        return total


class Return:
    def __init__(self, place, parts, pieces, land, sent, landed):
        self.place, self.parts, self.pieces = place, parts, pieces
        self.land, self.sent, self.landed = land, sent, landed
        self.size = land.shape[1] // pieces

    def rows(self, piece):
        return pl.ds(piece * self.size, self.size)

    def move(self, way, piece):
        place, rows = self.place, self.rows(piece)
        source = [
            self.parts[0].at[rows],
            self.parts[1].at[rows],
            self.parts[2].at[rows],
        ][way]
        return remote(
            source,
            self.land.at[way, rows],
            self.sent.at[way, piece],
            self.landed.at[way, piece],
            task=place.across if way == 2 else place.core,
        )

    def to_core(self, piece):
        self.move(0, piece).start()

    def by_core(self, piece):
        self.move(1, piece).start()

    def to_across(self, piece):
        rows = self.rows(piece)
        self.move(1, piece).wait_recv()
        joint = self.parts[2][rows, :].astype(f32)
        joint += self.land[1, rows, :].astype(f32)
        self.parts[2][rows, :] = joint.astype(bf16)
        self.move(2, piece).start()

    def finish(self, piece):
        rows = self.rows(piece)
        self.move(0, piece).wait()
        self.move(1, piece).wait_send()
        self.move(2, piece).wait()
        total = self.parts[3][rows, :].astype(f32)
        return total + self.land[0, rows, :].astype(f32) + self.land[2, rows, :].astype(f32)


def attend(packed, mixed, totals, index, between):
    zero = jnp.array(0, bf16)
    rows = rows_at(index, QUERY_FWD)

    def head_pair(pair, _):
        queries, keys, values = (rows_at(pair + part * (D // PAIR), PAIR) for part in range(3))
        key_rows, value_rows = packed[:, keys], packed[:, values]
        query_rows = packed[rows, queries] * jnp.array(HEAD_DIM**-0.5, bf16)
        outs, logs = [], []
        for half in range(2):
            own = jnp.where(half_lanes(QUERY_FWD, half), query_rows, zero)
            scores = dot_rt(own, key_rows)
            top = jnp.max(scores, axis=1, keepdims=True)
            weights = jnp.exp(scores - top)
            total = jnp.sum(weights, axis=1, keepdims=True)
            outs.append(dot(weights.astype(bf16), value_rows) * (1.0 / total))
            logs.append(top + jnp.log(total))
        mixed[rows, queries] = jnp.where(half_lanes(QUERY_FWD, 0), outs[0], outs[1]).astype(bf16)
        lanes = lax.broadcasted_iota(jnp.int32, (QUERY_FWD, 8), 1)
        totals[rows, :] = jnp.where(
            lanes == 2 * pair,
            logs[0],
            jnp.where(lanes == 2 * pair + 1, logs[1], totals[rows, :]),
        )
        between(index * (HEADS // 2) + pair)
        return 0

    lax.fori_loop(0, HEADS // 2, head_pair, 0)


def first_norm(image, gain, bias, normed_first):
    def block(index, _):
        rows = rows_at(index, ROWS)
        unit, _ = normalize(image[rows, :])
        normed_first[rows, :] = (unit * gain[0:1, :] + bias[0:1, :]).astype(bf16)
        return 0

    lax.fori_loop(0, SEQ // ROWS, block, 0)


def number_slots(choices, top_count, experts):
    named = choices[...].T
    numbers = lax.broadcasted_iota(jnp.int32, (experts, SEQ), 0)
    used = jnp.zeros((experts, SEQ), f32)
    for choice in range(TOPMAX):
        hit = (named[choice : choice + 1, :] == numbers) & (choice < top_count[0])
        used = used + jnp.where(hit, 1.0, 0.0)
    earlier = lax.broadcasted_iota(jnp.int32, (SEQ, SEQ), 0) < lax.broadcasted_iota(
        jnp.int32, (SEQ, SEQ), 1
    )
    before = dot(used.astype(bf16), jnp.where(earlier, 1.0, 0.0).astype(bf16))
    return jnp.where(used > 0, before, -1.0).astype(jnp.int32)


def mid_block(index, image, gain, bias, w_proj, router, mixed, mid, probs):
    rows = rows_at(index, QUERY_FWD)
    mid_rows = image[rows, :] + dot(mixed[rows, :], w_proj[...])
    mid[rows, :] = mid_rows
    unit, _ = normalize(mid_rows)
    normed_rows = unit * gain[1:2, :] + bias[1:2, :]
    logits = lax.dot_general(
        router[...],
        normed_rows,
        (((1,), (1,)), ((), ())),
        precision=HIGHEST,
        preferred_element_type=f32,
    )
    powers = jnp.exp(logits - jnp.max(logits, axis=0, keepdims=True))
    probs[:, rows] = powers / jnp.sum(powers, axis=0, keepdims=True)
    return normed_rows.astype(bf16)


def forward_kernel(
    top_count,
    image,
    gain,
    bias,
    w_qkv,
    w_proj,
    router,
    choices,
    mid,
    packed,
    mixed,
    logs,
    normed,
    slots,
    gates,
    probs,
    normed_first,
    totals,
):
    first_norm(image, gain, bias, normed_first)
    slots[...] = number_slots(choices, top_count, router.shape[0])
    packed[...] = dot(normed_first[...], w_qkv[...]).astype(bf16)
    totals[...] = jnp.zeros_like(totals)

    def block(index, _):
        attend(packed, mixed, totals, index, lambda point: None)
        normed[rows_at(index, QUERY_FWD), :] = mid_block(
            index, image, gain, bias, w_proj, router, mixed, mid, probs
        )
        return 0

    lax.fori_loop(0, SEQ // QUERY_FWD, block, 0)
    logs[...] = totals[...].T
    gates[...] = jnp.where(slots[...] >= 0, probs[...], 0.0)


def forward_part(top_count, image, gain, bias, w_qkv, w_proj, router, choices):
    experts = router.shape[0]
    return pl.pallas_call(
        forward_kernel,
        out_shape=(
            shape(SEQ, D),
            shape(SEQ, 3 * D, dtype=bf16),
            shape(SEQ, D, dtype=bf16),
            shape(8, SEQ),
            shape(SEQ, D, dtype=bf16),
            shape(experts, SEQ, dtype=jnp.int32),
            shape(experts, SEQ),
            shape(experts, SEQ),
        ),
        in_specs=[SMEM] + [VMEM] * 7,
        out_specs=[VMEM] * 8,
        scratch_shapes=[pltpu.VMEM((SEQ, D), bf16), pltpu.VMEM((SEQ, 8), f32)],
        compiler_params=params(),
    )(top_count, image, gain, bias, w_qkv, w_proj, router, choices)


def forward_sending_kernel(
    outers,
    top_count,
    image,
    cotangent,
    gain,
    bias,
    w_qkv,
    w_proj,
    w_in,
    w_out,
    router_columns,
    choices,
    mid,
    packed,
    mixed,
    logs,
    probs,
    normed_all,
    cot_all,
    slots_all,
    gates_all,
    quarters,
    full_in,
    full_out,
    normed_first,
    totals,
    router,
    own_quarter,
    sent,
    landed,
    stay,
    share_sent,
    share_landed,
):
    place = Place(outers)
    task = place.task
    for part in range(4):

        @pl.when(task == part)
        def _():
            own_quarter[...] = w_proj[...] if part == 3 else w_qkv[:, part * D : (part + 1) * D]

    shards = [(own_quarter, w_qkv.shape[0], quarters.at[task], "both")]
    for expert, kind in GATHER_WHOLE + GATHER_SPLIT:
        own, full = ((w_in, full_in), (w_out, full_out))[kind]
        mode = "line" if (expert, kind) in GATHER_SPLIT else "both"
        shards.append((own.at[expert], own.shape[1], full.at[expert], mode))
    gather = Gather(place, shards, sent, landed, stay)
    routed = range(1, len(shards))
    cot_all[task] = cotangent[...].astype(bf16)
    place.greet()
    gather.start(0)

    def share(index, view):
        return Share(place, view, share_sent.at[index], share_landed.at[index])

    cot = share(0, lambda source: cot_all.at[source])
    slot = share(1, lambda source: slots_all.at[source])
    gate = share(2, lambda source: gates_all.at[source])
    def run(acts):
        for unit, hop in acts:
            if unit < len(routed):
                gather.step(routed[unit], hop)

    for unit in routed[:AHEAD]:
        gather.start(unit)
    cot.start()
    router[...] = router_columns[...].T
    first_norm(image, gain, bias, normed_first)
    for hop in range(1, outers):
        gather.step(0, hop)
    for unit in routed[AHEAD:]:
        gather.start(unit)
    gather.finish(0)
    quarter = share(3 + SEQ // QUERY_FWD, lambda source: quarters.at[source])
    quarter.start()
    slots_all[task] = number_slots(choices, top_count, router.shape[0])
    slot.start()
    totals[...] = jnp.zeros_like(totals)
    run(FORWARD_FIRST)
    quarter.relay()
    quarter.finish()
    for part in range(3):
        packed[:, part * D : (part + 1) * D] = dot(normed_first[...], quarters[part]).astype(bf16)
    cot.relay()
    slot.relay()

    def chunk(index):
        return share(3 + index, lambda source: normed_all.at[source, rows_at(index, QUERY_FWD)])

    blocks = SEQ // QUERY_FWD

    def block(index, _):
        def between(point):
            for at, acts in FORWARD_POINTS.items():
                pl.when(point == at)(lambda acts=acts: run(acts))

        attend(packed, mixed, totals, index, between)
        normed_all[task, rows_at(index, QUERY_FWD), :] = mid_block(
            index, image, gain, bias, quarters.at[3], router, mixed, mid, probs
        )
        chunk(index).start()
        pl.when(index > 0)(lambda: chunk(index - 1).relay())
        return 0

    lax.fori_loop(0, blocks, block, 0)
    gates_all[task] = jnp.where(slots_all[task] >= 0, probs[...], 0.0)
    gate.start()
    logs[...] = totals[...].T
    run(FORWARD_THEN[0])
    chunk(blocks - 1).relay()
    gate.relay()
    run(FORWARD_THEN[1])
    for one in [cot, slot, gate] + [chunk(index) for index in range(blocks)]:
        one.finish()
    for unit in routed:
        gather.finish(unit)


def forward_sending(top_count, image, cotangent, gain, bias, shards, router, choices):
    w_qkv, w_proj, w_in, w_out = shards
    experts, size = router.shape[1], lax.axis_size("dp")
    groups, early = lax.axis_size("task"), 1 + GATHER_SPLIT[-1][0]
    units, shares = 1 + len(GATHER_WHOLE + GATHER_SPLIT), 4 + SEQ // QUERY_FWD
    return pl.pallas_call(
        functools.partial(forward_sending_kernel, size // 2),
        out_shape=(
            shape(SEQ, D),
            shape(SEQ, 3 * D, dtype=bf16),
            shape(SEQ, D, dtype=bf16),
            shape(8, SEQ),
            shape(experts, SEQ),
            shape(groups, SEQ, D, dtype=bf16),
            shape(groups, SEQ, D, dtype=bf16),
            shape(groups, experts, SEQ, dtype=jnp.int32),
            shape(groups, experts, SEQ),
            shape(groups, D, D, dtype=bf16),
            shape(early, D, FF, dtype=bf16),
            shape(early, FF, D, dtype=bf16),
        ),
        in_specs=[SMEM] + [VMEM] * 10,
        out_specs=[VMEM] * 10 + [ANY] * 2,
        scratch_shapes=[
            pltpu.VMEM((SEQ, D), bf16),
            pltpu.VMEM((SEQ, 8), f32),
            pltpu.VMEM((experts, D), f32),
            pltpu.VMEM(w_proj.shape, bf16),
            *gather_semaphores(units, size),
            pltpu.SemaphoreType.DMA((units,)),
            pltpu.SemaphoreType.DMA((shares, 3)),
            pltpu.SemaphoreType.DMA((shares, 3)),
        ],
        compiler_params=params(collective_id=0, has_side_effects=True),
    )(top_count, image, cotangent, gain, bias, w_qkv, w_proj, w_in, w_out, router, choices)


def slot_hits(slots, source, expert):
    return lax.broadcasted_iota(jnp.int32, (CAP, SEQ), 0) == slots[source, pl.ds(expert, 1), :]


def ones_at(hits):
    return jnp.where(hits, 1.0, 0.0).astype(bf16)


def dispatch(operands, work, expert, first, block, source):
    tokens, slots, gates = operands[:3]
    rows_in, rows_grad, rows_cot, rows_gate = work[:4]
    own = slice(block * CAP, (block + 1) * CAP)
    hits = slot_hits(slots, source, first + expert)
    both = dot(ones_at(hits), tokens[source])
    gate = jnp.sum(
        jnp.where(hits, gates[source, pl.ds(first + expert, 1), :], 0.0), axis=1, keepdims=True
    )
    rows_in[own, :] = both[:, :D].astype(bf16)
    rows_cot[own, :] = both[:, D:].astype(bf16)
    rows_grad[own, :] = (gate * both[:, D:]).astype(bf16)
    rows_gate[own, :] = jnp.broadcast_to(gate, (CAP, 128))


def hidden_tiles(operands, work, slot, start, count):
    w_in, w_out = operands[3:]
    rows_in, rows_grad, _, _, hidden, grad_pre, _ = work

    def tile(index, _):
        units = rows_at(index // count, FF_TILE)
        rows = rows_at(start + lax.rem(index, count), ROW_TILE)
        pre = dot(rows_in[rows, :], w_in[slot, :, units])
        grad_hidden = dot_rt(rows_grad[rows, :], w_out[slot, units, :])
        share = 0.5 * lax.erf(pre * ROOT_HALF) + 0.5
        slope = share + pre * (NORMAL * jnp.exp(-0.5 * pre * pre))
        hidden[rows, units] = (pre * share).astype(bf16)
        grad_pre[rows, units] = (grad_hidden * slope).astype(bf16)
        return 0

    lax.fori_loop(0, (FF // FF_TILE) * count, tile, 0)


def expert_rows_out(operands, work, grad_gates, expert, first, slot, block, source):
    slots, (w_in, w_out) = operands[1], operands[3:]
    _, _, rows_cot, rows_gate, hidden, grad_pre, sent = work
    own = slice(block * CAP, (block + 1) * CAP)
    kept = rows_at(expert, CAP)
    out_rows = dot(hidden[own, :], w_out[slot]).astype(bf16).astype(f32)
    sent[source, kept, :D] = (rows_gate[own, 0:1] * out_rows).astype(bf16)
    sent[source, kept, D:] = dot_rt(grad_pre[own, :], w_in[slot]).astype(bf16)
    grad_gate = jnp.sum(rows_cot[own, :].astype(f32) * out_rows, axis=1, keepdims=True)
    hits = slot_hits(slots, source, first + expert)
    grad_gates[source, pl.ds(expert, 1), :] = jnp.sum(
        jnp.where(hits, grad_gate, 0.0), axis=0, keepdims=True
    )


def weight_grads(work, grads, expert):
    rows_in, rows_grad, _, _, hidden, grad_pre, _ = work
    grads[0][expert] = dot_lt(rows_in[...], grad_pre[...]).astype(bf16)
    grads[1][expert] = dot_lt(rows_grad[...], hidden[...]).astype(bf16).T


def one_expert(operands, work, grads, expert, first, slot, sources, between, halfway=None):
    halves = 1 if halfway is None else 2
    size, tiles = len(sources) // halves, len(sources) * CAP // ROW_TILE // halves
    between(0)
    for block, source in enumerate(sources):
        dispatch(operands, work, expert, first, block, source)
    between(1)
    for half in range(halves):
        hidden_tiles(operands, work, slot, half * tiles, tiles)
        between(2 + half * 2)
        for block in range(half * size, (half + 1) * size):
            expert_rows_out(
                operands, work, grads[2], expert, first, slot, block, sources[block]
            )
        if half + 1 < halves:
            halfway()
    between(3 if halves == 1 else 5)
    weight_grads(work, grads, expert)
    between(4 if halves == 1 else 6)


def combine(slots, first, local_count, sent, columns, source, store):
    size = SEQ // RETURNS
    columns[...] = slots[source].T
    for piece in range(RETURNS):
        rows = pl.ds(piece * size, size)
        lanes = lax.broadcasted_iota(jnp.int32, (size, CAP), 1)
        mine = lax.broadcasted_iota(jnp.int32, (size, columns.shape[1]), 1)
        picks = []
        for expert in range(local_count):
            column = jnp.max(
                jnp.where(mine == first + expert, columns[rows, :], -1), axis=1, keepdims=True
            )
            picks.append(ones_at(lanes == column))
        back = dot(jnp.concatenate(picks, axis=1), sent[source])
        store(piece, rows, back[:, :D].astype(bf16), back[:, D:].astype(bf16))


def expert_scratch(groups, local_count, experts):
    width = groups * CAP
    return [
        pltpu.VMEM((width, D), bf16),
        pltpu.VMEM((width, D), bf16),
        pltpu.VMEM((width, D), bf16),
        pltpu.VMEM((width, 128), f32),
        pltpu.VMEM((width, FF), bf16),
        pltpu.VMEM((width, FF), bf16),
        pltpu.VMEM((groups, local_count * CAP, 2 * D), bf16),
        pltpu.VMEM((SEQ, experts), jnp.int32),
    ]


def expert_kernel(*refs):
    operands, grads, (mixes, grad_normed) = refs[:5], refs[5:8], refs[8:10]
    work, columns = refs[10:17], refs[17]
    groups, local_count = operands[0].shape[0], operands[3].shape[0]

    def body(expert, _):
        one_expert(
            operands, work, grads, expert, 0, expert, range(groups), lambda point: None
        )
        return 0

    lax.fori_loop(0, local_count, body, 0)
    for source in range(groups):

        def store(piece, rows, mix, grad, source=source):
            mixes[source, rows, :] = mix
            grad_normed[source, rows, :] = grad

        combine(operands[1], 0, local_count, work[6], columns, source, store)


def expert_part(*operands):
    groups, local_count = operands[0].shape[0], operands[3].shape[0]
    return pl.pallas_call(
        expert_kernel,
        out_shape=(
            shape(local_count, D, FF, dtype=bf16),
            shape(local_count, FF, D, dtype=bf16),
            shape(groups, local_count, SEQ),
            shape(groups, SEQ, D, dtype=bf16),
            shape(groups, SEQ, D, dtype=bf16),
        ),
        in_specs=[VMEM] * 5,
        out_specs=[VMEM] * 5,
        scratch_shapes=expert_scratch(groups, local_count, operands[1].shape[1]),
        compiler_params=params(),
    )(*operands)


def expert_sending_kernel(outers, *refs):
    normed_all, cot_all, slots, gates, early_in, early_out, w_in, w_out = refs[:8]
    late_in, late_out, gate_all, mixes, grad_rows, shard_in, shard_out, parts_in, parts_out = refs[8:17]
    full_in, full_out = refs[17:19]
    work, columns = refs[19:26], refs[26]
    both, slot_in, slot_out, grad_in, grad_out, grad_gates, land, first_parts = refs[27:35]
    sent, landed, gate_sent, gate_landed, mix_sem, late_sem, slot_sem, token_sem = refs[35:43]
    part_sem, gather_sems, scatter_refs = refs[43], refs[44:46], refs[46:]
    place = Place(outers)
    groups, local_count, size = both.shape[0], grad_in.shape[0], 2 * outers
    late = local_count - EARLY_EXPERTS
    first = place.task * local_count
    grads, shares = (grad_in, grad_out), (w_in.shape[1], w_out.shape[1])

    def tokens():
        return [
            pltpu.make_async_copy(
                whole.at[source],
                both.at[source, :, pl.ds(kind * D, D)],
                token_sem.at[kind, source],
            )
            for source in range(groups)
            for kind, whole in enumerate((normed_all, cot_all))
        ]

    def load(expert):
        slot, copies = expert % EARLY_EXPERTS, []
        for kind in range(2):
            target, sem = (slot_in, slot_out)[kind].at[slot], slot_sem.at[slot, kind]
            early, own = (early_in, early_out)[kind], (w_in, w_out)[kind]
            full = (full_in, full_out)[kind]
            if expert < EARLY_EXPERTS:
                copies.append(pltpu.make_async_copy(early.at[expert], target, sem.at[0]))
                continue
            for ahead in range(size):
                block = lax.rem(place.dp + ahead, size)
                rows = rows_at(block, shares[kind])
                source = full.at[expert - EARLY_EXPERTS, rows]
                if (expert, kind) in GATHER_SPLIT:
                    if ahead % 2 == 0:
                        source = early.at[expert, rows]
                elif ahead == 0:
                    source = own.at[expert]
                copies.append(pltpu.make_async_copy(source, target.at[rows], sem.at[ahead]))
        return copies

    def keep(expert):
        return [
            pltpu.make_async_copy(
                grads[kind].at[EARLY_EXPERTS + expert],
                (late_in, late_out)[kind].at[expert],
                late_sem.at[expert, kind],
            )
            for kind in range(2)
        ]

    for copy in tokens() + load(0):
        copy.start()
    place.greet(far=True)
    shards = []
    for expert, kind in GATHER_LATE + GATHER_SPLIT:
        full = (full_in, full_out)[kind].at[expert - EARLY_EXPERTS]
        if (expert, kind) in GATHER_SPLIT:
            shards.append(((early_in, early_out)[kind].at[expert], shares[kind], full, "side"))
        else:
            shards.append(((w_in, w_out)[kind].at[expert], shares[kind], full, "turned"))
    gather = Gather(place, shards, *gather_sems, None)
    turned = range(len(GATHER_LATE))
    for unit in range(len(shards)):
        gather.start(unit)
    for copy in load(1):
        copy.start()
    per_full, per_side = 6 * len(SCATTER_EARLY[1:]), 3 * len(SCATTER_SPLIT)

    def scatters(units, refs, **parts):
        return make_scatters(
            place,
            [blocks_of(place, grads[kind].at[expert], shares[kind]) for expert, kind in units],
            refs,
            **parts,
        )

    expert, kind = SCATTER_EARLY[0]
    turned_scatter = Turned(
        place,
        *blocks_of(place, grads[kind].at[expert], shares[kind]),
        scatter_refs[per_full + per_side :],
    )
    whole = [turned_scatter] + scatters(SCATTER_EARLY[1:], scatter_refs[:per_full])
    split = scatters(SCATTER_SPLIT, scatter_refs[per_full : per_full + per_side], line=False)
    stores, keeps = [], []
    for expert, kind in SCATTER_EARLY:

        def store(rows, shard=(shard_in, shard_out)[kind], expert=expert):
            shard[expert] = rows

        stores.append(store)
    for index, (_, kind) in enumerate(SCATTER_SPLIT):
        at = [other[1] for other in SCATTER_SPLIT[:index]].count(kind)

        keeps.append((parts_in, parts_out)[kind].at[at])
    steps = {}

    def plan(expert, point, *acts):
        steps.setdefault((expert, point), []).extend(acts)

    plan(0, 0, *[copy.wait for copy in tokens()])
    for expert in range(EARLY_EXPERTS):
        plan(expert, 1, *[copy.wait for copy in load(expert)])
    for unit in turned:
        for hop, at in enumerate(GATHER_POINTS[GATHER_LATE[unit][0]]):
            plan(*at, lambda unit=unit, hop=hop: gather.step(unit, hop))
    for expert in range(EARLY_EXPERTS, local_count):
        units = [
            unit
            for unit, (owner, _) in enumerate(GATHER_LATE + GATHER_SPLIT)
            if owner == expert
        ]
        plan(expert, 0, *[lambda unit=unit: gather.finish(unit) for unit in units])
        plan(expert, 0, *[copy.start for copy in load(expert)])
        plan(expert, 1, *[copy.wait for copy in load(expert)])
        point = 4 if expert < local_count - 1 else 6
        plan(expert, point, *[copy.start for copy in keep(expert - EARLY_EXPERTS)])
    for index, (expert, _) in enumerate(SCATTER_EARLY):
        plan(expert, 4, whole[index].start)
    for index, (expert, _) in enumerate(SCATTER_SPLIT):
        plan(expert, 4, split[index].start)
    for turn, at in SCATTER_POINTS.items():
        plan(*at, lambda turn=turn: scatter_turn(whole, stores, turn))

    operands = (both, slots, gates, slot_in, slot_out)
    every_grad = (grad_in, grad_out, grad_gates)
    sources = (place.far, place.across, place.core, place.task)

    def body(expert, _):
        def between(point):
            for at in range(local_count - 1):
                acts = steps.get((at, point))
                if acts:

                    @pl.when(expert == at)
                    def _():
                        for act in acts:
                            act()

        one_expert(
            operands,
            work,
            every_grad,
            expert,
            first,
            lax.rem(expert, EARLY_EXPERTS),
            sources,
            between,
        )
        return 0

    lax.fori_loop(0, local_count - 1, body, 0)
    hidden, grad_pre = work[4], work[5]

    def part(ref, block):
        return ref.at[pl.ds(0, SEQ), pl.ds(block * D, D)]

    parts = [first_parts.at[0], first_parts.at[1], part(hidden, 0), part(hidden, 1)]
    mix_parts = [first_parts.at[2], first_parts.at[2], part(grad_pre, 0), part(grad_pre, 1)]
    back = Return(
        place,
        (parts[2], parts[0], parts[1], parts[3]),
        RETURNS,
        land,
        sent,
        landed,
    )
    sends = (back.by_core, back.to_across, back.to_core, None)

    def mix_copy(block):
        return pltpu.make_async_copy(
            mix_parts[block], mixes.at[sources[block]], mix_sem.at[block]
        )

    def returned(block):
        def store(piece, rows, mix, grad):
            mix_parts[block][rows, :] = mix
            parts[block][rows, :] = grad
            if sends[block]:
                sends[block](piece)

        combine(slots, first, local_count, work[6], columns, sources[block], store)
        mix_copy(block).start()

    def halfway():
        returned(0)
        mix_copy(0).wait()
        returned(1)
        scatter_turn(whole, stores, 2)

    def last(point):
        for act in steps.get((local_count - 1, point), ()):
            act()

    one_expert(
        operands,
        work,
        every_grad,
        local_count - 1,
        first,
        (local_count - 1) % EARLY_EXPERTS,
        sources,
        last,
        halfway,
    )
    gate_all[place.task] = grad_gates[place.task]
    peers = (place.core, place.across, place.far)

    def gate_move(way):
        return remote(
            grad_gates.at[peers[way]],
            gate_all.at[place.task],
            gate_sent.at[way],
            gate_landed.at[way],
            task=peers[way],
        )

    for way in range(3):
        gate_move(way).start()
    returned(2)
    returned(3)
    for turn in range(4, len(whole) + outers - 1):
        scatter_turn(whole, stores, turn)
    expert, kind = SCATTER_EARLY[0]
    turned_scatter.add((shard_in, shard_out)[kind].at[expert])
    settled = [
        one.settle(keeps[index], part_sem.at[index]) for index, one in enumerate(split)
    ]
    for piece in range(RETURNS):
        grad_rows[back.rows(piece), :] = back.finish(piece)
    for way in range(3):
        gate_move(way).wait()
    for block in range(1, groups):
        mix_copy(block).wait()
    for expert in range(late):
        for copy in keep(expert):
            copy.wait()
    for copy in settled:
        copy.wait()


def kinds(units, kind):
    return sorted({unit[0] for unit in units if unit[1] == kind})


def expert_sending(*operands):
    groups, experts = operands[2].shape[:2]
    local_count, thin = operands[6].shape[:2]
    wide, size = operands[7].shape[1], lax.axis_size("dp")
    late, outers = local_count - EARLY_EXPERTS, size // 2
    tiles = ((thin, FF), (wide, D))
    return pl.pallas_call(
        functools.partial(expert_sending_kernel, outers),
        out_shape=(
            shape(late, D, FF, dtype=bf16),
            shape(late, FF, D, dtype=bf16),
            shape(groups, local_count, SEQ),
            shape(groups, SEQ, D, dtype=bf16),
            shape(SEQ, D),
            *[shape(len(kinds(SCATTER_EARLY, kind)), *tiles[kind]) for kind in range(2)],
            *[
                shape(len(kinds(SCATTER_SPLIT, kind)), outers, *tiles[kind], dtype=bf16)
                for kind in range(2)
            ],
            shape(late, D, FF, dtype=bf16),
            shape(late, FF, D, dtype=bf16),
        ),
        in_specs=[ANY] * 2 + [VMEM] * 2 + [ANY] * 4,
        out_specs=[ANY] * 2 + [VMEM, ANY] + [VMEM] * 3 + [ANY] * 4,
        scratch_shapes=expert_scratch(groups, local_count, experts)
        + [
            pltpu.VMEM((groups, SEQ, 2 * D), bf16),
            pltpu.VMEM((EARLY_EXPERTS, D, FF), bf16),
            pltpu.VMEM((EARLY_EXPERTS, FF, D), bf16),
            pltpu.VMEM((local_count, D, FF), bf16),
            pltpu.VMEM((local_count, FF, D), bf16),
            pltpu.VMEM((groups, local_count, SEQ), f32),
            pltpu.VMEM((3, SEQ, D), bf16),
            pltpu.VMEM((3, SEQ, D), bf16),
            pltpu.SemaphoreType.DMA((3, RETURNS)),
            pltpu.SemaphoreType.DMA((3, RETURNS)),
            pltpu.SemaphoreType.DMA((3,)),
            pltpu.SemaphoreType.DMA((3,)),
            pltpu.SemaphoreType.DMA((groups,)),
            pltpu.SemaphoreType.DMA((late, 2)),
            pltpu.SemaphoreType.DMA((EARLY_EXPERTS, 2, size)),
            pltpu.SemaphoreType.DMA((2, groups)),
            pltpu.SemaphoreType.DMA((len(SCATTER_SPLIT),)),
        ]
        + gather_semaphores(len(GATHER_LATE + GATHER_SPLIT), size)
        + scatter_scratch(SCATTER_EARLY[1:], outers, tiles)
        + scatter_scratch(SCATTER_SPLIT, outers, tiles, line=False)
        + turned_scratch(outers, tiles[SCATTER_EARLY[0][1]]),
        compiler_params=params(collective_id=1, has_side_effects=True),
    )(*operands)


def attend_back(packed, grad_mixed, logs, grad_packed, grad_keys, grad_values, between, done):
    zero = jnp.array(0, bf16)
    blocks = SEQ // QUERY_BWD

    def head_pair(pair):
        queries, keys, values = (
            slice(part * D + pair * PAIR, part * D + (pair + 1) * PAIR) for part in range(3)
        )
        key_rows, value_rows = packed[:, keys], packed[:, values]

        def block(index, _):
            rows = rows_at(index, QUERY_BWD)
            query_rows = packed[rows, queries] * jnp.array(HEAD_DIM**-0.5, bf16)
            grad_rows = grad_mixed[rows, queries]
            grad_query, part_keys, part_values = [], 0.0, 0.0
            for half in range(2):
                lanes = half_lanes(QUERY_BWD, half)
                own = jnp.where(lanes, query_rows, zero)
                own_grad = jnp.where(lanes, grad_rows, zero)
                head = 2 * pair + half
                probs = jnp.exp(dot_rt(key_rows, own) - logs[head : head + 1, rows])
                grad_probs = dot_rt(value_rows, own_grad)
                mean = jnp.sum(probs * grad_probs, axis=0, keepdims=True)
                grad_scores = (probs * (grad_probs - mean)).astype(bf16)
                part_values += dot(probs.astype(bf16), own_grad)
                part_keys += dot(grad_scores, own)
                grad_query.append(dot_lt(grad_scores, key_rows))
            grad_packed[rows, queries] = (
                jnp.where(half_lanes(QUERY_BWD, 0), grad_query[0], grad_query[1])
                * HEAD_DIM**-0.5
            ).astype(bf16)
            grad_keys[...] = jnp.where(index == 0, part_keys, grad_keys[...] + part_keys)
            grad_values[...] = jnp.where(index == 0, part_values, grad_values[...] + part_values)
            between(pair, index)
            return 0

        lax.fori_loop(0, blocks, block, 0)
        grad_packed[:, keys] = grad_keys[...].astype(bf16)
        grad_packed[:, values] = grad_values[...].astype(bf16)
        done(pair, (queries, keys, values))

    for pair in range(HEADS // 2):
        head_pair(pair)


def second_back(
    grad_rows, cotangent, gain, bias, mid, w_proj, router, grad_logits, grad_norm, grad_router, outs
):
    grad_mid, grad_low, grad_mixed = outs
    grad_norm[...] = jnp.zeros_like(grad_norm)
    grad_router[...] = jnp.zeros_like(grad_router)
    for index in range(SEQ // ROWS):
        rows = slice(index * ROWS, (index + 1) * ROWS)
        mid_rows = mid[rows, :]
        own_logits = grad_logits[:, rows]
        grad_in_rows = grad_rows(rows) + lax.dot_general(
            own_logits,
            router[...],
            (((0,), (0,)), ((), ())),
            precision=HIGHEST,
            preferred_element_type=f32,
        )
        grad_in, grad_gain, grad_bias, unit = norm_back(mid_rows, grad_in_rows, gain[1:2, :])
        grad_router[...] += jnp.dot(
            own_logits,
            unit * gain[1:2, :] + bias[1:2, :],
            precision=HIGHEST,
            preferred_element_type=f32,
        )
        grad_norm[1:2, :] += grad_gain
        grad_norm[3:4, :] += grad_bias
        grad_mid_rows = cotangent[rows, :] + grad_in
        grad_mid[rows, :] = grad_mid_rows
        low_rows = grad_mid_rows.astype(bf16)
        grad_low[rows, :] = low_rows
        grad_mixed[rows, :] = dot_rt(low_rows, w_proj[...]).astype(bf16)


def first_back(image, gain, parts, grad_packed, grad_mid, grad_image, grad_norm):
    def block(index, _):
        rows = rows_at(index, ROWS)
        grad_rows = sum(
            dot_rt(grad_packed[rows, part * D : (part + 1) * D], parts(part)) for part in range(3)
        )
        grad_in, grad_gain, grad_bias, _ = norm_back(image[rows, :], grad_rows, gain[0:1, :])
        grad_image[rows, :] = grad_mid[rows, :] + grad_in
        grad_norm[0:1, :] += grad_gain
        grad_norm[2:3, :] += grad_bias
        return 0

    lax.fori_loop(0, SEQ // ROWS, block, 0)


def logit_grads(probs, grad_gates):
    route = jnp.concatenate([grad_gates[group] for group in range(grad_gates.shape[0])], axis=0)
    return probs[...] * (route - jnp.sum(probs[...] * route, axis=0, keepdims=True))


def backward_scratch():
    return [
        pltpu.VMEM((SEQ, D), f32),
        pltpu.VMEM((SEQ, D), bf16),
        pltpu.VMEM((SEQ, D), bf16),
        pltpu.VMEM((SEQ, 3 * D), bf16),
        pltpu.VMEM((SEQ, PAIR), f32),
        pltpu.VMEM((SEQ, PAIR), f32),
        pltpu.VMEM((SEQ, D), bf16),
    ]


def backward_kernel(*refs):
    image, cotangent, gain, bias, mid, w_qkv, w_proj, router = refs[:8]
    packed, mixed, logs, mixes, grad_normed, grad_gates, probs = refs[8:15]
    activations, grad_image, grad_norm, grad_router, grad_shared = refs[15:20]
    grad_mid, grad_low, grad_mixed, grad_packed, grad_keys, grad_values, normed_first = refs[20:]
    groups = mixes.shape[0]

    def added(parts, rows):
        total = parts[0, rows, :].astype(f32)
        for source in range(1, groups):
            total += parts[source, rows, :].astype(f32)
        return total

    activations[...] = mid[...] + added(mixes, slice(None))
    second_back(
        lambda rows: added(grad_normed, rows),
        cotangent,
        gain,
        bias,
        mid,
        w_proj,
        router,
        logit_grads(probs, grad_gates),
        grad_norm,
        grad_router,
        (grad_mid, grad_low, grad_mixed),
    )
    first_norm(image, gain, bias, normed_first)
    grad_shared[:, 3 * D :] = dot_lt(mixed[...], grad_low[...]).astype(bf16)
    attend_back(
        packed,
        grad_mixed,
        logs,
        grad_packed,
        grad_keys,
        grad_values,
        lambda pair, index: None,
        lambda pair, columns: None,
    )
    first_back(
        image,
        gain,
        lambda part: w_qkv[:, part * D : (part + 1) * D],
        grad_packed,
        grad_mid,
        grad_image,
        grad_norm,
    )
    grad_shared[:, : 3 * D] = dot_lt(normed_first[...], grad_packed[...]).astype(bf16)


def backward_part(*operands):
    router = operands[7]
    return pl.pallas_call(
        backward_kernel,
        out_shape=(
            shape(SEQ, D),
            shape(SEQ, D),
            shape(4, D),
            shape(router.shape[0], D),
            shape(D, 4 * D, dtype=bf16),
        ),
        in_specs=[VMEM] * 15,
        out_specs=[VMEM] * 5,
        scratch_shapes=backward_scratch(),
        compiler_params=params(),
    )(*operands)


def backward_sending_kernel(outers, groups, *refs):
    whole, (gain, bias, router_columns, logs, grad_gates, probs) = refs[:9], refs[9:15]
    mixes_all, late_in, late_out = refs[15:18]
    activations, grad_image, grad_gain, grad_bias, grad_router, shard_qkv, shard_proj = refs[18:25]
    shard_in, shard_out = refs[25:27]
    grad_mid, grad_low, grad_mixed, grad_packed, grad_keys, grad_values, normed_first = refs[27:34]
    norm_sums, router_sums, shared, mixes, land, back_sent, back_landed = refs[34:41]
    router, own_shared, shared_land, shared_sent, shared_landed = refs[41:46]
    here, here_sem = refs[46:55], refs[55]
    parts_in, parts_out, image, cotangent, mid, quarters, packed, mixed, grad_rows = here
    refs = refs[56:]
    late_grads = sorted({unit[:2] for unit in SCATTER_LATE})
    mix_sem, grad_sem, grad_refs = refs[0], refs[1], refs[2 : 2 + len(late_grads)]
    refs = refs[2 + len(late_grads) :]
    inputs = [
        pltpu.make_async_copy(source, target, here_sem.at[index])
        for index, (source, target) in enumerate(zip(whole, here))
    ]
    place = Place(outers)
    size, pieces = 2 * outers, HEADS // 2 + 1
    shards = (shard_in, shard_out)
    loads = [
        pltpu.make_async_copy(
            (late_in, late_out)[kind].at[expert - EARLY_EXPERTS],
            grad_refs[index],
            grad_sem.at[index],
        )
        for index, (expert, kind) in enumerate(late_grads)
    ]
    mix_load = pltpu.make_async_copy(mixes_all, mixes, mix_sem)
    for copy in (*inputs[:2], *loads, *inputs[2:], mix_load):
        copy.start()
    place.greet_all(groups)
    at = 6 * len(SCATTER_LATE)
    late = make_scatters(
        place,
        [
            blocks_of(
                place, grad_refs[late_grads.index(unit[:2])], shards[unit[1]].shape[1], unit[2:]
            )
            for unit in SCATTER_LATE
        ],
        refs[:at],
    )
    split_blocks = []
    for index, (_, kind) in enumerate(SCATTER_SPLIT):
        number = [other[1] for other in SCATTER_SPLIT[:index]].count(kind)
        split_blocks.append(
            (
                lambda outer, parts=(parts_in, parts_out)[kind], number=number: parts.at[
                    number, outer
                ],
                None,
            )
        )
    split = make_scatters(place, split_blocks, refs[at:], side=False)
    at += 3 * len(SCATTER_SPLIT)
    small = make_scatters(place, [blocks_of(place, own_shared, shard_proj.shape[0])], refs[at:])
    at += 6
    norms = Spread("dp", place, size, *refs[at : at + 3])
    norms_task = Spread("task", place, groups, *refs[at + 3 : at + 6])
    routers = Spread("dp", place, size, *refs[at + 6 : at + 9])
    quarter = Spread("task", place, groups, *refs[at + 9 : at + 12])
    stores = []
    for unit in SCATTER_SPLIT + SCATTER_LATE:
        number = kinds(SCATTER_SPLIT + SCATTER_LATE, unit[1]).index(unit[0])

        def store(rows, shard=shards[unit[1]], number=number, half=unit[2:]):
            start = half[0] * rows.shape[0] if half else 0
            shard[number, start : start + rows.shape[0], :] = rows

        stores.append(store)
    for copy in inputs[:2]:
        copy.wait()
    for one in split:
        one.hop(0)
    for index, one in enumerate(late):
        unit = SCATTER_LATE[index]
        if unit[2:] in ((), (0,)):
            loads[late_grads.index(unit[:2])].wait()
        one.start()
    mix_load.wait()
    roles = (place.core, place.far, place.across, place.task)
    back = Return(
        place, [mixes.at[role] for role in roles], 1, land, back_sent, back_landed
    )
    back.by_core(0)
    back.to_core(0)
    router[...] = router_columns[...].T
    for copy in inputs[2:]:
        copy.wait()
    second_back(
        lambda rows: grad_rows[rows, :],
        cotangent,
        gain,
        bias,
        mid,
        quarters.at[3],
        router,
        logit_grads(probs, grad_gates),
        norm_sums,
        router_sums,
        (grad_mid, grad_low, grad_mixed),
    )
    back.to_across(0)
    first_norm(image, gain, bias, normed_first)
    shared[pieces - 1] = dot_lt(mixed[...], grad_low[...]).astype(bf16)
    routers.give(router_sums[...])
    blocks = SEQ // QUERY_BWD
    units, keeps = split + late, stores
    names = dict(zip("stuvwxyz", range(len(units))))
    names["0"] = len(units)
    units, keeps = units + small, keeps + [quarter.give]
    joined = Return(
        place,
        [shared.at[role] for role in roles],
        1,
        shared_land,
        shared_sent,
        shared_landed,
    )

    def run(acts):
        for act in acts:
            unit, hop = names[act[0]], int(act[1])
            if hop < outers - 1:
                units[unit].hop(hop)
            else:
                units[unit].finish(keeps[unit])

    def between(pair, index):
        for at, acts in BACKWARD_POINTS.items():
            if at // blocks == pair:
                pl.when(index == at % blocks)(lambda acts=acts: run(acts))

    def done(pair, columns):
        both = jnp.concatenate([grad_packed[:, part] for part in columns], axis=1)
        shared[pair] = dot_lt(normed_first[...], both).astype(bf16)

    attend_back(
        packed, grad_mixed, logs, grad_packed, grad_keys, grad_values, between, done
    )
    joined.by_core(0)
    joined.to_core(0)
    first_back(
        image,
        gain,
        lambda part: quarters[part],
        grad_packed,
        grad_mid,
        grad_image,
        norm_sums,
    )
    norms.give(norm_sums[...])
    joined.to_across(0)
    activations[...] = mid[...] + back.finish(0)
    run(BACKWARD_THEN[0])
    own_shared[...] = joined.finish(0).astype(bf16)
    small[0].start()
    grad_router[...] = routers.take().T
    norms_task.give(norms.take())
    run(BACKWARD_THEN[1])
    rows = norms_task.take()
    grad_gain[...] = rows[:2]
    grad_bias[...] = rows[2:4]
    quarter.arrive()
    shard_proj[...] = quarter.land[pieces - 1]
    for piece in range(pieces - 1):
        for part in range(3):
            column = part * D + piece * PAIR
            shard_qkv[:, column : column + PAIR] = quarter.land[
                piece, :, part * PAIR : (part + 1) * PAIR
            ]
    run(BACKWARD_THEN[2])


def backward_sending(*operands):
    router, whole = operands[11], operands[:9]
    experts, size = router.shape[1], lax.axis_size("dp")
    outers, thin, wide, pieces = size // 2, D // size, FF // size, HEADS // 2 + 1
    groups = lax.axis_size("task")
    tiles, wholes = ((thin, FF), (wide, D)), ((D, FF), (FF, D))
    ends = SCATTER_SPLIT + SCATTER_LATE
    late_grads = sorted({unit[:2] for unit in SCATTER_LATE})

    def spread(peers, *dims):
        return [pltpu.VMEM((peers, *dims), f32)] + [pltpu.SemaphoreType.DMA((peers - 1,))] * 2

    return pl.pallas_call(
        functools.partial(backward_sending_kernel, outers, groups),
        out_shape=(
            shape(SEQ, D),
            shape(SEQ, D),
            shape(2, D),
            shape(2, D),
            shape(D, experts),
            shape(thin, 3 * D),
            shape(thin, D),
            *[shape(len(kinds(ends, kind)), *tiles[kind]) for kind in range(2)],
        ),
        in_specs=[ANY] * 9 + [VMEM] * 6 + [ANY] * 3,
        out_specs=[VMEM] * 9,
        scratch_shapes=backward_scratch()
        + [
            pltpu.VMEM((8, D), f32),
            pltpu.VMEM((experts, D), f32),
            pltpu.VMEM((pieces, D, D), bf16),
            pltpu.VMEM((groups, SEQ, D), bf16),
            pltpu.VMEM((3, SEQ, D), bf16),
            pltpu.SemaphoreType.DMA((3, 1)),
            pltpu.SemaphoreType.DMA((3, 1)),
            pltpu.VMEM((experts, D), f32),
            pltpu.VMEM((D, D), bf16),
            pltpu.VMEM((3, D, D), bf16),
            pltpu.SemaphoreType.DMA((3, 1)),
            pltpu.SemaphoreType.DMA((3, 1)),
            *[pltpu.VMEM(operand.shape, operand.dtype) for operand in whole],
            pltpu.SemaphoreType.DMA((len(whole),)),
            pltpu.SemaphoreType.DMA,
            pltpu.SemaphoreType.DMA((len(late_grads),)),
        ]
        + [pltpu.VMEM(wholes[kind], bf16) for _, kind in late_grads]
        + scatter_scratch(SCATTER_LATE, outers, tiles)
        + scatter_scratch(SCATTER_SPLIT, outers, tiles, side=False)
        + scatter_scratch(range(1), outers, (thin, D))
        + spread(size, 8, D)
        + spread(groups, 8, D)
        + spread(size, experts, D)
        + spread(groups, thin, D),
        compiler_params=params(collective_id=2, has_side_effects=True),
    )(*operands)


def local(
    layer_input,
    cotangent,
    norm_gain,
    norm_bias,
    w_qkv,
    w_proj,
    router,
    w_in,
    w_out,
    choices,
    top_count,
):
    groups = lax.axis_size("task")
    local_count = w_in.shape[0]
    image = layer_input.reshape(SEQ, D)
    grad_rows = cotangent.reshape(SEQ, D)
    routes = choices.reshape(SEQ, TOPMAX)

    def swap(array):
        return lax.all_to_all(array, "task", split_axis=0, concat_axis=0, tiled=True)

    sending = groups == 4 and lax.axis_size("dp") == 8 and local_count == 4
    if sending:
        (
            mid,
            packed,
            mixed,
            logs,
            probs,
            normed,
            cot_rows,
            slots,
            gates,
            quarters,
            full_in,
            full_out,
        ) = forward_sending(
            top_count,
            image,
            grad_rows,
            norm_gain,
            norm_bias,
            (w_qkv, w_proj, w_in, w_out),
            router[0],
            routes,
        )
        (
            late_in,
            late_out,
            grad_gates,
            mixes,
            grad_normed,
            early_in,
            early_out,
            parts_in,
            parts_out,
            _,
            _,
        ) = expert_sending(normed, cot_rows, slots, gates, full_in, full_out, w_in, w_out)
        (
            activations,
            grad_image,
            grad_gain,
            grad_bias,
            grad_router,
            grad_qkv,
            grad_proj,
            grad_in,
            grad_out,
        ) = backward_sending(
            parts_in,
            parts_out,
            image,
            grad_rows,
            mid,
            quarters,
            packed,
            mixed,
            grad_normed,
            norm_gain,
            norm_bias,
            router[0],
            logs,
            grad_gates,
            probs,
            mixes,
            late_in,
            late_out,
        )
        grad_in = jnp.concatenate([early_in, grad_in], axis=0)
        grad_out = jnp.concatenate([early_out, grad_out], axis=0)
    else:
        router_rows = router[0].T
        full_qkv, full_proj, full_in, full_out = (
            lax.all_gather(w_qkv, "dp", axis=0, tiled=True),
            lax.all_gather(w_proj, "dp", axis=0, tiled=True),
            lax.all_gather(w_in, "dp", axis=1, tiled=True),
            lax.all_gather(w_out, "dp", axis=1, tiled=True),
        )
        mid, packed, mixed, logs, normed, slots, gates, probs = forward_part(
            top_count,
            image,
            norm_gain,
            norm_bias,
            full_qkv,
            full_proj,
            router_rows,
            routes,
        )
        normed = lax.all_gather(normed, "task")
        cot_rows = lax.all_gather(grad_rows.astype(bf16), "task")
        slots = swap(slots.reshape(groups, local_count, SEQ))
        gates = swap(gates.reshape(groups, local_count, SEQ))
        tokens = jnp.concatenate([normed, cot_rows], axis=-1)
        grad_in, grad_out, grad_gates, mixes, grad_normed = expert_part(
            tokens, slots, gates, full_in, full_out
        )
        activations, grad_image, grad_norm, grad_router, grad_shared = backward_part(
            image,
            grad_rows,
            norm_gain,
            norm_bias,
            mid,
            full_qkv,
            full_proj,
            router_rows,
            packed,
            mixed,
            logs,
            swap(mixes),
            swap(grad_normed),
            swap(grad_gates),
            probs,
        )
        grad_in = lax.psum_scatter(grad_in, "dp", scatter_dimension=1, tiled=True).astype(f32)
        grad_out = lax.psum_scatter(grad_out, "dp", scatter_dimension=1, tiled=True).astype(f32)
        grad_shared = lax.psum_scatter(grad_shared, "dp", scatter_dimension=0, tiled=True)
        grad_shared = lax.psum(grad_shared, "task").astype(f32)
        grad_qkv, grad_proj = grad_shared[:, : 3 * D], grad_shared[:, 3 * D :]
        grad_router = lax.psum(grad_router, "dp").T
        grad_norm = lax.psum(grad_norm, ("task", "dp"))
        grad_gain, grad_bias = grad_norm[:2], grad_norm[2:]
    return (
        activations.reshape(layer_input.shape),
        grad_image.reshape(layer_input.shape),
        grad_gain,
        grad_bias,
        grad_qkv,
        grad_proj,
        grad_router[None],
        grad_in,
        grad_out,
    )


def solution(mesh):
    tokens = P("task", "dp", None, None)
    rows = P("dp", None)
    blocks = P("task", "dp", None)
    routed = P("task", None, None)
    return jax.shard_map(
        local,
        mesh=mesh,
        in_specs=(tokens, tokens, P(), P(), rows, rows, routed, blocks, blocks, tokens, P("task")),
        out_specs=(tokens, tokens, P(), P(), rows, rows, routed, blocks, blocks),
        check_vma=False,
    )
```

```python
import functools

import jax
import jax.numpy as jnp
from jax import lax
from jax.experimental import pallas as pl
from jax.experimental.pallas import tpu as pltpu
from jax.sharding import PartitionSpec as P

D = 384
FF = 1536
HEADS = 6
HEAD_DIM = 64
PAIR = 2 * HEAD_DIM
TOPMAX = 4
SEQ = 1024
CAP = 320

f32 = jnp.float32
bf16 = jnp.bfloat16
HIGHEST = lax.Precision.HIGHEST
EPSILON = 1e-06
ROOT_HALF = 0.7071067811865476
NORMAL = 0.3989422804014327

FF_TILE = 512
ROW_TILE = 640
QUERY_FWD = 256
QUERY_BWD = 256
ROWS = 256
RETURNS = 2

GATHER_WHOLE = ((0, 0), (0, 1), (1, 0), (1, 1))
GATHER_SPLIT = ((2, 0), (2, 1))
GATHER_LATE = ((3, 0), (3, 1))
SCATTER_EARLY = ((0, 0), (0, 1), (1, 0))
SCATTER_SPLIT = ((1, 1), (2, 0))
SCATTER_LATE = ((2, 1), (3, 0), (3, 1, 0), (3, 1, 1))
EARLY_EXPERTS = 2

GATHER_POINTS = {2: ((0, 1), (0, 3), (1, 0), (1, 4)), 3: ((0, 2), (1, 1), (1, 4), (3, 0))}
SCATTER_POINTS = {1: (2, 4), 3: (3, 6)}

AHEAD = 2
FORWARD_FIRST = ((0, 1), (1, 1))
FORWARD_POINTS = {
    0: ((2, 1),),
    1: ((3, 1),),
    2: ((4, 1),),
    3: ((5, 1),),
    5: ((0, 2),),
    6: ((1, 2),),
    8: ((2, 2),),
    9: ((3, 2),),
    10: ((4, 2),),
    11: ((5, 2),),
}
FORWARD_THEN = (((0, 3), (1, 3)), ((2, 3), (3, 3), (4, 3), (5, 3)))

BACKWARD_POINTS = {
    3: ("s1", "u0",),
    8: ("t1", "s2", "v0",),
    11: ("u1",),
}
BACKWARD_THEN = (
    ("t2", "s3", "v1", "u2", "w0"),
    ("x0", "t3", "v2", "u3", "w1"),
    ("x1", "v3", "w2", "x2"),
    ("w3", "x3"),
)


VMEM = pl.BlockSpec(memory_space=pltpu.VMEM)
SMEM = pl.BlockSpec(memory_space=pltpu.SMEM)
ANY = pl.BlockSpec(memory_space=pl.ANY)


def shape(*dims, dtype=f32):
    return jax.ShapeDtypeStruct(dims, dtype)


def params(**more):
    return pltpu.CompilerParams(vmem_limit_bytes=63 * 2**20, **more)


def dot(a, b):
    return lax.dot_general(a, b, (((1,), (0,)), ((), ())), preferred_element_type=f32)


def dot_rt(a, b):
    return lax.dot_general(a, b, (((1,), (1,)), ((), ())), preferred_element_type=f32)


def dot_lt(a, b):
    return lax.dot_general(a, b, (((0,), (0,)), ((), ())), preferred_element_type=f32)


def rows_at(index, size):
    return pl.ds(pl.multiple_of(index * size, size), size)


def normalize(rows):
    centered = rows - jnp.mean(rows, axis=1, keepdims=True)
    scale = lax.rsqrt(jnp.mean(centered * centered, axis=1, keepdims=True) + EPSILON)
    return centered * scale, scale


def norm_back(rows, grad_rows, gain):
    unit, scale = normalize(rows)
    scaled = grad_rows * gain
    grad_in = scale * (
        scaled
        - jnp.mean(scaled, axis=1, keepdims=True)
        - unit * jnp.mean(scaled * unit, axis=1, keepdims=True)
    )
    grad_gain = jnp.sum(grad_rows * unit, axis=0, keepdims=True)
    return grad_in, grad_gain, jnp.sum(grad_rows, axis=0, keepdims=True), unit


def half_lanes(rows, half):
    lanes = lax.broadcasted_iota(jnp.int32, (rows, PAIR), 1)
    return (lanes < HEAD_DIM) if half == 0 else (lanes >= HEAD_DIM)


def remote(source, target, sent, landed, **device):
    return pltpu.make_async_remote_copy(
        src_ref=source,
        dst_ref=target,
        send_sem=sent,
        recv_sem=landed,
        device_id=device,
        device_id_type=pl.DeviceIdType.MESH,
    )


class Place:
    def __init__(self, outers):
        self.dp = lax.axis_index("dp")
        self.task = lax.axis_index("task")
        self.outers = outers
        self.outer, self.inner = self.dp // 2, self.dp % 2
        self.has_up, self.has_down = self.outer + 1 < outers, self.outer > 0
        self.up, self.down = self.dp + 2, self.dp - 2
        self.side = self.dp + 1 - 2 * self.inner
        self.core = self.task + 1 - 2 * (self.task % 2)
        self.across = self.task + 2 - 4 * (self.task // 2)
        self.far = self.across + 1 - 2 * (self.task % 2)

    def signal(self, **device):
        pl.semaphore_signal(
            pltpu.get_barrier_semaphore(),
            inc=1,
            device_id=device,
            device_id_type=pl.DeviceIdType.MESH,
        )

    def greet(self, far=False):
        pl.when(self.has_up)(lambda: self.signal(dp=self.up))
        pl.when(self.has_down)(lambda: self.signal(dp=self.down))
        self.signal(dp=self.side)
        self.signal(task=self.core)
        self.signal(task=self.across)
        if far:
            self.signal(task=self.far)
        others = 3 + int(far) + self.has_up.astype(jnp.int32) + self.has_down.astype(jnp.int32)
        pl.semaphore_wait(pltpu.get_barrier_semaphore(), others)

    def greet_all(self, groups):
        size = 2 * self.outers
        for ahead in range(1, size):
            self.signal(dp=lax.rem(self.dp + ahead, size))
        for ahead in range(1, groups):
            self.signal(task=lax.rem(self.task + ahead, groups))
        pl.semaphore_wait(pltpu.get_barrier_semaphore(), size + groups - 2)


class Gather:
    def __init__(self, place, shards, sent, landed, stay):
        self.place, self.shards = place, shards
        self.sent, self.landed, self.stay = sent, landed, stay

    def move(self, unit, source, way, device, first=None):
        _, size, full, _ = self.shards[unit]
        target = full.at[rows_at(source, size)]
        return remote(
            target if first is None else first,
            target,
            self.sent.at[unit, source, way],
            self.landed.at[unit, source],
            dp=device,
        )

    def local(self, unit):
        own, size, full, _ = self.shards[unit]
        target = full.at[rows_at(self.place.dp, size)]
        return pltpu.make_async_copy(own, target, self.stay.at[unit])

    def along(self, unit, source, up, down):
        place = self.place
        if up:
            pl.when(place.has_up)(lambda: self.move(unit, source, 0, place.up).start())
        if down:
            pl.when(place.has_down)(lambda: self.move(unit, source, 1, place.down).start())

    def to_side(self, unit, outer):
        own, size = self.shards[unit][:2]
        source = 2 * outer + self.place.inner
        return self.move(unit, source, 2, self.place.side, own.at[rows_at(source, size)])

    def start(self, unit):
        place = self.place
        own, mode = self.shards[unit][0], self.shards[unit][3]
        if mode == "side":
            for outer in range(place.outers):
                self.to_side(unit, outer).start()
            return
        if mode == "turned":
            self.move(unit, place.dp, 2, place.side, own).start()
        pl.when(place.has_up)(lambda: self.move(unit, place.dp, 0, place.up, own).start())
        pl.when(place.has_down)(lambda: self.move(unit, place.dp, 1, place.down, own).start())
        if mode == "both":
            self.move(unit, place.dp, 2, place.side, own).start()
        if self.stay is not None:
            self.local(unit).start()

    def step(self, unit, hop):
        place, mode = self.place, self.shards[unit][3]
        if hop == 0:
            self.move(unit, place.side, 0, place.dp).wait_recv()
            self.along(unit, place.side, True, True)
            return
        for column in (place.dp, place.side) if mode == "turned" else (place.dp,):

            @pl.when(place.outer >= hop)
            def _():
                self.move(unit, column - 2 * hop, 0, place.dp).wait_recv()
                self.along(unit, column - 2 * hop, True, False)
                if mode == "both":
                    self.move(unit, column - 2 * hop, 2, place.side).start()

            @pl.when(place.outer + hop < place.outers)
            def _():
                self.move(unit, column + 2 * hop, 1, place.dp).wait_recv()
                self.along(unit, column + 2 * hop, False, True)
                if mode == "both":
                    self.move(unit, column + 2 * hop, 2, place.side).start()

    def finish(self, unit):
        place, mode = self.place, self.shards[unit][3]
        if self.stay is not None:
            self.local(unit).wait()
        if mode == "turned":
            self.move(unit, place.dp, 2, place.side).wait_send()
        for outer in range(place.outers):
            own, other = 2 * outer + place.inner, 2 * outer + 1 - place.inner
            if mode in ("both", "side"):
                self.move(unit, other, 2, place.dp).wait_recv()
                self.move(unit, own, 2, place.side).wait_send()
            if mode == "side":
                continue
            for source in (own, other) if mode == "turned" else (own,):
                pl.when((outer <= place.outer) & place.has_up)(
                    lambda source=source: self.move(unit, source, 0, place.up).wait_send()
                )
                pl.when((outer >= place.outer) & place.has_down)(
                    lambda source=source: self.move(unit, source, 1, place.down).wait_send()
                )


def gather_semaphores(units, size):
    return [
        pltpu.SemaphoreType.DMA((units, size, 3)),
        pltpu.SemaphoreType.DMA((units, size)),
    ]


class Share:
    def __init__(self, place, view, sent, landed):
        self.place, self.view, self.sent, self.landed = place, view, sent, landed

    def move(self, source, way, **device):
        return remote(
            self.view(source),
            self.view(source),
            self.sent.at[way],
            self.landed.at[way],
            **device,
        )

    def start(self):
        place = self.place
        self.move(place.task, 0, task=place.across).start()
        self.move(place.task, 1, task=place.core).start()

    def relay(self):
        place = self.place
        self.move(place.across, 0, task=place.across).wait_recv()
        self.move(place.across, 2, task=place.core).start()

    def finish(self):
        place = self.place
        self.move(place.task, 0, task=place.across).wait_send()
        self.move(place.core, 1, task=place.core).wait()
        self.move(place.across, 2, task=place.core).wait()


class Scatter:
    def __init__(self, place, mine, theirs, side, line, sems):
        self.place, self.mine, self.theirs = place, mine, theirs
        self.side, self.line = side, line
        self.side_sent, self.side_landed, self.line_sent, self.line_landed = sems

    def to_side(self, outer):
        return remote(
            self.theirs(outer),
            self.side.at[outer],
            self.side_sent.at[outer],
            self.side_landed.at[outer],
            dp=self.place.side,
        )

    def fold(self, outer):
        return self.mine(outer) if self.side is None else self.side.at[outer]

    def along(self, outer, slot, device):
        return remote(
            self.fold(outer),
            self.line.at[slot],
            self.line_sent.at[outer],
            self.line_landed.at[slot],
            dp=device,
        )

    def start(self):
        outers = self.place.outers
        for near in range(outers // 2):
            self.to_side(outers - 1 - near).start()
            self.to_side(near).start()

    def total(self, outer, *slots):
        rows = self.mine(outer)[...].astype(f32)
        if self.side is not None:
            self.to_side(outer).wait_recv()
            rows += self.side[outer].astype(f32)
        for slot in slots:
            self.along(outer, slot, self.place.dp).wait_recv()
            rows += self.line[slot].astype(f32)
        return rows

    def settle(self, parts, sem):
        for outer in range(self.place.outers):
            self.fold(outer)[...] = self.total(outer).astype(bf16)
            self.to_side(outer).wait_send()
        copy = pltpu.make_async_copy(self.side, parts, sem)
        copy.start()
        return copy

    def hop(self, step):
        place, outers = self.place, self.place.outers

        @pl.when(place.outer == step)
        def _():
            for outer in range(outers - 1, step, -1):
                rows = self.total(outer, *([outer] if step else []))
                self.fold(outer)[...] = rows.astype(bf16)
                self.along(outer, outer, place.up).start()

        @pl.when(place.outer == outers - 1 - step)
        def _():
            for outer in range(outers - 1 - step):
                rows = self.total(outer, *([outer] if step else []))
                self.fold(outer)[...] = rows.astype(bf16)
                slot = outers if outer == outers - 2 - step else outer
                self.along(outer, slot, place.down).start()

    def finish(self, store):
        place, outers = self.place, self.place.outers
        for outer in range(outers):

            @pl.when(place.outer == outer)
            def _():
                below, above = [outer] * (outer > 0), [outers] * (outer < outers - 1)
                store(self.total(outer, *below, *above))
                for other in range(outers):
                    if other != outer:
                        self.along(other, other, place.dp).wait_send()

            if self.side is not None:
                self.to_side(outer).wait_send()


class Turned:
    def __init__(self, place, mine, theirs, refs):
        self.place = place
        self.own = Scatter(place, mine, None, None, refs[0], (None, None, *refs[1:3]))
        self.other = Scatter(place, theirs, None, None, refs[3], (None, None, *refs[4:6]))
        self.stage, self.land, self.sent, self.landed = refs[6:]

    def move(self):
        return remote(self.stage, self.land, self.sent, self.landed, dp=self.place.side)

    def start(self):
        self.own.hop(0)
        self.other.hop(0)

    def hop(self, step):
        if step:
            self.own.hop(step)
            self.other.hop(step)

    def finish(self, store):
        def send(rows):
            self.stage[...] = rows.astype(bf16)
            self.move().start()

        self.other.finish(send)
        self.own.finish(store)

    def add(self, shard):
        self.move().wait()
        shard[...] += self.land[...].astype(f32)


def turned_scratch(outers, tile):
    line = [pltpu.VMEM((outers + 1, *tile), bf16)]
    line += [pltpu.SemaphoreType.DMA((count,)) for count in (outers, outers + 1)]
    return line * 2 + [pltpu.VMEM(tile, bf16)] * 2 + [pltpu.SemaphoreType.DMA] * 2


def scatter_turn(units, stores, turn):
    outers = units[0].place.outers
    for step in range(outers - 1):
        if 0 <= turn - step < len(units):
            units[turn - step].hop(step)
    last = turn - outers + 1
    if 0 <= last < len(units):
        units[last].finish(stores[last])


def blocks_of(place, ref, size, half=()):
    def block(index):
        if half:
            return ref.at[rows_at(2 * index + half[0], size // 2)]
        return ref.at[rows_at(index, size)]

    return (
        lambda outer: block(2 * outer + place.inner),
        lambda outer: block(2 * outer + 1 - place.inner),
    )


def scatter_scratch(units, outers, tiles, side=True, line=True):
    scratch = []
    for unit in units:
        tile = tiles[unit[1]] if isinstance(unit, tuple) else tiles
        if isinstance(unit, tuple) and len(unit) > 2:
            tile = (tile[0] // 2, tile[1])
        for asked, slots in ((side, outers), (line, outers + 1)):
            if asked:
                scratch.append(pltpu.VMEM((slots, *tile), bf16))
        for asked, count in ((side, outers), (side, outers), (line, outers), (line, outers + 1)):
            if asked:
                scratch.append(pltpu.SemaphoreType.DMA((count,)))
    return scratch


def make_scatters(place, blocks, refs, side=True, line=True):
    count = 3 * side + 3 * line
    scatters = []
    for index, (mine, theirs) in enumerate(blocks):
        own = list(refs[index * count : (index + 1) * count])
        buffers = [own.pop(0) if asked else None for asked in (side, line)]
        sems = [own.pop(0) if asked else None for asked in (side, side, line, line)]
        scatters.append(Scatter(place, mine, theirs, *buffers, sems))
    return scatters


class Spread:
    def __init__(self, axis, place, count, land, sent, landed):
        self.axis, self.me, self.count = axis, getattr(place, axis), count
        self.land, self.sent, self.landed = land, sent, landed

    def move(self, source, ahead):
        return remote(
            self.land.at[source],
            self.land.at[source],
            self.sent.at[ahead - 1],
            self.landed.at[ahead - 1],
            **{self.axis: lax.rem(self.me + ahead, self.count)},
        )

    def give(self, rows):
        self.land[self.me] = rows.astype(self.land.dtype)
        for ahead in range(1, self.count):
            self.move(self.me, ahead).start()

    def arrive(self):
        for ahead in range(1, self.count):
            self.move(lax.rem(self.me + self.count - ahead, self.count), ahead).wait_recv()
            self.move(self.me, ahead).wait_send()

    def take(self):
        self.arrive()
        total = self.land[0].astype(f32)
        for index in range(1, self.count):
            total += self.land[index].astype(f32)
        return total


class Deal:
    def __init__(self, place, ref, size, land, sent, landed):
        self.place, self.ref, self.size = place, ref, size
        self.land, self.sent, self.landed = land, sent, landed
        self.count = land.shape[0]

    def block(self, index):
        return self.ref.at[rows_at(index, self.size)]

    def move(self, ahead):
        target = lax.rem(self.place.dp + ahead, self.count)
        return remote(
            self.block(target),
            self.land.at[self.place.dp],
            self.sent.at[ahead - 1],
            self.landed.at[ahead - 1],
            dp=target,
        )

    def start(self):
        for ahead in range(1, self.count):
            self.move(ahead).start()

    def total(self):
        rows = self.block(self.place.dp)[...].astype(f32)
        for ahead in range(1, self.count):
            self.move(ahead).wait()
            source = lax.rem(self.place.dp + self.count - ahead, self.count)
            rows += self.land[source].astype(f32)
        return rows


class Return:
    def __init__(self, place, parts, pieces, land, sent, landed):
        self.place, self.parts, self.pieces = place, parts, pieces
        self.land, self.sent, self.landed = land, sent, landed
        self.size = land.shape[1] // pieces

    def rows(self, piece):
        return pl.ds(piece * self.size, self.size)

    def move(self, way, piece):
        place, rows = self.place, self.rows(piece)
        source = [
            self.parts[0].at[rows],
            self.parts[1].at[rows],
            self.parts[2].at[rows],
        ][way]
        return remote(
            source,
            self.land.at[way, rows],
            self.sent.at[way, piece],
            self.landed.at[way, piece],
            task=place.across if way == 2 else place.core,
        )

    def to_core(self, piece):
        self.move(0, piece).start()

    def by_core(self, piece):
        self.move(1, piece).start()

    def to_across(self, piece):
        rows = self.rows(piece)
        self.move(1, piece).wait_recv()
        joint = self.parts[2][rows, :].astype(f32)
        joint += self.land[1, rows, :].astype(f32)
        self.parts[2][rows, :] = joint.astype(bf16)
        self.move(2, piece).start()

    def finish(self, piece):
        rows = self.rows(piece)
        self.move(0, piece).wait()
        self.move(1, piece).wait_send()
        self.move(2, piece).wait()
        total = self.parts[3][rows, :].astype(f32)
        return total + self.land[0, rows, :].astype(f32) + self.land[2, rows, :].astype(f32)


def attend(packed, mixed, totals, index, between):
    zero = jnp.array(0, bf16)
    rows = rows_at(index, QUERY_FWD)

    def head_pair(pair, _):
        queries, keys, values = (rows_at(pair + part * (D // PAIR), PAIR) for part in range(3))
        key_rows, value_rows = packed[:, keys], packed[:, values]
        query_rows = packed[rows, queries] * jnp.array(HEAD_DIM**-0.5, bf16)
        outs, logs = [], []
        for half in range(2):
            own = jnp.where(half_lanes(QUERY_FWD, half), query_rows, zero)
            scores = dot_rt(own, key_rows)
            top = jnp.max(scores, axis=1, keepdims=True)
            weights = jnp.exp(scores - top)
            total = jnp.sum(weights, axis=1, keepdims=True)
            outs.append(dot(weights.astype(bf16), value_rows) * (1.0 / total))
            logs.append(top + jnp.log(total))
        mixed[rows, queries] = jnp.where(half_lanes(QUERY_FWD, 0), outs[0], outs[1]).astype(bf16)
        lanes = lax.broadcasted_iota(jnp.int32, (QUERY_FWD, 8), 1)
        totals[rows, :] = jnp.where(
            lanes == 2 * pair,
            logs[0],
            jnp.where(lanes == 2 * pair + 1, logs[1], totals[rows, :]),
        )
        between(index * (HEADS // 2) + pair)
        return 0

    lax.fori_loop(0, HEADS // 2, head_pair, 0)


def first_norm(image, gain, bias, normed_first):
    def block(index, _):
        rows = rows_at(index, ROWS)
        unit, _ = normalize(image[rows, :])
        normed_first[rows, :] = (unit * gain[0:1, :] + bias[0:1, :]).astype(bf16)
        return 0

    lax.fori_loop(0, SEQ // ROWS, block, 0)


def number_slots(choices, top_count, experts):
    named = choices[...]
    numbers = lax.broadcasted_iota(jnp.int32, (experts, SEQ), 0)
    used = jnp.zeros((experts, SEQ), f32)
    for choice in range(TOPMAX):
        hit = (named[choice : choice + 1, :] == numbers) & (choice < top_count[0])
        used = used + jnp.where(hit, 1.0, 0.0)
    earlier = lax.broadcasted_iota(jnp.int32, (SEQ, SEQ), 0) < lax.broadcasted_iota(
        jnp.int32, (SEQ, SEQ), 1
    )
    before = dot(used.astype(bf16), jnp.where(earlier, 1.0, 0.0).astype(bf16))
    return jnp.where(used > 0, before, -1.0).astype(jnp.int32)


def mid_block(index, image, gain, bias, w_proj, router, mixed, mid, probs):
    rows = rows_at(index, QUERY_FWD)
    mid_rows = image[rows, :] + dot(mixed[rows, :], w_proj[...])
    mid[rows, :] = mid_rows
    unit, _ = normalize(mid_rows)
    normed_rows = unit * gain[1:2, :] + bias[1:2, :]
    logits = lax.dot_general(
        router[...],
        normed_rows,
        (((1,), (1,)), ((), ())),
        precision=HIGHEST,
        preferred_element_type=f32,
    )
    powers = jnp.exp(logits - jnp.max(logits, axis=0, keepdims=True))
    probs[:, rows] = powers / jnp.sum(powers, axis=0, keepdims=True)
    return normed_rows.astype(bf16)


def forward_kernel(
    top_count,
    image,
    gain,
    bias,
    w_qkv,
    w_proj,
    router,
    choices,
    mid,
    packed,
    mixed,
    logs,
    normed,
    slots,
    gates,
    probs,
    normed_first,
    totals,
):
    first_norm(image, gain, bias, normed_first)
    slots[...] = number_slots(choices, top_count, router.shape[0])
    packed[...] = dot(normed_first[...], w_qkv[...]).astype(bf16)
    totals[...] = jnp.zeros_like(totals)

    def block(index, _):
        attend(packed, mixed, totals, index, lambda point: None)
        normed[rows_at(index, QUERY_FWD), :] = mid_block(
            index, image, gain, bias, w_proj, router, mixed, mid, probs
        )
        return 0

    lax.fori_loop(0, SEQ // QUERY_FWD, block, 0)
    logs[...] = totals[...].T
    gates[...] = jnp.where(slots[...] >= 0, probs[...], 0.0)


def forward_part(top_count, image, gain, bias, w_qkv, w_proj, router, choices):
    experts = router.shape[0]
    return pl.pallas_call(
        forward_kernel,
        out_shape=(
            shape(SEQ, D),
            shape(SEQ, 3 * D, dtype=bf16),
            shape(SEQ, D, dtype=bf16),
            shape(8, SEQ),
            shape(SEQ, D, dtype=bf16),
            shape(experts, SEQ, dtype=jnp.int32),
            shape(experts, SEQ),
            shape(experts, SEQ),
        ),
        in_specs=[SMEM] + [VMEM] * 7,
        out_specs=[VMEM] * 8,
        scratch_shapes=[pltpu.VMEM((SEQ, D), bf16), pltpu.VMEM((SEQ, 8), f32)],
        compiler_params=params(),
    )(top_count, image, gain, bias, w_qkv, w_proj, router, choices)


def forward_sending_kernel(
    outers,
    top_count,
    image,
    cotangent,
    gain,
    bias,
    w_qkv,
    w_proj,
    w_in,
    w_out,
    router,
    choices,
    mid,
    packed,
    mixed,
    logs,
    probs,
    normed_all,
    cot_all,
    slots_all,
    gates_all,
    quarters,
    full_in,
    full_out,
    normed_first,
    totals,
    own_quarter,
    sent,
    landed,
    stay,
    share_sent,
    share_landed,
):
    place = Place(outers)
    task = place.task
    for part in range(4):

        @pl.when(task == part)
        def _():
            own_quarter[...] = w_proj[...] if part == 3 else w_qkv[:, part * D : (part + 1) * D]

    shards = [(own_quarter, w_qkv.shape[0], quarters.at[task], "both")]
    for expert, kind in GATHER_WHOLE + GATHER_SPLIT:
        own, full = ((w_in, full_in), (w_out, full_out))[kind]
        mode = "line" if (expert, kind) in GATHER_SPLIT else "both"
        shards.append((own.at[expert], own.shape[1], full.at[expert], mode))
    gather = Gather(place, shards, sent, landed, stay)
    routed = range(1, len(shards))
    cot_all[task] = cotangent[...].astype(bf16)
    place.greet()
    gather.start(0)

    def share(index, view):
        return Share(place, view, share_sent.at[index], share_landed.at[index])

    cot = share(0, lambda source: cot_all.at[source])
    slot = share(1, lambda source: slots_all.at[source])
    gate = share(2, lambda source: gates_all.at[source])
    def run(acts):
        for unit, hop in acts:
            if unit < len(routed):
                gather.step(routed[unit], hop)

    for unit in routed[:AHEAD]:
        gather.start(unit)
    cot.start()
    first_norm(image, gain, bias, normed_first)
    for hop in range(1, outers):
        gather.step(0, hop)
    for unit in routed[AHEAD:]:
        gather.start(unit)
    gather.finish(0)
    quarter = share(3 + SEQ // QUERY_FWD, lambda source: quarters.at[source])
    quarter.start()
    slots_all[task] = number_slots(choices, top_count, router.shape[0])
    slot.start()
    totals[...] = jnp.zeros_like(totals)
    run(FORWARD_FIRST)
    quarter.relay()
    quarter.finish()
    for part in range(3):
        packed[:, part * D : (part + 1) * D] = dot(normed_first[...], quarters[part]).astype(bf16)
    cot.relay()
    slot.relay()

    def chunk(index):
        return share(3 + index, lambda source: normed_all.at[source, rows_at(index, QUERY_FWD)])

    blocks = SEQ // QUERY_FWD

    def block(index, _):
        def between(point):
            for at, acts in FORWARD_POINTS.items():
                pl.when(point == at)(lambda acts=acts: run(acts))

        attend(packed, mixed, totals, index, between)
        normed_all[task, rows_at(index, QUERY_FWD), :] = mid_block(
            index, image, gain, bias, quarters.at[3], router, mixed, mid, probs
        )
        chunk(index).start()
        pl.when(index > 0)(lambda: chunk(index - 1).relay())
        return 0

    lax.fori_loop(0, blocks, block, 0)
    gates_all[task] = jnp.where(slots_all[task] >= 0, probs[...], 0.0)
    gate.start()
    logs[...] = totals[...].T
    run(FORWARD_THEN[0])
    chunk(blocks - 1).relay()
    gate.relay()
    run(FORWARD_THEN[1])
    for one in [cot, slot, gate] + [chunk(index) for index in range(blocks)]:
        one.finish()
    for unit in routed:
        gather.finish(unit)


def forward_sending(top_count, image, cotangent, gain, bias, shards, router, choices):
    w_qkv, w_proj, w_in, w_out = shards
    experts, size = router.shape[0], lax.axis_size("dp")
    groups, early = lax.axis_size("task"), 1 + GATHER_SPLIT[-1][0]
    units, shares = 1 + len(GATHER_WHOLE + GATHER_SPLIT), 4 + SEQ // QUERY_FWD
    return pl.pallas_call(
        functools.partial(forward_sending_kernel, size // 2),
        out_shape=(
            shape(SEQ, D),
            shape(SEQ, 3 * D, dtype=bf16),
            shape(SEQ, D, dtype=bf16),
            shape(8, SEQ),
            shape(experts, SEQ),
            shape(groups, SEQ, D, dtype=bf16),
            shape(groups, SEQ, D, dtype=bf16),
            shape(groups, experts, SEQ, dtype=jnp.int32),
            shape(groups, experts, SEQ),
            shape(groups, D, D, dtype=bf16),
            shape(early, D, FF, dtype=bf16),
            shape(early, FF, D, dtype=bf16),
        ),
        in_specs=[SMEM] + [VMEM] * 10,
        out_specs=[VMEM] * 10 + [ANY] * 2,
        scratch_shapes=[
            pltpu.VMEM((SEQ, D), bf16),
            pltpu.VMEM((SEQ, 8), f32),
            pltpu.VMEM(w_proj.shape, bf16),
            *gather_semaphores(units, size),
            pltpu.SemaphoreType.DMA((units,)),
            pltpu.SemaphoreType.DMA((shares, 3)),
            pltpu.SemaphoreType.DMA((shares, 3)),
        ],
        compiler_params=params(collective_id=0, has_side_effects=True),
    )(top_count, image, cotangent, gain, bias, w_qkv, w_proj, w_in, w_out, router, choices)


def slot_hits(slots, source, expert):
    return lax.broadcasted_iota(jnp.int32, (CAP, SEQ), 0) == slots[source, pl.ds(expert, 1), :]


def ones_at(hits):
    return jnp.where(hits, 1.0, 0.0).astype(bf16)


def dispatch(operands, work, expert, first, block, source):
    tokens, slots, gates = operands[:3]
    rows_in, rows_grad, rows_cot, rows_gate = work[:4]
    own = slice(block * CAP, (block + 1) * CAP)
    hits = slot_hits(slots, source, first + expert)
    both = dot(ones_at(hits), tokens[source])
    gate = jnp.sum(
        jnp.where(hits, gates[source, pl.ds(first + expert, 1), :], 0.0), axis=1, keepdims=True
    )
    rows_in[own, :] = both[:, :D].astype(bf16)
    rows_cot[own, :] = both[:, D:].astype(bf16)
    rows_grad[own, :] = (gate * both[:, D:]).astype(bf16)
    rows_gate[own, :] = jnp.broadcast_to(gate, (CAP, 128))


def hidden_tiles(operands, work, slot, start, count):
    w_in, w_out = operands[3:]
    rows_in, rows_grad, _, _, hidden, grad_pre, _ = work

    def tile(index, _):
        units = rows_at(index // count, FF_TILE)
        rows = rows_at(start + lax.rem(index, count), ROW_TILE)
        pre = dot(rows_in[rows, :], w_in[slot, :, units])
        grad_hidden = dot_rt(rows_grad[rows, :], w_out[slot, units, :])
        share = 0.5 * lax.erf(pre * ROOT_HALF) + 0.5
        slope = share + pre * (NORMAL * jnp.exp(-0.5 * pre * pre))
        hidden[rows, units] = (pre * share).astype(bf16)
        grad_pre[rows, units] = (grad_hidden * slope).astype(bf16)
        return 0

    lax.fori_loop(0, (FF // FF_TILE) * count, tile, 0)


def expert_rows_out(operands, work, grad_gates, expert, first, slot, block, source):
    slots, (w_in, w_out) = operands[1], operands[3:]
    _, _, rows_cot, rows_gate, hidden, grad_pre, sent = work
    own = slice(block * CAP, (block + 1) * CAP)
    kept = rows_at(expert, CAP)
    out_rows = dot(hidden[own, :], w_out[slot]).astype(bf16).astype(f32)
    sent[source, kept, :D] = (rows_gate[own, 0:1] * out_rows).astype(bf16)
    sent[source, kept, D:] = dot_rt(grad_pre[own, :], w_in[slot]).astype(bf16)
    grad_gate = jnp.sum(rows_cot[own, :].astype(f32) * out_rows, axis=1, keepdims=True)
    hits = slot_hits(slots, source, first + expert)
    grad_gates[source, pl.ds(expert, 1), :] = jnp.sum(
        jnp.where(hits, grad_gate, 0.0), axis=0, keepdims=True
    )


def weight_grads(work, grads, expert):
    rows_in, rows_grad, _, _, hidden, grad_pre, _ = work
    grads[0][expert] = dot_lt(rows_in[...], grad_pre[...]).astype(bf16)
    grads[1][expert] = dot_lt(rows_grad[...], hidden[...]).astype(bf16).T


def one_expert(operands, work, grads, expert, first, slot, sources, between, halfway=None):
    halves = 1 if halfway is None else 2
    size, tiles = len(sources) // halves, len(sources) * CAP // ROW_TILE // halves
    between(0)
    for block, source in enumerate(sources):
        dispatch(operands, work, expert, first, block, source)
    between(1)
    for half in range(halves):
        hidden_tiles(operands, work, slot, half * tiles, tiles)
        between(2 + half * 2)
        for block in range(half * size, (half + 1) * size):
            expert_rows_out(
                operands, work, grads[2], expert, first, slot, block, sources[block]
            )
        if half + 1 < halves:
            halfway()
    between(3 if halves == 1 else 5)
    weight_grads(work, grads, expert)
    between(4 if halves == 1 else 6)


def combine(slots, first, local_count, sent, columns, source, store):
    size = SEQ // RETURNS
    columns[...] = slots[source].T
    for piece in range(RETURNS):
        rows = pl.ds(piece * size, size)
        lanes = lax.broadcasted_iota(jnp.int32, (size, CAP), 1)
        mine = lax.broadcasted_iota(jnp.int32, (size, columns.shape[1]), 1)
        picks = []
        for expert in range(local_count):
            column = jnp.max(
                jnp.where(mine == first + expert, columns[rows, :], -1), axis=1, keepdims=True
            )
            picks.append(ones_at(lanes == column))
        back = dot(jnp.concatenate(picks, axis=1), sent[source])
        store(piece, rows, back[:, :D].astype(bf16), back[:, D:].astype(bf16))


def expert_scratch(groups, local_count, experts):
    width = groups * CAP
    return [
        pltpu.VMEM((width, D), bf16),
        pltpu.VMEM((width, D), bf16),
        pltpu.VMEM((width, D), bf16),
        pltpu.VMEM((width, 128), f32),
        pltpu.VMEM((width, FF), bf16),
        pltpu.VMEM((width, FF), bf16),
        pltpu.VMEM((groups, local_count * CAP, 2 * D), bf16),
        pltpu.VMEM((SEQ, experts), jnp.int32),
    ]


def expert_kernel(*refs):
    operands, grads, (mixes, grad_normed) = refs[:5], refs[5:8], refs[8:10]
    work, columns = refs[10:17], refs[17]
    groups, local_count = operands[0].shape[0], operands[3].shape[0]

    def body(expert, _):
        one_expert(
            operands, work, grads, expert, 0, expert, range(groups), lambda point: None
        )
        return 0

    lax.fori_loop(0, local_count, body, 0)
    for source in range(groups):

        def store(piece, rows, mix, grad, source=source):
            mixes[source, rows, :] = mix
            grad_normed[source, rows, :] = grad

        combine(operands[1], 0, local_count, work[6], columns, source, store)


def expert_part(*operands):
    groups, local_count = operands[0].shape[0], operands[3].shape[0]
    return pl.pallas_call(
        expert_kernel,
        out_shape=(
            shape(local_count, D, FF, dtype=bf16),
            shape(local_count, FF, D, dtype=bf16),
            shape(groups, local_count, SEQ),
            shape(groups, SEQ, D, dtype=bf16),
            shape(groups, SEQ, D, dtype=bf16),
        ),
        in_specs=[VMEM] * 5,
        out_specs=[VMEM] * 5,
        scratch_shapes=expert_scratch(groups, local_count, operands[1].shape[1]),
        compiler_params=params(),
    )(*operands)


def expert_sending_kernel(outers, *refs):
    normed_all, cot_all, slots, gates, early_in, early_out, w_in, w_out = refs[:8]
    late_in, late_out, gate_all, mixes, grad_rows, shard_in, shard_out, parts_in, parts_out = refs[8:17]
    full_in, full_out = refs[17:19]
    work, columns = refs[19:26], refs[26]
    both, slot_in, slot_out, grad_in, grad_out, grad_gates, land, first_parts = refs[27:35]
    sent, landed, gate_sent, gate_landed, mix_sem, late_sem, slot_sem, token_sem = refs[35:43]
    part_sem, gather_sems, scatter_refs = refs[43], refs[44:46], refs[46:]
    place = Place(outers)
    groups, local_count, size = both.shape[0], grad_in.shape[0], 2 * outers
    late = local_count - EARLY_EXPERTS
    first = place.task * local_count
    grads, shares = (grad_in, grad_out), (w_in.shape[1], w_out.shape[1])

    def tokens():
        return [
            pltpu.make_async_copy(
                whole.at[source],
                both.at[source, :, pl.ds(kind * D, D)],
                token_sem.at[kind, source],
            )
            for source in range(groups)
            for kind, whole in enumerate((normed_all, cot_all))
        ]

    def load(expert):
        slot, copies = expert % EARLY_EXPERTS, []
        for kind in range(2):
            target, sem = (slot_in, slot_out)[kind].at[slot], slot_sem.at[slot, kind]
            early, own = (early_in, early_out)[kind], (w_in, w_out)[kind]
            full = (full_in, full_out)[kind]
            if expert < EARLY_EXPERTS:
                copies.append(pltpu.make_async_copy(early.at[expert], target, sem.at[0]))
                continue
            for ahead in range(size):
                block = lax.rem(place.dp + ahead, size)
                rows = rows_at(block, shares[kind])
                source = full.at[expert - EARLY_EXPERTS, rows]
                if (expert, kind) in GATHER_SPLIT:
                    if ahead % 2 == 0:
                        source = early.at[expert, rows]
                elif ahead == 0:
                    source = own.at[expert]
                copies.append(pltpu.make_async_copy(source, target.at[rows], sem.at[ahead]))
        return copies

    def keep(expert):
        return [
            pltpu.make_async_copy(
                grads[kind].at[EARLY_EXPERTS + expert],
                (late_in, late_out)[kind].at[expert],
                late_sem.at[expert, kind],
            )
            for kind in range(2)
        ]

    for copy in tokens() + load(0):
        copy.start()
    place.greet(far=True)
    shards = []
    for expert, kind in GATHER_LATE + GATHER_SPLIT:
        full = (full_in, full_out)[kind].at[expert - EARLY_EXPERTS]
        if (expert, kind) in GATHER_SPLIT:
            shards.append(((early_in, early_out)[kind].at[expert], shares[kind], full, "side"))
        else:
            shards.append(((w_in, w_out)[kind].at[expert], shares[kind], full, "turned"))
    gather = Gather(place, shards, *gather_sems, None)
    turned = range(len(GATHER_LATE))
    for unit in range(len(shards)):
        gather.start(unit)
    for copy in load(1):
        copy.start()
    per_full, per_side = 6 * len(SCATTER_EARLY[1:]), 3 * len(SCATTER_SPLIT)

    def scatters(units, refs, **parts):
        return make_scatters(
            place,
            [blocks_of(place, grads[kind].at[expert], shares[kind]) for expert, kind in units],
            refs,
            **parts,
        )

    expert, kind = SCATTER_EARLY[0]
    turned_scatter = Turned(
        place,
        *blocks_of(place, grads[kind].at[expert], shares[kind]),
        scatter_refs[per_full + per_side :],
    )
    whole = [turned_scatter] + scatters(SCATTER_EARLY[1:], scatter_refs[:per_full])
    split = scatters(SCATTER_SPLIT, scatter_refs[per_full : per_full + per_side], line=False)
    stores, keeps = [], []
    for expert, kind in SCATTER_EARLY:

        def store(rows, shard=(shard_in, shard_out)[kind], expert=expert):
            shard[expert] = rows

        stores.append(store)
    for index, (_, kind) in enumerate(SCATTER_SPLIT):
        at = [other[1] for other in SCATTER_SPLIT[:index]].count(kind)

        keeps.append((parts_in, parts_out)[kind].at[at])
    steps = {}

    def plan(expert, point, *acts):
        steps.setdefault((expert, point), []).extend(acts)

    plan(0, 0, *[copy.wait for copy in tokens()])
    for expert in range(EARLY_EXPERTS):
        plan(expert, 1, *[copy.wait for copy in load(expert)])
    for unit in turned:
        for hop, at in enumerate(GATHER_POINTS[GATHER_LATE[unit][0]]):
            plan(*at, lambda unit=unit, hop=hop: gather.step(unit, hop))
    for expert in range(EARLY_EXPERTS, local_count):
        units = [
            unit
            for unit, (owner, _) in enumerate(GATHER_LATE + GATHER_SPLIT)
            if owner == expert
        ]
        plan(expert, 0, *[lambda unit=unit: gather.finish(unit) for unit in units])
        plan(expert, 0, *[copy.start for copy in load(expert)])
        plan(expert, 1, *[copy.wait for copy in load(expert)])
        point = 4 if expert < local_count - 1 else 6
        plan(expert, point, *[copy.start for copy in keep(expert - EARLY_EXPERTS)])
    for index, (expert, _) in enumerate(SCATTER_EARLY):
        plan(expert, 4, whole[index].start)
    for index, (expert, _) in enumerate(SCATTER_SPLIT):
        plan(expert, 4, split[index].start)
    for turn, at in SCATTER_POINTS.items():
        plan(*at, lambda turn=turn: scatter_turn(whole, stores, turn))

    operands = (both, slots, gates, slot_in, slot_out)
    every_grad = (grad_in, grad_out, grad_gates)
    sources = (place.far, place.across, place.core, place.task)

    def body(expert, _):
        def between(point):
            for at in range(local_count - 1):
                acts = steps.get((at, point))
                if acts:

                    @pl.when(expert == at)
                    def _():
                        for act in acts:
                            act()

        one_expert(
            operands,
            work,
            every_grad,
            expert,
            first,
            lax.rem(expert, EARLY_EXPERTS),
            sources,
            between,
        )
        return 0

    lax.fori_loop(0, local_count - 1, body, 0)
    hidden, grad_pre = work[4], work[5]

    def part(ref, block):
        return ref.at[pl.ds(0, SEQ), pl.ds(block * D, D)]

    parts = [first_parts.at[0], first_parts.at[1], part(hidden, 0), part(hidden, 1)]
    mix_parts = [first_parts.at[2], first_parts.at[2], part(grad_pre, 0), part(grad_pre, 1)]
    back = Return(
        place,
        (parts[2], parts[0], parts[1], parts[3]),
        RETURNS,
        land,
        sent,
        landed,
    )
    sends = (back.by_core, back.to_across, back.to_core, None)

    def mix_copy(block):
        return pltpu.make_async_copy(
            mix_parts[block], mixes.at[sources[block]], mix_sem.at[block]
        )

    def returned(block):
        def store(piece, rows, mix, grad):
            mix_parts[block][rows, :] = mix
            parts[block][rows, :] = grad
            if sends[block]:
                sends[block](piece)

        combine(slots, first, local_count, work[6], columns, sources[block], store)
        mix_copy(block).start()

    def halfway():
        returned(0)
        mix_copy(0).wait()
        returned(1)
        scatter_turn(whole, stores, 2)

    def last(point):
        for act in steps.get((local_count - 1, point), ()):
            act()

    one_expert(
        operands,
        work,
        every_grad,
        local_count - 1,
        first,
        (local_count - 1) % EARLY_EXPERTS,
        sources,
        last,
        halfway,
    )
    gate_all[place.task] = grad_gates[place.task]
    peers = (place.core, place.across, place.far)

    def gate_move(way):
        return remote(
            grad_gates.at[peers[way]],
            gate_all.at[place.task],
            gate_sent.at[way],
            gate_landed.at[way],
            task=peers[way],
        )

    for way in range(3):
        gate_move(way).start()
    returned(2)
    returned(3)
    for turn in range(4, len(whole) + outers - 1):
        scatter_turn(whole, stores, turn)
    expert, kind = SCATTER_EARLY[0]
    turned_scatter.add((shard_in, shard_out)[kind].at[expert])
    settled = [
        one.settle(keeps[index], part_sem.at[index]) for index, one in enumerate(split)
    ]
    for piece in range(RETURNS):
        grad_rows[back.rows(piece), :] = back.finish(piece)
    for way in range(3):
        gate_move(way).wait()
    for block in range(1, groups):
        mix_copy(block).wait()
    for expert in range(late):
        for copy in keep(expert):
            copy.wait()
    for copy in settled:
        copy.wait()


def kinds(units, kind):
    return sorted({unit[0] for unit in units if unit[1] == kind})


def expert_sending(*operands):
    groups, experts = operands[2].shape[:2]
    local_count, thin = operands[6].shape[:2]
    wide, size = operands[7].shape[1], lax.axis_size("dp")
    late, outers = local_count - EARLY_EXPERTS, size // 2
    tiles = ((thin, FF), (wide, D))
    return pl.pallas_call(
        functools.partial(expert_sending_kernel, outers),
        out_shape=(
            shape(late, D, FF, dtype=bf16),
            shape(late, FF, D, dtype=bf16),
            shape(groups, local_count, SEQ),
            shape(groups, SEQ, D, dtype=bf16),
            shape(SEQ, D),
            *[shape(len(kinds(SCATTER_EARLY, kind)), *tiles[kind]) for kind in range(2)],
            *[
                shape(len(kinds(SCATTER_SPLIT, kind)), outers, *tiles[kind], dtype=bf16)
                for kind in range(2)
            ],
            shape(late, D, FF, dtype=bf16),
            shape(late, FF, D, dtype=bf16),
        ),
        in_specs=[ANY] * 2 + [VMEM] * 2 + [ANY] * 4,
        out_specs=[ANY] * 2 + [VMEM, ANY] + [VMEM] * 3 + [ANY] * 4,
        scratch_shapes=expert_scratch(groups, local_count, experts)
        + [
            pltpu.VMEM((groups, SEQ, 2 * D), bf16),
            pltpu.VMEM((EARLY_EXPERTS, D, FF), bf16),
            pltpu.VMEM((EARLY_EXPERTS, FF, D), bf16),
            pltpu.VMEM((local_count, D, FF), bf16),
            pltpu.VMEM((local_count, FF, D), bf16),
            pltpu.VMEM((groups, local_count, SEQ), f32),
            pltpu.VMEM((3, SEQ, D), bf16),
            pltpu.VMEM((3, SEQ, D), bf16),
            pltpu.SemaphoreType.DMA((3, RETURNS)),
            pltpu.SemaphoreType.DMA((3, RETURNS)),
            pltpu.SemaphoreType.DMA((3,)),
            pltpu.SemaphoreType.DMA((3,)),
            pltpu.SemaphoreType.DMA((groups,)),
            pltpu.SemaphoreType.DMA((late, 2)),
            pltpu.SemaphoreType.DMA((EARLY_EXPERTS, 2, size)),
            pltpu.SemaphoreType.DMA((2, groups)),
            pltpu.SemaphoreType.DMA((len(SCATTER_SPLIT),)),
        ]
        + gather_semaphores(len(GATHER_LATE + GATHER_SPLIT), size)
        + scatter_scratch(SCATTER_EARLY[1:], outers, tiles)
        + scatter_scratch(SCATTER_SPLIT, outers, tiles, line=False)
        + turned_scratch(outers, tiles[SCATTER_EARLY[0][1]]),
        compiler_params=params(collective_id=1, has_side_effects=True),
    )(*operands)


def attend_back(packed, grad_mixed, logs, grad_packed, grad_keys, grad_values, between, done):
    zero = jnp.array(0, bf16)
    blocks = SEQ // QUERY_BWD

    def head_pair(pair):
        queries, keys, values = (
            slice(part * D + pair * PAIR, part * D + (pair + 1) * PAIR) for part in range(3)
        )
        key_rows, value_rows = packed[:, keys], packed[:, values]

        def block(index, _):
            rows = rows_at(index, QUERY_BWD)
            query_rows = packed[rows, queries] * jnp.array(HEAD_DIM**-0.5, bf16)
            grad_rows = grad_mixed[rows, queries]
            grad_query, part_keys, part_values = [], 0.0, 0.0
            for half in range(2):
                lanes = half_lanes(QUERY_BWD, half)
                own = jnp.where(lanes, query_rows, zero)
                own_grad = jnp.where(lanes, grad_rows, zero)
                head = 2 * pair + half
                probs = jnp.exp(dot_rt(key_rows, own) - logs[head : head + 1, rows])
                grad_probs = dot_rt(value_rows, own_grad)
                mean = jnp.sum(probs * grad_probs, axis=0, keepdims=True)
                grad_scores = (probs * (grad_probs - mean)).astype(bf16)
                part_values += dot(probs.astype(bf16), own_grad)
                part_keys += dot(grad_scores, own)
                grad_query.append(dot_lt(grad_scores, key_rows))
            grad_packed[rows, queries] = (
                jnp.where(half_lanes(QUERY_BWD, 0), grad_query[0], grad_query[1])
                * HEAD_DIM**-0.5
            ).astype(bf16)
            grad_keys[...] = jnp.where(index == 0, part_keys, grad_keys[...] + part_keys)
            grad_values[...] = jnp.where(index == 0, part_values, grad_values[...] + part_values)
            between(pair, index)
            return 0

        lax.fori_loop(0, blocks, block, 0)
        grad_packed[:, keys] = grad_keys[...].astype(bf16)
        grad_packed[:, values] = grad_values[...].astype(bf16)
        done(pair, (queries, keys, values))

    for pair in range(HEADS // 2):
        head_pair(pair)


def second_back(
    grad_rows, cotangent, gain, bias, mid, w_proj, router, grad_logits, grad_norm, grad_router, outs
):
    grad_mid, grad_low, grad_mixed = outs
    grad_norm[...] = jnp.zeros_like(grad_norm)
    grad_router[...] = jnp.zeros_like(grad_router)
    for index in range(SEQ // ROWS):
        rows = slice(index * ROWS, (index + 1) * ROWS)
        mid_rows = mid[rows, :]
        own_logits = grad_logits[:, rows]
        grad_in_rows = grad_rows(rows) + lax.dot_general(
            own_logits,
            router[...],
            (((0,), (0,)), ((), ())),
            precision=HIGHEST,
            preferred_element_type=f32,
        )
        grad_in, grad_gain, grad_bias, unit = norm_back(mid_rows, grad_in_rows, gain[1:2, :])
        grad_router[...] += jnp.dot(
            own_logits,
            unit * gain[1:2, :] + bias[1:2, :],
            precision=HIGHEST,
            preferred_element_type=f32,
        )
        grad_norm[1:2, :] += grad_gain
        grad_norm[3:4, :] += grad_bias
        grad_mid_rows = cotangent[rows, :] + grad_in
        grad_mid[rows, :] = grad_mid_rows
        low_rows = grad_mid_rows.astype(bf16)
        grad_low[rows, :] = low_rows
        grad_mixed[rows, :] = dot_rt(low_rows, w_proj[...]).astype(bf16)


def first_back(image, gain, parts, grad_packed, grad_mid, grad_image, grad_norm):
    def block(index, _):
        rows = rows_at(index, ROWS)
        grad_rows = sum(
            dot_rt(grad_packed[rows, part * D : (part + 1) * D], parts(part)) for part in range(3)
        )
        grad_in, grad_gain, grad_bias, _ = norm_back(image[rows, :], grad_rows, gain[0:1, :])
        grad_image[rows, :] = grad_mid[rows, :] + grad_in
        grad_norm[0:1, :] += grad_gain
        grad_norm[2:3, :] += grad_bias
        return 0

    lax.fori_loop(0, SEQ // ROWS, block, 0)


def logit_grads(probs, grad_gates):
    route = jnp.concatenate([grad_gates[group] for group in range(grad_gates.shape[0])], axis=0)
    return probs[...] * (route - jnp.sum(probs[...] * route, axis=0, keepdims=True))


def backward_scratch():
    return [
        pltpu.VMEM((SEQ, D), f32),
        pltpu.VMEM((SEQ, D), bf16),
        pltpu.VMEM((SEQ, D), bf16),
        pltpu.VMEM((SEQ, 3 * D), bf16),
        pltpu.VMEM((SEQ, PAIR), f32),
        pltpu.VMEM((SEQ, PAIR), f32),
        pltpu.VMEM((SEQ, D), bf16),
    ]


def backward_kernel(*refs):
    image, cotangent, gain, bias, mid, w_qkv, w_proj, router = refs[:8]
    packed, mixed, logs, mixes, grad_normed, grad_gates, probs = refs[8:15]
    activations, grad_image, grad_norm, grad_router, grad_shared = refs[15:20]
    grad_mid, grad_low, grad_mixed, grad_packed, grad_keys, grad_values, normed_first = refs[20:]
    groups = mixes.shape[0]

    def added(parts, rows):
        total = parts[0, rows, :].astype(f32)
        for source in range(1, groups):
            total += parts[source, rows, :].astype(f32)
        return total

    activations[...] = mid[...] + added(mixes, slice(None))
    second_back(
        lambda rows: added(grad_normed, rows),
        cotangent,
        gain,
        bias,
        mid,
        w_proj,
        router,
        logit_grads(probs, grad_gates),
        grad_norm,
        grad_router,
        (grad_mid, grad_low, grad_mixed),
    )
    first_norm(image, gain, bias, normed_first)
    grad_shared[:, 3 * D :] = dot_lt(mixed[...], grad_low[...]).astype(bf16)
    attend_back(
        packed,
        grad_mixed,
        logs,
        grad_packed,
        grad_keys,
        grad_values,
        lambda pair, index: None,
        lambda pair, columns: None,
    )
    first_back(
        image,
        gain,
        lambda part: w_qkv[:, part * D : (part + 1) * D],
        grad_packed,
        grad_mid,
        grad_image,
        grad_norm,
    )
    grad_shared[:, : 3 * D] = dot_lt(normed_first[...], grad_packed[...]).astype(bf16)


def backward_part(*operands):
    router = operands[7]
    return pl.pallas_call(
        backward_kernel,
        out_shape=(
            shape(SEQ, D),
            shape(SEQ, D),
            shape(4, D),
            shape(router.shape[0], D),
            shape(D, 4 * D, dtype=bf16),
        ),
        in_specs=[VMEM] * 15,
        out_specs=[VMEM] * 5,
        scratch_shapes=backward_scratch(),
        compiler_params=params(),
    )(*operands)


def backward_sending_kernel(outers, groups, *refs):
    whole, (gain, bias, router, logs, grad_gates, probs) = refs[:9], refs[9:15]
    mixes_all, late_in, late_out = refs[15:18]
    activations, grad_image, grad_gain, grad_bias, grad_router, shard_qkv, shard_proj = refs[18:25]
    shard_in, shard_out = refs[25:27]
    grad_mid, grad_low, grad_mixed, grad_packed, grad_keys, grad_values, normed_first = refs[27:34]
    norm_sums, router_sums, shared, mixes, land, back_sent, back_landed = refs[34:41]
    own_shared, shared_land, shared_sent, shared_landed = refs[41:45]
    here, here_sem = refs[45:54], refs[54]
    parts_in, parts_out, image, cotangent, mid, quarters, packed, mixed, grad_rows = here
    refs = refs[55:]
    late_grads = sorted({unit[:2] for unit in SCATTER_LATE})
    mix_sem, grad_sem, grad_refs = refs[0], refs[1], refs[2 : 2 + len(late_grads)]
    refs = refs[2 + len(late_grads) :]
    inputs = [
        pltpu.make_async_copy(source, target, here_sem.at[index])
        for index, (source, target) in enumerate(zip(whole, here))
    ]
    place = Place(outers)
    size, pieces = 2 * outers, HEADS // 2 + 1
    shards = (shard_in, shard_out)
    loads = [
        pltpu.make_async_copy(
            (late_in, late_out)[kind].at[expert - EARLY_EXPERTS],
            grad_refs[index],
            grad_sem.at[index],
        )
        for index, (expert, kind) in enumerate(late_grads)
    ]
    mix_load = pltpu.make_async_copy(mixes_all, mixes, mix_sem)
    for copy in (*inputs[:2], *loads, *inputs[2:], mix_load):
        copy.start()
    place.greet_all(groups)
    at = 6 * len(SCATTER_LATE)
    late = make_scatters(
        place,
        [
            blocks_of(
                place, grad_refs[late_grads.index(unit[:2])], shards[unit[1]].shape[1], unit[2:]
            )
            for unit in SCATTER_LATE
        ],
        refs[:at],
    )
    split_blocks = []
    for index, (_, kind) in enumerate(SCATTER_SPLIT):
        number = [other[1] for other in SCATTER_SPLIT[:index]].count(kind)
        split_blocks.append(
            (
                lambda outer, parts=(parts_in, parts_out)[kind], number=number: parts.at[
                    number, outer
                ],
                None,
            )
        )
    split = make_scatters(place, split_blocks, refs[at:], side=False)
    at += 3 * len(SCATTER_SPLIT)
    deal = Deal(place, own_shared, shard_proj.shape[0], *refs[at : at + 3])
    at += 3
    norms = Spread("dp", place, size, *refs[at : at + 3])
    norms_task = Spread("task", place, groups, *refs[at + 3 : at + 6])
    routers = Spread("dp", place, size, *refs[at + 6 : at + 9])
    quarter = Spread("task", place, groups, *refs[at + 9 : at + 12])
    stores = []
    for unit in SCATTER_SPLIT + SCATTER_LATE:
        number = kinds(SCATTER_SPLIT + SCATTER_LATE, unit[1]).index(unit[0])

        def store(rows, shard=shards[unit[1]], number=number, half=unit[2:]):
            start = half[0] * rows.shape[0] if half else 0
            shard[number, start : start + rows.shape[0], :] = rows

        stores.append(store)
    for copy in inputs[:2]:
        copy.wait()
    for one in split:
        one.hop(0)
    for index, one in enumerate(late):
        unit = SCATTER_LATE[index]
        if unit[2:] in ((), (0,)):
            loads[late_grads.index(unit[:2])].wait()
        one.start()
    mix_load.wait()
    roles = (place.core, place.far, place.across, place.task)
    back = Return(
        place, [mixes.at[role] for role in roles], 1, land, back_sent, back_landed
    )
    back.by_core(0)
    back.to_core(0)
    for copy in inputs[2:]:
        copy.wait()
    second_back(
        lambda rows: grad_rows[rows, :],
        cotangent,
        gain,
        bias,
        mid,
        quarters.at[3],
        router,
        logit_grads(probs, grad_gates),
        norm_sums,
        router_sums,
        (grad_mid, grad_low, grad_mixed),
    )
    back.to_across(0)
    first_norm(image, gain, bias, normed_first)
    shared[pieces - 1] = dot_lt(mixed[...], grad_low[...]).astype(bf16)
    routers.give(router_sums[...])
    blocks = SEQ // QUERY_BWD
    units, keeps = split + late, stores
    names = dict(zip("stuvwxyz", range(len(units))))
    joined = Return(
        place,
        [shared.at[role] for role in roles],
        1,
        shared_land,
        shared_sent,
        shared_landed,
    )

    def run(acts):
        for act in acts:
            unit, hop = names[act[0]], int(act[1])
            if hop < outers - 1:
                units[unit].hop(hop)
            else:
                units[unit].finish(keeps[unit])

    def between(pair, index):
        for at, acts in BACKWARD_POINTS.items():
            if at // blocks == pair:
                pl.when(index == at % blocks)(lambda acts=acts: run(acts))

    def done(pair, columns):
        both = jnp.concatenate([grad_packed[:, part] for part in columns], axis=1)
        shared[pair] = dot_lt(normed_first[...], both).astype(bf16)

    attend_back(
        packed, grad_mixed, logs, grad_packed, grad_keys, grad_values, between, done
    )
    joined.by_core(0)
    joined.to_core(0)
    first_back(
        image,
        gain,
        lambda part: quarters[part],
        grad_packed,
        grad_mid,
        grad_image,
        norm_sums,
    )
    norms.give(norm_sums[...])
    joined.to_across(0)
    activations[...] = mid[...] + back.finish(0)
    run(BACKWARD_THEN[0])
    own_shared[...] = joined.finish(0).astype(bf16)
    deal.start()
    grad_router[...] = routers.take()
    norms_task.give(norms.take())
    run(BACKWARD_THEN[1])
    quarter.give(deal.total())
    run(BACKWARD_THEN[2])
    rows = norms_task.take()
    grad_gain[...] = rows[:2]
    grad_bias[...] = rows[2:4]
    quarter.arrive()
    shard_proj[...] = quarter.land[pieces - 1]
    for piece in range(pieces - 1):
        for part in range(3):
            column = part * D + piece * PAIR
            shard_qkv[:, column : column + PAIR] = quarter.land[
                piece, :, part * PAIR : (part + 1) * PAIR
            ]
    run(BACKWARD_THEN[3])


def backward_sending(*operands):
    router, whole = operands[11], operands[:9]
    experts, size = router.shape[0], lax.axis_size("dp")
    outers, thin, wide, pieces = size // 2, D // size, FF // size, HEADS // 2 + 1
    groups = lax.axis_size("task")
    tiles, wholes = ((thin, FF), (wide, D)), ((D, FF), (FF, D))
    ends = SCATTER_SPLIT + SCATTER_LATE
    late_grads = sorted({unit[:2] for unit in SCATTER_LATE})

    def spread(peers, *dims):
        return [pltpu.VMEM((peers, *dims), f32)] + [pltpu.SemaphoreType.DMA((peers - 1,))] * 2

    return pl.pallas_call(
        functools.partial(backward_sending_kernel, outers, groups),
        out_shape=(
            shape(SEQ, D),
            shape(SEQ, D),
            shape(2, D),
            shape(2, D),
            shape(experts, D),
            shape(thin, 3 * D),
            shape(thin, D),
            *[shape(len(kinds(ends, kind)), *tiles[kind]) for kind in range(2)],
        ),
        in_specs=[ANY] * 9 + [VMEM] * 6 + [ANY] * 3,
        out_specs=[VMEM] * 9,
        scratch_shapes=backward_scratch()
        + [
            pltpu.VMEM((8, D), f32),
            pltpu.VMEM((experts, D), f32),
            pltpu.VMEM((pieces, D, D), bf16),
            pltpu.VMEM((groups, SEQ, D), bf16),
            pltpu.VMEM((3, SEQ, D), bf16),
            pltpu.SemaphoreType.DMA((3, 1)),
            pltpu.SemaphoreType.DMA((3, 1)),
            pltpu.VMEM((D, D), bf16),
            pltpu.VMEM((3, D, D), bf16),
            pltpu.SemaphoreType.DMA((3, 1)),
            pltpu.SemaphoreType.DMA((3, 1)),
            *[pltpu.VMEM(operand.shape, operand.dtype) for operand in whole],
            pltpu.SemaphoreType.DMA((len(whole),)),
            pltpu.SemaphoreType.DMA,
            pltpu.SemaphoreType.DMA((len(late_grads),)),
        ]
        + [pltpu.VMEM(wholes[kind], bf16) for _, kind in late_grads]
        + scatter_scratch(SCATTER_LATE, outers, tiles)
        + scatter_scratch(SCATTER_SPLIT, outers, tiles, side=False)
        + [
            pltpu.VMEM((size, thin, D), bf16),
            pltpu.SemaphoreType.DMA((size - 1,)),
            pltpu.SemaphoreType.DMA((size - 1,)),
        ]
        + spread(size, 8, D)
        + spread(groups, 8, D)
        + spread(size, experts, D)
        + spread(groups, thin, D),
        compiler_params=params(collective_id=2, has_side_effects=True),
    )(*operands)


def local(
    layer_input,
    cotangent,
    norm_gain,
    norm_bias,
    w_qkv,
    w_proj,
    router,
    w_in,
    w_out,
    choices,
    top_count,
):
    groups = lax.axis_size("task")
    local_count = w_in.shape[0]
    image = layer_input.reshape(SEQ, D)
    grad_rows = cotangent.reshape(SEQ, D)
    routes = choices.reshape(SEQ, TOPMAX).T
    router_rows = router[0].T

    def swap(array):
        return lax.all_to_all(array, "task", split_axis=0, concat_axis=0, tiled=True)

    sending = groups == 4 and lax.axis_size("dp") == 8 and local_count == 4
    if sending:
        (
            mid,
            packed,
            mixed,
            logs,
            probs,
            normed,
            cot_rows,
            slots,
            gates,
            quarters,
            full_in,
            full_out,
        ) = forward_sending(
            top_count,
            image,
            grad_rows,
            norm_gain,
            norm_bias,
            (w_qkv, w_proj, w_in, w_out),
            router_rows,
            routes,
        )
        (
            late_in,
            late_out,
            grad_gates,
            mixes,
            grad_normed,
            early_in,
            early_out,
            parts_in,
            parts_out,
            _,
            _,
        ) = expert_sending(normed, cot_rows, slots, gates, full_in, full_out, w_in, w_out)
        (
            activations,
            grad_image,
            grad_gain,
            grad_bias,
            grad_router,
            grad_qkv,
            grad_proj,
            grad_in,
            grad_out,
        ) = backward_sending(
            parts_in,
            parts_out,
            image,
            grad_rows,
            mid,
            quarters,
            packed,
            mixed,
            grad_normed,
            norm_gain,
            norm_bias,
            router_rows,
            logs,
            grad_gates,
            probs,
            mixes,
            late_in,
            late_out,
        )
        grad_in = jnp.concatenate([early_in, grad_in], axis=0)
        grad_out = jnp.concatenate([early_out, grad_out], axis=0)
    else:
        full_qkv, full_proj, full_in, full_out = (
            lax.all_gather(w_qkv, "dp", axis=0, tiled=True),
            lax.all_gather(w_proj, "dp", axis=0, tiled=True),
            lax.all_gather(w_in, "dp", axis=1, tiled=True),
            lax.all_gather(w_out, "dp", axis=1, tiled=True),
        )
        mid, packed, mixed, logs, normed, slots, gates, probs = forward_part(
            top_count,
            image,
            norm_gain,
            norm_bias,
            full_qkv,
            full_proj,
            router_rows,
            routes,
        )
        normed = lax.all_gather(normed, "task")
        cot_rows = lax.all_gather(grad_rows.astype(bf16), "task")
        slots = swap(slots.reshape(groups, local_count, SEQ))
        gates = swap(gates.reshape(groups, local_count, SEQ))
        tokens = jnp.concatenate([normed, cot_rows], axis=-1)
        grad_in, grad_out, grad_gates, mixes, grad_normed = expert_part(
            tokens, slots, gates, full_in, full_out
        )
        activations, grad_image, grad_norm, grad_router, grad_shared = backward_part(
            image,
            grad_rows,
            norm_gain,
            norm_bias,
            mid,
            full_qkv,
            full_proj,
            router_rows,
            packed,
            mixed,
            logs,
            swap(mixes),
            swap(grad_normed),
            swap(grad_gates),
            probs,
        )
        grad_in = lax.psum_scatter(grad_in, "dp", scatter_dimension=1, tiled=True).astype(f32)
        grad_out = lax.psum_scatter(grad_out, "dp", scatter_dimension=1, tiled=True).astype(f32)
        grad_shared = lax.psum_scatter(grad_shared, "dp", scatter_dimension=0, tiled=True)
        grad_shared = lax.psum(grad_shared, "task").astype(f32)
        grad_qkv, grad_proj = grad_shared[:, : 3 * D], grad_shared[:, 3 * D :]
        grad_router = lax.psum(grad_router, "dp")
        grad_norm = lax.psum(grad_norm, ("task", "dp"))
        grad_gain, grad_bias = grad_norm[:2], grad_norm[2:]
    return (
        activations.reshape(layer_input.shape),
        grad_image.reshape(layer_input.shape),
        grad_gain,
        grad_bias,
        grad_qkv,
        grad_proj,
        grad_router.T[None],
        grad_in,
        grad_out,
    )


def solution(mesh):
    tokens = P("task", "dp", None, None)
    rows = P("dp", None)
    blocks = P("task", "dp", None)
    routed = P("task", None, None)
    return jax.shard_map(
        local,
        mesh=mesh,
        in_specs=(tokens, tokens, P(), P(), rows, rows, routed, blocks, blocks, tokens, P("task")),
        out_specs=(tokens, tokens, P(), P(), rows, rows, routed, blocks, blocks),
        check_vma=False,
    )
```

```python
import functools

import jax
import jax.numpy as jnp
from jax import lax
from jax.experimental import pallas as pl
from jax.experimental.pallas import tpu as pltpu
from jax.sharding import PartitionSpec as P

D = 384
FF = 1536
HEADS = 6
HEAD_DIM = 64
PAIR = 2 * HEAD_DIM
TOPMAX = 4
SEQ = 1024
CAP = 320

f32 = jnp.float32
bf16 = jnp.bfloat16
HIGHEST = lax.Precision.HIGHEST
EPSILON = 1e-06
ROOT_HALF = 0.7071067811865476
NORMAL = 0.3989422804014327

FF_TILE = 512
ROW_TILE = 640
QUERY_FWD = 256
QUERY_BWD = 256
ROWS = 256
RETURNS = 2

GATHER_WHOLE = ((0, 0), (0, 1), (1, 0), (1, 1))
GATHER_SPLIT = ((2, 0), (2, 1))
GATHER_LATE = ((3, 0), (3, 1))
SCATTER_EARLY = ((0, 0), (0, 1), (1, 0))
SCATTER_SPLIT = ((1, 1), (2, 0))
SCATTER_LATE = ((2, 1), (3, 0), (3, 1, 0), (3, 1, 1))
EARLY_EXPERTS = 2

GATHER_POINTS = {2: ((0, 1), (0, 3), (1, 0), (1, 4)), 3: ((0, 2), (1, 1), (1, 4), (3, 0))}
SCATTER_POINTS = {1: (2, 4), 3: (3, 6)}

AHEAD, NEXT = 2, 4
FORWARD_FIRST = ((0, 1), (1, 1), (2, 1), (3, 1), (0, 2))
FORWARD_POINTS = {
    0: ((1, 2),),
    1: ((2, 2), (4, 0), (5, 0)),
    2: ((3, 2),),
    5: ((0, 3),),
    6: ((1, 3),),
    7: ((2, 3),),
    8: ((3, 3),),
    9: ((4, 1),),
    10: ((5, 1),),
}
FORWARD_THEN = (((4, 2), (5, 2)), ((4, 3), (5, 3)))

BACKWARD_POINTS = {
    3: ("s1", "u0",),
    8: ("t1", "s2", "v0",),
    11: ("u1",),
}
BACKWARD_THEN = (
    ("t2", "s3", "v1", "u2", "w0"),
    ("x0", "t3", "v2", "u3", "w1"),
    ("x1", "v3", "w2", "x2"),
    ("w3", "x3"),
)


VMEM = pl.BlockSpec(memory_space=pltpu.VMEM)
SMEM = pl.BlockSpec(memory_space=pltpu.SMEM)
ANY = pl.BlockSpec(memory_space=pl.ANY)


def shape(*dims, dtype=f32):
    return jax.ShapeDtypeStruct(dims, dtype)


def params(**more):
    return pltpu.CompilerParams(vmem_limit_bytes=63 * 2**20, **more)


def dot(a, b):
    return lax.dot_general(a, b, (((1,), (0,)), ((), ())), preferred_element_type=f32)


def dot_rt(a, b):
    return lax.dot_general(a, b, (((1,), (1,)), ((), ())), preferred_element_type=f32)


def dot_lt(a, b):
    return lax.dot_general(a, b, (((0,), (0,)), ((), ())), preferred_element_type=f32)


def rows_at(index, size):
    return pl.ds(pl.multiple_of(index * size, size), size)


def normalize(rows):
    centered = rows - jnp.mean(rows, axis=1, keepdims=True)
    scale = lax.rsqrt(jnp.mean(centered * centered, axis=1, keepdims=True) + EPSILON)
    return centered * scale, scale


def norm_back(rows, grad_rows, gain):
    unit, scale = normalize(rows)
    scaled = grad_rows * gain
    grad_in = scale * (
        scaled
        - jnp.mean(scaled, axis=1, keepdims=True)
        - unit * jnp.mean(scaled * unit, axis=1, keepdims=True)
    )
    grad_gain = jnp.sum(grad_rows * unit, axis=0, keepdims=True)
    return grad_in, grad_gain, jnp.sum(grad_rows, axis=0, keepdims=True), unit


def half_lanes(rows, half):
    lanes = lax.broadcasted_iota(jnp.int32, (rows, PAIR), 1)
    return (lanes < HEAD_DIM) if half == 0 else (lanes >= HEAD_DIM)


def remote(source, target, sent, landed, **device):
    return pltpu.make_async_remote_copy(
        src_ref=source,
        dst_ref=target,
        send_sem=sent,
        recv_sem=landed,
        device_id=device,
        device_id_type=pl.DeviceIdType.MESH,
    )


class Place:
    def __init__(self, outers):
        self.dp = lax.axis_index("dp")
        self.task = lax.axis_index("task")
        self.outers = outers
        self.outer, self.inner = self.dp // 2, self.dp % 2
        self.has_up, self.has_down = self.outer + 1 < outers, self.outer > 0
        self.up, self.down = self.dp + 2, self.dp - 2
        self.side = self.dp + 1 - 2 * self.inner
        self.core = self.task + 1 - 2 * (self.task % 2)
        self.across = self.task + 2 - 4 * (self.task // 2)
        self.far = self.across + 1 - 2 * (self.task % 2)

    def signal(self, **device):
        pl.semaphore_signal(
            pltpu.get_barrier_semaphore(),
            inc=1,
            device_id=device,
            device_id_type=pl.DeviceIdType.MESH,
        )

    def greet(self, far=False):
        pl.when(self.has_up)(lambda: self.signal(dp=self.up))
        pl.when(self.has_down)(lambda: self.signal(dp=self.down))
        self.signal(dp=self.side)
        self.signal(task=self.core)
        self.signal(task=self.across)
        if far:
            self.signal(task=self.far)
        others = 3 + int(far) + self.has_up.astype(jnp.int32) + self.has_down.astype(jnp.int32)
        pl.semaphore_wait(pltpu.get_barrier_semaphore(), others)

    def greet_all(self, groups):
        size = 2 * self.outers
        for ahead in range(1, size):
            self.signal(dp=lax.rem(self.dp + ahead, size))
        for ahead in range(1, groups):
            self.signal(task=lax.rem(self.task + ahead, groups))
        pl.semaphore_wait(pltpu.get_barrier_semaphore(), size + groups - 2)


class Gather:
    def __init__(self, place, shards, sent, landed, stay):
        self.place, self.shards = place, shards
        self.sent, self.landed, self.stay = sent, landed, stay

    def move(self, unit, source, way, device, first=None):
        _, size, full, _ = self.shards[unit]
        target = full.at[rows_at(source, size)]
        return remote(
            target if first is None else first,
            target,
            self.sent.at[unit, source, way],
            self.landed.at[unit, source],
            dp=device,
        )

    def local(self, unit):
        own, size, full, _ = self.shards[unit]
        target = full.at[rows_at(self.place.dp, size)]
        return pltpu.make_async_copy(own, target, self.stay.at[unit])

    def along(self, unit, source, up, down):
        place = self.place
        if up:
            pl.when(place.has_up)(lambda: self.move(unit, source, 0, place.up).start())
        if down:
            pl.when(place.has_down)(lambda: self.move(unit, source, 1, place.down).start())

    def to_side(self, unit, outer):
        own, size = self.shards[unit][:2]
        source = 2 * outer + self.place.inner
        return self.move(unit, source, 2, self.place.side, own.at[rows_at(source, size)])

    def start(self, unit):
        place = self.place
        own, mode = self.shards[unit][0], self.shards[unit][3]
        if mode == "side":
            for outer in range(place.outers):
                self.to_side(unit, outer).start()
            return
        if mode == "turned":
            self.move(unit, place.dp, 2, place.side, own).start()
        pl.when(place.has_up)(lambda: self.move(unit, place.dp, 0, place.up, own).start())
        pl.when(place.has_down)(lambda: self.move(unit, place.dp, 1, place.down, own).start())
        if mode == "both":
            self.move(unit, place.dp, 2, place.side, own).start()
        if self.stay is not None:
            self.local(unit).start()

    def step(self, unit, hop):
        place, mode = self.place, self.shards[unit][3]
        if hop == 0:
            self.move(unit, place.side, 0, place.dp).wait_recv()
            self.along(unit, place.side, True, True)
            return
        for column in (place.dp, place.side) if mode == "turned" else (place.dp,):

            @pl.when(place.outer >= hop)
            def _():
                self.move(unit, column - 2 * hop, 0, place.dp).wait_recv()
                self.along(unit, column - 2 * hop, True, False)
                if mode == "both":
                    self.move(unit, column - 2 * hop, 2, place.side).start()

            @pl.when(place.outer + hop < place.outers)
            def _():
                self.move(unit, column + 2 * hop, 1, place.dp).wait_recv()
                self.along(unit, column + 2 * hop, False, True)
                if mode == "both":
                    self.move(unit, column + 2 * hop, 2, place.side).start()

    def finish(self, unit):
        place, mode = self.place, self.shards[unit][3]
        if self.stay is not None:
            self.local(unit).wait()
        if mode == "turned":
            self.move(unit, place.dp, 2, place.side).wait_send()
        for outer in range(place.outers):
            own, other = 2 * outer + place.inner, 2 * outer + 1 - place.inner
            if mode in ("both", "side"):
                self.move(unit, other, 2, place.dp).wait_recv()
                self.move(unit, own, 2, place.side).wait_send()
            if mode == "side":
                continue
            for source in (own, other) if mode == "turned" else (own,):
                pl.when((outer <= place.outer) & place.has_up)(
                    lambda source=source: self.move(unit, source, 0, place.up).wait_send()
                )
                pl.when((outer >= place.outer) & place.has_down)(
                    lambda source=source: self.move(unit, source, 1, place.down).wait_send()
                )


def gather_semaphores(units, size):
    return [
        pltpu.SemaphoreType.DMA((units, size, 3)),
        pltpu.SemaphoreType.DMA((units, size)),
    ]


class Share:
    def __init__(self, place, view, sent, landed):
        self.place, self.view, self.sent, self.landed = place, view, sent, landed

    def move(self, source, way, **device):
        return remote(
            self.view(source),
            self.view(source),
            self.sent.at[way],
            self.landed.at[way],
            **device,
        )

    def start(self):
        place = self.place
        self.move(place.task, 0, task=place.across).start()
        self.move(place.task, 1, task=place.core).start()

    def relay(self):
        place = self.place
        self.move(place.across, 0, task=place.across).wait_recv()
        self.move(place.across, 2, task=place.core).start()

    def finish(self):
        place = self.place
        self.move(place.task, 0, task=place.across).wait_send()
        self.move(place.core, 1, task=place.core).wait()
        self.move(place.across, 2, task=place.core).wait()


class Scatter:
    def __init__(self, place, mine, theirs, side, line, sems):
        self.place, self.mine, self.theirs = place, mine, theirs
        self.side, self.line = side, line
        self.side_sent, self.side_landed, self.line_sent, self.line_landed = sems

    def to_side(self, outer):
        return remote(
            self.theirs(outer),
            self.side.at[outer],
            self.side_sent.at[outer],
            self.side_landed.at[outer],
            dp=self.place.side,
        )

    def fold(self, outer):
        return self.mine(outer) if self.side is None else self.side.at[outer]

    def along(self, outer, slot, device):
        return remote(
            self.fold(outer),
            self.line.at[slot],
            self.line_sent.at[outer],
            self.line_landed.at[slot],
            dp=device,
        )

    def start(self):
        outers = self.place.outers
        for near in range(outers // 2):
            self.to_side(outers - 1 - near).start()
            self.to_side(near).start()

    def total(self, outer, *slots):
        rows = self.mine(outer)[...].astype(f32)
        if self.side is not None:
            self.to_side(outer).wait_recv()
            rows += self.side[outer].astype(f32)
        for slot in slots:
            self.along(outer, slot, self.place.dp).wait_recv()
            rows += self.line[slot].astype(f32)
        return rows

    def settle(self, parts, sem):
        for outer in range(self.place.outers):
            self.fold(outer)[...] = self.total(outer).astype(bf16)
            self.to_side(outer).wait_send()
        copy = pltpu.make_async_copy(self.side, parts, sem)
        copy.start()
        return copy

    def hop(self, step):
        place, outers = self.place, self.place.outers

        @pl.when(place.outer == step)
        def _():
            for outer in range(outers - 1, step, -1):
                rows = self.total(outer, *([outer] if step else []))
                self.fold(outer)[...] = rows.astype(bf16)
                self.along(outer, outer, place.up).start()

        @pl.when(place.outer == outers - 1 - step)
        def _():
            for outer in range(outers - 1 - step):
                rows = self.total(outer, *([outer] if step else []))
                self.fold(outer)[...] = rows.astype(bf16)
                slot = outers if outer == outers - 2 - step else outer
                self.along(outer, slot, place.down).start()

    def finish(self, store):
        place, outers = self.place, self.place.outers
        for outer in range(outers):

            @pl.when(place.outer == outer)
            def _():
                below, above = [outer] * (outer > 0), [outers] * (outer < outers - 1)
                store(self.total(outer, *below, *above))
                for other in range(outers):
                    if other != outer:
                        self.along(other, other, place.dp).wait_send()

            if self.side is not None:
                self.to_side(outer).wait_send()


class Turned:
    def __init__(self, place, mine, theirs, refs):
        self.place = place
        self.own = Scatter(place, mine, None, None, refs[0], (None, None, *refs[1:3]))
        self.other = Scatter(place, theirs, None, None, refs[3], (None, None, *refs[4:6]))
        self.stage, self.land, self.sent, self.landed = refs[6:]

    def move(self):
        return remote(self.stage, self.land, self.sent, self.landed, dp=self.place.side)

    def start(self):
        self.own.hop(0)
        self.other.hop(0)

    def hop(self, step):
        if step:
            self.own.hop(step)
            self.other.hop(step)

    def finish(self, store):
        def send(rows):
            self.stage[...] = rows.astype(bf16)
            self.move().start()

        self.other.finish(send)
        self.own.finish(store)

    def add(self, shard):
        self.move().wait()
        shard[...] += self.land[...].astype(f32)


def turned_scratch(outers, tile):
    line = [pltpu.VMEM((outers + 1, *tile), bf16)]
    line += [pltpu.SemaphoreType.DMA((count,)) for count in (outers, outers + 1)]
    return line * 2 + [pltpu.VMEM(tile, bf16)] * 2 + [pltpu.SemaphoreType.DMA] * 2


def scatter_turn(units, stores, turn):
    outers = units[0].place.outers
    for step in range(outers - 1):
        if 0 <= turn - step < len(units):
            units[turn - step].hop(step)
    last = turn - outers + 1
    if 0 <= last < len(units):
        units[last].finish(stores[last])


def blocks_of(place, ref, size, half=()):
    def block(index):
        if half:
            return ref.at[rows_at(2 * index + half[0], size // 2)]
        return ref.at[rows_at(index, size)]

    return (
        lambda outer: block(2 * outer + place.inner),
        lambda outer: block(2 * outer + 1 - place.inner),
    )


def scatter_scratch(units, outers, tiles, side=True, line=True):
    scratch = []
    for unit in units:
        tile = tiles[unit[1]] if isinstance(unit, tuple) else tiles
        if isinstance(unit, tuple) and len(unit) > 2:
            tile = (tile[0] // 2, tile[1])
        for asked, slots in ((side, outers), (line, outers + 1)):
            if asked:
                scratch.append(pltpu.VMEM((slots, *tile), bf16))
        for asked, count in ((side, outers), (side, outers), (line, outers), (line, outers + 1)):
            if asked:
                scratch.append(pltpu.SemaphoreType.DMA((count,)))
    return scratch


def make_scatters(place, blocks, refs, side=True, line=True):
    count = 3 * side + 3 * line
    scatters = []
    for index, (mine, theirs) in enumerate(blocks):
        own = list(refs[index * count : (index + 1) * count])
        buffers = [own.pop(0) if asked else None for asked in (side, line)]
        sems = [own.pop(0) if asked else None for asked in (side, side, line, line)]
        scatters.append(Scatter(place, mine, theirs, *buffers, sems))
    return scatters


class Spread:
    def __init__(self, axis, place, count, land, sent, landed):
        self.axis, self.me, self.count = axis, getattr(place, axis), count
        self.land, self.sent, self.landed = land, sent, landed

    def move(self, source, ahead):
        return remote(
            self.land.at[source],
            self.land.at[source],
            self.sent.at[ahead - 1],
            self.landed.at[ahead - 1],
            **{self.axis: lax.rem(self.me + ahead, self.count)},
        )

    def give(self, rows):
        self.land[self.me] = rows.astype(self.land.dtype)
        for ahead in range(1, self.count):
            self.move(self.me, ahead).start()

    def arrive(self):
        for ahead in range(1, self.count):
            self.move(lax.rem(self.me + self.count - ahead, self.count), ahead).wait_recv()
            self.move(self.me, ahead).wait_send()

    def take(self):
        self.arrive()
        total = self.land[0].astype(f32)
        for index in range(1, self.count):
            total += self.land[index].astype(f32)
        return total


class Deal:
    def __init__(self, place, ref, size, land, sent, landed):
        self.place, self.ref, self.size = place, ref, size
        self.land, self.sent, self.landed = land, sent, landed
        self.count = land.shape[0]

    def block(self, index):
        return self.ref.at[rows_at(index, self.size)]

    def move(self, ahead):
        target = lax.rem(self.place.dp + ahead, self.count)
        return remote(
            self.block(target),
            self.land.at[self.place.dp],
            self.sent.at[ahead - 1],
            self.landed.at[ahead - 1],
            dp=target,
        )

    def start(self):
        for ahead in range(1, self.count):
            self.move(ahead).start()

    def total(self):
        rows = self.block(self.place.dp)[...].astype(f32)
        for ahead in range(1, self.count):
            self.move(ahead).wait()
            source = lax.rem(self.place.dp + self.count - ahead, self.count)
            rows += self.land[source].astype(f32)
        return rows


class Return:
    def __init__(self, place, parts, pieces, land, sent, landed):
        self.place, self.parts, self.pieces = place, parts, pieces
        self.land, self.sent, self.landed = land, sent, landed
        self.size = land.shape[1] // pieces

    def rows(self, piece):
        return pl.ds(piece * self.size, self.size)

    def move(self, way, piece):
        place, rows = self.place, self.rows(piece)
        source = [
            self.parts[0].at[rows],
            self.parts[1].at[rows],
            self.parts[2].at[rows],
        ][way]
        return remote(
            source,
            self.land.at[way, rows],
            self.sent.at[way, piece],
            self.landed.at[way, piece],
            task=place.across if way == 2 else place.core,
        )

    def to_core(self, piece):
        self.move(0, piece).start()

    def by_core(self, piece):
        self.move(1, piece).start()

    def to_across(self, piece):
        rows = self.rows(piece)
        self.move(1, piece).wait_recv()
        joint = self.parts[2][rows, :].astype(f32)
        joint += self.land[1, rows, :].astype(f32)
        self.parts[2][rows, :] = joint.astype(bf16)
        self.move(2, piece).start()

    def finish(self, piece):
        rows = self.rows(piece)
        self.move(0, piece).wait()
        self.move(1, piece).wait_send()
        self.move(2, piece).wait()
        total = self.parts[3][rows, :].astype(f32)
        return total + self.land[0, rows, :].astype(f32) + self.land[2, rows, :].astype(f32)


def attend(packed, mixed, totals, index, between):
    zero = jnp.array(0, bf16)
    rows = rows_at(index, QUERY_FWD)

    def head_pair(pair, _):
        queries, keys, values = (rows_at(pair + part * (D // PAIR), PAIR) for part in range(3))
        key_rows, value_rows = packed[:, keys], packed[:, values]
        query_rows = packed[rows, queries] * jnp.array(HEAD_DIM**-0.5, bf16)
        outs, logs = [], []
        for half in range(2):
            own = jnp.where(half_lanes(QUERY_FWD, half), query_rows, zero)
            scores = dot_rt(own, key_rows)
            top = jnp.max(scores, axis=1, keepdims=True)
            weights = jnp.exp(scores - top)
            total = jnp.sum(weights, axis=1, keepdims=True)
            outs.append(dot(weights.astype(bf16), value_rows) * (1.0 / total))
            logs.append(top + jnp.log(total))
        mixed[rows, queries] = jnp.where(half_lanes(QUERY_FWD, 0), outs[0], outs[1]).astype(bf16)
        lanes = lax.broadcasted_iota(jnp.int32, (QUERY_FWD, 8), 1)
        totals[rows, :] = jnp.where(
            lanes == 2 * pair,
            logs[0],
            jnp.where(lanes == 2 * pair + 1, logs[1], totals[rows, :]),
        )
        between(index * (HEADS // 2) + pair)
        return 0

    lax.fori_loop(0, HEADS // 2, head_pair, 0)


def first_norm(image, gain, bias, normed_first):
    def block(index, _):
        rows = rows_at(index, ROWS)
        unit, _ = normalize(image[rows, :])
        normed_first[rows, :] = (unit * gain[0:1, :] + bias[0:1, :]).astype(bf16)
        return 0

    lax.fori_loop(0, SEQ // ROWS, block, 0)


def number_slots(choices, top_count, experts):
    named = choices[...]
    numbers = lax.broadcasted_iota(jnp.int32, (experts, SEQ), 0)
    used = jnp.zeros((experts, SEQ), f32)
    for choice in range(TOPMAX):
        hit = (named[choice : choice + 1, :] == numbers) & (choice < top_count[0])
        used = used + jnp.where(hit, 1.0, 0.0)
    earlier = lax.broadcasted_iota(jnp.int32, (SEQ, SEQ), 0) < lax.broadcasted_iota(
        jnp.int32, (SEQ, SEQ), 1
    )
    before = dot(used.astype(bf16), jnp.where(earlier, 1.0, 0.0).astype(bf16))
    return jnp.where(used > 0, before, -1.0).astype(jnp.int32)


def mid_block(index, image, gain, bias, w_proj, router, mixed, mid, probs):
    rows = rows_at(index, QUERY_FWD)
    mid_rows = image[rows, :] + dot(mixed[rows, :], w_proj[...])
    mid[rows, :] = mid_rows
    unit, _ = normalize(mid_rows)
    normed_rows = unit * gain[1:2, :] + bias[1:2, :]
    logits = lax.dot_general(
        router[...],
        normed_rows,
        (((1,), (1,)), ((), ())),
        precision=HIGHEST,
        preferred_element_type=f32,
    )
    powers = jnp.exp(logits - jnp.max(logits, axis=0, keepdims=True))
    probs[:, rows] = powers / jnp.sum(powers, axis=0, keepdims=True)
    return normed_rows.astype(bf16)


def forward_kernel(
    top_count,
    image,
    gain,
    bias,
    w_qkv,
    w_proj,
    router,
    choices,
    mid,
    packed,
    mixed,
    logs,
    normed,
    slots,
    gates,
    probs,
    normed_first,
    totals,
):
    first_norm(image, gain, bias, normed_first)
    slots[...] = number_slots(choices, top_count, router.shape[0])
    packed[...] = dot(normed_first[...], w_qkv[...]).astype(bf16)
    totals[...] = jnp.zeros_like(totals)

    def block(index, _):
        attend(packed, mixed, totals, index, lambda point: None)
        normed[rows_at(index, QUERY_FWD), :] = mid_block(
            index, image, gain, bias, w_proj, router, mixed, mid, probs
        )
        return 0

    lax.fori_loop(0, SEQ // QUERY_FWD, block, 0)
    logs[...] = totals[...].T
    gates[...] = jnp.where(slots[...] >= 0, probs[...], 0.0)


def forward_part(top_count, image, gain, bias, w_qkv, w_proj, router, choices):
    experts = router.shape[0]
    return pl.pallas_call(
        forward_kernel,
        out_shape=(
            shape(SEQ, D),
            shape(SEQ, 3 * D, dtype=bf16),
            shape(SEQ, D, dtype=bf16),
            shape(8, SEQ),
            shape(SEQ, D, dtype=bf16),
            shape(experts, SEQ, dtype=jnp.int32),
            shape(experts, SEQ),
            shape(experts, SEQ),
        ),
        in_specs=[SMEM] + [VMEM] * 7,
        out_specs=[VMEM] * 8,
        scratch_shapes=[pltpu.VMEM((SEQ, D), bf16), pltpu.VMEM((SEQ, 8), f32)],
        compiler_params=params(),
    )(top_count, image, gain, bias, w_qkv, w_proj, router, choices)


def forward_sending_kernel(
    outers,
    top_count,
    image,
    cotangent,
    gain,
    bias,
    w_qkv,
    w_proj,
    w_in,
    w_out,
    router,
    choices,
    mid,
    packed,
    mixed,
    logs,
    probs,
    normed_all,
    cot_all,
    slots_all,
    gates_all,
    quarters,
    full_in,
    full_out,
    normed_first,
    totals,
    own_quarter,
    sent,
    landed,
    stay,
    share_sent,
    share_landed,
):
    place = Place(outers)
    task = place.task
    for part in range(4):

        @pl.when(task == part)
        def _():
            own_quarter[...] = w_proj[...] if part == 3 else w_qkv[:, part * D : (part + 1) * D]

    shards = [(own_quarter, w_qkv.shape[0], quarters.at[task], "both")]
    for expert, kind in GATHER_WHOLE + GATHER_SPLIT:
        own, full = ((w_in, full_in), (w_out, full_out))[kind]
        mode = "line" if (expert, kind) in GATHER_SPLIT else "both"
        shards.append((own.at[expert], own.shape[1], full.at[expert], mode))
    gather = Gather(place, shards, sent, landed, stay)
    routed = range(1, len(shards))
    cot_all[task] = cotangent[...].astype(bf16)
    place.greet()
    gather.start(0)

    def share(index, view):
        return Share(place, view, share_sent.at[index], share_landed.at[index])

    cot = share(0, lambda source: cot_all.at[source])
    slot = share(1, lambda source: slots_all.at[source])
    gate = share(2, lambda source: gates_all.at[source])
    def run(acts):
        for unit, hop in acts:
            if hop:
                gather.step(routed[unit], hop)
            else:
                gather.start(routed[unit])

    for unit in routed[:AHEAD]:
        gather.start(unit)
    cot.start()
    first_norm(image, gain, bias, normed_first)
    for hop in range(1, outers):
        gather.step(0, hop)
    for unit in routed[AHEAD:NEXT]:
        gather.start(unit)
    gather.finish(0)
    quarter = share(3 + SEQ // QUERY_FWD, lambda source: quarters.at[source])
    quarter.start()
    slots_all[task] = number_slots(choices, top_count, router.shape[0])
    slot.start()
    totals[...] = jnp.zeros_like(totals)
    run(FORWARD_FIRST)
    quarter.relay()
    quarter.finish()
    for part in range(3):
        packed[:, part * D : (part + 1) * D] = dot(normed_first[...], quarters[part]).astype(bf16)
    cot.relay()
    slot.relay()

    def chunk(index):
        return share(3 + index, lambda source: normed_all.at[source, rows_at(index, QUERY_FWD)])

    blocks = SEQ // QUERY_FWD

    def block(index, _):
        def between(point):
            for at, acts in FORWARD_POINTS.items():
                pl.when(point == at)(lambda acts=acts: run(acts))

        attend(packed, mixed, totals, index, between)
        normed_all[task, rows_at(index, QUERY_FWD), :] = mid_block(
            index, image, gain, bias, quarters.at[3], router, mixed, mid, probs
        )
        chunk(index).start()
        pl.when(index > 0)(lambda: chunk(index - 1).relay())
        return 0

    lax.fori_loop(0, blocks, block, 0)
    gates_all[task] = jnp.where(slots_all[task] >= 0, probs[...], 0.0)
    gate.start()
    logs[...] = totals[...].T
    run(FORWARD_THEN[0])
    chunk(blocks - 1).relay()
    gate.relay()
    run(FORWARD_THEN[1])
    for one in [cot, slot, gate] + [chunk(index) for index in range(blocks)]:
        one.finish()
    for unit in routed:
        gather.finish(unit)


def forward_sending(top_count, image, cotangent, gain, bias, shards, router, choices):
    w_qkv, w_proj, w_in, w_out = shards
    experts, size = router.shape[0], lax.axis_size("dp")
    groups, early = lax.axis_size("task"), 1 + GATHER_SPLIT[-1][0]
    units, shares = 1 + len(GATHER_WHOLE + GATHER_SPLIT), 4 + SEQ // QUERY_FWD
    return pl.pallas_call(
        functools.partial(forward_sending_kernel, size // 2),
        out_shape=(
            shape(SEQ, D),
            shape(SEQ, 3 * D, dtype=bf16),
            shape(SEQ, D, dtype=bf16),
            shape(8, SEQ),
            shape(experts, SEQ),
            shape(groups, SEQ, D, dtype=bf16),
            shape(groups, SEQ, D, dtype=bf16),
            shape(groups, experts, SEQ, dtype=jnp.int32),
            shape(groups, experts, SEQ),
            shape(groups, D, D, dtype=bf16),
            shape(early, D, FF, dtype=bf16),
            shape(early, FF, D, dtype=bf16),
        ),
        in_specs=[SMEM] + [VMEM] * 10,
        out_specs=[VMEM] * 10 + [ANY] * 2,
        scratch_shapes=[
            pltpu.VMEM((SEQ, D), bf16),
            pltpu.VMEM((SEQ, 8), f32),
            pltpu.VMEM(w_proj.shape, bf16),
            *gather_semaphores(units, size),
            pltpu.SemaphoreType.DMA((units,)),
            pltpu.SemaphoreType.DMA((shares, 3)),
            pltpu.SemaphoreType.DMA((shares, 3)),
        ],
        compiler_params=params(collective_id=0, has_side_effects=True),
    )(top_count, image, cotangent, gain, bias, w_qkv, w_proj, w_in, w_out, router, choices)


def slot_hits(slots, source, expert):
    return lax.broadcasted_iota(jnp.int32, (CAP, SEQ), 0) == slots[source, pl.ds(expert, 1), :]


def ones_at(hits):
    return jnp.where(hits, 1.0, 0.0).astype(bf16)


def dispatch(operands, work, expert, first, block, source):
    tokens, slots, gates = operands[:3]
    rows_in, rows_grad, rows_cot, rows_gate = work[:4]
    own = slice(block * CAP, (block + 1) * CAP)
    hits = slot_hits(slots, source, first + expert)
    both = dot(ones_at(hits), tokens[source])
    gate = jnp.sum(
        jnp.where(hits, gates[source, pl.ds(first + expert, 1), :], 0.0), axis=1, keepdims=True
    )
    rows_in[own, :] = both[:, :D].astype(bf16)
    rows_cot[own, :] = both[:, D:].astype(bf16)
    rows_grad[own, :] = (gate * both[:, D:]).astype(bf16)
    rows_gate[own, :] = jnp.broadcast_to(gate, (CAP, 128))


def hidden_tiles(operands, work, slot, start, count):
    w_in, w_out = operands[3:]
    rows_in, rows_grad, _, _, hidden, grad_pre, _ = work

    def tile(index, _):
        units = rows_at(index // count, FF_TILE)
        rows = rows_at(start + lax.rem(index, count), ROW_TILE)
        pre = dot(rows_in[rows, :], w_in[slot, :, units])
        grad_hidden = dot_rt(rows_grad[rows, :], w_out[slot, units, :])
        share = 0.5 * lax.erf(pre * ROOT_HALF) + 0.5
        slope = share + pre * (NORMAL * jnp.exp(-0.5 * pre * pre))
        hidden[rows, units] = (pre * share).astype(bf16)
        grad_pre[rows, units] = (grad_hidden * slope).astype(bf16)
        return 0

    lax.fori_loop(0, (FF // FF_TILE) * count, tile, 0)


def expert_rows_out(operands, work, grad_gates, expert, first, slot, block, source):
    slots, (w_in, w_out) = operands[1], operands[3:]
    _, _, rows_cot, rows_gate, hidden, grad_pre, sent = work
    own = slice(block * CAP, (block + 1) * CAP)
    kept = rows_at(expert, CAP)
    out_rows = dot(hidden[own, :], w_out[slot]).astype(bf16).astype(f32)
    sent[source, kept, :D] = (rows_gate[own, 0:1] * out_rows).astype(bf16)
    sent[source, kept, D:] = dot_rt(grad_pre[own, :], w_in[slot]).astype(bf16)
    grad_gate = jnp.sum(rows_cot[own, :].astype(f32) * out_rows, axis=1, keepdims=True)
    hits = slot_hits(slots, source, first + expert)
    grad_gates[source, pl.ds(expert, 1), :] = jnp.sum(
        jnp.where(hits, grad_gate, 0.0), axis=0, keepdims=True
    )


def weight_grads(work, grads, expert):
    rows_in, rows_grad, _, _, hidden, grad_pre, _ = work
    grads[0][expert] = dot_lt(rows_in[...], grad_pre[...]).astype(bf16)
    grads[1][expert] = dot_lt(rows_grad[...], hidden[...]).astype(bf16).T


def one_expert(operands, work, grads, expert, first, slot, sources, between, halfway=None):
    halves = 1 if halfway is None else 2
    size, tiles = len(sources) // halves, len(sources) * CAP // ROW_TILE // halves
    between(0)
    for block, source in enumerate(sources):
        dispatch(operands, work, expert, first, block, source)
    between(1)
    for half in range(halves):
        hidden_tiles(operands, work, slot, half * tiles, tiles)
        between(2 + half * 2)
        for block in range(half * size, (half + 1) * size):
            expert_rows_out(
                operands, work, grads[2], expert, first, slot, block, sources[block]
            )
        if half + 1 < halves:
            halfway()
    between(3 if halves == 1 else 5)
    weight_grads(work, grads, expert)
    between(4 if halves == 1 else 6)


def combine(slots, first, local_count, sent, columns, source, store):
    size = SEQ // RETURNS
    columns[...] = slots[source].T
    for piece in range(RETURNS):
        rows = pl.ds(piece * size, size)
        lanes = lax.broadcasted_iota(jnp.int32, (size, CAP), 1)
        mine = lax.broadcasted_iota(jnp.int32, (size, columns.shape[1]), 1)
        picks = []
        for expert in range(local_count):
            column = jnp.max(
                jnp.where(mine == first + expert, columns[rows, :], -1), axis=1, keepdims=True
            )
            picks.append(ones_at(lanes == column))
        back = dot(jnp.concatenate(picks, axis=1), sent[source])
        store(piece, rows, back[:, :D].astype(bf16), back[:, D:].astype(bf16))


def expert_scratch(groups, local_count, experts):
    width = groups * CAP
    return [
        pltpu.VMEM((width, D), bf16),
        pltpu.VMEM((width, D), bf16),
        pltpu.VMEM((width, D), bf16),
        pltpu.VMEM((width, 128), f32),
        pltpu.VMEM((width, FF), bf16),
        pltpu.VMEM((width, FF), bf16),
        pltpu.VMEM((groups, local_count * CAP, 2 * D), bf16),
        pltpu.VMEM((SEQ, experts), jnp.int32),
    ]


def expert_kernel(*refs):
    operands, grads, (mixes, grad_normed) = refs[:5], refs[5:8], refs[8:10]
    work, columns = refs[10:17], refs[17]
    groups, local_count = operands[0].shape[0], operands[3].shape[0]

    def body(expert, _):
        one_expert(
            operands, work, grads, expert, 0, expert, range(groups), lambda point: None
        )
        return 0

    lax.fori_loop(0, local_count, body, 0)
    for source in range(groups):

        def store(piece, rows, mix, grad, source=source):
            mixes[source, rows, :] = mix
            grad_normed[source, rows, :] = grad

        combine(operands[1], 0, local_count, work[6], columns, source, store)


def expert_part(*operands):
    groups, local_count = operands[0].shape[0], operands[3].shape[0]
    return pl.pallas_call(
        expert_kernel,
        out_shape=(
            shape(local_count, D, FF, dtype=bf16),
            shape(local_count, FF, D, dtype=bf16),
            shape(groups, local_count, SEQ),
            shape(groups, SEQ, D, dtype=bf16),
            shape(groups, SEQ, D, dtype=bf16),
        ),
        in_specs=[VMEM] * 5,
        out_specs=[VMEM] * 5,
        scratch_shapes=expert_scratch(groups, local_count, operands[1].shape[1]),
        compiler_params=params(),
    )(*operands)


def expert_sending_kernel(outers, *refs):
    normed_all, cot_all, slots, gates, early_in, early_out, w_in, w_out = refs[:8]
    late_in, late_out, gate_all, mixes, grad_rows, shard_in, shard_out, parts_in, parts_out = refs[8:17]
    full_in, full_out = refs[17:19]
    work, columns = refs[19:26], refs[26]
    both, slot_in, slot_out, grad_in, grad_out, grad_gates, land, first_parts = refs[27:35]
    sent, landed, gate_sent, gate_landed, mix_sem, late_sem, slot_sem, token_sem = refs[35:43]
    part_sem, gather_sems, scatter_refs = refs[43], refs[44:46], refs[46:]
    place = Place(outers)
    groups, local_count, size = both.shape[0], grad_in.shape[0], 2 * outers
    late = local_count - EARLY_EXPERTS
    first = place.task * local_count
    grads, shares = (grad_in, grad_out), (w_in.shape[1], w_out.shape[1])

    def tokens():
        return [
            pltpu.make_async_copy(
                whole.at[source],
                both.at[source, :, pl.ds(kind * D, D)],
                token_sem.at[kind, source],
            )
            for source in range(groups)
            for kind, whole in enumerate((normed_all, cot_all))
        ]

    def load(expert):
        slot, copies = expert % EARLY_EXPERTS, []
        for kind in range(2):
            target, sem = (slot_in, slot_out)[kind].at[slot], slot_sem.at[slot, kind]
            early, own = (early_in, early_out)[kind], (w_in, w_out)[kind]
            full = (full_in, full_out)[kind]
            if expert < EARLY_EXPERTS:
                copies.append(pltpu.make_async_copy(early.at[expert], target, sem.at[0]))
                continue
            for ahead in range(size):
                block = lax.rem(place.dp + ahead, size)
                rows = rows_at(block, shares[kind])
                source = full.at[expert - EARLY_EXPERTS, rows]
                if (expert, kind) in GATHER_SPLIT:
                    if ahead % 2 == 0:
                        source = early.at[expert, rows]
                elif ahead == 0:
                    source = own.at[expert]
                copies.append(pltpu.make_async_copy(source, target.at[rows], sem.at[ahead]))
        return copies

    def keep(expert):
        return [
            pltpu.make_async_copy(
                grads[kind].at[EARLY_EXPERTS + expert],
                (late_in, late_out)[kind].at[expert],
                late_sem.at[expert, kind],
            )
            for kind in range(2)
        ]

    for copy in tokens() + load(0):
        copy.start()
    place.greet(far=True)
    shards = []
    for expert, kind in GATHER_LATE + GATHER_SPLIT:
        full = (full_in, full_out)[kind].at[expert - EARLY_EXPERTS]
        if (expert, kind) in GATHER_SPLIT:
            shards.append(((early_in, early_out)[kind].at[expert], shares[kind], full, "side"))
        else:
            shards.append(((w_in, w_out)[kind].at[expert], shares[kind], full, "turned"))
    gather = Gather(place, shards, *gather_sems, None)
    turned = range(len(GATHER_LATE))
    for unit in range(len(shards)):
        gather.start(unit)
    for copy in load(1):
        copy.start()
    per_full, per_side = 6 * len(SCATTER_EARLY[1:]), 3 * len(SCATTER_SPLIT)

    def scatters(units, refs, **parts):
        return make_scatters(
            place,
            [blocks_of(place, grads[kind].at[expert], shares[kind]) for expert, kind in units],
            refs,
            **parts,
        )

    expert, kind = SCATTER_EARLY[0]
    turned_scatter = Turned(
        place,
        *blocks_of(place, grads[kind].at[expert], shares[kind]),
        scatter_refs[per_full + per_side :],
    )
    whole = [turned_scatter] + scatters(SCATTER_EARLY[1:], scatter_refs[:per_full])
    split = scatters(SCATTER_SPLIT, scatter_refs[per_full : per_full + per_side], line=False)
    stores, keeps = [], []
    for expert, kind in SCATTER_EARLY:

        def store(rows, shard=(shard_in, shard_out)[kind], expert=expert):
            shard[expert] = rows

        stores.append(store)
    for index, (_, kind) in enumerate(SCATTER_SPLIT):
        at = [other[1] for other in SCATTER_SPLIT[:index]].count(kind)

        keeps.append((parts_in, parts_out)[kind].at[at])
    steps = {}

    def plan(expert, point, *acts):
        steps.setdefault((expert, point), []).extend(acts)

    plan(0, 0, *[copy.wait for copy in tokens()])
    for expert in range(EARLY_EXPERTS):
        plan(expert, 1, *[copy.wait for copy in load(expert)])
    for unit in turned:
        for hop, at in enumerate(GATHER_POINTS[GATHER_LATE[unit][0]]):
            plan(*at, lambda unit=unit, hop=hop: gather.step(unit, hop))
    for expert in range(EARLY_EXPERTS, local_count):
        units = [
            unit
            for unit, (owner, _) in enumerate(GATHER_LATE + GATHER_SPLIT)
            if owner == expert
        ]
        plan(expert, 0, *[lambda unit=unit: gather.finish(unit) for unit in units])
        plan(expert, 0, *[copy.start for copy in load(expert)])
        plan(expert, 1, *[copy.wait for copy in load(expert)])
        point = 4 if expert < local_count - 1 else 6
        plan(expert, point, *[copy.start for copy in keep(expert - EARLY_EXPERTS)])
    for index, (expert, _) in enumerate(SCATTER_EARLY):
        plan(expert, 4, whole[index].start)
    for index, (expert, _) in enumerate(SCATTER_SPLIT):
        plan(expert, 4, split[index].start)
    for turn, at in SCATTER_POINTS.items():
        plan(*at, lambda turn=turn: scatter_turn(whole, stores, turn))

    operands = (both, slots, gates, slot_in, slot_out)
    every_grad = (grad_in, grad_out, grad_gates)
    sources = (place.far, place.across, place.core, place.task)

    def body(expert, _):
        def between(point):
            for at in range(local_count - 1):
                acts = steps.get((at, point))
                if acts:

                    @pl.when(expert == at)
                    def _():
                        for act in acts:
                            act()

        one_expert(
            operands,
            work,
            every_grad,
            expert,
            first,
            lax.rem(expert, EARLY_EXPERTS),
            sources,
            between,
        )
        return 0

    lax.fori_loop(0, local_count - 1, body, 0)
    hidden, grad_pre = work[4], work[5]

    def part(ref, block):
        return ref.at[pl.ds(0, SEQ), pl.ds(block * D, D)]

    parts = [first_parts.at[0], first_parts.at[1], part(hidden, 0), part(hidden, 1)]
    mix_parts = [first_parts.at[2], first_parts.at[2], part(grad_pre, 0), part(grad_pre, 1)]
    back = Return(
        place,
        (parts[2], parts[0], parts[1], parts[3]),
        RETURNS,
        land,
        sent,
        landed,
    )
    sends = (back.by_core, back.to_across, back.to_core, None)

    def mix_copy(block):
        return pltpu.make_async_copy(
            mix_parts[block], mixes.at[sources[block]], mix_sem.at[block]
        )

    def returned(block):
        def store(piece, rows, mix, grad):
            mix_parts[block][rows, :] = mix
            parts[block][rows, :] = grad
            if sends[block]:
                sends[block](piece)

        combine(slots, first, local_count, work[6], columns, sources[block], store)
        mix_copy(block).start()

    def halfway():
        returned(0)
        mix_copy(0).wait()
        returned(1)
        scatter_turn(whole, stores, 2)

    def last(point):
        for act in steps.get((local_count - 1, point), ()):
            act()

    one_expert(
        operands,
        work,
        every_grad,
        local_count - 1,
        first,
        (local_count - 1) % EARLY_EXPERTS,
        sources,
        last,
        halfway,
    )
    gate_all[place.task] = grad_gates[place.task]
    peers = (place.core, place.across, place.far)

    def gate_move(way):
        return remote(
            grad_gates.at[peers[way]],
            gate_all.at[place.task],
            gate_sent.at[way],
            gate_landed.at[way],
            task=peers[way],
        )

    for way in range(3):
        gate_move(way).start()
    returned(2)
    returned(3)
    for turn in range(4, len(whole) + outers - 1):
        scatter_turn(whole, stores, turn)
    expert, kind = SCATTER_EARLY[0]
    turned_scatter.add((shard_in, shard_out)[kind].at[expert])
    settled = [
        one.settle(keeps[index], part_sem.at[index]) for index, one in enumerate(split)
    ]
    for piece in range(RETURNS):
        grad_rows[back.rows(piece), :] = back.finish(piece)
    for way in range(3):
        gate_move(way).wait()
    for block in range(1, groups):
        mix_copy(block).wait()
    for expert in range(late):
        for copy in keep(expert):
            copy.wait()
    for copy in settled:
        copy.wait()


def kinds(units, kind):
    return sorted({unit[0] for unit in units if unit[1] == kind})


def expert_sending(*operands):
    groups, experts = operands[2].shape[:2]
    local_count, thin = operands[6].shape[:2]
    wide, size = operands[7].shape[1], lax.axis_size("dp")
    late, outers = local_count - EARLY_EXPERTS, size // 2
    tiles = ((thin, FF), (wide, D))
    return pl.pallas_call(
        functools.partial(expert_sending_kernel, outers),
        out_shape=(
            shape(late, D, FF, dtype=bf16),
            shape(late, FF, D, dtype=bf16),
            shape(groups, local_count, SEQ),
            shape(groups, SEQ, D, dtype=bf16),
            shape(SEQ, D),
            *[shape(len(kinds(SCATTER_EARLY, kind)), *tiles[kind]) for kind in range(2)],
            *[
                shape(len(kinds(SCATTER_SPLIT, kind)), outers, *tiles[kind], dtype=bf16)
                for kind in range(2)
            ],
            shape(late, D, FF, dtype=bf16),
            shape(late, FF, D, dtype=bf16),
        ),
        in_specs=[ANY] * 2 + [VMEM] * 2 + [ANY] * 4,
        out_specs=[ANY] * 2 + [VMEM, ANY] + [VMEM] * 3 + [ANY] * 4,
        scratch_shapes=expert_scratch(groups, local_count, experts)
        + [
            pltpu.VMEM((groups, SEQ, 2 * D), bf16),
            pltpu.VMEM((EARLY_EXPERTS, D, FF), bf16),
            pltpu.VMEM((EARLY_EXPERTS, FF, D), bf16),
            pltpu.VMEM((local_count, D, FF), bf16),
            pltpu.VMEM((local_count, FF, D), bf16),
            pltpu.VMEM((groups, local_count, SEQ), f32),
            pltpu.VMEM((3, SEQ, D), bf16),
            pltpu.VMEM((3, SEQ, D), bf16),
            pltpu.SemaphoreType.DMA((3, RETURNS)),
            pltpu.SemaphoreType.DMA((3, RETURNS)),
            pltpu.SemaphoreType.DMA((3,)),
            pltpu.SemaphoreType.DMA((3,)),
            pltpu.SemaphoreType.DMA((groups,)),
            pltpu.SemaphoreType.DMA((late, 2)),
            pltpu.SemaphoreType.DMA((EARLY_EXPERTS, 2, size)),
            pltpu.SemaphoreType.DMA((2, groups)),
            pltpu.SemaphoreType.DMA((len(SCATTER_SPLIT),)),
        ]
        + gather_semaphores(len(GATHER_LATE + GATHER_SPLIT), size)
        + scatter_scratch(SCATTER_EARLY[1:], outers, tiles)
        + scatter_scratch(SCATTER_SPLIT, outers, tiles, line=False)
        + turned_scratch(outers, tiles[SCATTER_EARLY[0][1]]),
        compiler_params=params(collective_id=1, has_side_effects=True),
    )(*operands)


def attend_back(packed, grad_mixed, logs, grad_packed, grad_keys, grad_values, between, done):
    zero = jnp.array(0, bf16)
    blocks = SEQ // QUERY_BWD

    def head_pair(pair):
        queries, keys, values = (
            slice(part * D + pair * PAIR, part * D + (pair + 1) * PAIR) for part in range(3)
        )
        key_rows, value_rows = packed[:, keys], packed[:, values]

        def block(index, _):
            rows = rows_at(index, QUERY_BWD)
            query_rows = packed[rows, queries] * jnp.array(HEAD_DIM**-0.5, bf16)
            grad_rows = grad_mixed[rows, queries]
            grad_query, part_keys, part_values = [], 0.0, 0.0
            for half in range(2):
                lanes = half_lanes(QUERY_BWD, half)
                own = jnp.where(lanes, query_rows, zero)
                own_grad = jnp.where(lanes, grad_rows, zero)
                head = 2 * pair + half
                probs = jnp.exp(dot_rt(key_rows, own) - logs[head : head + 1, rows])
                grad_probs = dot_rt(value_rows, own_grad)
                mean = jnp.sum(probs * grad_probs, axis=0, keepdims=True)
                grad_scores = (probs * (grad_probs - mean)).astype(bf16)
                part_values += dot(probs.astype(bf16), own_grad)
                part_keys += dot(grad_scores, own)
                grad_query.append(dot_lt(grad_scores, key_rows))
            grad_packed[rows, queries] = (
                jnp.where(half_lanes(QUERY_BWD, 0), grad_query[0], grad_query[1])
                * HEAD_DIM**-0.5
            ).astype(bf16)
            grad_keys[...] = jnp.where(index == 0, part_keys, grad_keys[...] + part_keys)
            grad_values[...] = jnp.where(index == 0, part_values, grad_values[...] + part_values)
            between(pair, index)
            return 0

        lax.fori_loop(0, blocks, block, 0)
        grad_packed[:, keys] = grad_keys[...].astype(bf16)
        grad_packed[:, values] = grad_values[...].astype(bf16)
        done(pair, (queries, keys, values))

    for pair in range(HEADS // 2):
        head_pair(pair)


def second_back(
    grad_rows, cotangent, gain, bias, mid, w_proj, router, grad_logits, grad_norm, grad_router, outs
):
    grad_mid, grad_low, grad_mixed = outs
    grad_norm[...] = jnp.zeros_like(grad_norm)
    grad_router[...] = jnp.zeros_like(grad_router)
    for index in range(SEQ // ROWS):
        rows = slice(index * ROWS, (index + 1) * ROWS)
        mid_rows = mid[rows, :]
        own_logits = grad_logits[:, rows]
        grad_in_rows = grad_rows(rows) + lax.dot_general(
            own_logits,
            router[...],
            (((0,), (0,)), ((), ())),
            precision=HIGHEST,
            preferred_element_type=f32,
        )
        grad_in, grad_gain, grad_bias, unit = norm_back(mid_rows, grad_in_rows, gain[1:2, :])
        grad_router[...] += jnp.dot(
            own_logits,
            unit * gain[1:2, :] + bias[1:2, :],
            precision=HIGHEST,
            preferred_element_type=f32,
        )
        grad_norm[1:2, :] += grad_gain
        grad_norm[3:4, :] += grad_bias
        grad_mid_rows = cotangent[rows, :] + grad_in
        grad_mid[rows, :] = grad_mid_rows
        low_rows = grad_mid_rows.astype(bf16)
        grad_low[rows, :] = low_rows
        grad_mixed[rows, :] = dot_rt(low_rows, w_proj[...]).astype(bf16)


def first_back(image, gain, parts, grad_packed, grad_mid, grad_image, grad_norm):
    def block(index, _):
        rows = rows_at(index, ROWS)
        grad_rows = sum(
            dot_rt(grad_packed[rows, part * D : (part + 1) * D], parts(part)) for part in range(3)
        )
        grad_in, grad_gain, grad_bias, _ = norm_back(image[rows, :], grad_rows, gain[0:1, :])
        grad_image[rows, :] = grad_mid[rows, :] + grad_in
        grad_norm[0:1, :] += grad_gain
        grad_norm[2:3, :] += grad_bias
        return 0

    lax.fori_loop(0, SEQ // ROWS, block, 0)


def logit_grads(probs, grad_gates):
    route = jnp.concatenate([grad_gates[group] for group in range(grad_gates.shape[0])], axis=0)
    return probs[...] * (route - jnp.sum(probs[...] * route, axis=0, keepdims=True))


def backward_scratch():
    return [
        pltpu.VMEM((SEQ, D), f32),
        pltpu.VMEM((SEQ, D), bf16),
        pltpu.VMEM((SEQ, D), bf16),
        pltpu.VMEM((SEQ, 3 * D), bf16),
        pltpu.VMEM((SEQ, PAIR), f32),
        pltpu.VMEM((SEQ, PAIR), f32),
        pltpu.VMEM((SEQ, D), bf16),
    ]


def backward_kernel(*refs):
    image, cotangent, gain, bias, mid, w_qkv, w_proj, router = refs[:8]
    packed, mixed, logs, mixes, grad_normed, grad_gates, probs = refs[8:15]
    activations, grad_image, grad_norm, grad_router, grad_shared = refs[15:20]
    grad_mid, grad_low, grad_mixed, grad_packed, grad_keys, grad_values, normed_first = refs[20:]
    groups = mixes.shape[0]

    def added(parts, rows):
        total = parts[0, rows, :].astype(f32)
        for source in range(1, groups):
            total += parts[source, rows, :].astype(f32)
        return total

    activations[...] = mid[...] + added(mixes, slice(None))
    second_back(
        lambda rows: added(grad_normed, rows),
        cotangent,
        gain,
        bias,
        mid,
        w_proj,
        router,
        logit_grads(probs, grad_gates),
        grad_norm,
        grad_router,
        (grad_mid, grad_low, grad_mixed),
    )
    first_norm(image, gain, bias, normed_first)
    grad_shared[:, 3 * D :] = dot_lt(mixed[...], grad_low[...]).astype(bf16)
    attend_back(
        packed,
        grad_mixed,
        logs,
        grad_packed,
        grad_keys,
        grad_values,
        lambda pair, index: None,
        lambda pair, columns: None,
    )
    first_back(
        image,
        gain,
        lambda part: w_qkv[:, part * D : (part + 1) * D],
        grad_packed,
        grad_mid,
        grad_image,
        grad_norm,
    )
    grad_shared[:, : 3 * D] = dot_lt(normed_first[...], grad_packed[...]).astype(bf16)


def backward_part(*operands):
    router = operands[7]
    return pl.pallas_call(
        backward_kernel,
        out_shape=(
            shape(SEQ, D),
            shape(SEQ, D),
            shape(4, D),
            shape(router.shape[0], D),
            shape(D, 4 * D, dtype=bf16),
        ),
        in_specs=[VMEM] * 15,
        out_specs=[VMEM] * 5,
        scratch_shapes=backward_scratch(),
        compiler_params=params(),
    )(*operands)


def backward_sending_kernel(outers, groups, *refs):
    whole, (gain, bias, router, logs, grad_gates, probs) = refs[:9], refs[9:15]
    mixes_all, late_in, late_out = refs[15:18]
    activations, grad_image, grad_gain, grad_bias, grad_router, shard_qkv, shard_proj = refs[18:25]
    shard_in, shard_out = refs[25:27]
    grad_mid, grad_low, grad_mixed, grad_packed, grad_keys, grad_values, normed_first = refs[27:34]
    norm_sums, router_sums, shared, mixes, land, back_sent, back_landed = refs[34:41]
    own_shared, shared_land, shared_sent, shared_landed = refs[41:45]
    here, here_sem, result_sem = refs[45:54], refs[54], refs[55]
    parts_in, parts_out, image, cotangent, mid, quarters, packed, mixed, grad_rows = here
    refs = refs[56:]
    late_grads = sorted({unit[:2] for unit in SCATTER_LATE})
    mix_sem, grad_sem, grad_refs = refs[0], refs[1], refs[2 : 2 + len(late_grads)]
    refs = refs[2 + len(late_grads) :]
    inputs = [
        pltpu.make_async_copy(source, target, here_sem.at[index])
        for index, (source, target) in enumerate(zip(whole, here))
    ]
    place = Place(outers)
    size, pieces = 2 * outers, HEADS // 2 + 1
    shards = (shard_in, shard_out)
    loads = [
        pltpu.make_async_copy(
            (late_in, late_out)[kind].at[expert - EARLY_EXPERTS],
            grad_refs[index],
            grad_sem.at[index],
        )
        for index, (expert, kind) in enumerate(late_grads)
    ]
    mix_load = pltpu.make_async_copy(mixes_all, mixes, mix_sem)
    for copy in (*inputs[:2], *loads, *inputs[2:], mix_load):
        copy.start()
    place.greet_all(groups)
    at = 6 * len(SCATTER_LATE)
    late = make_scatters(
        place,
        [
            blocks_of(
                place, grad_refs[late_grads.index(unit[:2])], shards[unit[1]].shape[1], unit[2:]
            )
            for unit in SCATTER_LATE
        ],
        refs[:at],
    )
    split_blocks = []
    for index, (_, kind) in enumerate(SCATTER_SPLIT):
        number = [other[1] for other in SCATTER_SPLIT[:index]].count(kind)
        split_blocks.append(
            (
                lambda outer, parts=(parts_in, parts_out)[kind], number=number: parts.at[
                    number, outer
                ],
                None,
            )
        )
    split = make_scatters(place, split_blocks, refs[at:], side=False)
    at += 3 * len(SCATTER_SPLIT)
    deal = Deal(place, own_shared, shard_proj.shape[0], *refs[at : at + 3])
    at += 3
    norms = Spread("dp", place, size, *refs[at : at + 3])
    norms_task = Spread("task", place, groups, *refs[at + 3 : at + 6])
    routers = Spread("dp", place, size, *refs[at + 6 : at + 9])
    quarter = Spread("task", place, groups, *refs[at + 9 : at + 12])
    stores = []
    for unit in SCATTER_SPLIT + SCATTER_LATE:
        number = kinds(SCATTER_SPLIT + SCATTER_LATE, unit[1]).index(unit[0])

        def store(rows, shard=shards[unit[1]], number=number, half=unit[2:]):
            start = half[0] * rows.shape[0] if half else 0
            shard[number, start : start + rows.shape[0], :] = rows

        stores.append(store)
    for copy in inputs[:2]:
        copy.wait()
    for one in split:
        one.hop(0)
    for index, one in enumerate(late):
        unit = SCATTER_LATE[index]
        if unit[2:] in ((), (0,)):
            loads[late_grads.index(unit[:2])].wait()
        one.start()
    mix_load.wait()
    roles = (place.core, place.far, place.across, place.task)
    back = Return(
        place, [mixes.at[role] for role in roles], 1, land, back_sent, back_landed
    )
    back.by_core(0)
    back.to_core(0)
    for copy in inputs[2:]:
        copy.wait()
    second_back(
        lambda rows: grad_rows[rows, :],
        cotangent,
        gain,
        bias,
        mid,
        quarters.at[3],
        router,
        logit_grads(probs, grad_gates),
        norm_sums,
        router_sums,
        (grad_mid, grad_low, grad_mixed),
    )
    back.to_across(0)
    first_norm(image, gain, bias, normed_first)
    shared[pieces - 1] = dot_lt(mixed[...], grad_low[...]).astype(bf16)
    routers.give(router_sums[...])
    blocks = SEQ // QUERY_BWD
    units, keeps = split + late, stores
    names = dict(zip("stuvwxyz", range(len(units))))
    joined = Return(
        place,
        [shared.at[role] for role in roles],
        1,
        shared_land,
        shared_sent,
        shared_landed,
    )

    def run(acts):
        for act in acts:
            unit, hop = names[act[0]], int(act[1])
            if hop < outers - 1:
                units[unit].hop(hop)
            else:
                units[unit].finish(keeps[unit])

    def between(pair, index):
        for at, acts in BACKWARD_POINTS.items():
            if at // blocks == pair:
                pl.when(index == at % blocks)(lambda acts=acts: run(acts))

    def done(pair, columns):
        both = jnp.concatenate([grad_packed[:, part] for part in columns], axis=1)
        shared[pair] = dot_lt(normed_first[...], both).astype(bf16)

    attend_back(
        packed, grad_mixed, logs, grad_packed, grad_keys, grad_values, between, done
    )
    joined.by_core(0)
    joined.to_core(0)
    first_back(
        image,
        gain,
        lambda part: quarters[part],
        grad_packed,
        grad_mid,
        grad_mid,
        norm_sums,
    )
    results = [
        pltpu.make_async_copy(grad_mid, grad_image, result_sem.at[0]),
        pltpu.make_async_copy(mid, activations, result_sem.at[1]),
    ]
    results[0].start()
    norms.give(norm_sums[...])
    joined.to_across(0)
    mid[...] = mid[...] + back.finish(0)
    results[1].start()
    run(BACKWARD_THEN[0])
    own_shared[...] = joined.finish(0).astype(bf16)
    deal.start()
    grad_router[...] = routers.take()
    norms_task.give(norms.take())
    run(BACKWARD_THEN[1])
    quarter.give(deal.total())
    run(BACKWARD_THEN[2])
    rows = norms_task.take()
    grad_gain[...] = rows[:2]
    grad_bias[...] = rows[2:4]
    quarter.arrive()
    shard_proj[...] = quarter.land[pieces - 1]
    for piece in range(pieces - 1):
        for part in range(3):
            column = part * D + piece * PAIR
            shard_qkv[:, column : column + PAIR] = quarter.land[
                piece, :, part * PAIR : (part + 1) * PAIR
            ]
    run(BACKWARD_THEN[3])
    for copy in results:
        copy.wait()


def backward_sending(*operands):
    router, whole = operands[11], operands[:9]
    experts, size = router.shape[0], lax.axis_size("dp")
    outers, thin, wide, pieces = size // 2, D // size, FF // size, HEADS // 2 + 1
    groups = lax.axis_size("task")
    tiles, wholes = ((thin, FF), (wide, D)), ((D, FF), (FF, D))
    ends = SCATTER_SPLIT + SCATTER_LATE
    late_grads = sorted({unit[:2] for unit in SCATTER_LATE})

    def spread(peers, *dims):
        return [pltpu.VMEM((peers, *dims), f32)] + [pltpu.SemaphoreType.DMA((peers - 1,))] * 2

    return pl.pallas_call(
        functools.partial(backward_sending_kernel, outers, groups),
        out_shape=(
            shape(SEQ, D),
            shape(SEQ, D),
            shape(2, D),
            shape(2, D),
            shape(experts, D),
            shape(thin, 3 * D),
            shape(thin, D),
            *[shape(len(kinds(ends, kind)), *tiles[kind]) for kind in range(2)],
        ),
        in_specs=[ANY] * 9 + [VMEM] * 6 + [ANY] * 3,
        out_specs=[ANY] * 2 + [VMEM] * 7,
        scratch_shapes=backward_scratch()
        + [
            pltpu.VMEM((8, D), f32),
            pltpu.VMEM((experts, D), f32),
            pltpu.VMEM((pieces, D, D), bf16),
            pltpu.VMEM((groups, SEQ, D), bf16),
            pltpu.VMEM((3, SEQ, D), bf16),
            pltpu.SemaphoreType.DMA((3, 1)),
            pltpu.SemaphoreType.DMA((3, 1)),
            pltpu.VMEM((D, D), bf16),
            pltpu.VMEM((3, D, D), bf16),
            pltpu.SemaphoreType.DMA((3, 1)),
            pltpu.SemaphoreType.DMA((3, 1)),
            *[pltpu.VMEM(operand.shape, operand.dtype) for operand in whole],
            pltpu.SemaphoreType.DMA((len(whole),)),
            pltpu.SemaphoreType.DMA((2,)),
            pltpu.SemaphoreType.DMA,
            pltpu.SemaphoreType.DMA((len(late_grads),)),
        ]
        + [pltpu.VMEM(wholes[kind], bf16) for _, kind in late_grads]
        + scatter_scratch(SCATTER_LATE, outers, tiles)
        + scatter_scratch(SCATTER_SPLIT, outers, tiles, side=False)
        + [
            pltpu.VMEM((size, thin, D), bf16),
            pltpu.SemaphoreType.DMA((size - 1,)),
            pltpu.SemaphoreType.DMA((size - 1,)),
        ]
        + spread(size, 8, D)
        + spread(groups, 8, D)
        + spread(size, experts, D)
        + spread(groups, thin, D),
        compiler_params=params(collective_id=2, has_side_effects=True),
    )(*operands)


def local(
    layer_input,
    cotangent,
    norm_gain,
    norm_bias,
    w_qkv,
    w_proj,
    router,
    w_in,
    w_out,
    choices,
    top_count,
):
    groups = lax.axis_size("task")
    local_count = w_in.shape[0]
    image = layer_input.reshape(SEQ, D)
    grad_rows = cotangent.reshape(SEQ, D)
    routes = choices.reshape(SEQ, TOPMAX).T
    router_rows = router[0].T

    def swap(array):
        return lax.all_to_all(array, "task", split_axis=0, concat_axis=0, tiled=True)

    sending = groups == 4 and lax.axis_size("dp") == 8 and local_count == 4
    if sending:
        (
            mid,
            packed,
            mixed,
            logs,
            probs,
            normed,
            cot_rows,
            slots,
            gates,
            quarters,
            full_in,
            full_out,
        ) = forward_sending(
            top_count,
            image,
            grad_rows,
            norm_gain,
            norm_bias,
            (w_qkv, w_proj, w_in, w_out),
            router_rows,
            routes,
        )
        (
            late_in,
            late_out,
            grad_gates,
            mixes,
            grad_normed,
            early_in,
            early_out,
            parts_in,
            parts_out,
            _,
            _,
        ) = expert_sending(normed, cot_rows, slots, gates, full_in, full_out, w_in, w_out)
        (
            activations,
            grad_image,
            grad_gain,
            grad_bias,
            grad_router,
            grad_qkv,
            grad_proj,
            grad_in,
            grad_out,
        ) = backward_sending(
            parts_in,
            parts_out,
            image,
            grad_rows,
            mid,
            quarters,
            packed,
            mixed,
            grad_normed,
            norm_gain,
            norm_bias,
            router_rows,
            logs,
            grad_gates,
            probs,
            mixes,
            late_in,
            late_out,
        )
        grad_in = jnp.concatenate([early_in, grad_in], axis=0)
        grad_out = jnp.concatenate([early_out, grad_out], axis=0)
    else:
        full_qkv, full_proj, full_in, full_out = (
            lax.all_gather(w_qkv, "dp", axis=0, tiled=True),
            lax.all_gather(w_proj, "dp", axis=0, tiled=True),
            lax.all_gather(w_in, "dp", axis=1, tiled=True),
            lax.all_gather(w_out, "dp", axis=1, tiled=True),
        )
        mid, packed, mixed, logs, normed, slots, gates, probs = forward_part(
            top_count,
            image,
            norm_gain,
            norm_bias,
            full_qkv,
            full_proj,
            router_rows,
            routes,
        )
        normed = lax.all_gather(normed, "task")
        cot_rows = lax.all_gather(grad_rows.astype(bf16), "task")
        slots = swap(slots.reshape(groups, local_count, SEQ))
        gates = swap(gates.reshape(groups, local_count, SEQ))
        tokens = jnp.concatenate([normed, cot_rows], axis=-1)
        grad_in, grad_out, grad_gates, mixes, grad_normed = expert_part(
            tokens, slots, gates, full_in, full_out
        )
        activations, grad_image, grad_norm, grad_router, grad_shared = backward_part(
            image,
            grad_rows,
            norm_gain,
            norm_bias,
            mid,
            full_qkv,
            full_proj,
            router_rows,
            packed,
            mixed,
            logs,
            swap(mixes),
            swap(grad_normed),
            swap(grad_gates),
            probs,
        )
        grad_in = lax.psum_scatter(grad_in, "dp", scatter_dimension=1, tiled=True).astype(f32)
        grad_out = lax.psum_scatter(grad_out, "dp", scatter_dimension=1, tiled=True).astype(f32)
        grad_shared = lax.psum_scatter(grad_shared, "dp", scatter_dimension=0, tiled=True)
        grad_shared = lax.psum(grad_shared, "task").astype(f32)
        grad_qkv, grad_proj = grad_shared[:, : 3 * D], grad_shared[:, 3 * D :]
        grad_router = lax.psum(grad_router, "dp")
        grad_norm = lax.psum(grad_norm, ("task", "dp"))
        grad_gain, grad_bias = grad_norm[:2], grad_norm[2:]
    return (
        activations.reshape(layer_input.shape),
        grad_image.reshape(layer_input.shape),
        grad_gain,
        grad_bias,
        grad_qkv,
        grad_proj,
        grad_router.T[None],
        grad_in,
        grad_out,
    )


def solution(mesh):
    tokens = P("task", "dp", None, None)
    rows = P("dp", None)
    blocks = P("task", "dp", None)
    routed = P("task", None, None)
    return jax.shard_map(
        local,
        mesh=mesh,
        in_specs=(tokens, tokens, P(), P(), rows, rows, routed, blocks, blocks, tokens, P("task")),
        out_specs=(tokens, tokens, P(), P(), rows, rows, routed, blocks, blocks),
        check_vma=False,
    )
```

```python
import functools

import jax
import jax.numpy as jnp
from jax import lax
from jax.experimental import pallas as pl
from jax.experimental.pallas import tpu as pltpu
from jax.sharding import PartitionSpec as P

D = 384
FF = 1536
HEADS = 6
HEAD_DIM = 64
PAIR = 2 * HEAD_DIM
TOPMAX = 4
SEQ = 1024
CAP = 320

f32 = jnp.float32
bf16 = jnp.bfloat16
HIGHEST = lax.Precision.HIGHEST
EPSILON = 1e-06
ROOT_HALF = 0.7071067811865476
NORMAL = 0.3989422804014327

FF_TILE = 512
ROW_TILE = 640
QUERY_FWD = 256
QUERY_BWD = 256
ROWS = 256
RETURNS = 2

GATHER_WHOLE = ((0, 0), (0, 1), (1, 0), (1, 1))
GATHER_SPLIT = ((2, 0), (2, 1))
GATHER_LATE = ((3, 0), (3, 1))
SCATTER_EARLY = ((0, 0), (0, 1), (1, 0))
SCATTER_SPLIT = ((1, 1), (2, 0))
SCATTER_LATE = ((2, 1), (3, 0), (3, 1, 0), (3, 1, 1))
EARLY_EXPERTS = 2

GATHER_POINTS = {2: ((0, 1), (0, 3), (1, 0), (1, 4)), 3: ((0, 2), (1, 1), (1, 4), (3, 0))}
SCATTER_POINTS = {1: (2, 4), 3: (3, 6)}

AHEAD, NEXT = 2, 4
FORWARD_FIRST = ((0, 1), (1, 1), (2, 1), (3, 1), (0, 2))
FORWARD_POINTS = {
    0: ((1, 2),),
    1: ((2, 2), (4, 0), (5, 0)),
    2: ((3, 2),),
    5: ((0, 3),),
    6: ((1, 3),),
    7: ((2, 3),),
    8: ((3, 3),),
    9: ((4, 1),),
    10: ((5, 1),),
}
FORWARD_THEN = (((4, 2), (5, 2)), ((4, 3), (5, 3)))

BACKWARD_POINTS = {
    3: ("s1", "u0",),
    8: ("t1", "s2", "v0",),
    11: ("u1",),
}
BACKWARD_THEN = (
    ("t2", "s3", "v1", "u2", "w0"),
    ("x0", "t3", "v2", "u3", "w1"),
    ("x1", "v3", "w2", "x2"),
    ("w3", "x3"),
)


VMEM = pl.BlockSpec(memory_space=pltpu.VMEM)
SMEM = pl.BlockSpec(memory_space=pltpu.SMEM)
ANY = pl.BlockSpec(memory_space=pl.ANY)


def shape(*dims, dtype=f32):
    return jax.ShapeDtypeStruct(dims, dtype)


def params(**more):
    return pltpu.CompilerParams(vmem_limit_bytes=63 * 2**20, **more)


def dot(a, b):
    return lax.dot_general(a, b, (((1,), (0,)), ((), ())), preferred_element_type=f32)


def dot_rt(a, b):
    return lax.dot_general(a, b, (((1,), (1,)), ((), ())), preferred_element_type=f32)


def dot_lt(a, b):
    return lax.dot_general(a, b, (((0,), (0,)), ((), ())), preferred_element_type=f32)


def rows_at(index, size):
    return pl.ds(pl.multiple_of(index * size, size), size)


def normalize(rows):
    centered = rows - jnp.mean(rows, axis=1, keepdims=True)
    scale = lax.rsqrt(jnp.mean(centered * centered, axis=1, keepdims=True) + EPSILON)
    return centered * scale, scale


def norm_back(rows, grad_rows, gain):
    unit, scale = normalize(rows)
    scaled = grad_rows * gain
    grad_in = scale * (
        scaled
        - jnp.mean(scaled, axis=1, keepdims=True)
        - unit * jnp.mean(scaled * unit, axis=1, keepdims=True)
    )
    grad_gain = jnp.sum(grad_rows * unit, axis=0, keepdims=True)
    return grad_in, grad_gain, jnp.sum(grad_rows, axis=0, keepdims=True), unit


def half_lanes(rows, half):
    lanes = lax.broadcasted_iota(jnp.int32, (rows, PAIR), 1)
    return (lanes < HEAD_DIM) if half == 0 else (lanes >= HEAD_DIM)


def remote(source, target, sent, landed, **device):
    return pltpu.make_async_remote_copy(
        src_ref=source,
        dst_ref=target,
        send_sem=sent,
        recv_sem=landed,
        device_id=device,
        device_id_type=pl.DeviceIdType.MESH,
    )


class Place:
    def __init__(self, outers):
        self.dp = lax.axis_index("dp")
        self.task = lax.axis_index("task")
        self.outers = outers
        self.outer, self.inner = self.dp // 2, self.dp % 2
        self.has_up, self.has_down = self.outer + 1 < outers, self.outer > 0
        self.up, self.down = self.dp + 2, self.dp - 2
        self.side = self.dp + 1 - 2 * self.inner
        self.core = self.task + 1 - 2 * (self.task % 2)
        self.across = self.task + 2 - 4 * (self.task // 2)
        self.far = self.across + 1 - 2 * (self.task % 2)

    def signal(self, **device):
        pl.semaphore_signal(
            pltpu.get_barrier_semaphore(),
            inc=1,
            device_id=device,
            device_id_type=pl.DeviceIdType.MESH,
        )

    def greet(self, far=False):
        pl.when(self.has_up)(lambda: self.signal(dp=self.up))
        pl.when(self.has_down)(lambda: self.signal(dp=self.down))
        self.signal(dp=self.side)
        self.signal(task=self.core)
        self.signal(task=self.across)
        if far:
            self.signal(task=self.far)
        others = 3 + int(far) + self.has_up.astype(jnp.int32) + self.has_down.astype(jnp.int32)
        pl.semaphore_wait(pltpu.get_barrier_semaphore(), others)

    def greet_all(self, groups):
        size = 2 * self.outers
        for ahead in range(1, size):
            self.signal(dp=lax.rem(self.dp + ahead, size))
        for ahead in range(1, groups):
            self.signal(task=lax.rem(self.task + ahead, groups))
        pl.semaphore_wait(pltpu.get_barrier_semaphore(), size + groups - 2)


class Gather:
    def __init__(self, place, shards, sent, landed, stay):
        self.place, self.shards = place, shards
        self.sent, self.landed, self.stay = sent, landed, stay

    def move(self, unit, source, way, device, first=None):
        _, size, full, _ = self.shards[unit]
        target = full.at[rows_at(source, size)]
        return remote(
            target if first is None else first,
            target,
            self.sent.at[unit, source, way],
            self.landed.at[unit, source],
            dp=device,
        )

    def local(self, unit):
        own, size, full, _ = self.shards[unit]
        target = full.at[rows_at(self.place.dp, size)]
        return pltpu.make_async_copy(own, target, self.stay.at[unit])

    def along(self, unit, source, up, down):
        place = self.place
        if up:
            pl.when(place.has_up)(lambda: self.move(unit, source, 0, place.up).start())
        if down:
            pl.when(place.has_down)(lambda: self.move(unit, source, 1, place.down).start())

    def to_side(self, unit, outer):
        own, size = self.shards[unit][:2]
        source = 2 * outer + self.place.inner
        return self.move(unit, source, 2, self.place.side, own.at[rows_at(source, size)])

    def start(self, unit):
        place = self.place
        own, mode = self.shards[unit][0], self.shards[unit][3]
        if mode == "side":
            for outer in range(place.outers):
                self.to_side(unit, outer).start()
            return
        if mode == "turned":
            self.move(unit, place.dp, 2, place.side, own).start()
        pl.when(place.has_up)(lambda: self.move(unit, place.dp, 0, place.up, own).start())
        pl.when(place.has_down)(lambda: self.move(unit, place.dp, 1, place.down, own).start())
        if mode == "both":
            self.move(unit, place.dp, 2, place.side, own).start()
        if self.stay is not None:
            self.local(unit).start()

    def step(self, unit, hop):
        place, mode = self.place, self.shards[unit][3]
        if hop == 0:
            self.move(unit, place.side, 0, place.dp).wait_recv()
            self.along(unit, place.side, True, True)
            return
        for column in (place.dp, place.side) if mode == "turned" else (place.dp,):

            @pl.when(place.outer >= hop)
            def _():
                self.move(unit, column - 2 * hop, 0, place.dp).wait_recv()
                self.along(unit, column - 2 * hop, True, False)
                if mode == "both":
                    self.move(unit, column - 2 * hop, 2, place.side).start()

            @pl.when(place.outer + hop < place.outers)
            def _():
                self.move(unit, column + 2 * hop, 1, place.dp).wait_recv()
                self.along(unit, column + 2 * hop, False, True)
                if mode == "both":
                    self.move(unit, column + 2 * hop, 2, place.side).start()

    def finish(self, unit):
        place, mode = self.place, self.shards[unit][3]
        if self.stay is not None:
            self.local(unit).wait()
        if mode == "turned":
            self.move(unit, place.dp, 2, place.side).wait_send()
        for outer in range(place.outers):
            own, other = 2 * outer + place.inner, 2 * outer + 1 - place.inner
            if mode in ("both", "side"):
                self.move(unit, other, 2, place.dp).wait_recv()
                self.move(unit, own, 2, place.side).wait_send()
            if mode == "side":
                continue
            for source in (own, other) if mode == "turned" else (own,):
                pl.when((outer <= place.outer) & place.has_up)(
                    lambda source=source: self.move(unit, source, 0, place.up).wait_send()
                )
                pl.when((outer >= place.outer) & place.has_down)(
                    lambda source=source: self.move(unit, source, 1, place.down).wait_send()
                )


def gather_semaphores(units, size):
    return [
        pltpu.SemaphoreType.DMA((units, size, 3)),
        pltpu.SemaphoreType.DMA((units, size)),
    ]


class Share:
    def __init__(self, place, view, sent, landed):
        self.place, self.view, self.sent, self.landed = place, view, sent, landed

    def move(self, source, way, **device):
        return remote(
            self.view(source),
            self.view(source),
            self.sent.at[way],
            self.landed.at[way],
            **device,
        )

    def start(self):
        place = self.place
        self.move(place.task, 0, task=place.across).start()
        self.move(place.task, 1, task=place.core).start()

    def relay(self):
        place = self.place
        self.move(place.across, 0, task=place.across).wait_recv()
        self.move(place.across, 2, task=place.core).start()

    def finish(self):
        place = self.place
        self.move(place.task, 0, task=place.across).wait_send()
        self.move(place.core, 1, task=place.core).wait()
        self.move(place.across, 2, task=place.core).wait()


class Scatter:
    def __init__(self, place, mine, theirs, side, line, sems):
        self.place, self.mine, self.theirs = place, mine, theirs
        self.side, self.line = side, line
        self.side_sent, self.side_landed, self.line_sent, self.line_landed = sems

    def to_side(self, outer):
        return remote(
            self.theirs(outer),
            self.side.at[outer],
            self.side_sent.at[outer],
            self.side_landed.at[outer],
            dp=self.place.side,
        )

    def fold(self, outer):
        return self.mine(outer) if self.side is None else self.side.at[outer]

    def along(self, outer, slot, device):
        return remote(
            self.fold(outer),
            self.line.at[slot],
            self.line_sent.at[outer],
            self.line_landed.at[slot],
            dp=device,
        )

    def start(self):
        outers = self.place.outers
        for near in range(outers // 2):
            self.to_side(outers - 1 - near).start()
            self.to_side(near).start()

    def total(self, outer, *slots):
        rows = self.mine(outer)[...].astype(f32)
        if self.side is not None:
            self.to_side(outer).wait_recv()
            rows += self.side[outer].astype(f32)
        for slot in slots:
            self.along(outer, slot, self.place.dp).wait_recv()
            rows += self.line[slot].astype(f32)
        return rows

    def settle(self, parts, sem):
        for outer in range(self.place.outers):
            self.fold(outer)[...] = self.total(outer).astype(bf16)
            self.to_side(outer).wait_send()
        copy = pltpu.make_async_copy(self.side, parts, sem)
        copy.start()
        return copy

    def hop(self, step):
        place, outers = self.place, self.place.outers

        @pl.when(place.outer == step)
        def _():
            for outer in range(outers - 1, step, -1):
                rows = self.total(outer, *([outer] if step else []))
                self.fold(outer)[...] = rows.astype(bf16)
                self.along(outer, outer, place.up).start()

        @pl.when(place.outer == outers - 1 - step)
        def _():
            for outer in range(outers - 1 - step):
                rows = self.total(outer, *([outer] if step else []))
                self.fold(outer)[...] = rows.astype(bf16)
                slot = outers if outer == outers - 2 - step else outer
                self.along(outer, slot, place.down).start()

    def finish(self, store):
        place, outers = self.place, self.place.outers
        for outer in range(outers):

            @pl.when(place.outer == outer)
            def _():
                below, above = [outer] * (outer > 0), [outers] * (outer < outers - 1)
                store(self.total(outer, *below, *above))
                for other in range(outers):
                    if other != outer:
                        self.along(other, other, place.dp).wait_send()

            if self.side is not None:
                self.to_side(outer).wait_send()


class Turned:
    def __init__(self, place, mine, theirs, refs):
        self.place = place
        self.own = Scatter(place, mine, None, None, refs[0], (None, None, *refs[1:3]))
        self.other = Scatter(place, theirs, None, None, refs[3], (None, None, *refs[4:6]))
        self.stage, self.land, self.sent, self.landed = refs[6:]

    def move(self):
        return remote(self.stage, self.land, self.sent, self.landed, dp=self.place.side)

    def start(self):
        self.own.hop(0)
        self.other.hop(0)

    def hop(self, step):
        if step:
            self.own.hop(step)
            self.other.hop(step)

    def finish(self, store):
        def send(rows):
            self.stage[...] = rows.astype(bf16)
            self.move().start()

        self.other.finish(send)
        self.own.finish(store)

    def add(self, shard):
        self.move().wait()
        shard[...] += self.land[...].astype(f32)


def turned_scratch(outers, tile):
    line = [pltpu.VMEM((outers + 1, *tile), bf16)]
    line += [pltpu.SemaphoreType.DMA((count,)) for count in (outers, outers + 1)]
    return line * 2 + [pltpu.VMEM(tile, bf16)] * 2 + [pltpu.SemaphoreType.DMA] * 2


def scatter_turn(units, stores, turn):
    outers = units[0].place.outers
    for step in range(outers - 1):
        if 0 <= turn - step < len(units):
            units[turn - step].hop(step)
    last = turn - outers + 1
    if 0 <= last < len(units):
        units[last].finish(stores[last])


def blocks_of(place, ref, size, half=()):
    def block(index):
        if half:
            return ref.at[rows_at(2 * index + half[0], size // 2)]
        return ref.at[rows_at(index, size)]

    return (
        lambda outer: block(2 * outer + place.inner),
        lambda outer: block(2 * outer + 1 - place.inner),
    )


def scatter_scratch(units, outers, tiles, side=True, line=True):
    scratch = []
    for unit in units:
        tile = tiles[unit[1]] if isinstance(unit, tuple) else tiles
        if isinstance(unit, tuple) and len(unit) > 2:
            tile = (tile[0] // 2, tile[1])
        for asked, slots in ((side, outers), (line, outers + 1)):
            if asked:
                scratch.append(pltpu.VMEM((slots, *tile), bf16))
        for asked, count in ((side, outers), (side, outers), (line, outers), (line, outers + 1)):
            if asked:
                scratch.append(pltpu.SemaphoreType.DMA((count,)))
    return scratch


def make_scatters(place, blocks, refs, side=True, line=True):
    count = 3 * side + 3 * line
    scatters = []
    for index, (mine, theirs) in enumerate(blocks):
        own = list(refs[index * count : (index + 1) * count])
        buffers = [own.pop(0) if asked else None for asked in (side, line)]
        sems = [own.pop(0) if asked else None for asked in (side, side, line, line)]
        scatters.append(Scatter(place, mine, theirs, *buffers, sems))
    return scatters


class Spread:
    def __init__(self, axis, place, count, land, sent, landed):
        self.axis, self.me, self.count = axis, getattr(place, axis), count
        self.land, self.sent, self.landed = land, sent, landed

    def move(self, source, ahead):
        return remote(
            self.land.at[source],
            self.land.at[source],
            self.sent.at[ahead - 1],
            self.landed.at[ahead - 1],
            **{self.axis: lax.rem(self.me + ahead, self.count)},
        )

    def give(self, rows):
        self.land[self.me] = rows.astype(self.land.dtype)
        for ahead in range(1, self.count):
            self.move(self.me, ahead).start()

    def arrive(self):
        for ahead in range(1, self.count):
            self.move(lax.rem(self.me + self.count - ahead, self.count), ahead).wait_recv()
            self.move(self.me, ahead).wait_send()

    def take(self):
        self.arrive()
        total = self.land[0].astype(f32)
        for index in range(1, self.count):
            total += self.land[index].astype(f32)
        return total


class Deal:
    def __init__(self, place, ref, size, land, sent, landed):
        self.place, self.ref, self.size = place, ref, size
        self.land, self.sent, self.landed = land, sent, landed
        self.count = land.shape[0]

    def block(self, index):
        return self.ref.at[rows_at(index, self.size)]

    def move(self, ahead):
        target = lax.rem(self.place.dp + ahead, self.count)
        return remote(
            self.block(target),
            self.land.at[self.place.dp],
            self.sent.at[ahead - 1],
            self.landed.at[ahead - 1],
            dp=target,
        )

    def start(self):
        for ahead in range(1, self.count):
            self.move(ahead).start()

    def total(self):
        rows = self.block(self.place.dp)[...].astype(f32)
        for ahead in range(1, self.count):
            self.move(ahead).wait()
            source = lax.rem(self.place.dp + self.count - ahead, self.count)
            rows += self.land[source].astype(f32)
        return rows


class Return:
    def __init__(self, place, parts, pieces, land, sent, landed):
        self.place, self.parts, self.pieces = place, parts, pieces
        self.land, self.sent, self.landed = land, sent, landed
        self.size = land.shape[1] // pieces

    def rows(self, piece):
        return pl.ds(piece * self.size, self.size)

    def move(self, way, piece):
        place, rows = self.place, self.rows(piece)
        source = [
            self.parts[0].at[rows],
            self.parts[1].at[rows],
            self.parts[2].at[rows],
        ][way]
        return remote(
            source,
            self.land.at[way, rows],
            self.sent.at[way, piece],
            self.landed.at[way, piece],
            task=place.across if way == 2 else place.core,
        )

    def to_core(self, piece):
        self.move(0, piece).start()

    def by_core(self, piece):
        self.move(1, piece).start()

    def to_across(self, piece):
        rows = self.rows(piece)
        self.move(1, piece).wait_recv()
        joint = self.parts[2][rows, :].astype(f32)
        joint += self.land[1, rows, :].astype(f32)
        self.parts[2][rows, :] = joint.astype(bf16)
        self.move(2, piece).start()

    def finish(self, piece):
        rows = self.rows(piece)
        self.move(0, piece).wait()
        self.move(1, piece).wait_send()
        self.move(2, piece).wait()
        total = self.parts[3][rows, :].astype(f32)
        return total + self.land[0, rows, :].astype(f32) + self.land[2, rows, :].astype(f32)


def attend(packed, mixed, totals, index, between):
    zero = jnp.array(0, bf16)
    rows = rows_at(index, QUERY_FWD)

    def head_pair(pair, _):
        queries, keys, values = (rows_at(pair + part * (D // PAIR), PAIR) for part in range(3))
        key_rows, value_rows = packed[:, keys], packed[:, values]
        query_rows = packed[rows, queries] * jnp.array(HEAD_DIM**-0.5, bf16)
        outs, logs = [], []
        for half in range(2):
            own = jnp.where(half_lanes(QUERY_FWD, half), query_rows, zero)
            scores = dot_rt(own, key_rows)
            top = jnp.max(scores, axis=1, keepdims=True)
            weights = jnp.exp(scores - top)
            total = jnp.sum(weights, axis=1, keepdims=True)
            outs.append(dot(weights.astype(bf16), value_rows) * (1.0 / total))
            logs.append(top + jnp.log(total))
        mixed[rows, queries] = jnp.where(half_lanes(QUERY_FWD, 0), outs[0], outs[1]).astype(bf16)
        lanes = lax.broadcasted_iota(jnp.int32, (QUERY_FWD, 8), 1)
        totals[rows, :] = jnp.where(
            lanes == 2 * pair,
            logs[0],
            jnp.where(lanes == 2 * pair + 1, logs[1], totals[rows, :]),
        )
        between(index * (HEADS // 2) + pair)
        return 0

    lax.fori_loop(0, HEADS // 2, head_pair, 0)


def first_norm(image, gain, bias, normed_first):
    def block(index, _):
        rows = rows_at(index, ROWS)
        unit, _ = normalize(image[rows, :])
        normed_first[rows, :] = (unit * gain[0:1, :] + bias[0:1, :]).astype(bf16)
        return 0

    lax.fori_loop(0, SEQ // ROWS, block, 0)


def number_slots(choices, top_count, experts):
    named = choices[...]
    numbers = lax.broadcasted_iota(jnp.int32, (experts, SEQ), 0)
    used = jnp.zeros((experts, SEQ), f32)
    for choice in range(TOPMAX):
        hit = (named[choice : choice + 1, :] == numbers) & (choice < top_count[0])
        used = used + jnp.where(hit, 1.0, 0.0)
    earlier = lax.broadcasted_iota(jnp.int32, (SEQ, SEQ), 0) < lax.broadcasted_iota(
        jnp.int32, (SEQ, SEQ), 1
    )
    before = dot(used.astype(bf16), jnp.where(earlier, 1.0, 0.0).astype(bf16))
    return jnp.where(used > 0, before, -1.0).astype(jnp.int32)


def mid_block(index, image, gain, bias, w_proj, router, mixed, mid, probs):
    rows = rows_at(index, QUERY_FWD)
    mid_rows = image[rows, :] + dot(mixed[rows, :], w_proj[...])
    mid[rows, :] = mid_rows
    unit, _ = normalize(mid_rows)
    normed_rows = unit * gain[1:2, :] + bias[1:2, :]
    logits = lax.dot_general(
        router[...],
        normed_rows,
        (((1,), (1,)), ((), ())),
        precision=HIGHEST,
        preferred_element_type=f32,
    )
    powers = jnp.exp(logits - jnp.max(logits, axis=0, keepdims=True))
    probs[:, rows] = powers / jnp.sum(powers, axis=0, keepdims=True)
    return normed_rows.astype(bf16)


def forward_kernel(
    top_count,
    image,
    gain,
    bias,
    w_qkv,
    w_proj,
    router,
    choices,
    mid,
    packed,
    mixed,
    logs,
    normed,
    slots,
    gates,
    probs,
    normed_first,
    totals,
):
    first_norm(image, gain, bias, normed_first)
    slots[...] = number_slots(choices, top_count, router.shape[0])
    packed[...] = dot(normed_first[...], w_qkv[...]).astype(bf16)
    totals[...] = jnp.zeros_like(totals)

    def block(index, _):
        attend(packed, mixed, totals, index, lambda point: None)
        normed[rows_at(index, QUERY_FWD), :] = mid_block(
            index, image, gain, bias, w_proj, router, mixed, mid, probs
        )
        return 0

    lax.fori_loop(0, SEQ // QUERY_FWD, block, 0)
    logs[...] = totals[...].T
    gates[...] = jnp.where(slots[...] >= 0, probs[...], 0.0)


def forward_part(top_count, image, gain, bias, w_qkv, w_proj, router, choices):
    experts = router.shape[0]
    return pl.pallas_call(
        forward_kernel,
        out_shape=(
            shape(SEQ, D),
            shape(SEQ, 3 * D, dtype=bf16),
            shape(SEQ, D, dtype=bf16),
            shape(8, SEQ),
            shape(SEQ, D, dtype=bf16),
            shape(experts, SEQ, dtype=jnp.int32),
            shape(experts, SEQ),
            shape(experts, SEQ),
        ),
        in_specs=[SMEM] + [VMEM] * 7,
        out_specs=[VMEM] * 8,
        scratch_shapes=[pltpu.VMEM((SEQ, D), bf16), pltpu.VMEM((SEQ, 8), f32)],
        compiler_params=params(),
    )(top_count, image, gain, bias, w_qkv, w_proj, router, choices)


def forward_sending_kernel(
    outers,
    top_count,
    image,
    cotangent,
    gain,
    bias,
    w_qkv,
    w_proj,
    w_in,
    w_out,
    router,
    choices,
    mid,
    packed,
    mixed,
    logs,
    probs,
    normed_all,
    cot_all,
    slots_all,
    gates_all,
    quarters,
    full_in,
    full_out,
    normed_first,
    totals,
    own_quarter,
    sent,
    landed,
    stay,
    share_sent,
    share_landed,
):
    place = Place(outers)
    task = place.task
    for part in range(4):

        @pl.when(task == part)
        def _():
            own_quarter[...] = w_proj[...] if part == 3 else w_qkv[:, part * D : (part + 1) * D]

    shards = [(own_quarter, w_qkv.shape[0], quarters.at[task], "both")]
    for expert, kind in GATHER_WHOLE + GATHER_SPLIT:
        own, full = ((w_in, full_in), (w_out, full_out))[kind]
        mode = "line" if (expert, kind) in GATHER_SPLIT else "both"
        shards.append((own.at[expert], own.shape[1], full.at[expert], mode))
    gather = Gather(place, shards, sent, landed, stay)
    routed = range(1, len(shards))
    cot_all[task] = cotangent[...].astype(bf16)
    place.greet()
    gather.start(0)

    def share(index, view):
        return Share(place, view, share_sent.at[index], share_landed.at[index])

    cot = share(0, lambda source: cot_all.at[source])
    slot = share(1, lambda source: slots_all.at[source])
    gate = share(2, lambda source: gates_all.at[source])
    def run(acts):
        for unit, hop in acts:
            if hop:
                gather.step(routed[unit], hop)
            else:
                gather.start(routed[unit])

    for unit in routed[:AHEAD]:
        gather.start(unit)
    cot.start()
    first_norm(image, gain, bias, normed_first)
    for hop in range(1, outers):
        gather.step(0, hop)
    for unit in routed[AHEAD:NEXT]:
        gather.start(unit)
    gather.finish(0)
    quarter = share(3 + SEQ // QUERY_FWD, lambda source: quarters.at[source])
    quarter.start()
    slots_all[task] = number_slots(choices, top_count, router.shape[0])
    slot.start()
    totals[...] = jnp.zeros_like(totals)
    run(FORWARD_FIRST)
    quarter.relay()
    quarter.finish()
    for part in range(3):
        packed[:, part * D : (part + 1) * D] = dot(normed_first[...], quarters[part]).astype(bf16)
    cot.relay()
    slot.relay()

    def chunk(index):
        return share(3 + index, lambda source: normed_all.at[source, rows_at(index, QUERY_FWD)])

    blocks = SEQ // QUERY_FWD

    def block(index, _):
        def between(point):
            for at, acts in FORWARD_POINTS.items():
                pl.when(point == at)(lambda acts=acts: run(acts))

        attend(packed, mixed, totals, index, between)
        normed_all[task, rows_at(index, QUERY_FWD), :] = mid_block(
            index, image, gain, bias, quarters.at[3], router, mixed, mid, probs
        )
        chunk(index).start()
        pl.when(index > 0)(lambda: chunk(index - 1).relay())
        return 0

    lax.fori_loop(0, blocks, block, 0)
    gates_all[task] = jnp.where(slots_all[task] >= 0, probs[...], 0.0)
    gate.start()
    logs[...] = totals[...].T
    run(FORWARD_THEN[0])
    chunk(blocks - 1).relay()
    gate.relay()
    run(FORWARD_THEN[1])
    for one in [cot, slot, gate] + [chunk(index) for index in range(blocks)]:
        one.finish()
    for unit in routed:
        gather.finish(unit)


def forward_sending(top_count, image, cotangent, gain, bias, shards, router, choices):
    w_qkv, w_proj, w_in, w_out = shards
    experts, size = router.shape[0], lax.axis_size("dp")
    groups, early = lax.axis_size("task"), 1 + GATHER_SPLIT[-1][0]
    units, shares = 1 + len(GATHER_WHOLE + GATHER_SPLIT), 4 + SEQ // QUERY_FWD
    return pl.pallas_call(
        functools.partial(forward_sending_kernel, size // 2),
        out_shape=(
            shape(SEQ, D),
            shape(SEQ, 3 * D, dtype=bf16),
            shape(SEQ, D, dtype=bf16),
            shape(8, SEQ),
            shape(experts, SEQ),
            shape(groups, SEQ, D, dtype=bf16),
            shape(groups, SEQ, D, dtype=bf16),
            shape(groups, experts, SEQ, dtype=jnp.int32),
            shape(groups, experts, SEQ),
            shape(groups, D, D, dtype=bf16),
            shape(early, D, FF, dtype=bf16),
            shape(early, FF, D, dtype=bf16),
        ),
        in_specs=[SMEM] + [VMEM] * 10,
        out_specs=[VMEM] * 10 + [ANY] * 2,
        scratch_shapes=[
            pltpu.VMEM((SEQ, D), bf16),
            pltpu.VMEM((SEQ, 8), f32),
            pltpu.VMEM(w_proj.shape, bf16),
            *gather_semaphores(units, size),
            pltpu.SemaphoreType.DMA((units,)),
            pltpu.SemaphoreType.DMA((shares, 3)),
            pltpu.SemaphoreType.DMA((shares, 3)),
        ],
        compiler_params=params(collective_id=0, has_side_effects=True),
    )(top_count, image, cotangent, gain, bias, w_qkv, w_proj, w_in, w_out, router, choices)


def slot_hits(slots, source, expert):
    return lax.broadcasted_iota(jnp.int32, (CAP, SEQ), 0) == slots[source, pl.ds(expert, 1), :]


def ones_at(hits):
    return jnp.where(hits, 1.0, 0.0).astype(bf16)


def dispatch(operands, work, expert, first, block, source):
    tokens, slots, gates = operands[:3]
    rows_in, rows_grad, rows_cot, rows_gate = work[:4]
    own = slice(block * CAP, (block + 1) * CAP)
    hits = slot_hits(slots, source, first + expert)
    both = dot(ones_at(hits), tokens[source])
    gate = jnp.sum(
        jnp.where(hits, gates[source, pl.ds(first + expert, 1), :], 0.0), axis=1, keepdims=True
    )
    rows_in[own, :] = both[:, :D].astype(bf16)
    rows_cot[own, :] = both[:, D:].astype(bf16)
    rows_grad[own, :] = (gate * both[:, D:]).astype(bf16)
    rows_gate[own, :] = jnp.broadcast_to(gate, (CAP, 128))


def hidden_tiles(operands, work, slot, start, count):
    w_in, w_out = operands[3:]
    rows_in, rows_grad, _, _, hidden, grad_pre, _ = work

    def tile(index, _):
        units = rows_at(index // count, FF_TILE)
        rows = rows_at(start + lax.rem(index, count), ROW_TILE)
        pre = dot(rows_in[rows, :], w_in[slot, :, units])
        grad_hidden = dot_rt(rows_grad[rows, :], w_out[slot, units, :])
        share = 0.5 * lax.erf(pre * ROOT_HALF) + 0.5
        slope = share + pre * (NORMAL * jnp.exp(-0.5 * pre * pre))
        hidden[rows, units] = (pre * share).astype(bf16)
        grad_pre[rows, units] = (grad_hidden * slope).astype(bf16)
        return 0

    lax.fori_loop(0, (FF // FF_TILE) * count, tile, 0)


def expert_rows_out(operands, work, grad_gates, expert, first, slot, block, source):
    slots, (w_in, w_out) = operands[1], operands[3:]
    _, _, rows_cot, rows_gate, hidden, grad_pre, sent = work
    own = slice(block * CAP, (block + 1) * CAP)
    kept = rows_at(expert, CAP)
    out_rows = dot(hidden[own, :], w_out[slot]).astype(bf16).astype(f32)
    sent[source, kept, :D] = (rows_gate[own, 0:1] * out_rows).astype(bf16)
    sent[source, kept, D:] = dot_rt(grad_pre[own, :], w_in[slot]).astype(bf16)
    grad_gate = jnp.sum(rows_cot[own, :].astype(f32) * out_rows, axis=1, keepdims=True)
    hits = slot_hits(slots, source, first + expert)
    grad_gates[source, pl.ds(expert, 1), :] = jnp.sum(
        jnp.where(hits, grad_gate, 0.0), axis=0, keepdims=True
    )


def weight_grads(work, grads, expert):
    rows_in, rows_grad, _, _, hidden, grad_pre, _ = work
    grads[0][expert] = dot_lt(rows_in[...], grad_pre[...]).astype(bf16)
    grads[1][expert] = dot_lt(rows_grad[...], hidden[...]).astype(bf16).T


def one_expert(operands, work, grads, expert, first, slot, sources, between, halfway=None):
    halves = 1 if halfway is None else 2
    size, tiles = len(sources) // halves, len(sources) * CAP // ROW_TILE // halves
    between(0)
    for block, source in enumerate(sources):
        dispatch(operands, work, expert, first, block, source)
    between(1)
    for half in range(halves):
        hidden_tiles(operands, work, slot, half * tiles, tiles)
        between(2 + half * 2)
        for block in range(half * size, (half + 1) * size):
            expert_rows_out(
                operands, work, grads[2], expert, first, slot, block, sources[block]
            )
        if half + 1 < halves:
            halfway()
    between(3 if halves == 1 else 5)
    weight_grads(work, grads, expert)
    between(4 if halves == 1 else 6)


def combine(slots, first, local_count, sent, columns, source, store):
    size = SEQ // RETURNS
    mine = [slots[source, pl.ds(first + expert, 1), :] for expert in range(local_count)]
    columns[...] = jnp.concatenate(mine, axis=0).T
    for piece in range(RETURNS):
        rows = pl.ds(piece * size, size)
        lanes = lax.broadcasted_iota(jnp.int32, (size, CAP), 1)
        picks = [
            ones_at(lanes == columns[rows, expert : expert + 1]) for expert in range(local_count)
        ]
        back = dot(jnp.concatenate(picks, axis=1), sent[source])
        store(piece, rows, back[:, :D].astype(bf16), back[:, D:].astype(bf16))


def expert_scratch(groups, local_count, experts):
    width = groups * CAP
    return [
        pltpu.VMEM((width, D), bf16),
        pltpu.VMEM((width, D), bf16),
        pltpu.VMEM((width, D), bf16),
        pltpu.VMEM((width, 128), f32),
        pltpu.VMEM((width, FF), bf16),
        pltpu.VMEM((width, FF), bf16),
        pltpu.VMEM((groups, local_count * CAP, 2 * D), bf16),
        pltpu.VMEM((SEQ, local_count), jnp.int32),
    ]


def expert_kernel(*refs):
    operands, grads, (mixes, grad_normed) = refs[:5], refs[5:8], refs[8:10]
    work, columns = refs[10:17], refs[17]
    groups, local_count = operands[0].shape[0], operands[3].shape[0]

    def body(expert, _):
        one_expert(
            operands, work, grads, expert, 0, expert, range(groups), lambda point: None
        )
        return 0

    lax.fori_loop(0, local_count, body, 0)
    for source in range(groups):

        def store(piece, rows, mix, grad, source=source):
            mixes[source, rows, :] = mix
            grad_normed[source, rows, :] = grad

        combine(operands[1], 0, local_count, work[6], columns, source, store)


def expert_part(*operands):
    groups, local_count = operands[0].shape[0], operands[3].shape[0]
    return pl.pallas_call(
        expert_kernel,
        out_shape=(
            shape(local_count, D, FF, dtype=bf16),
            shape(local_count, FF, D, dtype=bf16),
            shape(groups, local_count, SEQ),
            shape(groups, SEQ, D, dtype=bf16),
            shape(groups, SEQ, D, dtype=bf16),
        ),
        in_specs=[VMEM] * 5,
        out_specs=[VMEM] * 5,
        scratch_shapes=expert_scratch(groups, local_count, operands[1].shape[1]),
        compiler_params=params(),
    )(*operands)


def expert_sending_kernel(outers, *refs):
    normed_all, cot_all, slots, gates, early_in, early_out, w_in, w_out = refs[:8]
    late_in, late_out, gate_all, mixes, grad_rows, shard_in, shard_out, parts_in, parts_out = refs[8:17]
    full_in, full_out = refs[17:19]
    work, columns = refs[19:26], refs[26]
    both, slot_in, slot_out, grad_in, grad_out, grad_gates, land, first_parts = refs[27:35]
    sent, landed, gate_sent, gate_landed, mix_sem, late_sem, slot_sem, token_sem = refs[35:43]
    part_sem, gather_sems, scatter_refs = refs[43], refs[44:46], refs[46:]
    place = Place(outers)
    groups, local_count, size = both.shape[0], grad_in.shape[0], 2 * outers
    late = local_count - EARLY_EXPERTS
    first = place.task * local_count
    grads, shares = (grad_in, grad_out), (w_in.shape[1], w_out.shape[1])

    def tokens():
        return [
            pltpu.make_async_copy(
                whole.at[source],
                both.at[source, :, pl.ds(kind * D, D)],
                token_sem.at[kind, source],
            )
            for source in range(groups)
            for kind, whole in enumerate((normed_all, cot_all))
        ]

    def load(expert):
        slot, copies = expert % EARLY_EXPERTS, []
        for kind in range(2):
            target, sem = (slot_in, slot_out)[kind].at[slot], slot_sem.at[slot, kind]
            early, own = (early_in, early_out)[kind], (w_in, w_out)[kind]
            full = (full_in, full_out)[kind]
            if expert < EARLY_EXPERTS:
                copies.append(pltpu.make_async_copy(early.at[expert], target, sem.at[0]))
                continue
            for ahead in range(size):
                block = lax.rem(place.dp + ahead, size)
                rows = rows_at(block, shares[kind])
                source = full.at[expert - EARLY_EXPERTS, rows]
                if (expert, kind) in GATHER_SPLIT:
                    if ahead % 2 == 0:
                        source = early.at[expert, rows]
                elif ahead == 0:
                    source = own.at[expert]
                copies.append(pltpu.make_async_copy(source, target.at[rows], sem.at[ahead]))
        return copies

    def keep(expert):
        return [
            pltpu.make_async_copy(
                grads[kind].at[EARLY_EXPERTS + expert],
                (late_in, late_out)[kind].at[expert],
                late_sem.at[expert, kind],
            )
            for kind in range(2)
        ]

    for copy in tokens() + load(0):
        copy.start()
    place.greet(far=True)
    shards = []
    for expert, kind in GATHER_LATE + GATHER_SPLIT:
        full = (full_in, full_out)[kind].at[expert - EARLY_EXPERTS]
        if (expert, kind) in GATHER_SPLIT:
            shards.append(((early_in, early_out)[kind].at[expert], shares[kind], full, "side"))
        else:
            shards.append(((w_in, w_out)[kind].at[expert], shares[kind], full, "turned"))
    gather = Gather(place, shards, *gather_sems, None)
    turned = range(len(GATHER_LATE))
    for unit in range(len(shards)):
        gather.start(unit)
    for copy in load(1):
        copy.start()
    per_full, per_side = 6 * len(SCATTER_EARLY[1:]), 3 * len(SCATTER_SPLIT)

    def scatters(units, refs, **parts):
        return make_scatters(
            place,
            [blocks_of(place, grads[kind].at[expert], shares[kind]) for expert, kind in units],
            refs,
            **parts,
        )

    expert, kind = SCATTER_EARLY[0]
    turned_scatter = Turned(
        place,
        *blocks_of(place, grads[kind].at[expert], shares[kind]),
        scatter_refs[per_full + per_side :],
    )
    whole = [turned_scatter] + scatters(SCATTER_EARLY[1:], scatter_refs[:per_full])
    split = scatters(SCATTER_SPLIT, scatter_refs[per_full : per_full + per_side], line=False)
    stores, keeps = [], []
    for expert, kind in SCATTER_EARLY:

        def store(rows, shard=(shard_in, shard_out)[kind], expert=expert):
            shard[expert] = rows

        stores.append(store)
    for index, (_, kind) in enumerate(SCATTER_SPLIT):
        at = [other[1] for other in SCATTER_SPLIT[:index]].count(kind)

        keeps.append((parts_in, parts_out)[kind].at[at])
    steps = {}

    def plan(expert, point, *acts):
        steps.setdefault((expert, point), []).extend(acts)

    plan(0, 0, *[copy.wait for copy in tokens()])
    for expert in range(EARLY_EXPERTS):
        plan(expert, 1, *[copy.wait for copy in load(expert)])
    for unit in turned:
        for hop, at in enumerate(GATHER_POINTS[GATHER_LATE[unit][0]]):
            plan(*at, lambda unit=unit, hop=hop: gather.step(unit, hop))
    for expert in range(EARLY_EXPERTS, local_count):
        units = [
            unit
            for unit, (owner, _) in enumerate(GATHER_LATE + GATHER_SPLIT)
            if owner == expert
        ]
        plan(expert, 0, *[lambda unit=unit: gather.finish(unit) for unit in units])
        plan(expert, 0, *[copy.start for copy in load(expert)])
        plan(expert, 1, *[copy.wait for copy in load(expert)])
        point = 4 if expert < local_count - 1 else 6
        plan(expert, point, *[copy.start for copy in keep(expert - EARLY_EXPERTS)])
    for index, (expert, _) in enumerate(SCATTER_EARLY):
        plan(expert, 4, whole[index].start)
    for index, (expert, _) in enumerate(SCATTER_SPLIT):
        plan(expert, 4, split[index].start)
    for turn, at in SCATTER_POINTS.items():
        plan(*at, lambda turn=turn: scatter_turn(whole, stores, turn))

    operands = (both, slots, gates, slot_in, slot_out)
    every_grad = (grad_in, grad_out, grad_gates)
    sources = (place.far, place.across, place.core, place.task)

    def body(expert, _):
        def between(point):
            for at in range(local_count - 1):
                acts = steps.get((at, point))
                if acts:

                    @pl.when(expert == at)
                    def _():
                        for act in acts:
                            act()

        one_expert(
            operands,
            work,
            every_grad,
            expert,
            first,
            lax.rem(expert, EARLY_EXPERTS),
            sources,
            between,
        )
        return 0

    lax.fori_loop(0, local_count - 1, body, 0)
    hidden, grad_pre = work[4], work[5]

    def part(ref, block):
        return ref.at[pl.ds(0, SEQ), pl.ds(block * D, D)]

    parts = [first_parts.at[0], first_parts.at[1], part(hidden, 0), part(hidden, 1)]
    mix_parts = [first_parts.at[2], first_parts.at[2], part(grad_pre, 0), part(grad_pre, 1)]
    back = Return(
        place,
        (parts[2], parts[0], parts[1], parts[3]),
        RETURNS,
        land,
        sent,
        landed,
    )
    sends = (back.by_core, back.to_across, back.to_core, None)

    def mix_copy(block):
        return pltpu.make_async_copy(
            mix_parts[block], mixes.at[sources[block]], mix_sem.at[block]
        )

    def returned(block):
        def store(piece, rows, mix, grad):
            mix_parts[block][rows, :] = mix
            parts[block][rows, :] = grad
            if sends[block]:
                sends[block](piece)

        combine(slots, first, local_count, work[6], columns, sources[block], store)
        mix_copy(block).start()

    def halfway():
        returned(0)
        mix_copy(0).wait()
        returned(1)
        scatter_turn(whole, stores, 2)

    def last(point):
        for act in steps.get((local_count - 1, point), ()):
            act()

    one_expert(
        operands,
        work,
        every_grad,
        local_count - 1,
        first,
        (local_count - 1) % EARLY_EXPERTS,
        sources,
        last,
        halfway,
    )
    gate_all[place.task] = grad_gates[place.task]
    peers = (place.core, place.across, place.far)

    def gate_move(way):
        return remote(
            grad_gates.at[peers[way]],
            gate_all.at[place.task],
            gate_sent.at[way],
            gate_landed.at[way],
            task=peers[way],
        )

    for way in range(3):
        gate_move(way).start()
    returned(2)
    returned(3)
    for turn in range(4, len(whole) + outers - 1):
        scatter_turn(whole, stores, turn)
    expert, kind = SCATTER_EARLY[0]
    turned_scatter.add((shard_in, shard_out)[kind].at[expert])
    settled = [
        one.settle(keeps[index], part_sem.at[index]) for index, one in enumerate(split)
    ]
    for piece in range(RETURNS):
        grad_rows[back.rows(piece), :] = back.finish(piece)
    for way in range(3):
        gate_move(way).wait()
    for block in range(1, groups):
        mix_copy(block).wait()
    for expert in range(late):
        for copy in keep(expert):
            copy.wait()
    for copy in settled:
        copy.wait()


def kinds(units, kind):
    return sorted({unit[0] for unit in units if unit[1] == kind})


def expert_sending(*operands):
    groups, experts = operands[2].shape[:2]
    local_count, thin = operands[6].shape[:2]
    wide, size = operands[7].shape[1], lax.axis_size("dp")
    late, outers = local_count - EARLY_EXPERTS, size // 2
    tiles = ((thin, FF), (wide, D))
    return pl.pallas_call(
        functools.partial(expert_sending_kernel, outers),
        out_shape=(
            shape(late, D, FF, dtype=bf16),
            shape(late, FF, D, dtype=bf16),
            shape(groups, local_count, SEQ),
            shape(groups, SEQ, D, dtype=bf16),
            shape(SEQ, D),
            *[shape(len(kinds(SCATTER_EARLY, kind)), *tiles[kind]) for kind in range(2)],
            *[
                shape(len(kinds(SCATTER_SPLIT, kind)), outers, *tiles[kind], dtype=bf16)
                for kind in range(2)
            ],
            shape(late, D, FF, dtype=bf16),
            shape(late, FF, D, dtype=bf16),
        ),
        in_specs=[ANY] * 2 + [VMEM] * 2 + [ANY] * 4,
        out_specs=[ANY] * 2 + [VMEM, ANY] + [VMEM] * 3 + [ANY] * 4,
        scratch_shapes=expert_scratch(groups, local_count, experts)
        + [
            pltpu.VMEM((groups, SEQ, 2 * D), bf16),
            pltpu.VMEM((EARLY_EXPERTS, D, FF), bf16),
            pltpu.VMEM((EARLY_EXPERTS, FF, D), bf16),
            pltpu.VMEM((local_count, D, FF), bf16),
            pltpu.VMEM((local_count, FF, D), bf16),
            pltpu.VMEM((groups, local_count, SEQ), f32),
            pltpu.VMEM((3, SEQ, D), bf16),
            pltpu.VMEM((3, SEQ, D), bf16),
            pltpu.SemaphoreType.DMA((3, RETURNS)),
            pltpu.SemaphoreType.DMA((3, RETURNS)),
            pltpu.SemaphoreType.DMA((3,)),
            pltpu.SemaphoreType.DMA((3,)),
            pltpu.SemaphoreType.DMA((groups,)),
            pltpu.SemaphoreType.DMA((late, 2)),
            pltpu.SemaphoreType.DMA((EARLY_EXPERTS, 2, size)),
            pltpu.SemaphoreType.DMA((2, groups)),
            pltpu.SemaphoreType.DMA((len(SCATTER_SPLIT),)),
        ]
        + gather_semaphores(len(GATHER_LATE + GATHER_SPLIT), size)
        + scatter_scratch(SCATTER_EARLY[1:], outers, tiles)
        + scatter_scratch(SCATTER_SPLIT, outers, tiles, line=False)
        + turned_scratch(outers, tiles[SCATTER_EARLY[0][1]]),
        compiler_params=params(collective_id=1, has_side_effects=True),
    )(*operands)


def attend_back(packed, grad_mixed, logs, grad_packed, grad_keys, grad_values, between, done):
    zero = jnp.array(0, bf16)
    blocks = SEQ // QUERY_BWD

    def head_pair(pair):
        queries, keys, values = (
            slice(part * D + pair * PAIR, part * D + (pair + 1) * PAIR) for part in range(3)
        )
        key_rows, value_rows = packed[:, keys], packed[:, values]

        def block(index, _):
            rows = rows_at(index, QUERY_BWD)
            query_rows = packed[rows, queries] * jnp.array(HEAD_DIM**-0.5, bf16)
            grad_rows = grad_mixed[rows, queries]
            grad_query, part_keys, part_values = [], 0.0, 0.0
            for half in range(2):
                lanes = half_lanes(QUERY_BWD, half)
                own = jnp.where(lanes, query_rows, zero)
                own_grad = jnp.where(lanes, grad_rows, zero)
                head = 2 * pair + half
                probs = jnp.exp(dot_rt(key_rows, own) - logs[head : head + 1, rows])
                grad_probs = dot_rt(value_rows, own_grad)
                mean = jnp.sum(probs * grad_probs, axis=0, keepdims=True)
                grad_scores = (probs * (grad_probs - mean)).astype(bf16)
                part_values += dot(probs.astype(bf16), own_grad)
                part_keys += dot(grad_scores, own)
                grad_query.append(dot_lt(grad_scores, key_rows))
            grad_packed[rows, queries] = (
                jnp.where(half_lanes(QUERY_BWD, 0), grad_query[0], grad_query[1])
                * HEAD_DIM**-0.5
            ).astype(bf16)
            grad_keys[...] = jnp.where(index == 0, part_keys, grad_keys[...] + part_keys)
            grad_values[...] = jnp.where(index == 0, part_values, grad_values[...] + part_values)
            between(pair, index)
            return 0

        lax.fori_loop(0, blocks, block, 0)
        grad_packed[:, keys] = grad_keys[...].astype(bf16)
        grad_packed[:, values] = grad_values[...].astype(bf16)
        done(pair, (queries, keys, values))

    for pair in range(HEADS // 2):
        head_pair(pair)


def second_back(
    grad_rows, cotangent, gain, bias, mid, w_proj, router, grad_logits, grad_norm, grad_router, outs
):
    grad_mid, grad_low, grad_mixed = outs
    grad_norm[...] = jnp.zeros_like(grad_norm)
    grad_router[...] = jnp.zeros_like(grad_router)
    for index in range(SEQ // ROWS):
        rows = slice(index * ROWS, (index + 1) * ROWS)
        mid_rows = mid[rows, :]
        own_logits = grad_logits[:, rows]
        grad_in_rows = grad_rows(rows) + lax.dot_general(
            own_logits,
            router[...],
            (((0,), (0,)), ((), ())),
            precision=HIGHEST,
            preferred_element_type=f32,
        )
        grad_in, grad_gain, grad_bias, unit = norm_back(mid_rows, grad_in_rows, gain[1:2, :])
        grad_router[...] += jnp.dot(
            own_logits,
            unit * gain[1:2, :] + bias[1:2, :],
            precision=HIGHEST,
            preferred_element_type=f32,
        )
        grad_norm[1:2, :] += grad_gain
        grad_norm[3:4, :] += grad_bias
        grad_mid_rows = cotangent[rows, :] + grad_in
        grad_mid[rows, :] = grad_mid_rows
        low_rows = grad_mid_rows.astype(bf16)
        grad_low[rows, :] = low_rows
        grad_mixed[rows, :] = dot_rt(low_rows, w_proj[...]).astype(bf16)


def first_back(image, gain, parts, grad_packed, grad_mid, grad_image, grad_norm):
    def block(index, _):
        rows = rows_at(index, ROWS)
        grad_rows = sum(
            dot_rt(grad_packed[rows, part * D : (part + 1) * D], parts(part)) for part in range(3)
        )
        grad_in, grad_gain, grad_bias, _ = norm_back(image[rows, :], grad_rows, gain[0:1, :])
        grad_image[rows, :] = grad_mid[rows, :] + grad_in
        grad_norm[0:1, :] += grad_gain
        grad_norm[2:3, :] += grad_bias
        return 0

    lax.fori_loop(0, SEQ // ROWS, block, 0)


def logit_grads(probs, grad_gates):
    route = jnp.concatenate([grad_gates[group] for group in range(grad_gates.shape[0])], axis=0)
    return probs[...] * (route - jnp.sum(probs[...] * route, axis=0, keepdims=True))


def backward_scratch():
    return [
        pltpu.VMEM((SEQ, D), f32),
        pltpu.VMEM((SEQ, D), bf16),
        pltpu.VMEM((SEQ, D), bf16),
        pltpu.VMEM((SEQ, 3 * D), bf16),
        pltpu.VMEM((SEQ, PAIR), f32),
        pltpu.VMEM((SEQ, PAIR), f32),
        pltpu.VMEM((SEQ, D), bf16),
    ]


def backward_kernel(*refs):
    image, cotangent, gain, bias, mid, w_qkv, w_proj, router = refs[:8]
    packed, mixed, logs, mixes, grad_normed, grad_gates, probs = refs[8:15]
    activations, grad_image, grad_norm, grad_router, grad_shared = refs[15:20]
    grad_mid, grad_low, grad_mixed, grad_packed, grad_keys, grad_values, normed_first = refs[20:]
    groups = mixes.shape[0]

    def added(parts, rows):
        total = parts[0, rows, :].astype(f32)
        for source in range(1, groups):
            total += parts[source, rows, :].astype(f32)
        return total

    activations[...] = mid[...] + added(mixes, slice(None))
    second_back(
        lambda rows: added(grad_normed, rows),
        cotangent,
        gain,
        bias,
        mid,
        w_proj,
        router,
        logit_grads(probs, grad_gates),
        grad_norm,
        grad_router,
        (grad_mid, grad_low, grad_mixed),
    )
    first_norm(image, gain, bias, normed_first)
    grad_shared[:, 3 * D :] = dot_lt(mixed[...], grad_low[...]).astype(bf16)
    attend_back(
        packed,
        grad_mixed,
        logs,
        grad_packed,
        grad_keys,
        grad_values,
        lambda pair, index: None,
        lambda pair, columns: None,
    )
    first_back(
        image,
        gain,
        lambda part: w_qkv[:, part * D : (part + 1) * D],
        grad_packed,
        grad_mid,
        grad_image,
        grad_norm,
    )
    grad_shared[:, : 3 * D] = dot_lt(normed_first[...], grad_packed[...]).astype(bf16)


def backward_part(*operands):
    router = operands[7]
    return pl.pallas_call(
        backward_kernel,
        out_shape=(
            shape(SEQ, D),
            shape(SEQ, D),
            shape(4, D),
            shape(router.shape[0], D),
            shape(D, 4 * D, dtype=bf16),
        ),
        in_specs=[VMEM] * 15,
        out_specs=[VMEM] * 5,
        scratch_shapes=backward_scratch(),
        compiler_params=params(),
    )(*operands)


def backward_sending_kernel(outers, groups, *refs):
    whole, (gain, bias, router, logs, grad_gates, probs) = refs[:9], refs[9:15]
    mixes_all, late_in, late_out = refs[15:18]
    activations, grad_image, grad_gain, grad_bias, grad_router, shard_qkv, shard_proj = refs[18:25]
    shard_in, shard_out = refs[25:27]
    grad_mid, grad_low, grad_mixed, grad_packed, grad_keys, grad_values, normed_first = refs[27:34]
    norm_sums, router_sums, shared, mixes, land, back_sent, back_landed = refs[34:41]
    own_shared, shared_land, shared_sent, shared_landed = refs[41:45]
    here, here_sem, result_sem = refs[45:54], refs[54], refs[55]
    parts_in, parts_out, image, cotangent, mid, quarters, packed, mixed, grad_rows = here
    refs = refs[56:]
    late_grads = sorted({unit[:2] for unit in SCATTER_LATE})
    mix_sem, grad_sem, grad_refs = refs[0], refs[1], refs[2 : 2 + len(late_grads)]
    refs = refs[2 + len(late_grads) :]
    inputs = [
        pltpu.make_async_copy(source, target, here_sem.at[index])
        for index, (source, target) in enumerate(zip(whole, here))
    ]
    place = Place(outers)
    size, pieces = 2 * outers, HEADS // 2 + 1
    shards = (shard_in, shard_out)
    loads = [
        pltpu.make_async_copy(
            (late_in, late_out)[kind].at[expert - EARLY_EXPERTS],
            grad_refs[index],
            grad_sem.at[index],
        )
        for index, (expert, kind) in enumerate(late_grads)
    ]
    mix_load = pltpu.make_async_copy(mixes_all, mixes, mix_sem)
    for copy in (*inputs[:2], *loads, *inputs[2:], mix_load):
        copy.start()
    place.greet_all(groups)
    at = 6 * len(SCATTER_LATE)
    late = make_scatters(
        place,
        [
            blocks_of(
                place, grad_refs[late_grads.index(unit[:2])], shards[unit[1]].shape[1], unit[2:]
            )
            for unit in SCATTER_LATE
        ],
        refs[:at],
    )
    split_blocks = []
    for index, (_, kind) in enumerate(SCATTER_SPLIT):
        number = [other[1] for other in SCATTER_SPLIT[:index]].count(kind)
        split_blocks.append(
            (
                lambda outer, parts=(parts_in, parts_out)[kind], number=number: parts.at[
                    number, outer
                ],
                None,
            )
        )
    split = make_scatters(place, split_blocks, refs[at:], side=False)
    at += 3 * len(SCATTER_SPLIT)
    deal = Deal(place, own_shared, shard_proj.shape[0], *refs[at : at + 3])
    at += 3
    norms = Spread("dp", place, size, *refs[at : at + 3])
    norms_task = Spread("task", place, groups, *refs[at + 3 : at + 6])
    routers = Spread("dp", place, size, *refs[at + 6 : at + 9])
    quarter = Spread("task", place, groups, *refs[at + 9 : at + 12])
    stores = []
    for unit in SCATTER_SPLIT + SCATTER_LATE:
        number = kinds(SCATTER_SPLIT + SCATTER_LATE, unit[1]).index(unit[0])

        def store(rows, shard=shards[unit[1]], number=number, half=unit[2:]):
            start = half[0] * rows.shape[0] if half else 0
            shard[number, start : start + rows.shape[0], :] = rows

        stores.append(store)
    for copy in inputs[:2]:
        copy.wait()
    for one in split:
        one.hop(0)
    for index, one in enumerate(late):
        unit = SCATTER_LATE[index]
        if unit[2:] in ((), (0,)):
            loads[late_grads.index(unit[:2])].wait()
        one.start()
    mix_load.wait()
    roles = (place.core, place.far, place.across, place.task)
    back = Return(
        place, [mixes.at[role] for role in roles], 1, land, back_sent, back_landed
    )
    back.by_core(0)
    back.to_core(0)
    for copy in inputs[2:]:
        copy.wait()
    second_back(
        lambda rows: grad_rows[rows, :],
        cotangent,
        gain,
        bias,
        mid,
        quarters.at[3],
        router,
        logit_grads(probs, grad_gates),
        norm_sums,
        router_sums,
        (grad_mid, grad_low, grad_mixed),
    )
    back.to_across(0)
    first_norm(image, gain, bias, normed_first)
    shared[pieces - 1] = dot_lt(mixed[...], grad_low[...]).astype(bf16)
    routers.give(router_sums[...])
    blocks = SEQ // QUERY_BWD
    units, keeps = split + late, stores
    names = dict(zip("stuvwxyz", range(len(units))))
    joined = Return(
        place,
        [shared.at[role] for role in roles],
        1,
        shared_land,
        shared_sent,
        shared_landed,
    )

    def run(acts):
        for act in acts:
            unit, hop = names[act[0]], int(act[1])
            if hop < outers - 1:
                units[unit].hop(hop)
            else:
                units[unit].finish(keeps[unit])

    def between(pair, index):
        for at, acts in BACKWARD_POINTS.items():
            if at // blocks == pair:
                pl.when(index == at % blocks)(lambda acts=acts: run(acts))

    def done(pair, columns):
        both = jnp.concatenate([grad_packed[:, part] for part in columns], axis=1)
        shared[pair] = dot_lt(normed_first[...], both).astype(bf16)

    attend_back(
        packed, grad_mixed, logs, grad_packed, grad_keys, grad_values, between, done
    )
    joined.by_core(0)
    joined.to_core(0)
    first_back(
        image,
        gain,
        lambda part: quarters[part],
        grad_packed,
        grad_mid,
        grad_mid,
        norm_sums,
    )
    results = [
        pltpu.make_async_copy(grad_mid, grad_image, result_sem.at[0]),
        pltpu.make_async_copy(mid, activations, result_sem.at[1]),
    ]
    results[0].start()
    norms.give(norm_sums[...])
    joined.to_across(0)
    mid[...] = mid[...] + back.finish(0)
    results[1].start()
    run(BACKWARD_THEN[0])
    own_shared[...] = joined.finish(0).astype(bf16)
    deal.start()
    grad_router[...] = routers.take()
    norms_task.give(norms.take())
    run(BACKWARD_THEN[1])
    quarter.give(deal.total())
    run(BACKWARD_THEN[2])
    rows = norms_task.take()
    grad_gain[...] = rows[:2]
    grad_bias[...] = rows[2:4]
    quarter.arrive()
    shard_proj[...] = quarter.land[pieces - 1]
    for piece in range(pieces - 1):
        for part in range(3):
            column = part * D + piece * PAIR
            shard_qkv[:, column : column + PAIR] = quarter.land[
                piece, :, part * PAIR : (part + 1) * PAIR
            ]
    run(BACKWARD_THEN[3])
    for copy in results:
        copy.wait()


def backward_sending(*operands):
    router, whole = operands[11], operands[:9]
    experts, size = router.shape[0], lax.axis_size("dp")
    outers, thin, wide, pieces = size // 2, D // size, FF // size, HEADS // 2 + 1
    groups = lax.axis_size("task")
    tiles, wholes = ((thin, FF), (wide, D)), ((D, FF), (FF, D))
    ends = SCATTER_SPLIT + SCATTER_LATE
    late_grads = sorted({unit[:2] for unit in SCATTER_LATE})

    def spread(peers, *dims):
        return [pltpu.VMEM((peers, *dims), f32)] + [pltpu.SemaphoreType.DMA((peers - 1,))] * 2

    return pl.pallas_call(
        functools.partial(backward_sending_kernel, outers, groups),
        out_shape=(
            shape(SEQ, D),
            shape(SEQ, D),
            shape(2, D),
            shape(2, D),
            shape(experts, D),
            shape(thin, 3 * D),
            shape(thin, D),
            *[shape(len(kinds(ends, kind)), *tiles[kind]) for kind in range(2)],
        ),
        in_specs=[ANY] * 9 + [VMEM] * 6 + [ANY] * 3,
        out_specs=[ANY] * 2 + [VMEM] * 7,
        scratch_shapes=backward_scratch()
        + [
            pltpu.VMEM((8, D), f32),
            pltpu.VMEM((experts, D), f32),
            pltpu.VMEM((pieces, D, D), bf16),
            pltpu.VMEM((groups, SEQ, D), bf16),
            pltpu.VMEM((3, SEQ, D), bf16),
            pltpu.SemaphoreType.DMA((3, 1)),
            pltpu.SemaphoreType.DMA((3, 1)),
            pltpu.VMEM((D, D), bf16),
            pltpu.VMEM((3, D, D), bf16),
            pltpu.SemaphoreType.DMA((3, 1)),
            pltpu.SemaphoreType.DMA((3, 1)),
            *[pltpu.VMEM(operand.shape, operand.dtype) for operand in whole],
            pltpu.SemaphoreType.DMA((len(whole),)),
            pltpu.SemaphoreType.DMA((2,)),
            pltpu.SemaphoreType.DMA,
            pltpu.SemaphoreType.DMA((len(late_grads),)),
        ]
        + [pltpu.VMEM(wholes[kind], bf16) for _, kind in late_grads]
        + scatter_scratch(SCATTER_LATE, outers, tiles)
        + scatter_scratch(SCATTER_SPLIT, outers, tiles, side=False)
        + [
            pltpu.VMEM((size, thin, D), bf16),
            pltpu.SemaphoreType.DMA((size - 1,)),
            pltpu.SemaphoreType.DMA((size - 1,)),
        ]
        + spread(size, 8, D)
        + spread(groups, 8, D)
        + spread(size, experts, D)
        + spread(groups, thin, D),
        compiler_params=params(collective_id=2, has_side_effects=True),
    )(*operands)


def local(
    layer_input,
    cotangent,
    norm_gain,
    norm_bias,
    w_qkv,
    w_proj,
    router,
    w_in,
    w_out,
    choices,
    top_count,
):
    groups = lax.axis_size("task")
    local_count = w_in.shape[0]
    image = layer_input.reshape(SEQ, D)
    grad_rows = cotangent.reshape(SEQ, D)
    routes = choices.reshape(SEQ, TOPMAX).T
    router_rows = router[0].T

    def swap(array):
        return lax.all_to_all(array, "task", split_axis=0, concat_axis=0, tiled=True)

    sending = groups == 4 and lax.axis_size("dp") == 8 and local_count == 4
    if sending:
        (
            mid,
            packed,
            mixed,
            logs,
            probs,
            normed,
            cot_rows,
            slots,
            gates,
            quarters,
            full_in,
            full_out,
        ) = forward_sending(
            top_count,
            image,
            grad_rows,
            norm_gain,
            norm_bias,
            (w_qkv, w_proj, w_in, w_out),
            router_rows,
            routes,
        )
        (
            late_in,
            late_out,
            grad_gates,
            mixes,
            grad_normed,
            early_in,
            early_out,
            parts_in,
            parts_out,
            _,
            _,
        ) = expert_sending(normed, cot_rows, slots, gates, full_in, full_out, w_in, w_out)
        (
            activations,
            grad_image,
            grad_gain,
            grad_bias,
            grad_router,
            grad_qkv,
            grad_proj,
            grad_in,
            grad_out,
        ) = backward_sending(
            parts_in,
            parts_out,
            image,
            grad_rows,
            mid,
            quarters,
            packed,
            mixed,
            grad_normed,
            norm_gain,
            norm_bias,
            router_rows,
            logs,
            grad_gates,
            probs,
            mixes,
            late_in,
            late_out,
        )
        grad_in = jnp.concatenate([early_in, grad_in], axis=0)
        grad_out = jnp.concatenate([early_out, grad_out], axis=0)
    else:
        full_qkv, full_proj, full_in, full_out = (
            lax.all_gather(w_qkv, "dp", axis=0, tiled=True),
            lax.all_gather(w_proj, "dp", axis=0, tiled=True),
            lax.all_gather(w_in, "dp", axis=1, tiled=True),
            lax.all_gather(w_out, "dp", axis=1, tiled=True),
        )
        mid, packed, mixed, logs, normed, slots, gates, probs = forward_part(
            top_count,
            image,
            norm_gain,
            norm_bias,
            full_qkv,
            full_proj,
            router_rows,
            routes,
        )
        normed = lax.all_gather(normed, "task")
        cot_rows = lax.all_gather(grad_rows.astype(bf16), "task")
        slots = swap(slots.reshape(groups, local_count, SEQ))
        gates = swap(gates.reshape(groups, local_count, SEQ))
        tokens = jnp.concatenate([normed, cot_rows], axis=-1)
        grad_in, grad_out, grad_gates, mixes, grad_normed = expert_part(
            tokens, slots, gates, full_in, full_out
        )
        activations, grad_image, grad_norm, grad_router, grad_shared = backward_part(
            image,
            grad_rows,
            norm_gain,
            norm_bias,
            mid,
            full_qkv,
            full_proj,
            router_rows,
            packed,
            mixed,
            logs,
            swap(mixes),
            swap(grad_normed),
            swap(grad_gates),
            probs,
        )
        grad_in = lax.psum_scatter(grad_in, "dp", scatter_dimension=1, tiled=True).astype(f32)
        grad_out = lax.psum_scatter(grad_out, "dp", scatter_dimension=1, tiled=True).astype(f32)
        grad_shared = lax.psum_scatter(grad_shared, "dp", scatter_dimension=0, tiled=True)
        grad_shared = lax.psum(grad_shared, "task").astype(f32)
        grad_qkv, grad_proj = grad_shared[:, : 3 * D], grad_shared[:, 3 * D :]
        grad_router = lax.psum(grad_router, "dp")
        grad_norm = lax.psum(grad_norm, ("task", "dp"))
        grad_gain, grad_bias = grad_norm[:2], grad_norm[2:]
    return (
        activations.reshape(layer_input.shape),
        grad_image.reshape(layer_input.shape),
        grad_gain,
        grad_bias,
        grad_qkv,
        grad_proj,
        grad_router.T[None],
        grad_in,
        grad_out,
    )


def solution(mesh):
    tokens = P("task", "dp", None, None)
    rows = P("dp", None)
    blocks = P("task", "dp", None)
    routed = P("task", None, None)
    return jax.shard_map(
        local,
        mesh=mesh,
        in_specs=(tokens, tokens, P(), P(), rows, rows, routed, blocks, blocks, tokens, P("task")),
        out_specs=(tokens, tokens, P(), P(), rows, rows, routed, blocks, blocks),
        check_vma=False,
    )
```
